32 devices in a mesh: grp: 2 (over core), dp: 16 (over z, y, x).
Axes of the slice: x: 2, y: 2, z: 4, core: 2. Of those that a mesh axis runs over, the one named last changes fastest.
Arguments:
- tokens: bfloat16 [32768, 768], P(('grp', 'dp')), may hold values from -6 to 6
- out_grad: bfloat16 [32768, 768], P(('grp', 'dp')), may hold values from -6 to 6
- image_counts: int32 [32, 32], P(('grp', 'dp')), may hold values from 0 to 98, as said below
- group_of_device: int32 [32], P(('grp', 'dp')), may hold values from 0 to 2, as said below
- group_weight: int32 [3], replicated, may hold values from 1 to 4
- norm1_gain: bfloat16 [768], replicated, may hold values from 0.5 to 1.5
- norm1_bias: bfloat16 [768], replicated, may hold values from -4 to 4
- qkv_weight: bfloat16 [768, 2304], replicated, may hold values from -0.21875 to 0.21875
- qkv_bias: bfloat16 [2304], replicated, may hold values from -4 to 4
- proj_weight: bfloat16 [768, 768], replicated, may hold values from -0.875 to 0.875
- proj_bias: bfloat16 [768], replicated, may hold values from -4 to 4
- norm2_gain: bfloat16 [768], replicated, may hold values from 0.5 to 1.5
- norm2_bias: bfloat16 [768], replicated, may hold values from -4 to 4
- fc1_weight: bfloat16 [768, 3072], replicated, may hold values from -0.21875 to 0.21875
- fc1_bias: bfloat16 [3072], replicated, may hold values from -4 to 4
- fc2_weight: bfloat16 [3072, 768], replicated, may hold values from -0.109375 to 0.109375
- fc2_bias: bfloat16 [768], replicated, may hold values from -4 to 4
- first_moment: float32 [16, 442992], P('dp'), may hold values from -2.5 to 2.5
- second_moment: float32 [16, 442992], P('dp'), may hold values from 1e-05 to 0.001
Outputs:
- block_out: bfloat16 [32768, 768], P(('grp', 'dp'))
- input_grad: bfloat16 [32768, 768], P(('grp', 'dp'))
- weight_grads: float32 [16, 442992], P('dp')
- new_weights: bfloat16 [16, 442992], replicated
- new_first: float32 [16, 442992], P('dp')
- new_second: float32 [16, 442992], P('dp')
- fc2_bias_grad: float32 [768], P('dp')
The draws below stay inside these ranges and needn't reach their ends.
Inputs may be any that keep to these rules, and one draw needn't show every extreme that they name: `group_of_device`: each of the 3 groups holds some devices: about a half, a third and a sixth of them. `image_counts`: in each device's row the live images come first, at least one, each with 30 to 98 visible patches, summing to at most 1024; the remaining slots are 0.
All inputs are finite; a program needn't handle non-finite values.
Results may differ from the reference program's by a relative error of at most 0.012.
Values may be sent and summed in bfloat16 or wider, within the bound.
No kernel may reach another device: no remote copies, remote signals or barrier semaphores. Data moves between devices by JAX's collectives and lax.ppermute only.
A program may use at most 320 MiB of HBM per device.

```python
import math
import jax
import jax.numpy as jnp
from jax import lax

D = 768
HEADS = 12
HEAD_DIM = 64
FF = 3072
TOK_DEV = 1024
IMG_SLOTS = 32
NGROUPS = 3
TOKENS = 32768
PARAM_ROW = 442992
N_GRP = 2
N_DP = 16


def draw_image_counts(key, part):
    device_count = N_GRP * N_DP
    raw_counts = jax.random.randint(key, (device_count, IMG_SLOTS), 30, 99, dtype=jnp.int32)
    raw_counts = raw_counts.at[0, 0].set(98).at[device_count - 1, 0].set(30)
    running = jnp.cumsum(raw_counts, axis=1)
    kept_counts = jnp.where(running <= TOK_DEV, raw_counts, 0)
    return kept_counts.at[0, IMG_SLOTS - 1].set(0).astype(jnp.int32)


def draw_group_of_device(key, part):
    device_count = N_GRP * N_DP
    ranking = jax.random.permutation(key, device_count).astype(jnp.int32)
    middle_group = jnp.where(6 * ranking < 5 * device_count, 1, 2)
    return jnp.where(6 * ranking < 3 * device_count, 0, middle_group).astype(jnp.int32)


def steps_of(stream_key, extent, split, low, largest):
    def one(dim, shards_of):
        steps = jax.random.uniform(jax.random.fold_in(jax.random.fold_in(stream_key, 6), dim), (shards_of,), jnp.float32, low / len(split), largest / len(split))
        return jnp.repeat(jnp.exp(steps), extent[dim] // shards_of).reshape((-1,) + (1,) * (len(extent) - dim - 1))

    factor_of = one(*split[0])
    for cut in split[1:]:
        factor_of = factor_of * one(*cut)
    return factor_of


def bell_draw(rng, extent, scale, limit, split=(), kind=jnp.bfloat16):
    factor_of = steps_of(rng, extent, split, -0.22, 0.18) if split else 1.0
    drawn = jax.random.normal(rng, extent, jnp.float32) * scale * factor_of
    return jnp.minimum(jnp.maximum(drawn, -limit), limit).astype(kind)


def setup_inputs(seed: int = 0) -> dict:
    splits = jax.random.split(jax.random.key(seed), 20)
    tokens = bell_draw(splits[0], (TOKENS, D), 1.0, 6.0, ((0, 32),))
    out_grad = bell_draw(splits[1], (TOKENS, D), 1.0, 6.0, ((0, 32),))
    image_counts = draw_image_counts(jax.random.fold_in(splits[19], 71), 0)
    group_of_device = draw_group_of_device(jax.random.fold_in(splits[19], 71), 0)
    group_weight = jax.random.randint(splits[4], (NGROUPS,), 1, 5).astype(jnp.int32)
    norm1_gain = jnp.clip(1.0 + 0.1 * jax.random.normal(splits[5], (D,), jnp.float32), 0.5, 1.5).astype(jnp.bfloat16)
    norm1_bias = bell_draw(splits[6], (D,), 0.3, 4.0)
    qkv_weight = bell_draw(splits[7], (D, 3 * D), D ** -0.5, 0.21875)
    qkv_bias = bell_draw(splits[8], (3 * D,), 0.3, 4.0)
    proj_weight = bell_draw(splits[9], (D, D), (D // 16) ** -0.5, 0.875)
    proj_bias = bell_draw(splits[10], (D,), 0.3, 4.0)
    norm2_gain = jnp.clip(1.0 + 0.1 * jax.random.normal(splits[11], (D,), jnp.float32), 0.5, 1.5).astype(jnp.bfloat16)
    norm2_bias = bell_draw(splits[12], (D,), 0.3, 4.0)
    fc1_weight = bell_draw(splits[13], (D, FF), D ** -0.5, 0.21875)
    fc1_bias = bell_draw(splits[14], (FF,), 0.3, 4.0)
    fc2_weight = bell_draw(splits[15], (FF, D), FF ** -0.5, 0.109375)
    fc2_bias = bell_draw(splits[16], (D,), 0.3, 4.0)
    first_moment = bell_draw(splits[17], (N_DP, PARAM_ROW), 0.4, 2.5, ((0, 16),), jnp.float32)
    second_moment = jnp.clip(jnp.exp(math.log(0.001) - 4.6051703 * jax.random.uniform(splits[18], (N_DP, PARAM_ROW), jnp.float32) ** steps_of(splits[18], (N_DP, PARAM_ROW), ((0, 16),), -0.2, 0.2)), 9.999999747378752e-06, 0.001)
    return dict(tokens=tokens, out_grad=out_grad, image_counts=image_counts, group_of_device=group_of_device, group_weight=group_weight, norm1_gain=norm1_gain, norm1_bias=norm1_bias, qkv_weight=qkv_weight, qkv_bias=qkv_bias, proj_weight=proj_weight, proj_bias=proj_bias, norm2_gain=norm2_gain, norm2_bias=norm2_bias, fc1_weight=fc1_weight, fc1_bias=fc1_bias, fc2_weight=fc2_weight, fc2_bias=fc2_bias, first_moment=first_moment, second_moment=second_moment)


@jax.custom_vjp
def low(v):
    return lax.optimization_barrier(v.astype(jnp.bfloat16)).astype(jnp.float32)

@jax.custom_vjp
def low_back(v):
    return v

def low_keep(v):
    return (low(v), None)

def low_pass(kept, grad):
    return (grad,)

def back_keep(v):
    return (v, None)

def back_low(kept, grad):
    return (low(grad),)
low.defvjp(low_keep, low_pass)
low_back.defvjp(back_keep, back_low)
beta_one = 0.9
beta_two = 0.999
adam_eps = 1e-08
decay_rate = 0.05
step_count = 10.0
learn_rate = 0.004 * 0.75 ** 1
norm_eps = 1e-06
neg_fill = -1e+30
decay_flags = (0.0, 0.0, 1.0, 0.0, 1.0, 0.0, 0.0, 0.0, 1.0, 0.0, 1.0, 0.0)

def layer_norm(values, gain, shift):
    center = values - lax.optimization_barrier(jnp.mean(values, axis=-1, keepdims=True))
    spread = lax.optimization_barrier(jnp.mean(center * center, axis=-1, keepdims=True))
    return center * lax.rsqrt(spread + norm_eps) * gain + shift

def gelu_tanh(values):
    return jax.nn.gelu(values, approximate=True)

def matmul(first_op, second_op):
    return jnp.dot(first_op, second_op, precision=lax.Precision.HIGHEST, preferred_element_type=jnp.float32)

def segment_info(counts_row, length):
    segment_ends = jnp.cumsum(counts_row)
    position = lax.iota(jnp.int32, length)
    segment = lax.optimization_barrier(jnp.sum((position[:, None] >= segment_ends[None, :]).astype(jnp.int32), axis=1))
    return (segment, position < segment_ends[-1])

def adam_step(current, grads, first, second, decay):
    first_new = beta_one * first + (1.0 - beta_one) * grads
    second_new = beta_two * second + (1.0 - beta_two) * grads * grads
    ratio = first_new / (1.0 - beta_one ** step_count) / (jnp.sqrt(second_new / (1.0 - beta_two ** step_count)) + adam_eps)
    updated = current - learn_rate * (ratio + decay_rate * decay * current)
    return (updated.astype(jnp.bfloat16), first_new, second_new)

def forward(inputs, same_segment, params):
    gain_one, shift_one, qkv_weight, qkv_bias, proj_weight, proj_bias, gain_two, shift_two, fc1_weight, fc1_bias, fc2_weight, fc2_bias = params
    length = inputs.shape[0]
    block_rows = min(512, length)
    blocks = length // block_rows
    normed_one = low(layer_norm(inputs, gain_one, shift_one))
    projected = low(low_back(matmul(normed_one, qkv_weight) + qkv_bias))
    query_rows = projected[:, :D].reshape(blocks, block_rows, HEADS, HEAD_DIM)
    key_rows = projected[:, D:2 * D].reshape(length, HEADS, HEAD_DIM)
    value_rows = projected[:, 2 * D:].reshape(length, HEADS, HEAD_DIM)
    masks = same_segment.reshape(blocks, block_rows, length)

    def attend(pieces):
        query_part, mask_part = pieces
        raw = jnp.einsum('qhd,khd->hqk', query_part, key_rows, precision=lax.Precision.HIGHEST) * 0.125
        scores = jnp.where(mask_part[None], low_back(raw), neg_fill)
        row_max = lax.optimization_barrier(jnp.max(scores, axis=-1, keepdims=True))
        exponent = jnp.exp(scores - row_max)
        attn_probs = exponent / lax.optimization_barrier(jnp.sum(exponent, axis=-1, keepdims=True))
        return jnp.einsum('hqk,khd->qhd', low(attn_probs), value_rows, precision=lax.Precision.HIGHEST)
    context = lax.map(jax.checkpoint(attend), (query_rows, masks)).reshape(length, D)
    context = low(low_back(context))
    middle = inputs + low_back(matmul(context, proj_weight) + proj_bias)
    normed_two = low(layer_norm(middle, gain_two, shift_two))
    hidden = low_back(matmul(normed_two, fc1_weight) + fc1_bias)
    activated = low(gelu_tanh(hidden))
    return middle + matmul(activated, fc2_weight) + fc2_bias

def reference(tokens, out_grad, image_counts, group_of_device, group_weight, norm1_gain, norm1_bias, qkv_weight, qkv_bias, proj_weight, proj_bias, norm2_gain, norm2_bias, fc1_weight, fc1_bias, fc2_weight, fc2_bias, first_moment, second_moment):
    weight_list = (norm1_gain, norm1_bias, qkv_weight, qkv_bias, proj_weight, proj_bias, norm2_gain, norm2_bias, fc1_weight, fc1_bias, fc2_weight, fc2_bias)
    params = tuple((item.astype(jnp.float32) for item in weight_list))
    device_count = N_GRP * N_DP
    images = lax.optimization_barrier(jnp.sum((image_counts > 0).astype(jnp.int32), axis=1))
    member = (group_of_device[:, None] == jnp.arange(NGROUPS, dtype=jnp.int32)[None, :]).astype(jnp.int32)
    totals = lax.optimization_barrier(jnp.sum(member * images[:, None], axis=0))
    shares = lax.optimization_barrier(jnp.sum(member * group_weight[None, :], axis=1)).astype(jnp.float32)
    own_totals = lax.optimization_barrier(jnp.sum(member * totals[None, :], axis=1)).astype(jnp.float32)
    factors = shares / own_totals

    def one_device(carry, pieces):
        token_part, grad_part, count_part, factor = pieces
        segment, valid_rows = segment_info(count_part, TOK_DEV)
        same_segment = segment[:, None] == segment[None, :]
        inputs = token_part.astype(jnp.float32)
        result, backward = jax.vjp(lambda values, weights_in: forward(values, same_segment, weights_in), inputs, params)
        cotangent = grad_part.astype(jnp.float32) * valid_rows[:, None].astype(jnp.float32)
        input_part, param_grads = backward(cotangent)
        carry = tuple((total + factor * item for total, item in zip(carry, param_grads)))
        return (carry, (result.astype(jnp.bfloat16), input_part.astype(jnp.bfloat16)))
    start_sums = tuple((jnp.zeros(item.shape, jnp.float32) for item in weight_list))
    summed, (block_rows_out, input_rows) = lax.scan(one_device, start_sums, (tokens.reshape(device_count, TOK_DEV, D), out_grad.reshape(device_count, TOK_DEV, D), image_counts, factors))
    weight_grads = jnp.concatenate([item.reshape(N_DP, -1) for item in summed], axis=1)
    current = jnp.concatenate([item.reshape(N_DP, -1) for item in params], axis=1)
    decay = jnp.concatenate([jnp.full((1, item.size // N_DP), flag, jnp.float32) for item, flag in zip(weight_list, decay_flags)], axis=1)
    new_weights, new_first, new_second = adam_step(current, weight_grads, first_moment, second_moment, decay)
    block_out = block_rows_out.reshape(TOKENS, D)
    input_grad = input_rows.reshape(TOKENS, D)
    fc2_bias_grad = summed[11]
    return (block_out, input_grad, weight_grads, new_weights, new_first, new_second, fc2_bias_grad)
```

```python
import jax
import jax.numpy as jnp
from jax import lax
from jax.sharding import PartitionSpec as P

D = 768
HEADS = 12
HEAD_DIM = 64
NGROUPS = 3


beta_one = 0.9
beta_two = 0.999
adam_eps = 1e-08
decay_rate = 0.05
step_count = 10.0
learn_rate = 0.004 * 0.75**1
norm_eps = 1e-06
neg_fill = -1e30
decay_flags = (0.0, 0.0, 1.0, 0.0, 1.0, 0.0, 0.0, 0.0, 1.0, 0.0, 1.0, 0.0)


def layer_norm(values, gain, shift):
    center = values - jnp.mean(values, axis=-1, keepdims=True)
    spread = jnp.mean(center * center, axis=-1, keepdims=True)
    return center * lax.rsqrt(spread + norm_eps) * gain + shift


def gelu_tanh(values):
    return jax.nn.gelu(values, approximate=True)


def contract_rows(first_op, second_op):
    return lax.dot_general(
        first_op, second_op, (((0,), (0,)), ((), ())), preferred_element_type=jnp.float32
    )


def contract_cols(first_op, second_op):
    return lax.dot_general(
        first_op, second_op, (((1,), (1,)), ((), ())), preferred_element_type=jnp.float32
    )


def segment_info(counts_row, length):
    slots = lax.iota(jnp.int32, counts_row.shape[0])
    segment_ends = jnp.sum(
        jnp.where(slots[:, None] <= slots[None, :], counts_row[:, None], 0), axis=0
    )
    position = lax.iota(jnp.int32, length)
    segment = jnp.sum((position[:, None] >= segment_ends[None, :]).astype(jnp.int32), axis=1)
    return (segment, position < segment_ends[-1])


def score_block(query_part, key_rows, same_segment):
    raw = (
        jnp.einsum("qhd,khd->hqk", query_part, key_rows, preferred_element_type=jnp.float32) * 0.125
    )
    return jnp.where(same_segment[None], raw, neg_fill)


def on_device(
    tokens,
    out_grad,
    image_counts,
    group_of_device,
    group_weight,
    norm1_gain,
    norm1_bias,
    qkv_weight,
    qkv_bias,
    proj_weight,
    proj_bias,
    norm2_gain,
    norm2_bias,
    fc1_weight,
    fc1_bias,
    fc2_weight,
    fc2_bias,
    first_moment,
    second_moment,
):
    length = tokens.shape[0]
    segment, valid_rows = segment_info(image_counts[0], length)
    images = jnp.sum((image_counts[0] > 0).astype(jnp.int32))
    member = (group_of_device[0] == lax.iota(jnp.int32, NGROUPS)).astype(jnp.int32)
    totals = lax.psum(member * images, ("grp", "dp"))
    factor = jnp.sum(member * group_weight).astype(jnp.float32) / jnp.sum(member * totals).astype(
        jnp.float32
    )
    inputs = tokens.astype(jnp.float32)
    normed_one, norm_one_back = jax.vjp(
        layer_norm, inputs, norm1_gain.astype(jnp.float32), norm1_bias.astype(jnp.float32)
    )
    normed_one_low = normed_one.astype(jnp.bfloat16)
    projected = (
        jnp.dot(normed_one_low, qkv_weight, preferred_element_type=jnp.float32)
        + qkv_bias.astype(jnp.float32)
    ).astype(jnp.bfloat16)
    query_rows = projected[:, :D].reshape(length, HEADS, HEAD_DIM)
    key_rows = projected[:, D : 2 * D].reshape(length, HEADS, HEAD_DIM)
    value_rows = projected[:, 2 * D :].reshape(length, HEADS, HEAD_DIM)
    block_rows = min(512, length)
    offsets = list(range(0, length, block_rows))
    context_parts = []
    log_sums = []
    for offset in offsets:
        same_segment = segment[offset : offset + block_rows, None] == segment[None, :]
        scores = score_block(query_rows[offset : offset + block_rows], key_rows, same_segment)
        row_max = jnp.max(scores, axis=-1, keepdims=True)
        exponent = jnp.exp(scores - row_max)
        row_sum = jnp.sum(exponent, axis=-1, keepdims=True)
        attn_probs = exponent / row_sum
        log_sums.append(row_max + jnp.log(row_sum))
        context_parts.append(
            jnp.einsum(
                "hqk,khd->qhd",
                attn_probs.astype(jnp.bfloat16),
                value_rows,
                preferred_element_type=jnp.float32,
            )
        )
    context = jnp.concatenate(context_parts, axis=0).reshape(length, D).astype(jnp.bfloat16)
    middle = inputs + (
        jnp.dot(context, proj_weight, preferred_element_type=jnp.float32)
        + proj_bias.astype(jnp.float32)
    )
    normed_two, norm_two_back = jax.vjp(
        layer_norm, middle, norm2_gain.astype(jnp.float32), norm2_bias.astype(jnp.float32)
    )
    normed_two_low = normed_two.astype(jnp.bfloat16)
    hidden = jnp.dot(
        normed_two_low, fc1_weight, preferred_element_type=jnp.float32
    ) + fc1_bias.astype(jnp.float32)
    activated, gelu_back = jax.vjp(gelu_tanh, hidden)
    activated_low = activated.astype(jnp.bfloat16)
    block_out = (
        middle
        + (
            jnp.dot(activated_low, fc2_weight, preferred_element_type=jnp.float32)
            + fc2_bias.astype(jnp.float32)
        )
    ).astype(jnp.bfloat16)
    grad_out = out_grad.astype(jnp.float32) * valid_rows[:, None].astype(jnp.float32)
    grad_out_low = grad_out.astype(jnp.bfloat16)
    fc2_grad = contract_rows(activated_low, grad_out_low)
    fc2_bias_grad = jnp.sum(grad_out, axis=0)
    grad_hidden = gelu_back(contract_cols(grad_out_low, fc2_weight))[0].astype(jnp.bfloat16)
    fc1_grad = contract_rows(normed_two_low, grad_hidden)
    fc1_bias_grad = jnp.sum(grad_hidden.astype(jnp.float32), axis=0)
    grad_middle_norm, gain_two_grad, shift_two_grad = norm_two_back(
        contract_cols(grad_hidden, fc1_weight)
    )
    grad_middle = grad_out + grad_middle_norm
    grad_branch = grad_middle.astype(jnp.bfloat16)
    proj_grad = contract_rows(context, grad_branch)
    proj_bias_grad = jnp.sum(grad_branch.astype(jnp.float32), axis=0)
    grad_context = (
        contract_cols(grad_branch, proj_weight)
        .astype(jnp.bfloat16)
        .reshape(length, HEADS, HEAD_DIM)
    )
    grad_keys = jnp.zeros((length, HEADS, HEAD_DIM), jnp.float32)
    grad_values = jnp.zeros((length, HEADS, HEAD_DIM), jnp.float32)
    query_grads = []
    for piece_index, offset in enumerate(offsets):
        query_part = query_rows[offset : offset + block_rows]
        context_grad_part = grad_context[offset : offset + block_rows]
        same_segment = segment[offset : offset + block_rows, None] == segment[None, :]
        attn_probs = jnp.exp(
            score_block(query_part, key_rows, same_segment) - log_sums[piece_index]
        )
        grad_probs = jnp.einsum(
            "qhd,khd->hqk", context_grad_part, value_rows, preferred_element_type=jnp.float32
        )
        grad_scores = (
            attn_probs * (grad_probs - jnp.sum(attn_probs * grad_probs, axis=-1, keepdims=True))
        ).astype(jnp.bfloat16)
        query_grads.append(
            jnp.einsum("hqk,khd->qhd", grad_scores, key_rows, preferred_element_type=jnp.float32)
            * 0.125
        )
        grad_keys = (
            grad_keys
            + jnp.einsum(
                "hqk,qhd->khd", grad_scores, query_part, preferred_element_type=jnp.float32
            )
            * 0.125
        )
        grad_values = grad_values + jnp.einsum(
            "hqk,qhd->khd",
            attn_probs.astype(jnp.bfloat16),
            context_grad_part,
            preferred_element_type=jnp.float32,
        )
    grad_projected = jnp.concatenate(
        [
            jnp.concatenate(query_grads, axis=0).reshape(length, D),
            grad_keys.reshape(length, D),
            grad_values.reshape(length, D),
        ],
        axis=1,
    ).astype(jnp.bfloat16)
    qkv_grad = contract_rows(normed_one_low, grad_projected)
    qkv_bias_grad = jnp.sum(grad_projected.astype(jnp.float32), axis=0)
    grad_input_norm, gain_one_grad, shift_one_grad = norm_one_back(
        contract_cols(grad_projected, qkv_weight)
    )
    input_grad = (grad_middle + grad_input_norm).astype(jnp.bfloat16)
    moments = (first_moment, second_moment)
    mlp_summed, rest_summed = exchange_grads(
        (gain_one_grad, shift_one_grad, qkv_grad, qkv_bias_grad, proj_grad, proj_bias_grad),
        (gain_two_grad, shift_two_grad, fc1_grad, fc1_bias_grad, fc2_grad, fc2_bias_grad),
        factor,
    )
    row_count = lax.axis_size("dp")
    own_index = lax.axis_index("dp")
    weight_list = (
        norm1_gain,
        norm1_bias,
        qkv_weight,
        qkv_bias,
        proj_weight,
        proj_bias,
        norm2_gain,
        norm2_bias,
        fc1_weight,
        fc1_bias,
        fc2_weight,
        fc2_bias,
    )
    own_weights = [
        lax.dynamic_slice_in_dim(item.reshape(row_count, -1), own_index, 1, 0)[0]
        for item in weight_list
    ]
    rows = D // row_count
    fc1_sum = mlp_summed[0].reshape(4, rows, D).transpose(1, 0, 2).reshape(-1)
    fc2_sum = mlp_summed[1].reshape(-1)
    qkv_sum = jnp.concatenate(
        [rest_summed[0, :rows], rest_summed[0, rows : 2 * rows], rest_summed[1, :rows]], axis=1
    ).reshape(-1)
    proj_sum = rest_summed[1, rows : 2 * rows].reshape(-1)
    small = rest_summed[0, 2 * rows]
    widths = [item.size // row_count for item in weight_list]
    small_parts = {}
    start = 0
    for index, flag in enumerate(decay_flags):
        if flag == 0.0:
            small_parts[index] = small[start : start + widths[index]]
            start += widths[index]
    large_parts = {2: qkv_sum, 4: proj_sum, 8: fc1_sum, 10: fc2_sum}
    pieces = [
        small_parts[index] if index in small_parts else large_parts[index] for index in range(12)
    ]
    split = sum(widths[:8])
    grads_out, first_out, second_out, fresh = [], [], [], []
    for lead, tail, begin, end in ((8, 12, split, sum(widths)), (0, 8, 0, split)):
        summed_part = jnp.concatenate(pieces[lead:tail])
        current = jnp.concatenate(own_weights[lead:tail]).astype(jnp.float32)
        decay = jnp.concatenate(
            [
                jnp.full((width,), flag, jnp.float32)
                for width, flag in zip(widths[lead:tail], decay_flags[lead:tail])
            ]
        )
        new_first = beta_one * moments[0][0, begin:end] + (1.0 - beta_one) * summed_part
        new_second = (
            beta_two * moments[1][0, begin:end] + (1.0 - beta_two) * summed_part * summed_part
        )
        ratio = (
            new_first
            / (1.0 - beta_one**step_count)
            / (jnp.sqrt(new_second / (1.0 - beta_two**step_count)) + adam_eps)
        )
        fresh_low = (current - learn_rate * (ratio + decay_rate * decay * current)).astype(
            jnp.bfloat16
        )
        grads_out.insert(0, summed_part)
        first_out.insert(0, new_first)
        second_out.insert(0, new_second)
        fresh.insert(0, gather_rows(fresh_low))
    summed = jnp.concatenate(grads_out)[None]
    new_first = jnp.concatenate(first_out)[None]
    new_second = jnp.concatenate(second_out)[None]
    new_weights = jnp.concatenate(fresh, axis=1)
    summed_bias = pieces[11]
    return (block_out, input_grad, summed, new_weights, new_first, new_second, summed_bias)


AXES = ("grp", "dp")


def swap(values, bit):
    count = lax.axis_size("grp") * lax.axis_size("dp")
    return lax.ppermute(values, AXES, [(i, i ^ bit) for i in range(count)])


def bit_of(position):
    return (lax.axis_index("dp") >> position) & 1


def add_low(kept, came):
    return (kept.astype(jnp.float32) + came.astype(jnp.float32)).astype(jnp.bfloat16)


def halve(values, position, positions):
    axis = positions.index(position)
    own = bit_of(position)
    sent = lax.dynamic_index_in_dim(values, 1 - own, axis, keepdims=False)
    kept = lax.dynamic_index_in_dim(values, own, axis, keepdims=False)
    return kept, swap(sent, 1 << position), [p for p in positions if p != position]


def reduce_rows(values):
    count = lax.axis_size("dp")
    grp = lax.axis_index("grp")
    kept = lax.dynamic_index_in_dim(values, grp, 0, keepdims=False)
    came = swap(lax.dynamic_index_in_dim(values, 1 - grp, 0, keepdims=False), count)
    kept = add_low(kept, came)
    depth = count.bit_length() - 1
    positions = list(range(depth))[::-1]
    rows = kept.shape[1]
    parts = [kept[:, : rows // 2], kept[:, rows // 2 :]]
    left = [positions, positions]
    parts = [part.reshape((2,) * depth + part.shape[1:]) for part in parts]
    for order in ((0, 1), (1, 0)):
        for index in (0, 1):
            part, came, left[index] = halve(parts[index], order[index], left[index])
            parts[index] = add_low(part, came)
    whole = jnp.concatenate(parts, axis=depth - 2)
    rest = left[0]
    for position in range(2, depth):
        part, came, rest = halve(whole, position, rest)
        if rest:
            whole = add_low(part, came)
        else:
            whole = part.astype(jnp.float32) + came.astype(jnp.float32)
    other = swap(whole, count)
    return jnp.where(grp == 0, jnp.stack([whole, other]), jnp.stack([other, whole]))


def join(own, came, bit):
    return jnp.where(bit == 0, jnp.stack([own, came]), jnp.stack([came, own]))


def gather_rows(values):
    count = lax.axis_size("dp")
    depth = count.bit_length() - 1
    grp = lax.axis_index("grp")
    width = values.shape[0]
    padded = -(-width // 4096) * 4096
    halves = jnp.pad(values, (0, padded - width)).reshape(2, 2, padded // 512, 128)
    own = lax.dynamic_index_in_dim(halves, grp, 0, keepdims=False)
    for position in range(2, depth)[::-1]:
        own = join(own, swap(own, 1 << position), bit_of(position))
    lead = own.ndim - 3
    parts = [lax.index_in_dim(own, i, lead, keepdims=False) for i in (0, 1)]
    for order in ((1, 0), (0, 1)):
        for index in (0, 1):
            position = order[index]
            parts[index] = join(
                parts[index], swap(parts[index], 1 << position), bit_of(position)
            )
    parts[1] = jnp.swapaxes(parts[1], 0, 1)
    full = jnp.stack(parts, axis=depth)
    full = full.transpose(tuple(range(depth))[::-1] + tuple(range(depth, full.ndim)))
    full = full.reshape((count,) + full.shape[depth:])
    other = swap(full, count)
    whole = jnp.where(
        grp == 0, jnp.stack([full, other], axis=1), jnp.stack([other, full], axis=1)
    )
    return whole.reshape(count, padded)[:, :width]


def exchange_grads(front, back, factor):
    gain_one, shift_one, qkv, qkv_bias, proj, proj_bias = front
    gain_two, shift_two, fc1, fc1_bias, fc2, fc2_bias = back
    count = lax.axis_size("dp")
    rows = D // count
    fc1_blocks = fc1.reshape(count, rows, 4, D).transpose(0, 2, 1, 3).reshape(count, 4 * rows, D)
    fc2_blocks = fc2.reshape(count, 4 * rows, D)
    mlp = (jnp.stack([fc1_blocks, fc2_blocks]) * factor).astype(jnp.bfloat16)
    small = jnp.concatenate(
        [
            item.reshape(count, -1)
            for item in (
                gain_one,
                shift_one,
                qkv_bias,
                proj_bias,
                gain_two,
                shift_two,
                fc1_bias,
                fc2_bias,
            )
        ],
        axis=1,
    )
    small = jnp.pad(small, ((0, 0), (0, D - small.shape[1])))[:, None]
    small = jnp.pad(small, ((0, 0), (0, 7), (0, 0)))
    qkv_blocks = qkv.reshape(count, rows, 3, D)
    first_half = jnp.concatenate([qkv_blocks[:, :, 0], qkv_blocks[:, :, 1], small], axis=1)
    second_half = jnp.concatenate(
        [qkv_blocks[:, :, 2], proj.reshape(count, rows, D), jnp.zeros_like(small)], axis=1
    )
    rest = (jnp.stack([first_half, second_half]) * factor).astype(jnp.bfloat16)
    return reduce_rows(mlp), reduce_rows(rest)


def solution(mesh):
    in_specs = (
        P(("grp", "dp"), None),
        P(("grp", "dp"), None),
        P(("grp", "dp"), None),
        P(("grp", "dp")),
        P(),
        P(),
        P(),
        P(),
        P(),
        P(),
        P(),
        P(),
        P(),
        P(),
        P(),
        P(),
        P(),
        P("dp", None),
        P("dp", None),
    )
    out_specs = (
        P(("grp", "dp"), None),
        P(("grp", "dp"), None),
        P("dp", None),
        P(),
        P("dp", None),
        P("dp", None),
        P("dp"),
    )
    return jax.shard_map(
        on_device, mesh=mesh, in_specs=in_specs, out_specs=out_specs, check_vma=False
    )
```

```python
import jax
import jax.numpy as jnp
from jax import lax
from jax.experimental import pallas as pl
from jax.experimental.pallas import tpu as pltpu
from jax.sharding import PartitionSpec as P

D = 768
HEADS = 12
HEAD_DIM = 64
NGROUPS = 3


beta_one = 0.9
beta_two = 0.999
adam_eps = 1e-08
decay_rate = 0.05
step_count = 10.0
learn_rate = 0.004 * 0.75**1
norm_eps = 1e-06
neg_fill = -1e30
decay_flags = (0.0, 0.0, 1.0, 0.0, 1.0, 0.0, 0.0, 0.0, 1.0, 0.0, 1.0, 0.0)


def layer_norm(values, gain, shift):
    center = values - jnp.mean(values, axis=-1, keepdims=True)
    spread = jnp.mean(center * center, axis=-1, keepdims=True)
    return center * lax.rsqrt(spread + norm_eps) * gain + shift


def gelu_tanh(values):
    return jax.nn.gelu(values, approximate=True)


def contract_rows(first_op, second_op):
    return lax.dot_general(
        first_op, second_op, (((0,), (0,)), ((), ())), preferred_element_type=jnp.float32
    )


def contract_cols(first_op, second_op):
    return lax.dot_general(
        first_op, second_op, (((1,), (1,)), ((), ())), preferred_element_type=jnp.float32
    )


def segment_info(counts_row, length):
    slots = lax.iota(jnp.int32, counts_row.shape[0])
    segment_ends = jnp.sum(
        jnp.where(slots[:, None] <= slots[None, :], counts_row[:, None], 0), axis=0
    )
    position = lax.iota(jnp.int32, length)
    segment = jnp.sum((position[:, None] >= segment_ends[None, :]).astype(jnp.int32), axis=1)
    return (segment, position < segment_ends[-1])


TILE = 128
WINDOW = 3 * TILE


def window_start(tile, tiles):
    return min(max(tile - 1, 0), tiles - 3) * TILE


def dot_nt(first, second):
    return lax.dot_general(first, second, (((1,), (1,)), ((), ())), preferred_element_type=jnp.float32)


def dot_tn(first, second):
    return lax.dot_general(first, second, (((0,), (0,)), ((), ())), preferred_element_type=jnp.float32)


def dot_nn(first, second):
    return jnp.dot(first, second, preferred_element_type=jnp.float32)


def stack_heads(block, low):
    zero = jnp.zeros_like(block)
    return jnp.concatenate([jnp.where(low, block, zero), jnp.where(low, zero, block)], axis=0)


def merge_heads(block, low):
    return jnp.where(low, block[:TILE], block[TILE:])


def fill_masks(bias_ref, seg_col_ref, seg_row_ref, tiles):
    for tile in range(tiles):
        start = window_start(tile, tiles)
        same = (
            seg_col_ref[tile * TILE : (tile + 1) * TILE, :]
            == seg_row_ref[:, start : start + WINDOW]
        )
        bias_ref[tile] = jnp.where(same, 0.0, neg_fill)


def soft_probs(scores):
    row_max = jnp.max(scores, axis=1, keepdims=True)
    exponent = jnp.exp(scores - row_max)
    return exponent * (1.0 / jnp.sum(exponent, axis=1, keepdims=True))


def attn_forward_kernel(
    pad_ref, query_ref, key_ref, value_ref, seg_col_ref, seg_row_ref, out_ref, bias_ref
):
    length = query_ref.shape[0]
    tiles = length // TILE

    @pl.when(pl.program_id(0) == 0)
    def _():
        fill_masks(bias_ref, seg_col_ref, seg_row_ref, tiles)

    low = lax.broadcasted_iota(jnp.int32, (TILE, 128), 1) < 64
    scale = jnp.asarray(0.125, jnp.bfloat16)

    for tile in range(tiles):
        start = window_start(tile, tiles)
        queries = stack_heads(query_ref[tile * TILE : (tile + 1) * TILE, :] * scale, low)
        bias = bias_ref[tile]
        scores = dot_nt(queries, key_ref[start : start + WINDOW, :]) + jnp.concatenate(
            [bias, bias], axis=0
        )
        probs = soft_probs(scores).astype(jnp.bfloat16)
        mixed = dot_nn(probs, value_ref[start : start + WINDOW, :])
        out_ref[tile * TILE : (tile + 1) * TILE, :] = merge_heads(mixed, low).astype(jnp.bfloat16)

    @pl.loop(0, tiles)
    def _(tile):
        start = jnp.minimum(jnp.maximum(tile - 1, 0), tiles - 3) * TILE
        padding = (tile + 1) * TILE > pad_ref[0]
        outside = (pad_ref[0] < start) | (start + WINDOW < length)

        @pl.when(padding & outside)
        def _():
            rows = pl.ds(pl.multiple_of(tile * TILE, TILE), TILE)
            queries = stack_heads(query_ref[rows, :] * scale, low)
            same = seg_col_ref[rows, :] == seg_row_ref[...]
            bias = jnp.where(same, 0.0, neg_fill)
            scores = dot_nt(queries, key_ref[...]) + jnp.concatenate([bias, bias], axis=0)
            probs = soft_probs(scores).astype(jnp.bfloat16)
            out_ref[rows, :] = merge_heads(dot_nn(probs, value_ref[...]), low).astype(jnp.bfloat16)


def attn_forward(projected, seg_col, seg_row, pad_start):
    length, width = projected.shape
    pairs = width // 3 // 128
    tiles = length // TILE

    def part(offset):
        return pl.BlockSpec((length, 128), lambda pair, pad: (0, offset * pairs + pair))

    return pl.pallas_call(
        attn_forward_kernel,
        out_shape=jax.ShapeDtypeStruct((length, width // 3), jnp.bfloat16),
        grid_spec=pltpu.PrefetchScalarGridSpec(
            num_scalar_prefetch=1,
            grid=(pairs,),
            in_specs=[
                part(0),
                part(1),
                part(2),
                pl.BlockSpec((length, 1), lambda pair, pad: (0, 0)),
                pl.BlockSpec((1, length), lambda pair, pad: (0, 0)),
            ],
            out_specs=pl.BlockSpec((length, 128), lambda pair, pad: (0, pair)),
            scratch_shapes=[pltpu.VMEM((tiles, TILE, WINDOW), jnp.float32)],
        ),
        compiler_params=pltpu.CompilerParams(vmem_limit_bytes=40 * 2**20),
        cost_estimate=pl.CostEstimate(
            flops=4 * length * WINDOW * width // 3,
            bytes_accessed=8 * length * width // 3,
            transcendentals=length * WINDOW * 12,
        ),
        name="attn_forward",
    )(pad_start, projected, projected, projected, seg_col, seg_row)


def attn_backward_kernel(
    query_ref, key_ref, value_ref, grad_ref, seg_col_ref, seg_row_ref,
    query_out, key_out, value_out, bias_ref, key_sum, value_sum,
):
    length = query_ref.shape[0]
    tiles = length // TILE

    @pl.when(pl.program_id(0) == 0)
    def _():
        fill_masks(bias_ref, seg_col_ref, seg_row_ref, tiles)

    low = lax.broadcasted_iota(jnp.int32, (TILE, 128), 1) < 64
    scale = jnp.asarray(0.125, jnp.bfloat16)
    key_sum[...] = jnp.zeros_like(key_sum)
    value_sum[...] = jnp.zeros_like(value_sum)

    for tile in range(tiles):
        start = window_start(tile, tiles)
        rows = slice(tile * TILE, (tile + 1) * TILE)
        span = slice(start, start + WINDOW)
        queries = stack_heads(query_ref[rows, :] * scale, low)
        grads = stack_heads(grad_ref[rows, :], low)
        bias = bias_ref[tile]
        keys = key_ref[span, :]
        scores = dot_nt(queries, keys) + jnp.concatenate([bias, bias], axis=0)
        probs = soft_probs(scores)
        grad_probs = dot_nt(grads, value_ref[span, :])
        delta = jnp.sum(probs * grad_probs, axis=1, keepdims=True)
        grad_scores = (probs * (grad_probs - delta)).astype(jnp.bfloat16)
        query_out[rows, :] = (merge_heads(dot_nn(grad_scores, keys), low) * 0.125).astype(
            jnp.bfloat16
        )
        key_sum[span, :] += dot_tn(grad_scores, queries)
        value_sum[span, :] += dot_tn(probs.astype(jnp.bfloat16), grads)
    key_out[...] = key_sum[...].astype(jnp.bfloat16)
    value_out[...] = value_sum[...].astype(jnp.bfloat16)


def attn_backward(projected, grad_context, seg_col, seg_row):
    length, width = projected.shape
    pairs = width // 3 // 128
    tiles = length // TILE

    def part(offset):
        return pl.BlockSpec((length, 128), lambda pair: (0, offset * pairs + pair))

    return pl.pallas_call(
        attn_backward_kernel,
        out_shape=[jax.ShapeDtypeStruct((length, width // 3), jnp.bfloat16)] * 3,
        grid_spec=pltpu.PrefetchScalarGridSpec(
            num_scalar_prefetch=0,
            grid=(pairs,),
            in_specs=[
                part(0),
                part(1),
                part(2),
                part(0),
                pl.BlockSpec((length, 1), lambda pair: (0, 0)),
                pl.BlockSpec((1, length), lambda pair: (0, 0)),
            ],
            out_specs=[part(0)] * 3,
            scratch_shapes=[
                pltpu.VMEM((tiles, TILE, WINDOW), jnp.float32),
                pltpu.VMEM((length, 128), jnp.float32),
                pltpu.VMEM((length, 128), jnp.float32),
            ],
        ),
        compiler_params=pltpu.CompilerParams(vmem_limit_bytes=40 * 2**20),
        cost_estimate=pl.CostEstimate(
            flops=10 * length * WINDOW * width // 3,
            bytes_accessed=14 * length * width // 3,
            transcendentals=length * WINDOW * 12,
        ),
        name="attn_backward",
    )(projected, projected, projected, grad_context, seg_col, seg_row)


def on_device(
    tokens,
    out_grad,
    image_counts,
    group_of_device,
    group_weight,
    norm1_gain,
    norm1_bias,
    qkv_weight,
    qkv_bias,
    proj_weight,
    proj_bias,
    norm2_gain,
    norm2_bias,
    fc1_weight,
    fc1_bias,
    fc2_weight,
    fc2_bias,
    first_moment,
    second_moment,
):
    length = tokens.shape[0]
    segment, valid_rows = segment_info(image_counts[0], length)
    images = jnp.sum((image_counts[0] > 0).astype(jnp.int32))
    member = (group_of_device[0] == lax.iota(jnp.int32, NGROUPS)).astype(jnp.int32)
    totals = member * images
    for position in range((lax.axis_size("grp") * lax.axis_size("dp")).bit_length() - 1):
        totals = totals + swap(totals, 1 << position)
    factor = jnp.sum(member * group_weight).astype(jnp.float32) / jnp.sum(member * totals).astype(
        jnp.float32
    )
    inputs = tokens.astype(jnp.float32)
    normed_one, norm_one_back = jax.vjp(
        layer_norm, inputs, norm1_gain.astype(jnp.float32), norm1_bias.astype(jnp.float32)
    )
    normed_one_low = normed_one.astype(jnp.bfloat16)
    projected = (
        jnp.dot(normed_one_low, qkv_weight, preferred_element_type=jnp.float32)
        + qkv_bias.astype(jnp.float32)
    ).astype(jnp.bfloat16)
    seg_col, seg_row = segment[:, None], segment[None, :]
    pad_start = jnp.sum(image_counts[0], keepdims=True)
    context = attn_forward(projected, seg_col, seg_row, pad_start)
    middle = inputs + (
        jnp.dot(context, proj_weight, preferred_element_type=jnp.float32)
        + proj_bias.astype(jnp.float32)
    )
    normed_two, norm_two_back = jax.vjp(
        layer_norm, middle, norm2_gain.astype(jnp.float32), norm2_bias.astype(jnp.float32)
    )
    normed_two_low = normed_two.astype(jnp.bfloat16)
    hidden = jnp.dot(
        normed_two_low, fc1_weight, preferred_element_type=jnp.float32
    ) + fc1_bias.astype(jnp.float32)
    activated, gelu_back = jax.vjp(gelu_tanh, hidden)
    activated_low = activated.astype(jnp.bfloat16)
    block_out = (
        middle
        + (
            jnp.dot(activated_low, fc2_weight, preferred_element_type=jnp.float32)
            + fc2_bias.astype(jnp.float32)
        )
    ).astype(jnp.bfloat16)
    grad_out = out_grad.astype(jnp.float32) * valid_rows[:, None].astype(jnp.float32)
    grad_out_low = grad_out.astype(jnp.bfloat16)
    fc2_grad = contract_rows(activated_low, grad_out_low)
    fc2_bias_grad = jnp.sum(grad_out, axis=0)
    grad_hidden = gelu_back(contract_cols(grad_out_low, fc2_weight))[0].astype(jnp.bfloat16)
    fc1_grad = contract_rows(normed_two_low, grad_hidden)
    fc1_bias_grad = jnp.sum(grad_hidden.astype(jnp.float32), axis=0)
    grad_middle_norm, gain_two_grad, shift_two_grad = norm_two_back(
        contract_cols(grad_hidden, fc1_weight)
    )
    grad_middle = grad_out + grad_middle_norm
    grad_branch = grad_middle.astype(jnp.bfloat16)
    proj_grad = contract_rows(context, grad_branch)
    proj_bias_grad = jnp.sum(grad_branch.astype(jnp.float32), axis=0)
    grad_context = contract_cols(grad_branch, proj_weight).astype(jnp.bfloat16)
    grad_projected = jnp.concatenate(
        attn_backward(projected, grad_context, seg_col, seg_row), axis=1
    )
    qkv_grad = contract_rows(normed_one_low, grad_projected)
    qkv_bias_grad = jnp.sum(grad_projected.astype(jnp.float32), axis=0)
    grad_input_norm, gain_one_grad, shift_one_grad = norm_one_back(
        contract_cols(grad_projected, qkv_weight)
    )
    input_grad = (grad_middle + grad_input_norm).astype(jnp.bfloat16)
    moments = (first_moment, second_moment)
    mlp_summed, rest_summed = exchange_grads(
        (gain_one_grad, shift_one_grad, qkv_grad, qkv_bias_grad, proj_grad, proj_bias_grad),
        (gain_two_grad, shift_two_grad, fc1_grad, fc1_bias_grad, fc2_grad, fc2_bias_grad),
        factor,
    )
    row_count = lax.axis_size("dp")
    own_index = lax.axis_index("dp")
    weight_list = (
        norm1_gain,
        norm1_bias,
        qkv_weight,
        qkv_bias,
        proj_weight,
        proj_bias,
        norm2_gain,
        norm2_bias,
        fc1_weight,
        fc1_bias,
        fc2_weight,
        fc2_bias,
    )
    own_weights = [
        lax.dynamic_slice_in_dim(item.reshape(row_count, -1), own_index, 1, 0)[0]
        for item in weight_list
    ]
    rows = D // row_count
    fc1_sum = mlp_summed[0].reshape(4, rows, D).transpose(1, 0, 2).reshape(-1)
    fc2_sum = mlp_summed[1].reshape(-1)
    qkv_sum = jnp.concatenate(
        [rest_summed[0, :rows], rest_summed[0, rows : 2 * rows], rest_summed[1, :rows]], axis=1
    ).reshape(-1)
    proj_sum = rest_summed[1, rows : 2 * rows].reshape(-1)
    small = rest_summed[0, 2 * rows]
    widths = [item.size // row_count for item in weight_list]
    small_parts = {}
    start = 0
    for index, flag in enumerate(decay_flags):
        if flag == 0.0:
            small_parts[index] = small[start : start + widths[index]]
            start += widths[index]
    large_parts = {2: qkv_sum, 4: proj_sum, 8: fc1_sum, 10: fc2_sum}
    pieces = [
        small_parts[index] if index in small_parts else large_parts[index] for index in range(12)
    ]
    split = sum(widths[:8])
    grads_out, first_out, second_out, fresh = [], [], [], []
    for lead, tail, begin, end in ((8, 12, split, sum(widths)), (0, 8, 0, split)):
        summed_part = jnp.concatenate(pieces[lead:tail])
        current = jnp.concatenate(own_weights[lead:tail]).astype(jnp.float32)
        decay = jnp.concatenate(
            [
                jnp.full((width,), flag, jnp.float32)
                for width, flag in zip(widths[lead:tail], decay_flags[lead:tail])
            ]
        )
        new_first = beta_one * moments[0][0, begin:end] + (1.0 - beta_one) * summed_part
        new_second = (
            beta_two * moments[1][0, begin:end] + (1.0 - beta_two) * summed_part * summed_part
        )
        ratio = (
            new_first
            / (1.0 - beta_one**step_count)
            / (jnp.sqrt(new_second / (1.0 - beta_two**step_count)) + adam_eps)
        )
        fresh_low = (current - learn_rate * (ratio + decay_rate * decay * current)).astype(
            jnp.bfloat16
        )
        grads_out.insert(0, summed_part)
        first_out.insert(0, new_first)
        second_out.insert(0, new_second)
        fresh.insert(0, gather_rows(fresh_low))
    summed = jnp.concatenate(grads_out)[None]
    new_first = jnp.concatenate(first_out)[None]
    new_second = jnp.concatenate(second_out)[None]
    new_weights = jnp.concatenate(fresh, axis=1)
    summed_bias = pieces[11]
    return (block_out, input_grad, summed, new_weights, new_first, new_second, summed_bias)


AXES = ("grp", "dp")


def swap(values, bit):
    count = lax.axis_size("grp") * lax.axis_size("dp")
    return lax.ppermute(values, AXES, [(i, i ^ bit) for i in range(count)])


def bit_of(position):
    return (lax.axis_index("dp") >> position) & 1


def add_low(kept, came):
    return (kept.astype(jnp.float32) + came.astype(jnp.float32)).astype(jnp.bfloat16)


def halve(values, position, positions):
    axis = positions.index(position)
    own = bit_of(position)
    sent = lax.dynamic_index_in_dim(values, 1 - own, axis, keepdims=False)
    kept = lax.dynamic_index_in_dim(values, own, axis, keepdims=False)
    return kept, swap(sent, 1 << position), [p for p in positions if p != position]


def reduce_rows(values):
    count = lax.axis_size("dp")
    grp = lax.axis_index("grp")
    kept = lax.dynamic_index_in_dim(values, grp, 0, keepdims=False)
    came = swap(lax.dynamic_index_in_dim(values, 1 - grp, 0, keepdims=False), count)
    kept = add_low(kept, came)
    depth = count.bit_length() - 1
    positions = list(range(depth))[::-1]
    rows = kept.shape[1]
    parts = [kept[:, : rows // 2], kept[:, rows // 2 :]]
    left = [positions, positions]
    parts = [part.reshape((2,) * depth + part.shape[1:]) for part in parts]
    for order in ((0, 1), (1, 0)):
        for index in (0, 1):
            part, came, left[index] = halve(parts[index], order[index], left[index])
            parts[index] = add_low(part, came)
    whole = jnp.concatenate(parts, axis=depth - 2)
    rest = left[0]
    for position in range(2, depth):
        part, came, rest = halve(whole, position, rest)
        if rest:
            whole = add_low(part, came)
        else:
            whole = part.astype(jnp.float32) + came.astype(jnp.float32)
    other = swap(whole, count)
    return jnp.where(grp == 0, jnp.stack([whole, other]), jnp.stack([other, whole]))


def join(own, came, bit):
    return jnp.where(bit == 0, jnp.stack([own, came]), jnp.stack([came, own]))


def gather_rows(values):
    count = lax.axis_size("dp")
    depth = count.bit_length() - 1
    grp = lax.axis_index("grp")
    width = values.shape[0]
    padded = -(-width // 4096) * 4096
    halves = jnp.pad(values, (0, padded - width)).reshape(2, 2, padded // 512, 128)
    own = lax.dynamic_index_in_dim(halves, grp, 0, keepdims=False)
    for position in range(2, depth)[::-1]:
        own = join(own, swap(own, 1 << position), bit_of(position))
    lead = own.ndim - 3
    parts = [lax.index_in_dim(own, i, lead, keepdims=False) for i in (0, 1)]
    for order in ((1, 0), (0, 1)):
        for index in (0, 1):
            position = order[index]
            parts[index] = join(
                parts[index], swap(parts[index], 1 << position), bit_of(position)
            )
    parts[1] = jnp.swapaxes(parts[1], 0, 1)
    full = jnp.stack(parts, axis=depth)
    full = full.transpose(tuple(range(depth))[::-1] + tuple(range(depth, full.ndim)))
    full = full.reshape((count,) + full.shape[depth:])
    other = swap(full, count)
    whole = jnp.where(
        grp == 0, jnp.stack([full, other], axis=1), jnp.stack([other, full], axis=1)
    )
    return whole.reshape(count, padded)[:, :width]


def exchange_grads(front, back, factor):
    gain_one, shift_one, qkv, qkv_bias, proj, proj_bias = front
    gain_two, shift_two, fc1, fc1_bias, fc2, fc2_bias = back
    count = lax.axis_size("dp")
    rows = D // count
    fc1_blocks = fc1.reshape(count, rows, 4, D).transpose(0, 2, 1, 3).reshape(count, 4 * rows, D)
    fc2_blocks = fc2.reshape(count, 4 * rows, D)
    mlp = (jnp.stack([fc1_blocks, fc2_blocks]) * factor).astype(jnp.bfloat16)
    small = jnp.concatenate(
        [
            item.reshape(count, -1)
            for item in (
                gain_one,
                shift_one,
                qkv_bias,
                proj_bias,
                gain_two,
                shift_two,
                fc1_bias,
                fc2_bias,
            )
        ],
        axis=1,
    )
    small = jnp.pad(small, ((0, 0), (0, D - small.shape[1])))[:, None]
    small = jnp.pad(small, ((0, 0), (0, 7), (0, 0)))
    qkv_blocks = qkv.reshape(count, rows, 3, D)
    first_half = jnp.concatenate([qkv_blocks[:, :, 0], qkv_blocks[:, :, 1], small], axis=1)
    second_half = jnp.concatenate(
        [qkv_blocks[:, :, 2], proj.reshape(count, rows, D), jnp.zeros_like(small)], axis=1
    )
    rest = (jnp.stack([first_half, second_half]) * factor).astype(jnp.bfloat16)
    return reduce_rows(mlp), reduce_rows(rest)


def solution(mesh):
    in_specs = (
        P(("grp", "dp"), None),
        P(("grp", "dp"), None),
        P(("grp", "dp"), None),
        P(("grp", "dp")),
        P(),
        P(),
        P(),
        P(),
        P(),
        P(),
        P(),
        P(),
        P(),
        P(),
        P(),
        P(),
        P(),
        P("dp", None),
        P("dp", None),
    )
    out_specs = (
        P(("grp", "dp"), None),
        P(("grp", "dp"), None),
        P("dp", None),
        P(),
        P("dp", None),
        P("dp", None),
        P("dp"),
    )
    return jax.shard_map(
        on_device, mesh=mesh, in_specs=in_specs, out_specs=out_specs, check_vma=False
    )
```

```python
import functools

import jax
import jax.numpy as jnp
from jax import lax
from jax.experimental import pallas as pl
from jax.experimental.pallas import tpu as pltpu
from jax.sharding import PartitionSpec as P

D = 768
HEADS = 12
HEAD_DIM = 64
NGROUPS = 3


beta_one = 0.9
beta_two = 0.999
adam_eps = 1e-08
decay_rate = 0.05
step_count = 10.0
learn_rate = 0.004 * 0.75**1
norm_eps = 1e-06
neg_fill = -1e30
decay_flags = (0.0, 0.0, 1.0, 0.0, 1.0, 0.0, 0.0, 0.0, 1.0, 0.0, 1.0, 0.0)


def layer_norm(values, gain, shift):
    center = values - jnp.mean(values, axis=-1, keepdims=True)
    spread = jnp.mean(center * center, axis=-1, keepdims=True)
    return center * lax.rsqrt(spread + norm_eps) * gain + shift


def gelu_tanh(values):
    return jax.nn.gelu(values, approximate=True)


def contract_rows(first_op, second_op):
    return lax.dot_general(
        first_op, second_op, (((0,), (0,)), ((), ())), preferred_element_type=jnp.float32
    )


def contract_cols(first_op, second_op):
    return lax.dot_general(
        first_op, second_op, (((1,), (1,)), ((), ())), preferred_element_type=jnp.float32
    )


def segment_info(counts_row, length):
    slots = lax.iota(jnp.int32, counts_row.shape[0])
    segment_ends = jnp.sum(
        jnp.where(slots[:, None] <= slots[None, :], counts_row[:, None], 0), axis=0
    )
    position = lax.iota(jnp.int32, length)
    segment = jnp.sum((position[:, None] >= segment_ends[None, :]).astype(jnp.int32), axis=1)
    return (segment, position < segment_ends[-1])


TILE = 128
WINDOW = 3 * TILE


def window_start(tile, tiles):
    return min(max(tile - 1, 0), tiles - 3) * TILE


def dot_nt(first, second):
    return lax.dot_general(first, second, (((1,), (1,)), ((), ())), preferred_element_type=jnp.float32)


def dot_tn(first, second):
    return lax.dot_general(first, second, (((0,), (0,)), ((), ())), preferred_element_type=jnp.float32)


def dot_nn(first, second):
    return jnp.dot(first, second, preferred_element_type=jnp.float32)


def stack_heads(block, low):
    zero = jnp.zeros_like(block)
    return jnp.concatenate([jnp.where(low, block, zero), jnp.where(low, zero, block)], axis=0)


def merge_heads(block, low):
    return jnp.where(low, block[:TILE], block[TILE:])


def fill_masks(bias_ref, seg_col_ref, seg_row_ref, tiles):
    for tile in range(tiles):
        start = window_start(tile, tiles)
        same = (
            seg_col_ref[tile * TILE : (tile + 1) * TILE, :]
            == seg_row_ref[:, start : start + WINDOW]
        )
        bias_ref[tile] = jnp.where(same, 0.0, neg_fill)


def soft_probs(scores):
    row_max = jnp.max(scores, axis=1, keepdims=True)
    exponent = jnp.exp(scores - row_max)
    return exponent * (1.0 / jnp.sum(exponent, axis=1, keepdims=True))


def attn_forward_kernel(
    pad_ref, query_ref, key_ref, value_ref, seg_col_ref, seg_row_ref, out_ref, bias_ref
):
    length = query_ref.shape[0]
    tiles = length // TILE

    @pl.when(pl.program_id(0) == 0)
    def _():
        fill_masks(bias_ref, seg_col_ref, seg_row_ref, tiles)

    low = lax.broadcasted_iota(jnp.int32, (TILE, 128), 1) < 64
    scale = jnp.asarray(0.125, jnp.bfloat16)

    for tile in range(tiles):
        start = window_start(tile, tiles)
        queries = stack_heads(query_ref[tile * TILE : (tile + 1) * TILE, :] * scale, low)
        bias = bias_ref[tile]
        scores = dot_nt(queries, key_ref[start : start + WINDOW, :]) + jnp.concatenate(
            [bias, bias], axis=0
        )
        probs = soft_probs(scores).astype(jnp.bfloat16)
        mixed = dot_nn(probs, value_ref[start : start + WINDOW, :])
        out_ref[tile * TILE : (tile + 1) * TILE, :] = merge_heads(mixed, low).astype(jnp.bfloat16)

    @pl.loop(0, tiles)
    def _(tile):
        start = jnp.minimum(jnp.maximum(tile - 1, 0), tiles - 3) * TILE
        padding = (tile + 1) * TILE > pad_ref[0]
        outside = (pad_ref[0] < start) | (start + WINDOW < length)

        @pl.when(padding & outside)
        def _():
            rows = pl.ds(pl.multiple_of(tile * TILE, TILE), TILE)
            queries = stack_heads(query_ref[rows, :] * scale, low)
            same = seg_col_ref[rows, :] == seg_row_ref[...]
            bias = jnp.where(same, 0.0, neg_fill)
            scores = dot_nt(queries, key_ref[...]) + jnp.concatenate([bias, bias], axis=0)
            probs = soft_probs(scores).astype(jnp.bfloat16)
            out_ref[rows, :] = merge_heads(dot_nn(probs, value_ref[...]), low).astype(jnp.bfloat16)


def attn_forward(projected, seg_col, seg_row, pad_start):
    length, width = projected.shape
    pairs = width // 3 // 128
    tiles = length // TILE

    def part(offset):
        return pl.BlockSpec((length, 128), lambda pair, pad: (0, offset * pairs + pair))

    return pl.pallas_call(
        attn_forward_kernel,
        out_shape=jax.ShapeDtypeStruct((length, width // 3), jnp.bfloat16),
        grid_spec=pltpu.PrefetchScalarGridSpec(
            num_scalar_prefetch=1,
            grid=(pairs,),
            in_specs=[
                part(0),
                part(1),
                part(2),
                pl.BlockSpec((length, 1), lambda pair, pad: (0, 0)),
                pl.BlockSpec((1, length), lambda pair, pad: (0, 0)),
            ],
            out_specs=pl.BlockSpec((length, 128), lambda pair, pad: (0, pair)),
            scratch_shapes=[pltpu.VMEM((tiles, TILE, WINDOW), jnp.float32)],
        ),
        compiler_params=pltpu.CompilerParams(vmem_limit_bytes=40 * 2**20),
        cost_estimate=pl.CostEstimate(
            flops=4 * length * WINDOW * width // 3,
            bytes_accessed=8 * length * width // 3,
            transcendentals=length * WINDOW * 12,
        ),
        name="attn_forward",
    )(pad_start, projected, projected, projected, seg_col, seg_row)


def attn_backward_kernel(
    query_ref, key_ref, value_ref, grad_ref, seg_col_ref, seg_row_ref,
    query_out, key_out, value_out, bias_ref, key_sum, value_sum,
):
    length = query_ref.shape[0]
    tiles = length // TILE

    @pl.when(pl.program_id(0) == 0)
    def _():
        fill_masks(bias_ref, seg_col_ref, seg_row_ref, tiles)

    low = lax.broadcasted_iota(jnp.int32, (TILE, 128), 1) < 64
    scale = jnp.asarray(0.125, jnp.bfloat16)
    key_sum[...] = jnp.zeros_like(key_sum)
    value_sum[...] = jnp.zeros_like(value_sum)

    for tile in range(tiles):
        start = window_start(tile, tiles)
        rows = slice(tile * TILE, (tile + 1) * TILE)
        span = slice(start, start + WINDOW)
        queries = stack_heads(query_ref[rows, :] * scale, low)
        grads = stack_heads(grad_ref[rows, :], low)
        bias = bias_ref[tile]
        keys = key_ref[span, :]
        scores = dot_nt(queries, keys) + jnp.concatenate([bias, bias], axis=0)
        probs = soft_probs(scores)
        grad_probs = dot_nt(grads, value_ref[span, :])
        delta = jnp.sum(probs * grad_probs, axis=1, keepdims=True)
        grad_scores = (probs * (grad_probs - delta)).astype(jnp.bfloat16)
        query_out[rows, :] = (merge_heads(dot_nn(grad_scores, keys), low) * 0.125).astype(
            jnp.bfloat16
        )
        key_sum[span, :] += dot_tn(grad_scores, queries)
        value_sum[span, :] += dot_tn(probs.astype(jnp.bfloat16), grads)
    key_out[...] = key_sum[...].astype(jnp.bfloat16)
    value_out[...] = value_sum[...].astype(jnp.bfloat16)


def attn_backward(projected, grad_context, seg_col, seg_row):
    length, width = projected.shape
    pairs = width // 3 // 128
    tiles = length // TILE

    def part(offset):
        return pl.BlockSpec((length, 128), lambda pair: (0, offset * pairs + pair))

    return pl.pallas_call(
        attn_backward_kernel,
        out_shape=[jax.ShapeDtypeStruct((length, width // 3), jnp.bfloat16)] * 3,
        grid_spec=pltpu.PrefetchScalarGridSpec(
            num_scalar_prefetch=0,
            grid=(pairs,),
            in_specs=[
                part(0),
                part(1),
                part(2),
                part(0),
                pl.BlockSpec((length, 1), lambda pair: (0, 0)),
                pl.BlockSpec((1, length), lambda pair: (0, 0)),
            ],
            out_specs=[part(0)] * 3,
            scratch_shapes=[
                pltpu.VMEM((tiles, TILE, WINDOW), jnp.float32),
                pltpu.VMEM((length, 128), jnp.float32),
                pltpu.VMEM((length, 128), jnp.float32),
            ],
        ),
        compiler_params=pltpu.CompilerParams(vmem_limit_bytes=40 * 2**20),
        cost_estimate=pl.CostEstimate(
            flops=10 * length * WINDOW * width // 3,
            bytes_accessed=14 * length * width // 3,
            transcendentals=length * WINDOW * 12,
        ),
        name="attn_backward",
    )(projected, projected, projected, grad_context, seg_col, seg_row)


AXES = ("grp", "dp")
VMEM_BYTES = 56 * 2**20


def swap(values, bit):
    count = lax.axis_size("grp") * lax.axis_size("dp")
    return lax.ppermute(values, AXES, [(i, i ^ bit) for i in range(count)])


def add_low(kept, came):
    return (kept.astype(jnp.float32) + came.astype(jnp.float32)).astype(jnp.bfloat16)


def pick(values, axis, index):
    return lax.index_in_dim(values, index, axis, keepdims=False)


def column_sums(block):
    ones = jnp.ones((8, block.shape[0]), jnp.bfloat16)
    return dot_nn(ones, block)


def mlp_grads_kernel(
    info, factor_ref, normed_ref, hidden_ref, active_ref, grad_ref, out_ref, bias_ref, small_ref
):
    step = pl.program_id(0)
    last = step == pl.num_programs(0) - 1
    own = info[1]
    count = out_ref.shape[0]
    rows = D // count
    factor = factor_ref[0]

    @pl.when(info[0] == 0)
    def _():
        grads = (dot_tn(normed_ref[...], hidden_ref[...]) * factor).astype(jnp.bfloat16)
        place = pl.ds(pl.multiple_of(step * rows, rows), rows)
        for dest in range(count):
            out_ref[dest ^ own, place, :] = grads[dest * rows : (dest + 1) * rows]
        bias_ref[:, pl.ds(pl.multiple_of(step * D, D), D)] = (
            column_sums(hidden_ref[...]) * factor
        )

        @pl.when(last)
        def _():
            small_ref[...] = jnp.zeros_like(small_ref)
            for dest in range(count):
                small_ref[0:1, 0 : 4 * rows] = bias_ref[
                    0:1, dest * 4 * rows : (dest + 1) * 4 * rows
                ]
                out_ref[dest ^ own, 4 * rows :, :] = small_ref[...].astype(jnp.bfloat16)

    @pl.when(info[0] == 1)
    def _():
        grads = (dot_tn(active_ref[...], grad_ref[...]) * factor).astype(jnp.bfloat16)
        per = count // 4
        for part in range(per):
            out_ref[(step * per + part) ^ own, 0 : 4 * rows, :] = grads[
                part * 4 * rows : (part + 1) * 4 * rows
            ]

        @pl.when(last)
        def _():
            bias_ref[:, 0:D] = column_sums(grad_ref[...]) * factor
            small_ref[...] = jnp.zeros_like(small_ref)
            for dest in range(count):
                small_ref[0:1, 0:rows] = bias_ref[0:1, dest * rows : (dest + 1) * rows]
                out_ref[dest ^ own, 4 * rows :, :] = small_ref[...].astype(jnp.bfloat16)


def mlp_grads(half, own, count, factor, normed, grad_hidden, active, grad_out):
    length = normed.shape[0]
    rows = D // count
    steps = grad_hidden.shape[1] // D
    return pl.pallas_call(
        mlp_grads_kernel,
        out_shape=jax.ShapeDtypeStruct((count, 4 * rows + 8, D), jnp.bfloat16),
        grid_spec=pltpu.PrefetchScalarGridSpec(
            num_scalar_prefetch=1,
            grid=(steps,),
            in_specs=[
                pl.BlockSpec(memory_space=pltpu.SMEM),
                pl.BlockSpec((length, D), lambda i, info: (0, 0)),
                pl.BlockSpec((length, D), lambda i, info: (0, i * (1 - info[0]))),
                pl.BlockSpec((length, D), lambda i, info: (0, i * info[0])),
                pl.BlockSpec((length, D), lambda i, info: (0, 0)),
            ],
            out_specs=pl.BlockSpec((count, 4 * rows + 8, D), lambda i, info: (0, 0, 0)),
            scratch_shapes=[
                pltpu.VMEM((8, steps * D), jnp.float32),
                pltpu.VMEM((8, D), jnp.float32),
            ],
        ),
        compiler_params=pltpu.CompilerParams(vmem_limit_bytes=VMEM_BYTES),
        cost_estimate=pl.CostEstimate(
            flops=2 * length * D * D * steps, bytes_accessed=16 * 2**20, transcendentals=0
        ),
        name="mlp_grads",
    )(jnp.stack([half, own]), factor, normed, grad_hidden, active, grad_out)


def rest_grads_kernel(
    info,
    factor_ref,
    normed_ref,
    context_ref,
    query_ref,
    key_ref,
    value_ref,
    branch_ref,
    gain_one_ref,
    shift_one_ref,
    proj_bias_ref,
    gain_two_ref,
    shift_two_ref,
    out_ref,
    bias_ref,
    small_ref,
):
    step = pl.program_id(0)
    own = info[1]
    count = out_ref.shape[0]
    rows = D // count
    factor = factor_ref[0]

    def block(first_ref, second_ref, position):
        grads = (dot_tn(first_ref[...], second_ref[...]) * factor).astype(jnp.bfloat16)
        for dest in range(count):
            out_ref[dest ^ own, position * rows : (position + 1) * rows, :] = grads[
                dest * rows : (dest + 1) * rows
            ]

    @pl.when((info[0] == 0) & (step == 0))
    def _():
        block(normed_ref, query_ref, 0)

    @pl.when((info[0] == 0) & (step == 1))
    def _():
        block(normed_ref, key_ref, 1)
        for index, ref in enumerate((query_ref, key_ref, value_ref)):
            bias_ref[:, index * D : (index + 1) * D] = column_sums(ref[...])
        small_ref[...] = jnp.zeros_like(small_ref)
        for dest in range(count):
            part = slice(dest * rows, (dest + 1) * rows)
            wide = slice(dest * 3 * rows, (dest + 1) * 3 * rows)
            small_ref[0:1, 0:rows] = gain_one_ref[0:1, part]
            small_ref[0:1, rows : 2 * rows] = shift_one_ref[0:1, part]
            small_ref[0:1, 2 * rows : 5 * rows] = bias_ref[0:1, wide]
            small_ref[0:1, 5 * rows : 6 * rows] = proj_bias_ref[0:1, part]
            small_ref[0:1, 6 * rows : 7 * rows] = gain_two_ref[0:1, part]
            small_ref[0:1, 7 * rows : 8 * rows] = shift_two_ref[0:1, part]
            out_ref[dest ^ own, 2 * rows :, :] = (small_ref[...] * factor).astype(jnp.bfloat16)

    @pl.when((info[0] == 1) & (step == 0))
    def _():
        block(normed_ref, value_ref, 0)

    @pl.when((info[0] == 1) & (step == 1))
    def _():
        block(context_ref, branch_ref, 1)
        for dest in range(count):
            out_ref[dest, 2 * rows :, :] = jnp.zeros((8, D), jnp.bfloat16)


def rest_grads(half, own, count, factor, normed, context, query, key, value, branch, vectors):
    length = normed.shape[0]
    rows = D // count
    full = pl.BlockSpec((length, D), lambda i, info: (0, 0))
    line = pl.BlockSpec((1, D), lambda i, info: (0, 0))
    return pl.pallas_call(
        rest_grads_kernel,
        out_shape=jax.ShapeDtypeStruct((count, 2 * rows + 8, D), jnp.bfloat16),
        grid_spec=pltpu.PrefetchScalarGridSpec(
            num_scalar_prefetch=1,
            grid=(2,),
            in_specs=[pl.BlockSpec(memory_space=pltpu.SMEM)] + [full] * 6 + [line] * 5,
            out_specs=pl.BlockSpec((count, 2 * rows + 8, D), lambda i, info: (0, 0, 0)),
            scratch_shapes=[
                pltpu.VMEM((8, 3 * D), jnp.float32),
                pltpu.VMEM((8, D), jnp.float32),
            ],
        ),
        compiler_params=pltpu.CompilerParams(vmem_limit_bytes=VMEM_BYTES),
        cost_estimate=pl.CostEstimate(
            flops=4 * length * D * D, bytes_accessed=12 * 2**20, transcendentals=0
        ),
        name="rest_grads",
    )(
        jnp.stack([half, own]),
        factor,
        normed,
        context,
        query,
        key,
        value,
        branch,
        *[item.reshape(1, D) for item in vectors],
    )


def reduce_blocks(sent, kept):
    count = lax.axis_size("dp")
    depth = count.bit_length() - 1
    came = swap(sent, count)
    rows = kept.shape[1]
    cut = (rows - 8) // 2
    lead = (2,) * depth
    parts = []
    for span, order in ((slice(0, cut), (0, 1)), (slice(cut, rows), (1, 0))):
        own_part = kept[:, span].reshape(lead + (-1, D))
        came_part = came[:, span].reshape(lead + (-1, D))
        parts.append((own_part, came_part, order))
    for turn in (0, 1):
        following = []
        for own_part, came_part, order in parts:
            axis = depth - 1 - order[0] if turn == 0 else depth - 2
            away = add_low(pick(own_part, axis, 1), pick(came_part, axis, 1))
            stay = add_low(pick(own_part, axis, 0), pick(came_part, axis, 0))
            following.append((stay, swap(away, 1 << order[turn]), order))
        parts = following
    for position in range(2, depth):
        axis = depth - 1 - position
        away, stay = (
            jnp.concatenate(
                [add_low(pick(one, axis, i), pick(two, axis, i)) for one, two, _ in parts], axis=-2
            )
            for i in (1, 0)
        )
        parts = [(stay, swap(away, 1 << position), None)]
    return parts[0][0].astype(jnp.float32) + parts[0][1].astype(jnp.float32)


def gather_blocks(values):
    count = lax.axis_size("dp")
    depth = count.bit_length() - 1
    held = [values.reshape(1, 2, -1, 128)]
    slots = [0]
    for position in range(2, depth)[::-1]:
        block = held[0] if len(held) == 1 else jnp.concatenate(held, axis=0)
        held = [block, swap(block, 1 << position)]
        slots = slots + [slot ^ (1 << position) for slot in slots]
    arrays, lists = [], []
    for index, order in ((0, (1, 0)), (1, (0, 1))):
        block = jnp.concatenate([item[:, index] for item in held], axis=0)
        block = jnp.concatenate([block, swap(block, 1 << order[0])], axis=0)
        names = slots + [slot ^ (1 << order[0]) for slot in slots]
        arrays += [block, swap(block, 1 << order[1])]
        lists += [names, [name ^ (1 << order[1]) for name in names]]
    return arrays, lists


def place(target, source_ref, rows, offset):
    row, lane = divmod(offset, 128)
    if lane == 0:
        target[row : row + rows, :] = source_ref[0:rows, :]
        return
    rolled = pltpu.roll(source_ref[0:rows, :], lane, 1)
    lanes = lax.broadcasted_iota(jnp.int32, (rows, 128), 1)
    target[row : row + rows, :] = jnp.where(lanes >= lane, rolled, target[row : row + rows, :])
    target[row + 1 : row + 1 + rows, :] = jnp.where(
        lanes < lane, rolled, target[row + 1 : row + 1 + rows, :]
    )


def place_line(target, line, offset):
    start, width = 0, line.shape[1]
    while start < width:
        row, lane = divmod(offset + start, 128)
        step = min(128 - lane, width - start)
        target[row : row + 1, lane : lane + step] = line[:, start : start + step]
        start += step


def spread(target, block, first, stride):
    for piece in range(block.shape[1] // 128):
        target[pl.ds(first + piece, block.shape[0], stride=stride), :] = block[
            :, piece * 128 : (piece + 1) * 128
        ]


def adam_rows(grads_ref, current_ref, first_ref, second_ref, outs, fresh_ref, start, width, plain):
    sum_out, first_out, second_out = outs

    def update(grads, current, old_first, old_second, position):
        new_first = beta_one * old_first + (1.0 - beta_one) * grads
        new_second = beta_two * old_second + (1.0 - beta_two) * grads * grads
        ratio = (
            new_first
            / (1.0 - beta_one**step_count)
            / (jnp.sqrt(new_second / (1.0 - beta_two**step_count)) + adam_eps)
        )
        decays = jnp.ones(grads.shape, jnp.bool_)
        for low, high in plain:
            decays = decays & ((position < low) | (position >= high))
        decay = jnp.where(decays, decay_rate, 0.0)
        fresh = current - learn_rate * (ratio + decay * current)
        return new_first, new_second, fresh

    group = 64
    loops = width // (group * 128)

    @pl.loop(0, loops)
    def _(index):
        rows = pl.ds(pl.multiple_of(index * group, group), group)
        begin = pl.multiple_of(index * (group * 128), 1024)
        there = pl.ds(pl.multiple_of(start + begin, 128), group * 128)
        here = pl.ds(begin, group * 128)
        shape = (group, 128)
        position = (
            begin
            + lax.broadcasted_iota(jnp.int32, shape, 0) * 128
            + lax.broadcasted_iota(jnp.int32, shape, 1)
        )
        grads = grads_ref[rows, :]
        new_first, new_second, fresh = update(
            grads,
            current_ref[rows, :],
            first_ref[0:1, there].reshape(shape),
            second_ref[0:1, there].reshape(shape),
            position,
        )
        sum_out[0:1, here] = grads.reshape(1, group * 128)
        first_out[0:1, here] = new_first.reshape(1, group * 128)
        second_out[0:1, here] = new_second.reshape(1, group * 128)
        fresh_ref[rows, :] = fresh

    begin = loops * group * 128
    while begin < width:
        size = min(128, width - begin)
        row = begin // 128
        grads = grads_ref[row : row + 1, 0:size]
        position = begin + lax.broadcasted_iota(jnp.int32, (1, size), 1)
        new_first, new_second, fresh = update(
            grads,
            current_ref[row : row + 1, 0:size],
            first_ref[0:1, start + begin : start + begin + size],
            second_ref[0:1, start + begin : start + begin + size],
            position,
        )
        sum_out[0:1, begin : begin + size] = grads
        first_out[0:1, begin : begin + size] = new_first
        second_out[0:1, begin : begin + size] = new_second
        fresh_ref[row : row + 1, 0:size] = fresh
        begin += size


def own_lines(target, info, count, lines, part_widths, offsets):
    for dest in range(count):

        @pl.when(info[1] == dest)
        def _():
            for line, width, offset in zip(lines, part_widths, offsets):
                place_line(
                    target,
                    line[:, dest * width : (dest + 1) * width].astype(jnp.float32),
                    offset,
                )


def send_half(info, fresh_ref, fresh_out):
    rows = fresh_out.shape[0]
    fresh_out[...] = fresh_ref[pl.ds(pl.multiple_of(info[0] * rows, 16), rows), :].astype(
        jnp.bfloat16
    )


def mlp_update_kernel(
    start,
    info,
    mine_ref,
    other_ref,
    fc1_ref,
    fc1_bias_ref,
    fc2_ref,
    fc2_bias_ref,
    first_ref,
    second_ref,
    sum_out,
    first_out,
    second_out,
    fresh_out,
    grads_ref,
    current_ref,
    fresh_ref,
    line_ref,
):
    rows = fc1_ref.shape[0]
    count = D // rows
    tiles = D // 128
    large = rows * 4 * D
    second = large + 4 * rows
    end = second + large

    def fill(fc1_half, fc2_half):
        for part in range(4):
            spread(
                grads_ref, fc1_half[part * rows : (part + 1) * rows, :], part * tiles, 4 * tiles
            )
        spread(line_ref, fc2_half[0 : 4 * rows, :], 0, tiles)
        place(grads_ref, line_ref, large // 128, second)
        place_line(grads_ref, fc1_half[4 * rows : 4 * rows + 1, 0 : 4 * rows], large)
        place_line(grads_ref, fc2_half[4 * rows : 4 * rows + 1, 0:rows], end)

    @pl.when(info[0] == 0)
    def _():
        fill(mine_ref, other_ref)

    @pl.when(info[0] != 0)
    def _():
        fill(other_ref, mine_ref)

    spread(current_ref, fc1_ref[...].astype(jnp.float32), 0, 4 * tiles)
    spread(line_ref, fc2_ref[...].astype(jnp.float32), 0, tiles)
    place(current_ref, line_ref, large // 128, second)
    own_lines(
        current_ref,
        info,
        count,
        (fc1_bias_ref[...], fc2_bias_ref[...]),
        (4 * rows, rows),
        (large, end),
    )
    adam_rows(
        grads_ref,
        current_ref,
        first_ref,
        second_ref,
        (sum_out, first_out, second_out),
        fresh_ref,
        start,
        end + rows,
        ((large, second), (end, end + rows)),
    )
    send_half(info, fresh_ref, fresh_out)


def rest_update_kernel(
    info,
    mine_ref,
    other_ref,
    qkv_ref,
    proj_ref,
    gain_one_ref,
    shift_one_ref,
    qkv_bias_ref,
    proj_bias_ref,
    gain_two_ref,
    shift_two_ref,
    first_ref,
    second_ref,
    sum_out,
    first_out,
    second_out,
    fresh_out,
    grads_ref,
    current_ref,
    fresh_ref,
    line_ref,
):
    rows = qkv_ref.shape[0]
    count = D // rows
    tiles = D // 128
    qkv_at = 2 * rows
    qkv_bias_at = qkv_at + 3 * rows * D
    proj_at = qkv_bias_at + 3 * rows
    proj_bias_at = proj_at + rows * D
    end = proj_bias_at + 3 * rows
    small = (0, rows, qkv_bias_at, proj_bias_at, proj_bias_at + rows, proj_bias_at + 2 * rows)
    widths = (rows, rows, 3 * rows, rows, rows, rows)

    def fill(first_half, second_half):
        spread(line_ref, first_half[0:rows, :], 0, 3 * tiles)
        spread(line_ref, first_half[rows : 2 * rows, :], tiles, 3 * tiles)
        spread(line_ref, second_half[0:rows, :], 2 * tiles, 3 * tiles)
        place(grads_ref, line_ref, 3 * rows * tiles, qkv_at)
        spread(line_ref, second_half[rows : 2 * rows, :], 0, tiles)
        place(grads_ref, line_ref, rows * tiles, proj_at)
        begin = 0
        for width, offset in zip(widths, small):
            place_line(
                grads_ref, first_half[2 * rows : 2 * rows + 1, begin : begin + width], offset
            )
            begin += width

    @pl.when(info[0] == 0)
    def _():
        fill(mine_ref, other_ref)

    @pl.when(info[0] != 0)
    def _():
        fill(other_ref, mine_ref)

    spread(line_ref, qkv_ref[...].astype(jnp.float32), 0, 3 * tiles)
    place(current_ref, line_ref, 3 * rows * tiles, qkv_at)
    spread(line_ref, proj_ref[...].astype(jnp.float32), 0, tiles)
    place(current_ref, line_ref, rows * tiles, proj_at)
    lines = (
        gain_one_ref[...],
        shift_one_ref[...],
        qkv_bias_ref[...],
        proj_bias_ref[...],
        gain_two_ref[...],
        shift_two_ref[...],
    )
    own_lines(current_ref, info, count, lines, widths, small)
    adam_rows(
        grads_ref,
        current_ref,
        first_ref,
        second_ref,
        (sum_out, first_out, second_out),
        fresh_ref,
        0,
        end,
        ((0, qkv_at), (qkv_bias_at, proj_at), (proj_bias_at, end)),
    )
    send_half(info, fresh_ref, fresh_out)


def update_call(kernel, name, info, mine, other, matrices, small, moments, width, order):
    count = lax.axis_size("dp")
    half_rows = -(-width // 4096) * 16
    tall = 2 * half_rows

    def whole(item):
        return pl.BlockSpec(item.shape, lambda i, info: (0,) * item.ndim)

    operands = {("half", 0): (mine, whole(mine)), ("half", 1): (other, whole(other))}
    for index, item in enumerate(matrices):
        operands["matrix", index] = (
            item,
            pl.BlockSpec((item.shape[0] // count, item.shape[1]), lambda i, info: (info[1], 0)),
        )
    for index, item in enumerate(small):
        line = item.reshape(1, -1)
        operands["small", index] = (line, whole(line))
    for index, item in enumerate(moments):
        operands["moment", index] = (item, whole(item))
    chosen = [operands[key] for key in order]
    line_out = pl.BlockSpec((1, width), lambda i, info: (0, 0))
    return pl.pallas_call(
        kernel,
        out_shape=[jax.ShapeDtypeStruct((1, width), jnp.float32)] * 3
        + [jax.ShapeDtypeStruct((half_rows, 128), jnp.bfloat16)],
        grid_spec=pltpu.PrefetchScalarGridSpec(
            num_scalar_prefetch=1,
            grid=(1,),
            in_specs=[spec for _, spec in chosen],
            out_specs=[line_out] * 3 + [pl.BlockSpec((half_rows, 128), lambda i, info: (0, 0))],
            scratch_shapes=[pltpu.VMEM((tall + 8, 128), jnp.float32) for _ in range(4)],
        ),
        compiler_params=pltpu.CompilerParams(vmem_limit_bytes=VMEM_BYTES),
        cost_estimate=pl.CostEstimate(flops=2**20, bytes_accessed=24 * 2**20, transcendentals=0),
        name=name,
    )(info, *[item for item, _ in chosen])


def assemble_kernel(lists, start, width, aliased, info, *refs):
    mine, other = refs[0:4], refs[4:8]
    refs = refs[8 + aliased :]
    out_ref, refs = refs[0], refs[1:]
    tail = width % 128
    if tail:
        tail_ref, refs = refs[0], refs[1:]
    held, wide, in_sems, out_sems = refs
    count, rows = held.shape[1], held.shape[2]
    half = count // 2

    def arrivals(segment, begin):
        core, part = divmod(segment, 2)
        for index in range(count):
            array, slot = divmod(index, half)
            place = lists[2 * part + array][slot] ^ info[1]

            def copy(sources):
                return pltpu.make_async_copy(
                    sources[2 * part + array].at[slot],
                    held.at[segment, place],
                    in_sems.at[segment, index],
                )

            if begin:

                @pl.when(info[0] == core)
                def _():
                    copy(mine).start()

                @pl.when(info[0] != core)
                def _():
                    copy(other).start()

            else:
                copy(mine).wait()

    def departure(segment):
        length = min(rows * 128, width - tail - segment * rows * 128)
        return pltpu.make_async_copy(
            wide.at[segment % 2, :, pl.ds(0, length)],
            out_ref.at[:, pl.ds(start + segment * rows * 128, length)],
            out_sems.at[segment],
        )

    for segment in range(4):
        arrivals(segment, True)
    for segment in range(4):
        arrivals(segment, False)
        if segment >= 2:
            departure(segment - 2).wait()
        wide[segment % 2] = held[segment].reshape(count, rows * 128)
        departure(segment).start()
        if segment == 3 and tail:
            at = width - tail - segment * rows * 128
            tail_ref[...] = wide[segment % 2, :, at : at + 128]
    departure(2).wait()
    departure(3).wait()


def assemble(info, arrays, others, lists, start, width, total, target=None):
    count = lax.axis_size("dp")
    rows = arrays[0].shape[1]
    anywhere = pl.BlockSpec(memory_space=pl.ANY)
    aliased = 0 if target is None else 1
    tail = width % 128
    out_shape = [jax.ShapeDtypeStruct((count, total), jnp.bfloat16)]
    out_specs = [anywhere]
    if tail:
        out_shape.append(jax.ShapeDtypeStruct((count, 128), jnp.bfloat16))
        out_specs.append(pl.BlockSpec((count, 128), lambda i, info: (0, 0)))
    outs = pl.pallas_call(
        functools.partial(assemble_kernel, lists, start, width, aliased),
        out_shape=out_shape,
        grid_spec=pltpu.PrefetchScalarGridSpec(
            num_scalar_prefetch=1,
            grid=(1,),
            in_specs=[anywhere] * (8 + aliased),
            out_specs=out_specs,
            scratch_shapes=[
                pltpu.VMEM((4, count, rows, 128), jnp.bfloat16),
                pltpu.VMEM((2, count, rows * 128), jnp.bfloat16),
                pltpu.SemaphoreType.DMA((4, count)),
                pltpu.SemaphoreType.DMA((4,)),
            ],
        ),
        input_output_aliases={9: 0} if aliased else {},
        compiler_params=pltpu.CompilerParams(vmem_limit_bytes=VMEM_BYTES),
        cost_estimate=pl.CostEstimate(
            flops=2**20, bytes_accessed=4 * count * width, transcendentals=0
        ),
        name="assemble",
    )(info, *arrays, *others, *(() if target is None else (target,)))
    if tail:
        whole = lax.dynamic_update_slice(outs[0], outs[1][:, :tail], (0, start + width - tail))
        return whole
    return outs[0]


def join_kernel(*refs):
    for index in range(3):
        low, high, out = refs[index], refs[3 + index], refs[6 + index]
        width = low.shape[1]
        out[0:1, 0:width] = low[...]
        out[0:1, width:] = high[...]


def join_lines(lows, highs):
    total = lows[0].shape[1] + highs[0].shape[1]
    return pl.pallas_call(
        join_kernel,
        out_shape=[jax.ShapeDtypeStruct((1, total), jnp.float32)] * 3,
        compiler_params=pltpu.CompilerParams(vmem_limit_bytes=VMEM_BYTES),
        cost_estimate=pl.CostEstimate(flops=0, bytes_accessed=24 * total, transcendentals=0),
        name="join_lines",
    )(*lows, *highs)


MLP_ORDER = (
    ("half", 0),
    ("half", 1),
    ("matrix", 0),
    ("small", 0),
    ("matrix", 1),
    ("small", 1),
    ("moment", 0),
    ("moment", 1),
)
REST_ORDER = (
    (("half", 0), ("half", 1), ("matrix", 0), ("matrix", 1))
    + tuple(("small", index) for index in range(6))
    + (("moment", 0), ("moment", 1))
)


def reduce_pair(make, core):
    sent = make(1 - core)
    kept = make(core)
    mine = reduce_blocks(sent, kept)
    return mine, swap(mine, lax.axis_size("dp"))


def on_device(
    tokens,
    out_grad,
    image_counts,
    group_of_device,
    group_weight,
    norm1_gain,
    norm1_bias,
    qkv_weight,
    qkv_bias,
    proj_weight,
    proj_bias,
    norm2_gain,
    norm2_bias,
    fc1_weight,
    fc1_bias,
    fc2_weight,
    fc2_bias,
    first_moment,
    second_moment,
):
    length = tokens.shape[0]
    segment, valid_rows = segment_info(image_counts[0], length)
    images = jnp.sum((image_counts[0] > 0).astype(jnp.int32))
    member = (group_of_device[0] == lax.iota(jnp.int32, NGROUPS)).astype(jnp.int32)
    totals = member * images
    for position in range((lax.axis_size("grp") * lax.axis_size("dp")).bit_length() - 1):
        totals = totals + swap(totals, 1 << position)
    factor = jnp.sum(member * group_weight).astype(jnp.float32) / jnp.sum(member * totals).astype(
        jnp.float32
    )
    inputs = tokens.astype(jnp.float32)
    normed_one, norm_one_back = jax.vjp(
        layer_norm, inputs, norm1_gain.astype(jnp.float32), norm1_bias.astype(jnp.float32)
    )
    normed_one_low = normed_one.astype(jnp.bfloat16)
    projected = (
        jnp.dot(normed_one_low, qkv_weight, preferred_element_type=jnp.float32)
        + qkv_bias.astype(jnp.float32)
    ).astype(jnp.bfloat16)
    seg_col, seg_row = segment[:, None], segment[None, :]
    pad_start = jnp.sum(image_counts[0], keepdims=True)
    context = attn_forward(projected, seg_col, seg_row, pad_start)
    middle = inputs + (
        jnp.dot(context, proj_weight, preferred_element_type=jnp.float32)
        + proj_bias.astype(jnp.float32)
    )
    normed_two, norm_two_back = jax.vjp(
        layer_norm, middle, norm2_gain.astype(jnp.float32), norm2_bias.astype(jnp.float32)
    )
    normed_two_low = normed_two.astype(jnp.bfloat16)
    hidden = jnp.dot(
        normed_two_low, fc1_weight, preferred_element_type=jnp.float32
    ) + fc1_bias.astype(jnp.float32)
    activated, gelu_back = jax.vjp(gelu_tanh, hidden)
    activated_low = activated.astype(jnp.bfloat16)
    block_out = (
        middle
        + (
            jnp.dot(activated_low, fc2_weight, preferred_element_type=jnp.float32)
            + fc2_bias.astype(jnp.float32)
        )
    ).astype(jnp.bfloat16)
    grad_out = out_grad.astype(jnp.float32) * valid_rows[:, None].astype(jnp.float32)
    grad_out_low = grad_out.astype(jnp.bfloat16)
    fc2_grad = contract_rows(activated_low, grad_out_low)
    fc2_bias_grad = jnp.sum(grad_out, axis=0)
    grad_hidden = gelu_back(contract_cols(grad_out_low, fc2_weight))[0].astype(jnp.bfloat16)
    fc1_grad = contract_rows(normed_two_low, grad_hidden)
    fc1_bias_grad = jnp.sum(grad_hidden.astype(jnp.float32), axis=0)
    grad_middle_norm, gain_two_grad, shift_two_grad = norm_two_back(
        contract_cols(grad_hidden, fc1_weight)
    )
    grad_middle = grad_out + grad_middle_norm
    grad_branch = grad_middle.astype(jnp.bfloat16)
    proj_grad = contract_rows(context, grad_branch)
    proj_bias_grad = jnp.sum(grad_branch.astype(jnp.float32), axis=0)
    grad_context = contract_cols(grad_branch, proj_weight).astype(jnp.bfloat16)
    query_grad, key_grad, value_grad = attn_backward(projected, grad_context, seg_col, seg_row)
    grad_projected = jnp.concatenate([query_grad, key_grad, value_grad], axis=1)
    qkv_grad = contract_rows(normed_one_low, grad_projected)
    qkv_bias_grad = jnp.sum(grad_projected.astype(jnp.float32), axis=0)
    grad_input_norm, gain_one_grad, shift_one_grad = norm_one_back(
        contract_cols(grad_projected, qkv_weight)
    )
    input_grad = (grad_middle + grad_input_norm).astype(jnp.bfloat16)
    moments = (first_moment, second_moment)
    count = lax.axis_size("dp")
    if D // count % 16 == 0 and 8 * (D // count) <= D:
        core = lax.axis_index("grp")
        own = lax.axis_index("dp")
        info = jnp.stack([core, own])
        factor_line = factor.reshape(1)
        mlp_parts = reduce_pair(
                functools.partial(
                    mlp_grads,
                    own=own,
                    count=count,
                    factor=factor_line,
                    normed=normed_two_low,
                    grad_hidden=grad_hidden,
                    active=activated_low,
                    grad_out=grad_out_low,
                ),
                core,
            )
        vectors = (gain_one_grad, shift_one_grad, proj_bias_grad, gain_two_grad, shift_two_grad)
        rest_parts = reduce_pair(
            functools.partial(
                rest_grads,
                own=own,
                count=count,
                factor=factor_line,
                normed=normed_one_low,
                context=context,
                query=query_grad,
                key=key_grad,
                value=value_grad,
                branch=grad_branch,
                vectors=vectors,
            ),
            core,
        )
        total = first_moment.shape[1]
        rest_width = (3 * D * D + D * D + 3 * D + 5 * D) // count
        mlp_width = total - rest_width
        *mlp_lines, mlp_fresh = update_call(
            functools.partial(mlp_update_kernel, rest_width),
            "mlp_update",
            info,
            *mlp_parts,
            (fc1_weight, fc2_weight),
            (fc1_bias, fc2_bias),
            moments,
            mlp_width,
            MLP_ORDER,
        )
        mlp_arrays, lists = gather_blocks(mlp_fresh)
        new_weights = assemble(
            info,
            mlp_arrays,
            [swap(item, count) for item in mlp_arrays],
            lists,
            rest_width,
            mlp_width,
            total,
        )
        *rest_lines, rest_fresh = update_call(
            rest_update_kernel,
            "rest_update",
            info,
            *rest_parts,
            (qkv_weight, proj_weight),
            (norm1_gain, norm1_bias, qkv_bias, proj_bias, norm2_gain, norm2_bias),
            moments,
            rest_width,
            REST_ORDER,
        )
        rest_arrays, lists = gather_blocks(rest_fresh)
        new_weights = assemble(
            info,
            rest_arrays,
            [swap(item, count) for item in rest_arrays],
            lists,
            0,
            rest_width,
            total,
            new_weights,
        )
        summed, new_first, new_second = join_lines(rest_lines, mlp_lines)
        summed_bias = mlp_lines[0][0, mlp_width - D // count :]
        return (block_out, input_grad, summed, new_weights, new_first, new_second, summed_bias)
    mlp_summed, rest_summed = exchange_grads(
        (gain_one_grad, shift_one_grad, qkv_grad, qkv_bias_grad, proj_grad, proj_bias_grad),
        (gain_two_grad, shift_two_grad, fc1_grad, fc1_bias_grad, fc2_grad, fc2_bias_grad),
        factor,
    )
    row_count = lax.axis_size("dp")
    own_index = lax.axis_index("dp")
    weight_list = (
        norm1_gain,
        norm1_bias,
        qkv_weight,
        qkv_bias,
        proj_weight,
        proj_bias,
        norm2_gain,
        norm2_bias,
        fc1_weight,
        fc1_bias,
        fc2_weight,
        fc2_bias,
    )
    own_weights = [
        lax.dynamic_slice_in_dim(item.reshape(row_count, -1), own_index, 1, 0)[0]
        for item in weight_list
    ]
    rows = D // row_count
    fc1_sum = mlp_summed[0].reshape(4, rows, D).transpose(1, 0, 2).reshape(-1)
    fc2_sum = mlp_summed[1].reshape(-1)
    qkv_sum = jnp.concatenate(
        [rest_summed[0, :rows], rest_summed[0, rows : 2 * rows], rest_summed[1, :rows]], axis=1
    ).reshape(-1)
    proj_sum = rest_summed[1, rows : 2 * rows].reshape(-1)
    small = rest_summed[0, 2 * rows]
    widths = [item.size // row_count for item in weight_list]
    small_parts = {}
    start = 0
    for index, flag in enumerate(decay_flags):
        if flag == 0.0:
            small_parts[index] = small[start : start + widths[index]]
            start += widths[index]
    large_parts = {2: qkv_sum, 4: proj_sum, 8: fc1_sum, 10: fc2_sum}
    pieces = [
        small_parts[index] if index in small_parts else large_parts[index] for index in range(12)
    ]
    split = sum(widths[:8])
    grads_out, first_out, second_out, fresh = [], [], [], []
    for lead, tail, begin, end in ((8, 12, split, sum(widths)), (0, 8, 0, split)):
        summed_part = jnp.concatenate(pieces[lead:tail])
        current = jnp.concatenate(own_weights[lead:tail]).astype(jnp.float32)
        decay = jnp.concatenate(
            [
                jnp.full((width,), flag, jnp.float32)
                for width, flag in zip(widths[lead:tail], decay_flags[lead:tail])
            ]
        )
        new_first = beta_one * moments[0][0, begin:end] + (1.0 - beta_one) * summed_part
        new_second = (
            beta_two * moments[1][0, begin:end] + (1.0 - beta_two) * summed_part * summed_part
        )
        ratio = (
            new_first
            / (1.0 - beta_one**step_count)
            / (jnp.sqrt(new_second / (1.0 - beta_two**step_count)) + adam_eps)
        )
        fresh_low = (current - learn_rate * (ratio + decay_rate * decay * current)).astype(
            jnp.bfloat16
        )
        grads_out.insert(0, summed_part)
        first_out.insert(0, new_first)
        second_out.insert(0, new_second)
        fresh.insert(0, gather_rows(fresh_low))
    summed = jnp.concatenate(grads_out)[None]
    new_first = jnp.concatenate(first_out)[None]
    new_second = jnp.concatenate(second_out)[None]
    new_weights = jnp.concatenate(fresh, axis=1)
    summed_bias = pieces[11]
    return (block_out, input_grad, summed, new_weights, new_first, new_second, summed_bias)


def bit_of(position):
    return (lax.axis_index("dp") >> position) & 1


def halve(values, position, positions):
    axis = positions.index(position)
    own = bit_of(position)
    sent = lax.dynamic_index_in_dim(values, 1 - own, axis, keepdims=False)
    kept = lax.dynamic_index_in_dim(values, own, axis, keepdims=False)
    return kept, swap(sent, 1 << position), [p for p in positions if p != position]


def reduce_rows(values):
    count = lax.axis_size("dp")
    grp = lax.axis_index("grp")
    kept = lax.dynamic_index_in_dim(values, grp, 0, keepdims=False)
    came = swap(lax.dynamic_index_in_dim(values, 1 - grp, 0, keepdims=False), count)
    kept = add_low(kept, came)
    depth = count.bit_length() - 1
    positions = list(range(depth))[::-1]
    rows = kept.shape[1]
    parts = [kept[:, : rows // 2], kept[:, rows // 2 :]]
    left = [positions, positions]
    parts = [part.reshape((2,) * depth + part.shape[1:]) for part in parts]
    for order in ((0, 1), (1, 0)):
        for index in (0, 1):
            part, came, left[index] = halve(parts[index], order[index], left[index])
            parts[index] = add_low(part, came)
    whole = jnp.concatenate(parts, axis=depth - 2)
    rest = left[0]
    for position in range(2, depth):
        part, came, rest = halve(whole, position, rest)
        if rest:
            whole = add_low(part, came)
        else:
            whole = part.astype(jnp.float32) + came.astype(jnp.float32)
    other = swap(whole, count)
    return jnp.where(grp == 0, jnp.stack([whole, other]), jnp.stack([other, whole]))


def join(own, came, bit):
    return jnp.where(bit == 0, jnp.stack([own, came]), jnp.stack([came, own]))


def gather_rows(values):
    count = lax.axis_size("dp")
    depth = count.bit_length() - 1
    grp = lax.axis_index("grp")
    width = values.shape[0]
    padded = -(-width // 4096) * 4096
    halves = jnp.pad(values, (0, padded - width)).reshape(2, 2, padded // 512, 128)
    own = lax.dynamic_index_in_dim(halves, grp, 0, keepdims=False)
    for position in range(2, depth)[::-1]:
        own = join(own, swap(own, 1 << position), bit_of(position))
    lead = own.ndim - 3
    parts = [lax.index_in_dim(own, i, lead, keepdims=False) for i in (0, 1)]
    for order in ((1, 0), (0, 1)):
        for index in (0, 1):
            position = order[index]
            parts[index] = join(
                parts[index], swap(parts[index], 1 << position), bit_of(position)
            )
    parts[1] = jnp.swapaxes(parts[1], 0, 1)
    full = jnp.stack(parts, axis=depth)
    full = full.transpose(tuple(range(depth))[::-1] + tuple(range(depth, full.ndim)))
    full = full.reshape((count,) + full.shape[depth:])
    other = swap(full, count)
    whole = jnp.where(
        grp == 0, jnp.stack([full, other], axis=1), jnp.stack([other, full], axis=1)
    )
    return whole.reshape(count, padded)[:, :width]


def exchange_grads(front, back, factor):
    gain_one, shift_one, qkv, qkv_bias, proj, proj_bias = front
    gain_two, shift_two, fc1, fc1_bias, fc2, fc2_bias = back
    count = lax.axis_size("dp")
    rows = D // count
    fc1_blocks = fc1.reshape(count, rows, 4, D).transpose(0, 2, 1, 3).reshape(count, 4 * rows, D)
    fc2_blocks = fc2.reshape(count, 4 * rows, D)
    mlp = (jnp.stack([fc1_blocks, fc2_blocks]) * factor).astype(jnp.bfloat16)
    small = jnp.concatenate(
        [
            item.reshape(count, -1)
            for item in (
                gain_one,
                shift_one,
                qkv_bias,
                proj_bias,
                gain_two,
                shift_two,
                fc1_bias,
                fc2_bias,
            )
        ],
        axis=1,
    )
    small = jnp.pad(small, ((0, 0), (0, D - small.shape[1])))[:, None]
    small = jnp.pad(small, ((0, 0), (0, 7), (0, 0)))
    qkv_blocks = qkv.reshape(count, rows, 3, D)
    first_half = jnp.concatenate([qkv_blocks[:, :, 0], qkv_blocks[:, :, 1], small], axis=1)
    second_half = jnp.concatenate(
        [qkv_blocks[:, :, 2], proj.reshape(count, rows, D), jnp.zeros_like(small)], axis=1
    )
    rest = (jnp.stack([first_half, second_half]) * factor).astype(jnp.bfloat16)
    return reduce_rows(mlp), reduce_rows(rest)


def solution(mesh):
    in_specs = (
        P(("grp", "dp"), None),
        P(("grp", "dp"), None),
        P(("grp", "dp"), None),
        P(("grp", "dp")),
        P(),
        P(),
        P(),
        P(),
        P(),
        P(),
        P(),
        P(),
        P(),
        P(),
        P(),
        P(),
        P(),
        P("dp", None),
        P("dp", None),
    )
    out_specs = (
        P(("grp", "dp"), None),
        P(("grp", "dp"), None),
        P("dp", None),
        P(),
        P("dp", None),
        P("dp", None),
        P("dp"),
    )
    return jax.shard_map(
        on_device, mesh=mesh, in_specs=in_specs, out_specs=out_specs, check_vma=False
    )
```

```python
import functools

import jax
import jax.numpy as jnp
from jax import lax
from jax.experimental import pallas as pl
from jax.experimental.pallas import tpu as pltpu
from jax.sharding import PartitionSpec as P

D = 768
HEADS = 12
HEAD_DIM = 64
NGROUPS = 3


beta_one = 0.9
beta_two = 0.999
adam_eps = 1e-08
decay_rate = 0.05
step_count = 10.0
learn_rate = 0.004 * 0.75**1
norm_eps = 1e-06
neg_fill = -1e30
decay_flags = (0.0, 0.0, 1.0, 0.0, 1.0, 0.0, 0.0, 0.0, 1.0, 0.0, 1.0, 0.0)


def layer_norm(values, gain, shift):
    center = values - jnp.mean(values, axis=-1, keepdims=True)
    spread = jnp.mean(center * center, axis=-1, keepdims=True)
    return center * lax.rsqrt(spread + norm_eps) * gain + shift


def gelu_tanh(values):
    return jax.nn.gelu(values, approximate=True)


def contract_rows(first_op, second_op):
    return lax.dot_general(
        first_op, second_op, (((0,), (0,)), ((), ())), preferred_element_type=jnp.float32
    )


def contract_cols(first_op, second_op):
    return lax.dot_general(
        first_op, second_op, (((1,), (1,)), ((), ())), preferred_element_type=jnp.float32
    )


def segment_info(counts_row, length):
    slots = lax.iota(jnp.int32, counts_row.shape[0])
    segment_ends = jnp.sum(
        jnp.where(slots[:, None] <= slots[None, :], counts_row[:, None], 0), axis=0
    )
    position = lax.iota(jnp.int32, length)
    segment = jnp.sum((position[:, None] >= segment_ends[None, :]).astype(jnp.int32), axis=1)
    return (segment, position < segment_ends[-1])


TILE = 128
WINDOW = 3 * TILE


def window_start(tile, tiles):
    return min(max(tile - 1, 0), tiles - 3) * TILE


def dot_nt(first, second):
    return lax.dot_general(first, second, (((1,), (1,)), ((), ())), preferred_element_type=jnp.float32)


def dot_tn(first, second):
    return lax.dot_general(first, second, (((0,), (0,)), ((), ())), preferred_element_type=jnp.float32)


def dot_nn(first, second):
    return jnp.dot(first, second, preferred_element_type=jnp.float32)


def stack_heads(block, low):
    zero = jnp.zeros_like(block)
    return jnp.concatenate([jnp.where(low, block, zero), jnp.where(low, zero, block)], axis=0)


def merge_heads(block, low):
    return jnp.where(low, block[:TILE], block[TILE:])


def fill_masks(bias_ref, seg_col_ref, seg_row_ref, tiles):
    for tile in range(tiles):
        start = window_start(tile, tiles)
        same = (
            seg_col_ref[tile * TILE : (tile + 1) * TILE, :]
            == seg_row_ref[:, start : start + WINDOW]
        )
        bias_ref[tile] = jnp.where(same, 0.0, neg_fill)


ANYWHERE = pl.BlockSpec(memory_space=pl.ANY)
VMEM_BYTES = 56 * 2**20


def ordered_kernel(kernel, first, extra, outs, *refs):
    token = refs[first + extra + outs]
    token[...] = jnp.zeros_like(token)
    kernel(*refs[:first], *refs[first + extra : first + extra + outs], *refs[first + extra + outs + 1 :])


def ordered_call(
    kernel, operands, in_specs, out_shape, out_specs, after=(), grid=(1,), scalars=(), scratch=(),
    cost=(0, 0, 0), aliases=None, name=None,
):
    call = pl.pallas_call(
        functools.partial(
            ordered_kernel, kernel, len(scalars) + len(operands), len(after), len(out_shape)
        ),
        out_shape=[*out_shape, jax.ShapeDtypeStruct((8, 128), jnp.float32)],
        grid_spec=pltpu.PrefetchScalarGridSpec(
            num_scalar_prefetch=len(scalars),
            grid=grid,
            in_specs=[*in_specs] + [ANYWHERE] * len(after),
            out_specs=[*out_specs, pl.BlockSpec((8, 128), lambda *_: (0, 0))],
            scratch_shapes=list(scratch),
        ),
        input_output_aliases=aliases or {},
        compiler_params=pltpu.CompilerParams(vmem_limit_bytes=VMEM_BYTES),
        cost_estimate=pl.CostEstimate(
            flops=cost[0], bytes_accessed=cost[1], transcendentals=cost[2]
        ),
        name=name,
    )
    return call(*scalars, *operands, *after)


def whole(item):
    return pl.BlockSpec(item.shape, lambda *_: (0,) * len(item.shape))


def floats(*shape):
    return jax.ShapeDtypeStruct(shape, jnp.float32)


def halves(*shape):
    return jax.ShapeDtypeStruct(shape, jnp.bfloat16)


def attn_forward_kernel(
    pad_ref,
    query_ref,
    key_ref,
    value_ref,
    seg_col_ref,
    seg_row_ref,
    out_ref,
    weight_out,
    scale_out,
    bias_ref,
):
    length = query_ref.shape[0]
    tiles = length // TILE

    @pl.when(pl.program_id(0) == 0)
    def _():
        fill_masks(bias_ref, seg_col_ref, seg_row_ref, tiles)

    low = lax.broadcasted_iota(jnp.int32, (TILE, 128), 1) < 64
    scale = jnp.asarray(0.125, jnp.bfloat16)

    def head_rows(queries, keys, values, bias):
        scores = dot_nt(queries, keys) + bias
        weights = jnp.exp(scores - jnp.max(scores, axis=1, keepdims=True)).astype(jnp.bfloat16)
        ones = jnp.ones((values.shape[0], 128), jnp.bfloat16)
        mixed = dot_nn(weights, jnp.concatenate([values, ones], axis=1))
        inverse = 1.0 / mixed[:, 128:]
        return weights, mixed[:, :128] * inverse, inverse

    for tile in range(tiles):
        span = pl.ds(window_start(tile, tiles), WINDOW)
        rows = slice(tile * TILE, (tile + 1) * TILE)
        queries = query_ref[rows, :] * scale
        zero = jnp.zeros_like(queries)
        first, second = (
            head_rows(part, key_ref[span, :], value_ref[span, :], bias_ref[tile])
            for part in (jnp.where(low, queries, zero), jnp.where(low, zero, queries))
        )
        weight_out[0, tile, 0:TILE, :] = first[0]
        weight_out[0, tile, TILE:, :] = second[0]
        out_ref[rows, :] = jnp.where(low, first[1], second[1]).astype(jnp.bfloat16)
        scale_out[rows, :] = jnp.where(low, first[2], second[2])

    @pl.loop(0, tiles)
    def _(tile):
        start = jnp.minimum(jnp.maximum(tile - 1, 0), tiles - 3) * TILE
        padding = (tile + 1) * TILE > pad_ref[0]
        outside = (pad_ref[0] < start) | (start + WINDOW < length)

        @pl.when(padding & outside)
        def _():
            rows = pl.ds(pl.multiple_of(tile * TILE, TILE), TILE)
            queries = query_ref[rows, :] * scale
            zero = jnp.zeros_like(queries)
            bias = jnp.where(seg_col_ref[rows, :] == seg_row_ref[...], 0.0, neg_fill)
            first, second = (
                head_rows(part, key_ref[...], value_ref[...], bias)
                for part in (jnp.where(low, queries, zero), jnp.where(low, zero, queries))
            )
            out_ref[rows, :] = jnp.where(low, first[1], second[1]).astype(jnp.bfloat16)


def attn_forward(projected, seg_col, seg_row, pad_start):
    length, width = projected.shape
    pairs = width // 3 // 128
    tiles = length // TILE

    def part(offset):
        return pl.BlockSpec((length, 128), lambda pair, pad: (0, offset * pairs + pair))

    return ordered_call(
        attn_forward_kernel,
        (projected, projected, projected, seg_col, seg_row),
        [part(0), part(1), part(2), whole(seg_col), whole(seg_row)],
        [
            halves(length, width // 3),
            halves(pairs, tiles, 2 * TILE, WINDOW),
            floats(length, width // 3),
        ],
        [
            part(0),
            pl.BlockSpec((1, tiles, 2 * TILE, WINDOW), lambda pair, pad: (pair, 0, 0, 0)),
            part(0),
        ],
        grid=(pairs,),
        scalars=(pad_start,),
        scratch=[pltpu.VMEM((tiles, TILE, WINDOW), jnp.float32)],
        cost=(
            16 * length * WINDOW * width // 3,
            14 * length * width // 3,
            length * WINDOW * 12,
        ),
        name="attn_forward",
    )


def attn_backward_kernel(
    query_ref,
    key_ref,
    value_ref,
    context_ref,
    grad_ref,
    weight_ref,
    scale_ref,
    query_out,
    key_out,
    value_out,
    key_sum,
    value_sum,
):
    length = query_ref.shape[0]
    tiles = length // TILE
    low = lax.broadcasted_iota(jnp.int32, (TILE, 128), 1) < 64
    scale = jnp.asarray(0.125, jnp.bfloat16)
    key_sum[...] = jnp.zeros_like(key_sum)
    value_sum[...] = jnp.zeros_like(value_sum)

    for tile in range(tiles):
        rows = slice(tile * TILE, (tile + 1) * TILE)
        span = pl.ds(window_start(tile, tiles), WINDOW)
        queries = stack_heads(query_ref[rows, :] * scale, low)
        scaled = grad_ref[rows, :].astype(jnp.float32) * scale_ref[rows, :]
        product = stack_heads(scaled * context_ref[rows, :].astype(jnp.float32), low)
        delta = jnp.sum(product, axis=1, keepdims=True)
        grads = stack_heads(scaled.astype(jnp.bfloat16), low)
        keys = key_ref[span, :]
        weights = weight_ref[0, tile]
        grad_probs = dot_nt(grads, value_ref[span, :])
        grad_scores = (weights.astype(jnp.float32) * (grad_probs - delta)).astype(jnp.bfloat16)
        query_out[rows, :] = (merge_heads(dot_nn(grad_scores, keys), low) * 0.125).astype(
            jnp.bfloat16
        )
        key_sum[span, :] += dot_tn(grad_scores, queries)
        value_sum[span, :] += dot_tn(weights, grads)
    key_out[...] = key_sum[...].astype(jnp.bfloat16)
    value_out[...] = value_sum[...].astype(jnp.bfloat16)


def attn_backward(projected, context, context_grad, weights, scales, begin, pairs, after=()):
    length, width = projected.shape
    wide = width // 3 // 128
    tiles = length // TILE

    def part(offset):
        return pl.BlockSpec((length, 128), lambda pair: (0, offset * wide + begin + pair))

    out = halves(length, pairs * 128)
    *grads, token = ordered_call(
        attn_backward_kernel,
        (projected, projected, projected, context, context_grad, weights, scales),
        [
            part(0),
            part(1),
            part(2),
            part(0),
            part(0),
            pl.BlockSpec((1, tiles, 2 * TILE, WINDOW), lambda pair: (begin + pair, 0, 0, 0)),
            part(0),
        ],
        [out] * 3,
        [pl.BlockSpec((length, 128), lambda pair: (0, pair))] * 3,
        after,
        grid=(pairs,),
        scratch=[
            pltpu.VMEM((length, 128), jnp.float32),
            pltpu.VMEM((length, 128), jnp.float32),
        ],
        cost=(40 * length * WINDOW * pairs * 128, 16 * length * pairs * 128, 0),
        name="attn_backward",
    )
    return grads, token


AXES = ("grp", "dp")


def swap(values, bit):
    count = lax.axis_size("grp") * lax.axis_size("dp")
    return lax.ppermute(values, AXES, [(i, i ^ bit) for i in range(count)])


def add_low(kept, came):
    return (kept.astype(jnp.float32) + came.astype(jnp.float32)).astype(jnp.bfloat16)


def pick(values, axis, index):
    return lax.index_in_dim(values, index, axis, keepdims=False)


def column_sums(block):
    ones = jnp.ones((8, block.shape[0]), jnp.bfloat16)
    return dot_nn(ones, block)


def mlp_grads_kernel(
    info, factor_ref, normed_ref, hidden_ref, active_ref, grad_ref, out_ref, bias_ref, small_ref
):
    step = pl.program_id(0)
    last = step == pl.num_programs(0) - 1
    own = info[1]
    count = out_ref.shape[0]
    rows = D // count
    factor = factor_ref[0]

    @pl.when(info[0] == 0)
    def _():
        grads = (dot_tn(normed_ref[...], hidden_ref[...]) * factor).astype(jnp.bfloat16)
        place = pl.ds(pl.multiple_of(step * rows, rows), rows)
        for dest in range(count):
            out_ref[dest ^ own, place, :] = grads[dest * rows : (dest + 1) * rows]
        bias_ref[:, pl.ds(pl.multiple_of(step * D, D), D)] = (
            column_sums(hidden_ref[...]) * factor
        )

        @pl.when(last)
        def _():
            small_ref[...] = jnp.zeros_like(small_ref)
            for dest in range(count):
                small_ref[0:1, 0 : 4 * rows] = bias_ref[
                    0:1, dest * 4 * rows : (dest + 1) * 4 * rows
                ]
                out_ref[dest ^ own, 4 * rows :, :] = small_ref[...].astype(jnp.bfloat16)

    @pl.when(info[0] == 1)
    def _():
        grads = (dot_tn(active_ref[...], grad_ref[...]) * factor).astype(jnp.bfloat16)
        per = count // 4
        for part in range(per):
            out_ref[(step * per + part) ^ own, 0 : 4 * rows, :] = grads[
                part * 4 * rows : (part + 1) * 4 * rows
            ]

        @pl.when(last)
        def _():
            bias_ref[:, 0:D] = column_sums(grad_ref[...]) * factor
            small_ref[...] = jnp.zeros_like(small_ref)
            for dest in range(count):
                small_ref[0:1, 0:rows] = bias_ref[0:1, dest * rows : (dest + 1) * rows]
                out_ref[dest ^ own, 4 * rows :, :] = small_ref[...].astype(jnp.bfloat16)


def mlp_grads(half, own, count, factor, normed, grad_hidden, active, grad_out, after=()):
    length = normed.shape[0]
    rows = D // count
    steps = grad_hidden.shape[1] // D
    shape = (count, 4 * rows + 8, D)
    return ordered_call(
        mlp_grads_kernel,
        (factor, normed, grad_hidden, active, grad_out),
        [
            pl.BlockSpec(memory_space=pltpu.SMEM),
            whole(normed),
            pl.BlockSpec((length, D), lambda i, info: (0, i * (1 - info[0]))),
            pl.BlockSpec((length, D), lambda i, info: (0, i * info[0])),
            whole(grad_out),
        ],
        [jax.ShapeDtypeStruct(shape, jnp.bfloat16)],
        [pl.BlockSpec(shape, lambda *_: (0, 0, 0))],
        after,
        grid=(steps,),
        scalars=(jnp.stack([half, own]),),
        scratch=[pltpu.VMEM((8, steps * D), jnp.float32), pltpu.VMEM((8, D), jnp.float32)],
        cost=(6 * length * D * D * steps, 16 * 2**20, 0),
        name="mlp_grads",
    )


def rest_grads_kernel(parts, info, factor_ref, normed_ref, context_ref, *refs):
    query_refs, refs = refs[:parts], refs[parts:]
    key_refs, refs = refs[:parts], refs[parts:]
    value_refs, refs = refs[:parts], refs[parts:]
    branch_ref, gain_one_ref, shift_one_ref, proj_bias_ref, gain_two_ref, shift_two_ref = refs[:6]
    out_ref, bias_ref, small_ref = refs[-3:]
    step = pl.program_id(0)
    own = info[1]
    count = out_ref.shape[0]
    rows = D // count
    factor = factor_ref[0]

    def block(first_ref, second_refs, position):
        begin = 0
        for second_ref in second_refs:
            end = begin + second_ref.shape[1]
            grads = (dot_tn(first_ref[...], second_ref[...]) * factor).astype(jnp.bfloat16)
            for dest in range(count):
                out_ref[dest ^ own, position * rows : (position + 1) * rows, begin:end] = grads[
                    dest * rows : (dest + 1) * rows
                ]
            begin = end

    @pl.when((info[0] == 0) & (step == 0))
    def _():
        block(normed_ref, query_refs, 0)

    @pl.when((info[0] == 0) & (step == 1))
    def _():
        block(normed_ref, key_refs, 1)
        begin = 0
        for ref in query_refs + key_refs + value_refs:
            end = begin + ref.shape[1]
            bias_ref[:, begin:end] = column_sums(ref[...])
            begin = end
        small_ref[...] = jnp.zeros_like(small_ref)
        for dest in range(count):
            part = slice(dest * rows, (dest + 1) * rows)
            wide = slice(dest * 3 * rows, (dest + 1) * 3 * rows)
            small_ref[0:1, 0:rows] = gain_one_ref[0:1, part]
            small_ref[0:1, rows : 2 * rows] = shift_one_ref[0:1, part]
            small_ref[0:1, 2 * rows : 5 * rows] = bias_ref[0:1, wide]
            small_ref[0:1, 5 * rows : 6 * rows] = proj_bias_ref[0:1, part]
            small_ref[0:1, 6 * rows : 7 * rows] = gain_two_ref[0:1, part]
            small_ref[0:1, 7 * rows : 8 * rows] = shift_two_ref[0:1, part]
            out_ref[dest ^ own, 2 * rows :, :] = (small_ref[...] * factor).astype(jnp.bfloat16)

    @pl.when((info[0] == 1) & (step == 0))
    def _():
        block(normed_ref, value_refs, 0)

    @pl.when((info[0] == 1) & (step == 1))
    def _():
        block(context_ref, (branch_ref,), 1)
        for dest in range(count):
            out_ref[dest, 2 * rows :, :] = jnp.zeros((8, D), jnp.bfloat16)


def rest_grads(
    half, own, count, factor, normed, context, query, key, value, branch, vectors, after=()
):
    length = normed.shape[0]
    rows = D // count
    operands = [normed, context, *query, *key, *value, branch]
    operands += vectors
    shape = (count, 2 * rows + 8, D)
    return ordered_call(
        functools.partial(rest_grads_kernel, len(query)),
        (factor, *operands),
        [pl.BlockSpec(memory_space=pltpu.SMEM)] + [whole(item) for item in operands],
        [jax.ShapeDtypeStruct(shape, jnp.bfloat16)],
        [pl.BlockSpec(shape, lambda *_: (0, 0, 0))],
        after,
        grid=(2,),
        scalars=(jnp.stack([half, own]),),
        scratch=[pltpu.VMEM((8, 3 * D), jnp.float32), pltpu.VMEM((8, D), jnp.float32)],
        cost=(16 * length * D * D, 12 * 2**20, 0),
        name="rest_grads",
    )


def first_split_kernel(cut, kept_ref, came_ref, *refs):
    first_stay, first_away, second_stay, second_away = refs
    for index in range(4):
        low, high = index % 2, index // 2
        target = first_away if low else first_stay
        target[high] = add_low(kept_ref[index, 0:cut, :], came_ref[index, 0:cut, :])
        target = second_away if high else second_stay
        target[low] = add_low(kept_ref[index, cut:, :], came_ref[index, cut:, :])


def first_split(kept, came, cut, after=()):
    count, rows, width = kept.shape
    sizes = (cut, cut, rows - cut, rows - cut)
    return ordered_call(
        functools.partial(first_split_kernel, cut),
        (kept, came),
        [pl.BlockSpec((4, rows, width), lambda i: (i, 0, 0))] * 2,
        [jax.ShapeDtypeStruct((count // 2, size, width), kept.dtype) for size in sizes],
        [pl.BlockSpec((2, size, width), lambda i: (i, 0, 0)) for size in sizes],
        after,
        grid=(count // 4,),
        cost=(count * rows * width, 6 * count * rows * width, 0),
        name="first_split",
    )


def next_split_kernel(parts, *refs):
    outs = refs[-2:] if parts == 1 else refs[-4:]
    for index in range(parts):
        kept_ref, came_ref = refs[2 * index : 2 * index + 2]
        for side in (0, 1):
            outs[2 * index + side][0] = add_low(kept_ref[side], came_ref[side])


def join_split_kernel(cut, *refs):
    first_kept, first_came, second_kept, second_came = refs[:4]
    for side, out in enumerate(refs[-2:]):
        out[0, 0:cut, :] = add_low(first_kept[side], first_came[side])
        out[0, cut:, :] = add_low(second_kept[side], second_came[side])


def next_split(pairs, joined, after=()):
    lead, _, width = pairs[0][0].shape
    heights = [kept.shape[1] for kept, _ in pairs]
    operands = [item for pair in pairs for item in pair]
    sizes = [sum(heights)] * 2 if joined else [size for size in heights for _ in (0, 1)]
    kernel = (
        functools.partial(join_split_kernel, heights[0])
        if joined
        else functools.partial(next_split_kernel, len(pairs))
    )
    total = lead * sum(heights) * width
    return ordered_call(
        kernel,
        operands,
        [pl.BlockSpec((2,) + item.shape[1:], lambda i: (i, 0, 0)) for item in operands],
        [jax.ShapeDtypeStruct((lead // 2, size, width), jnp.bfloat16) for size in sizes],
        [pl.BlockSpec((1, size, width), lambda i: (i, 0, 0)) for size in sizes],
        after,
        grid=(lead // 2,),
        cost=(total, 6 * total, 0),
        name="next_split",
    )


def reduce_blocks(came, kept):
    count = lax.axis_size("dp")
    depth = count.bit_length() - 1
    after = yield None
    cut = (kept.shape[1] - 8) // 2
    first, first_away, second, second_away, token = first_split(kept, came, cut, after)
    pairs = [(first, swap(first_away, 1)), (second, swap(second_away, 2))]
    after = yield token
    first, first_away, second, second_away, token = next_split(pairs, False, after)
    pairs = [(first, swap(first_away, 2)), (second, swap(second_away, 1))]
    after = yield token
    for position in range(2, depth):
        stay, away, token = next_split(pairs, position == 2, after)
        pairs = [(stay, swap(away, 1 << position))]
        after = yield token
    ((stay, came),) = pairs
    return final_sum(stay, came, after)


def finish(steps, works, sending):
    works = list(works)
    while True:
        after = (works.pop(0)(sending),) if works else ()
        try:
            sending = steps.send(after)
        except StopIteration as stop:
            for work in works:
                work(None)
            return stop.value


def final_sum_kernel(kept_ref, came_ref, out_ref):
    out_ref[...] = kept_ref[0].astype(jnp.float32) + came_ref[0].astype(jnp.float32)


def final_sum(kept, came, after=()):
    shape = jax.ShapeDtypeStruct(kept.shape[1:], jnp.float32)
    return ordered_call(
        final_sum_kernel,
        (kept, came),
        [whole(kept), whole(came)],
        [shape],
        [whole(shape)],
        after,
        name="final_sum",
    )


def tie_kernel(*refs):
    pass


def tie(values, *after):
    return pl.pallas_call(
        tie_kernel,
        out_shape=jax.ShapeDtypeStruct(values.shape, values.dtype),
        in_specs=[ANYWHERE] * (1 + len(after)),
        out_specs=ANYWHERE,
        input_output_aliases={0: 0},
        name="tie",
    )(values, *after)


def join_kernel(split, *refs):
    sems = refs[-1]
    ins = refs[: 2 if split else 4]
    outs = refs[len(ins) : -1]
    copies = []
    for index, out in enumerate(outs):
        for side in (0, 1):
            source = ins[side].at[:, index] if split else ins[2 * index + side]
            place = pl.ds(side * source.shape[0], source.shape[0])
            copies.append(pltpu.make_async_copy(source, out.at[place], sems.at[index, side]))
    for copy in copies:
        copy.start()
    for copy in copies:
        copy.wait()


def join_whole_kernel(first_ref, second_ref, out_ref, sems):
    copies = [
        pltpu.make_async_copy(
            ref, out_ref.at[pl.ds(side * ref.shape[0], ref.shape[0])], sems.at[0, side]
        )
        for side, ref in enumerate((first_ref, second_ref))
    ]
    for copy in copies:
        copy.start()
    for copy in copies:
        copy.wait()


def join_blocks(pairs, after=(), split=False):
    operands = [item for pair in pairs for item in pair]
    if split:
        lead, _, *rest = operands[0].shape
        shapes = [(2 * lead, *rest)] * 2
    else:
        shapes = [(2 * pair[0].shape[0], *pair[0].shape[1:]) for pair in pairs]
    shapes = [jax.ShapeDtypeStruct(shape, jnp.bfloat16) for shape in shapes]
    return ordered_call(
        join_whole_kernel if len(shapes) == 1 else functools.partial(join_kernel, split),
        operands,
        [ANYWHERE] * len(operands),
        shapes,
        [whole(shape) for shape in shapes],
        after,
        scratch=[pltpu.SemaphoreType.DMA((2, 2))],
        cost=(0, 4 * sum(shape.size for shape in shapes), 0),
        name="join_blocks",
    )


class Gather:
    def __init__(self, values):
        self.depth = lax.axis_size("dp").bit_length() - 1
        self.block = values.reshape(1, 2, -1, 128)
        self.slots = [0]
        self.position = self.depth - 1
        self.came = swap(self.block, 1 << self.position)

    def _grow(self, slots, position):
        return slots + [slot ^ (1 << position) for slot in slots]

    def outer(self, after=()):
        self.slots = self._grow(self.slots, self.position)
        if self.position > 2:
            self.block, token = join_blocks([(self.block, self.came)], after)
            self.position -= 1
            self.came = swap(self.block, 1 << self.position)
            return token
        *self.parts, token = join_blocks([(self.block, self.came)], after, split=True)
        self.came = [swap(self.parts[0], 2), swap(self.parts[1], 1)]
        return token

    def inner(self, after=()):
        *self.parts, token = join_blocks(list(zip(self.parts, self.came)), after)
        self.came = [swap(self.parts[0], 1), swap(self.parts[1], 2)]
        return token

    def others(self):
        count = lax.axis_size("dp")
        self.parts_other = [swap(part, count) for part in self.parts]

    def result(self, after=()):
        count = lax.axis_size("dp")
        came = [tie(item, *after) for item in self.came] if after else self.came
        came_other = [swap(item, count) for item in came]
        names = [self._grow(self.slots, 1), self._grow(self.slots, 0)]
        lists = []
        for name, bit in zip(names, (1, 2)):
            lists += [name, [slot ^ bit for slot in name]]
        arrays = [self.parts[0], came[0], self.parts[1], came[1]]
        others = [self.parts_other[0], came_other[0], self.parts_other[1], came_other[1]]
        return arrays, others, lists


def place(target, source_ref, rows, offset):
    row, lane = divmod(offset, 128)
    if lane == 0:
        target[row : row + rows, :] = source_ref[0:rows, :]
        return
    rolled = pltpu.roll(source_ref[0:rows, :], lane, 1)
    lanes = lax.broadcasted_iota(jnp.int32, (rows, 128), 1)
    target[row : row + rows, :] = jnp.where(lanes >= lane, rolled, target[row : row + rows, :])
    target[row + 1 : row + 1 + rows, :] = jnp.where(
        lanes < lane, rolled, target[row + 1 : row + 1 + rows, :]
    )


def place_line(target, line, offset):
    start, width = 0, line.shape[1]
    while start < width:
        row, lane = divmod(offset + start, 128)
        step = min(128 - lane, width - start)
        target[row : row + 1, lane : lane + step] = line[:, start : start + step]
        start += step


def spread(target, block, first, stride):
    for piece in range(block.shape[1] // 128):
        target[pl.ds(first + piece, block.shape[0], stride=stride), :] = block[
            :, piece * 128 : (piece + 1) * 128
        ]


def adam_rows(grads_ref, current_ref, first_ref, second_ref, outs, fresh_ref, start, width, plain):
    sum_out, first_out, second_out = outs

    def update(grads, current, old_first, old_second, position):
        new_first = beta_one * old_first + (1.0 - beta_one) * grads
        new_second = beta_two * old_second + (1.0 - beta_two) * grads * grads
        ratio = (
            new_first
            / (1.0 - beta_one**step_count)
            / (jnp.sqrt(new_second / (1.0 - beta_two**step_count)) + adam_eps)
        )
        decays = jnp.ones(grads.shape, jnp.bool_)
        for low, high in plain:
            decays = decays & ((position < low) | (position >= high))
        decay = jnp.where(decays, decay_rate, 0.0)
        fresh = current - learn_rate * (ratio + decay * current)
        return new_first, new_second, fresh

    group = 64
    loops = width // (group * 128)

    @pl.loop(0, loops)
    def _(index):
        rows = pl.ds(pl.multiple_of(index * group, group), group)
        begin = pl.multiple_of(index * (group * 128), 1024)
        there = pl.ds(pl.multiple_of(start + begin, 128), group * 128)
        here = pl.ds(begin, group * 128)
        shape = (group, 128)
        position = (
            begin
            + lax.broadcasted_iota(jnp.int32, shape, 0) * 128
            + lax.broadcasted_iota(jnp.int32, shape, 1)
        )
        grads = grads_ref[rows, :]
        new_first, new_second, fresh = update(
            grads,
            current_ref[rows, :],
            first_ref[0:1, there].reshape(shape),
            second_ref[0:1, there].reshape(shape),
            position,
        )
        sum_out[0:1, here] = grads.reshape(1, group * 128)
        first_out[0:1, here] = new_first.reshape(1, group * 128)
        second_out[0:1, here] = new_second.reshape(1, group * 128)
        fresh_ref[rows, :] = fresh

    begin = loops * group * 128
    while begin < width:
        size = min(128, width - begin)
        row = begin // 128
        grads = grads_ref[row : row + 1, 0:size]
        position = begin + lax.broadcasted_iota(jnp.int32, (1, size), 1)
        new_first, new_second, fresh = update(
            grads,
            current_ref[row : row + 1, 0:size],
            first_ref[0:1, start + begin : start + begin + size],
            second_ref[0:1, start + begin : start + begin + size],
            position,
        )
        sum_out[0:1, begin : begin + size] = grads
        first_out[0:1, begin : begin + size] = new_first
        second_out[0:1, begin : begin + size] = new_second
        fresh_ref[row : row + 1, 0:size] = fresh
        begin += size


def own_lines(target, info, count, lines, part_widths, offsets):
    for dest in range(count):

        @pl.when(info[1] == dest)
        def _():
            for line, width, offset in zip(lines, part_widths, offsets):
                place_line(
                    target,
                    line[:, dest * width : (dest + 1) * width].astype(jnp.float32),
                    offset,
                )


def send_half(info, fresh_ref, fresh_out):
    rows = fresh_out.shape[0]
    fresh_out[...] = fresh_ref[pl.ds(pl.multiple_of(info[0] * rows, 16), rows), :].astype(
        jnp.bfloat16
    )


def mlp_update_kernel(
    start,
    info,
    mine_ref,
    other_ref,
    fc1_ref,
    fc1_bias_ref,
    fc2_ref,
    fc2_bias_ref,
    first_ref,
    second_ref,
    sum_out,
    first_out,
    second_out,
    fresh_out,
    grads_ref,
    current_ref,
    fresh_ref,
    line_ref,
):
    rows = fc1_ref.shape[0]
    count = D // rows
    tiles = D // 128
    large = rows * 4 * D
    second = large + 4 * rows
    end = second + large

    def fill(fc1_half, fc2_half):
        for part in range(4):
            spread(
                grads_ref, fc1_half[part * rows : (part + 1) * rows, :], part * tiles, 4 * tiles
            )
        spread(line_ref, fc2_half[0 : 4 * rows, :], 0, tiles)
        place(grads_ref, line_ref, large // 128, second)
        place_line(grads_ref, fc1_half[4 * rows : 4 * rows + 1, 0 : 4 * rows], large)
        place_line(grads_ref, fc2_half[4 * rows : 4 * rows + 1, 0:rows], end)

    @pl.when(info[0] == 0)
    def _():
        fill(mine_ref, other_ref)

    @pl.when(info[0] != 0)
    def _():
        fill(other_ref, mine_ref)

    spread(current_ref, fc1_ref[...].astype(jnp.float32), 0, 4 * tiles)
    spread(line_ref, fc2_ref[...].astype(jnp.float32), 0, tiles)
    place(current_ref, line_ref, large // 128, second)
    own_lines(
        current_ref,
        info,
        count,
        (fc1_bias_ref[...], fc2_bias_ref[...]),
        (4 * rows, rows),
        (large, end),
    )
    adam_rows(
        grads_ref,
        current_ref,
        first_ref,
        second_ref,
        (sum_out, first_out, second_out),
        fresh_ref,
        start,
        end + rows,
        ((large, second), (end, end + rows)),
    )
    send_half(info, fresh_ref, fresh_out)


def rest_update_kernel(
    info,
    mine_ref,
    other_ref,
    qkv_ref,
    proj_ref,
    gain_one_ref,
    shift_one_ref,
    qkv_bias_ref,
    proj_bias_ref,
    gain_two_ref,
    shift_two_ref,
    first_ref,
    second_ref,
    sum_out,
    first_out,
    second_out,
    fresh_out,
    grads_ref,
    current_ref,
    fresh_ref,
    line_ref,
):
    rows = qkv_ref.shape[0]
    count = D // rows
    tiles = D // 128
    qkv_at = 2 * rows
    qkv_bias_at = qkv_at + 3 * rows * D
    proj_at = qkv_bias_at + 3 * rows
    proj_bias_at = proj_at + rows * D
    end = proj_bias_at + 3 * rows
    small = (0, rows, qkv_bias_at, proj_bias_at, proj_bias_at + rows, proj_bias_at + 2 * rows)
    widths = (rows, rows, 3 * rows, rows, rows, rows)

    def fill(first_half, second_half):
        spread(line_ref, first_half[0:rows, :], 0, 3 * tiles)
        spread(line_ref, first_half[rows : 2 * rows, :], tiles, 3 * tiles)
        spread(line_ref, second_half[0:rows, :], 2 * tiles, 3 * tiles)
        place(grads_ref, line_ref, 3 * rows * tiles, qkv_at)
        spread(line_ref, second_half[rows : 2 * rows, :], 0, tiles)
        place(grads_ref, line_ref, rows * tiles, proj_at)
        begin = 0
        for width, offset in zip(widths, small):
            place_line(
                grads_ref, first_half[2 * rows : 2 * rows + 1, begin : begin + width], offset
            )
            begin += width

    @pl.when(info[0] == 0)
    def _():
        fill(mine_ref, other_ref)

    @pl.when(info[0] != 0)
    def _():
        fill(other_ref, mine_ref)

    spread(line_ref, qkv_ref[...].astype(jnp.float32), 0, 3 * tiles)
    place(current_ref, line_ref, 3 * rows * tiles, qkv_at)
    spread(line_ref, proj_ref[...].astype(jnp.float32), 0, tiles)
    place(current_ref, line_ref, rows * tiles, proj_at)
    lines = (
        gain_one_ref[...],
        shift_one_ref[...],
        qkv_bias_ref[...],
        proj_bias_ref[...],
        gain_two_ref[...],
        shift_two_ref[...],
    )
    own_lines(current_ref, info, count, lines, widths, small)
    adam_rows(
        grads_ref,
        current_ref,
        first_ref,
        second_ref,
        (sum_out, first_out, second_out),
        fresh_ref,
        0,
        end,
        ((0, qkv_at), (qkv_bias_at, proj_at), (proj_bias_at, end)),
    )
    send_half(info, fresh_ref, fresh_out)


def update_call(
    kernel, name, info, mine, other, matrices, small, moments, width, order, after=()
):
    count = lax.axis_size("dp")
    half_rows = -(-width // 4096) * 16
    tall = 2 * half_rows

    operands = {("half", 0): (mine, whole(mine)), ("half", 1): (other, whole(other))}
    for index, item in enumerate(matrices):
        operands["matrix", index] = (
            item,
            pl.BlockSpec((item.shape[0] // count, item.shape[1]), lambda i, info: (info[1], 0)),
        )
    for index, item in enumerate(small):
        line = item.reshape(1, -1)
        operands["small", index] = (line, whole(line))
    for index, item in enumerate(moments):
        operands["moment", index] = (item, whole(item))
    chosen = [operands[key] for key in order]
    line = jax.ShapeDtypeStruct((1, width), jnp.float32)
    half_out = jax.ShapeDtypeStruct((half_rows, 128), jnp.bfloat16)
    return ordered_call(
        kernel,
        [item for item, _ in chosen],
        [spec for _, spec in chosen],
        [line, line, line, half_out],
        [whole(line)] * 3 + [whole(half_out)],
        after,
        scalars=(info,),
        scratch=[pltpu.VMEM((tall + 8, 128), jnp.float32) for _ in range(4)],
        cost=(2**20, 24 * 2**20, 0),
        name=name,
    )


def assemble_kernel(lists, start, width, extra, info, *refs):
    each = 1 if lists is None else 4
    mine, other = refs[0:each], refs[each : 2 * each]
    refs = refs[2 * each + extra :]
    out_ref, refs = refs[0], refs[1:]
    tail = width % 128
    if tail:
        tail_ref, refs = refs[0], refs[1:]
    held, wide, in_sems, out_sems = refs
    count, rows = held.shape[1], held.shape[2]

    def pieces(segment):
        part = segment % 2
        if lists is None:
            whole_part = pl.ds(part * rows, rows)
            return [(lambda refs: refs[0].at[:, whole_part], held.at[segment], 0)]
        found = []
        for index in range(count):
            array, slot = divmod(index, count // 2)
            array += 2 * part
            target = held.at[segment, lists[array][slot] ^ info[1]]
            found.append(
                (lambda refs, array=array, slot=slot: refs[array].at[slot], target, index)
            )
        return found

    def arrivals(segment, begin):
        for source, target, index in pieces(segment):

            def copy(refs):
                return pltpu.make_async_copy(source(refs), target, in_sems.at[segment, index])

            if begin:

                @pl.when(info[0] == segment // 2)
                def _():
                    copy(mine).start()

                @pl.when(info[0] != segment // 2)
                def _():
                    copy(other).start()

            else:
                copy(mine).wait()

    def departure(segment):
        length = min(rows * 128, width - tail - segment * rows * 128)
        return pltpu.make_async_copy(
            wide.at[segment % 2, :, pl.ds(0, length)],
            out_ref.at[:, pl.ds(start + segment * rows * 128, length)],
            out_sems.at[segment],
        )

    for segment in range(4):
        arrivals(segment, True)
    for segment in range(4):
        arrivals(segment, False)
        if segment >= 2:
            departure(segment - 2).wait()
        wide[segment % 2] = held[segment].reshape(count, rows * 128)
        departure(segment).start()
        if segment == 3 and tail:
            at = width - tail - segment * rows * 128
            tail_ref[...] = wide[segment % 2, :, at : at + 128]
    departure(2).wait()
    departure(3).wait()


def assemble(info, arrays, others, lists, start, width, total, target=None, after=()):
    count = lax.axis_size("dp")
    rows = arrays[0].shape[1] // (2 if lists is None else 1)
    aliased = 0 if target is None else 1
    tail = width % 128
    out_shape = [jax.ShapeDtypeStruct((count, total), jnp.bfloat16)]
    out_specs = [ANYWHERE]
    if tail:
        out_shape.append(jax.ShapeDtypeStruct((count, 128), jnp.bfloat16))
        out_specs.append(whole(out_shape[-1]))
    operands = (*arrays, *others, *(() if target is None else (target,)))
    *outs, token = ordered_call(
        functools.partial(assemble_kernel, lists, start, width, aliased),
        operands,
        [ANYWHERE] * len(operands),
        out_shape,
        out_specs,
        after,
        scalars=(info,),
        scratch=[
            pltpu.VMEM((4, count, rows, 128), jnp.bfloat16),
            pltpu.VMEM((2, count, rows * 128), jnp.bfloat16),
            pltpu.SemaphoreType.DMA((4, count)),
            pltpu.SemaphoreType.DMA((4,)),
        ],
        cost=(2**20, 4 * count * width, 0),
        aliases={len(operands): 0} if aliased else {},
        name="assemble",
    )
    if tail:
        filled = lax.dynamic_update_slice(outs[0], outs[1][:, :tail], (0, start + width - tail))
        return filled, token
    return outs[0], token


def join_lines_kernel(*refs):
    for index in range(3):
        low, high, out = refs[index], refs[3 + index], refs[6 + index]
        width = low.shape[1]
        out[0:1, 0:width] = low[...]
        out[0:1, width:] = high[...]


def join_lines(lows, highs, after=()):
    operands = (*lows, *highs)
    line = jax.ShapeDtypeStruct((1, lows[0].shape[1] + highs[0].shape[1]), jnp.float32)
    return ordered_call(
        join_lines_kernel,
        operands,
        [whole(item) for item in operands],
        [line] * 3,
        [whole(line)] * 3,
        after,
        cost=(0, 24 * line.size, 0),
        name="join_lines",
    )


MLP_ORDER = (
    ("half", 0),
    ("half", 1),
    ("matrix", 0),
    ("small", 0),
    ("matrix", 1),
    ("small", 1),
    ("moment", 0),
    ("moment", 1),
)
REST_ORDER = (
    (("half", 0), ("half", 1), ("matrix", 0), ("matrix", 1))
    + tuple(("small", index) for index in range(6))
    + (("moment", 0), ("moment", 1))
)


ROWS = 256


def norm_rows(values):
    center = values - jnp.mean(values, axis=-1, keepdims=True)
    spread = lax.rsqrt(jnp.mean(center * center, axis=-1, keepdims=True) + norm_eps)
    return center * spread, spread


def norm_back(grads, gain, hat, spread):
    scaled = grads * gain
    inner = scaled - jnp.mean(scaled, axis=-1, keepdims=True)
    inner = inner - hat * jnp.mean(scaled * hat, axis=-1, keepdims=True)
    return (
        spread * inner,
        jnp.sum(grads * hat, axis=0, keepdims=True),
        jnp.sum(grads, axis=0, keepdims=True),
    )


def add_lines(refs, lines):
    first = pl.program_id(0) == 0

    @pl.when(first)
    def _():
        for ref, line in zip(refs, lines):
            ref[...] = line

    @pl.when(jnp.logical_not(first))
    def _():
        for ref, line in zip(refs, lines):
            ref[...] += line


def rows_of(item):
    return pl.BlockSpec((ROWS, item.shape[1]), lambda i, *_: (i, 0))


def first_part_kernel(tokens_ref, gain_ref, bias_ref, weight_ref, shift_ref, normed_out, out_ref):
    hat, _ = norm_rows(tokens_ref[...].astype(jnp.float32))
    normed = (
        hat * gain_ref[...].astype(jnp.float32) + bias_ref[...].astype(jnp.float32)
    ).astype(jnp.bfloat16)
    normed_out[...] = normed
    out_ref[...] = (
        dot_nn(normed, weight_ref[...]) + shift_ref[...].astype(jnp.float32)
    ).astype(jnp.bfloat16)


def first_part(tokens, gain, bias, weight, shift):
    length = tokens.shape[0]
    operands = (tokens, gain, bias, weight, shift)
    outs = [halves(length, D), halves(length, weight.shape[1])]
    return ordered_call(
        first_part_kernel,
        operands,
        [rows_of(tokens)] + [whole(item) for item in operands[1:]],
        outs,
        [rows_of(item) for item in outs],
        grid=(length // ROWS,),
        cost=(2 * length * weight.size, 8 * 2**20, 0),
        name="norm_qkv",
    )


def second_part_kernel(
    tokens_ref, context_ref, weight_ref, shift_ref, gain_ref, bias_ref, middle_out, normed_out
):
    middle = tokens_ref[...].astype(jnp.float32) + (
        dot_nn(context_ref[...], weight_ref[...]) + shift_ref[...].astype(jnp.float32)
    )
    middle_out[...] = middle
    hat, _ = norm_rows(middle)
    normed_out[...] = (
        hat * gain_ref[...].astype(jnp.float32) + bias_ref[...].astype(jnp.float32)
    ).astype(jnp.bfloat16)


def second_part(tokens, context, weight, shift, gain, bias):
    length = tokens.shape[0]
    operands = (tokens, context, weight, shift, gain, bias)
    outs = [floats(length, D), halves(length, D)]
    return ordered_call(
        second_part_kernel,
        operands,
        [rows_of(tokens), rows_of(context)] + [whole(item) for item in operands[2:]],
        outs,
        [rows_of(item) for item in outs],
        grid=(length // ROWS,),
        cost=(2 * length * weight.size, 8 * 2**20, 0),
        name="proj_norm",
    )


def mlp_part_kernel(
    normed_ref, grad_ref, first_ref, shift_ref, second_ref, active_out, hidden_grad_out
):
    root = 0.7978845608028654
    for begin in range(0, normed_ref.shape[0], ROWS):
        rows = slice(begin, begin + ROWS)
        hidden = dot_nn(normed_ref[rows, :], first_ref[...]) + shift_ref[...].astype(jnp.float32)
        grad_active = dot_nt(grad_ref[rows, :], second_ref[...])
        square = hidden * hidden
        slope = jnp.tanh(hidden * (root + (root * 0.044715) * square))
        half = 0.5 + 0.5 * slope
        active_out[rows, :] = (hidden * half).astype(jnp.bfloat16)
        rise = half + (0.5 * hidden) * (1.0 - slope * slope) * (
            root + (3.0 * root * 0.044715) * square
        )
        hidden_grad_out[rows, :] = (grad_active * rise).astype(jnp.bfloat16)


def mlp_part(normed, grad_out, first, shift, second):
    length, width = normed.shape[0], first.shape[1]
    step = D
    columns = pl.BlockSpec((length, step), lambda i: (0, i))
    outs = [halves(length, width)] * 2
    return ordered_call(
        mlp_part_kernel,
        (normed, grad_out, first, shift, second),
        [
            whole(normed),
            whole(grad_out),
            pl.BlockSpec((D, step), lambda i: (0, i)),
            pl.BlockSpec((1, step), lambda i: (0, i)),
            pl.BlockSpec((step, D), lambda i: (i, 0)),
        ],
        outs,
        [columns, columns],
        grid=(width // step,),
        cost=(4 * length * D * width, 24 * 2**20, length * width),
        name="mlp_part",
    )


def middle_back_kernel(
    hidden_grad_ref,
    first_ref,
    middle_ref,
    gain_ref,
    grad_out_ref,
    proj_ref,
    middle_grad_out,
    branch_out,
    context_grad_out,
    gain_sum,
    bias_sum,
    proj_bias_sum,
):
    grads = dot_nt(hidden_grad_ref[...], first_ref[...])
    hat, spread = norm_rows(middle_ref[...])
    back, gain_line, bias_line = norm_back(
        grads, gain_ref[...].astype(jnp.float32), hat, spread
    )
    middle_grad = grad_out_ref[...].astype(jnp.float32) + back
    middle_grad_out[...] = middle_grad
    branch = middle_grad.astype(jnp.bfloat16)
    branch_out[...] = branch
    context_grad_out[...] = dot_nt(branch, proj_ref[...]).astype(jnp.bfloat16)
    proj_line = jnp.sum(branch.astype(jnp.float32), axis=0, keepdims=True)
    add_lines((gain_sum, bias_sum, proj_bias_sum), (gain_line, bias_line, proj_line))


def middle_back(hidden_grad, first, middle, gain, grad_out, proj, after=()):
    length = middle.shape[0]
    line = floats(1, D)
    outs = [floats(length, D), halves(length, D), halves(length, D)]
    return ordered_call(
        middle_back_kernel,
        (hidden_grad, first, middle, gain, grad_out, proj),
        [
            rows_of(hidden_grad),
            whole(first),
            rows_of(middle),
            whole(gain),
            rows_of(grad_out),
            whole(proj),
        ],
        outs + [line] * 3,
        [rows_of(item) for item in outs] + [whole(line)] * 3,
        after,
        grid=(length // ROWS,),
        cost=(2 * length * (first.size + proj.size), 24 * 2**20, 0),
        name="middle_back",
    )


def input_back_kernel(parts, tokens_ref, gain_ref, weight_ref, middle_grad_ref, *refs):
    pieces, (out_ref, gain_sum, bias_sum) = refs[: 3 * parts], refs[3 * parts :]
    joined = jnp.concatenate([piece[...] for piece in pieces], axis=1)
    grads = dot_nt(joined, weight_ref[...])
    hat, spread = norm_rows(tokens_ref[...].astype(jnp.float32))
    back, gain_line, bias_line = norm_back(
        grads, gain_ref[...].astype(jnp.float32), hat, spread
    )
    out_ref[...] = (middle_grad_ref[...] + back).astype(jnp.bfloat16)
    add_lines((gain_sum, bias_sum), (gain_line, bias_line))


def input_back(tokens, gain, weight, middle_grad, pieces, after=()):
    length = tokens.shape[0]
    line = floats(1, D)
    out = halves(length, D)
    return ordered_call(
        functools.partial(input_back_kernel, len(pieces) // 3),
        (tokens, gain, weight, middle_grad, *pieces),
        [rows_of(tokens), whole(gain), whole(weight), rows_of(middle_grad)]
        + [rows_of(item) for item in pieces],
        [out, line, line],
        [rows_of(out), whole(line), whole(line)],
        after,
        grid=(length // ROWS,),
        cost=(2 * length * weight.size, 16 * 2**20, 0),
        name="input_back",
    )


def block_out_kernel(active_ref, weight_ref, shift_ref, middle_ref, out_ref):
    out_ref[...] = (
        middle_ref[...]
        + (dot_nn(active_ref[...], weight_ref[...]) + shift_ref[...].astype(jnp.float32))
    ).astype(jnp.bfloat16)


def block_out_rows(active, weight, shift, middle, after=()):
    length = middle.shape[0]
    out = halves(length, D)
    return ordered_call(
        block_out_kernel,
        (active, weight, shift, middle),
        [rows_of(active), whole(weight), whole(shift), rows_of(middle)],
        [out],
        [rows_of(out)],
        after,
        grid=(length // ROWS,),
        cost=(2 * length * weight.size, 16 * 2**20, 0),
        name="block_out",
    )


def on_device(
    tokens,
    out_grad,
    image_counts,
    group_of_device,
    group_weight,
    norm1_gain,
    norm1_bias,
    qkv_weight,
    qkv_bias,
    proj_weight,
    proj_bias,
    norm2_gain,
    norm2_bias,
    fc1_weight,
    fc1_bias,
    fc2_weight,
    fc2_bias,
    first_moment,
    second_moment,
):
    count = lax.axis_size("dp")
    core = lax.axis_index("grp")
    own = lax.axis_index("dp")
    info = jnp.stack([core, own])
    length = tokens.shape[0]
    counts_row = image_counts[0]
    segment, valid_rows = segment_info(counts_row, length)
    seg_col, seg_row = segment[:, None], segment[None, :]
    pad_start = jnp.sum(counts_row, keepdims=True)
    factor = device_factor(counts_row, group_of_device, group_weight).reshape(1)
    gain_one, shift_one, qkv_shift, proj_shift, gain_two, shift_two, fc1_shift, fc2_shift = (
        item.reshape(1, -1)
        for item in (
            norm1_gain,
            norm1_bias,
            qkv_bias,
            proj_bias,
            norm2_gain,
            norm2_bias,
            fc1_bias,
            fc2_bias,
        )
    )
    grad_out = jnp.where(valid_rows[:, None], out_grad, jnp.zeros_like(out_grad))

    normed_one, projected, _ = first_part(tokens, gain_one, shift_one, qkv_weight, qkv_shift)
    context, weights, scales, _ = attn_forward(projected, seg_col, seg_row, pad_start)
    middle, normed_two, _ = second_part(
        tokens, context, proj_weight, proj_shift, gain_two, shift_two
    )
    active, grad_hidden, _ = mlp_part(normed_two, grad_out, fc1_weight, fc1_shift, fc2_weight)

    mlp_make = functools.partial(
        mlp_grads,
        own=own,
        count=count,
        factor=factor,
        normed=normed_two,
        grad_hidden=grad_hidden,
        active=active,
        grad_out=grad_out,
    )
    sent, token = mlp_make(1 - core)
    came = swap(sent, count)
    middle_grad, branch, context_grad, gain_two_sum, shift_two_sum, proj_bias_sum, token = (
        middle_back(grad_hidden, fc1_weight, middle, gain_two, grad_out, proj_weight, (token,))
    )
    kept, _ = mlp_make(core, after=(token,))
    mlp_steps = reduce_blocks(came, kept)
    next(mlp_steps)
    sending = mlp_steps.send(())
    pieces = []
    wide = D // 128
    third = wide // 3
    for begin in (0, third, 2 * third):
        grads, token = attn_backward(
            projected,
            context,
            context_grad,
            weights,
            scales,
            begin,
            third if begin < 2 * third else wide - begin,
            after=(sending,),
        )
        pieces.append(grads)
        if begin < 2 * third:
            sending = mlp_steps.send((token,))
    last_attend = token
    query_grad, key_grad, value_grad = zip(*pieces)
    input_state = []

    def back_to_input(sending):
        after = () if sending is None else (sending,)
        input_state.extend(
            input_back(
                tokens,
                gain_one,
                qkv_weight,
                middle_grad,
                query_grad + key_grad + value_grad,
                after,
            )
        )
        return input_state[-1]

    mlp_mine, token = finish(mlp_steps, [lambda sending: last_attend, back_to_input], sending)
    input_grad, gain_one_sum, shift_one_sum, _ = input_state
    mlp_parts = (mlp_mine, swap(mlp_mine, count))

    rest_make = functools.partial(
        rest_grads,
        own=own,
        count=count,
        factor=factor,
        normed=normed_one,
        context=context,
        query=query_grad,
        key=key_grad,
        value=value_grad,
        branch=branch,
        vectors=(gain_one_sum, shift_one_sum, proj_bias_sum, gain_two_sum, shift_two_sum),
    )
    sent, token = rest_make(1 - core, after=(token,))
    came = swap(sent, count)
    moments = (first_moment, second_moment)
    total = first_moment.shape[1]
    rest_width = (3 * D * D + D * D + 3 * D + 5 * D) // count
    mlp_width = total - rest_width
    *mlp_lines, mlp_fresh, update_token = update_call(
        functools.partial(mlp_update_kernel, rest_width),
        "mlp_update",
        info,
        *mlp_parts,
        (fc1_weight, fc2_weight),
        (fc1_bias, fc2_bias),
        moments,
        mlp_width,
        MLP_ORDER,
        after=(token,),
    )
    mlp_gathered = lax.all_gather(mlp_fresh, "dp")
    kept, token = rest_make(core, after=(update_token,))
    rest_steps = reduce_blocks(came, kept)
    next(rest_steps)
    sending = rest_steps.send(())
    block_state = []

    def block_rows(sending):
        block_state.extend(
            block_out_rows(active, fc2_weight, fc2_shift, middle, (sending,))
        )
        return block_state[-1]

    rest_mine, _ = finish(rest_steps, [block_rows], sending)
    block_out, _ = block_state
    rest_parts = (rest_mine, swap(rest_mine, count))
    *rest_lines, rest_fresh, token = update_call(
        rest_update_kernel,
        "rest_update",
        info,
        *rest_parts,
        (qkv_weight, proj_weight),
        (norm1_gain, norm1_bias, qkv_bias, proj_bias, norm2_gain, norm2_bias),
        moments,
        rest_width,
        REST_ORDER,
    )
    rest_gather = Gather(rest_fresh)
    mlp_gathered = tie(mlp_gathered, token)
    summed, new_first, new_second, token = join_lines(rest_lines, mlp_lines, (token,))
    mlp_other = swap(mlp_gathered, count)
    after = (token,)
    while rest_gather.position > 2:
        rest_gather.outer(after)
        after = ()
    token = rest_gather.outer(after)
    new_weights, token = assemble(
        info,
        [mlp_gathered],
        [mlp_other],
        None,
        rest_width,
        mlp_width,
        total,
        after=(token,),
    )
    rest_gather.inner((token,))
    rest_gather.others()
    new_weights, _ = assemble(info, *rest_gather.result(), 0, rest_width, total, new_weights)
    summed_bias = mlp_lines[0][0, mlp_width - D // count :]
    return (block_out, input_grad, summed, new_weights, new_first, new_second, summed_bias)


def device_factor(counts_row, group_of_device, group_weight):
    images = jnp.sum((counts_row > 0).astype(jnp.int32))
    member = (group_of_device[0] == lax.iota(jnp.int32, NGROUPS)).astype(jnp.int32)
    totals = member * images
    for position in range((lax.axis_size("grp") * lax.axis_size("dp")).bit_length() - 1):
        totals = totals + swap(totals, 1 << position)
    return jnp.sum(member * group_weight).astype(jnp.float32) / jnp.sum(member * totals).astype(
        jnp.float32
    )


def general_device(
    tokens,
    out_grad,
    image_counts,
    group_of_device,
    group_weight,
    norm1_gain,
    norm1_bias,
    qkv_weight,
    qkv_bias,
    proj_weight,
    proj_bias,
    norm2_gain,
    norm2_bias,
    fc1_weight,
    fc1_bias,
    fc2_weight,
    fc2_bias,
    first_moment,
    second_moment,
):
    length = tokens.shape[0]
    segment, valid_rows = segment_info(image_counts[0], length)
    factor = device_factor(image_counts[0], group_of_device, group_weight)
    inputs = tokens.astype(jnp.float32)
    normed_one, norm_one_back = jax.vjp(
        layer_norm, inputs, norm1_gain.astype(jnp.float32), norm1_bias.astype(jnp.float32)
    )
    normed_one_low = normed_one.astype(jnp.bfloat16)
    projected = (
        jnp.dot(normed_one_low, qkv_weight, preferred_element_type=jnp.float32)
        + qkv_bias.astype(jnp.float32)
    ).astype(jnp.bfloat16)
    seg_col, seg_row = segment[:, None], segment[None, :]
    pad_start = jnp.sum(image_counts[0], keepdims=True)
    context, weights, scales, _ = attn_forward(projected, seg_col, seg_row, pad_start)
    middle = inputs + (
        jnp.dot(context, proj_weight, preferred_element_type=jnp.float32)
        + proj_bias.astype(jnp.float32)
    )
    normed_two, norm_two_back = jax.vjp(
        layer_norm, middle, norm2_gain.astype(jnp.float32), norm2_bias.astype(jnp.float32)
    )
    normed_two_low = normed_two.astype(jnp.bfloat16)
    hidden = jnp.dot(
        normed_two_low, fc1_weight, preferred_element_type=jnp.float32
    ) + fc1_bias.astype(jnp.float32)
    activated, gelu_back = jax.vjp(gelu_tanh, hidden)
    activated_low = activated.astype(jnp.bfloat16)
    block_out = (
        middle
        + (
            jnp.dot(activated_low, fc2_weight, preferred_element_type=jnp.float32)
            + fc2_bias.astype(jnp.float32)
        )
    ).astype(jnp.bfloat16)
    grad_out = out_grad.astype(jnp.float32) * valid_rows[:, None].astype(jnp.float32)
    grad_out_low = grad_out.astype(jnp.bfloat16)
    fc2_grad = contract_rows(activated_low, grad_out_low)
    fc2_bias_grad = jnp.sum(grad_out, axis=0)
    grad_hidden = gelu_back(contract_cols(grad_out_low, fc2_weight))[0].astype(jnp.bfloat16)
    fc1_grad = contract_rows(normed_two_low, grad_hidden)
    fc1_bias_grad = jnp.sum(grad_hidden.astype(jnp.float32), axis=0)
    grad_middle_norm, gain_two_grad, shift_two_grad = norm_two_back(
        contract_cols(grad_hidden, fc1_weight)
    )
    grad_middle = grad_out + grad_middle_norm
    grad_branch = grad_middle.astype(jnp.bfloat16)
    proj_grad = contract_rows(context, grad_branch)
    proj_bias_grad = jnp.sum(grad_branch.astype(jnp.float32), axis=0)
    grad_context = contract_cols(grad_branch, proj_weight).astype(jnp.bfloat16)
    (query_grad, key_grad, value_grad), _ = attn_backward(
        projected, context, grad_context, weights, scales, 0, D // 128
    )
    grad_projected = jnp.concatenate([query_grad, key_grad, value_grad], axis=1)
    qkv_grad = contract_rows(normed_one_low, grad_projected)
    qkv_bias_grad = jnp.sum(grad_projected.astype(jnp.float32), axis=0)
    grad_input_norm, gain_one_grad, shift_one_grad = norm_one_back(
        contract_cols(grad_projected, qkv_weight)
    )
    input_grad = (grad_middle + grad_input_norm).astype(jnp.bfloat16)
    moments = (first_moment, second_moment)
    mlp_summed, rest_summed = exchange_grads(
        (gain_one_grad, shift_one_grad, qkv_grad, qkv_bias_grad, proj_grad, proj_bias_grad),
        (gain_two_grad, shift_two_grad, fc1_grad, fc1_bias_grad, fc2_grad, fc2_bias_grad),
        factor,
    )
    row_count = lax.axis_size("dp")
    own_index = lax.axis_index("dp")
    weight_list = (
        norm1_gain,
        norm1_bias,
        qkv_weight,
        qkv_bias,
        proj_weight,
        proj_bias,
        norm2_gain,
        norm2_bias,
        fc1_weight,
        fc1_bias,
        fc2_weight,
        fc2_bias,
    )
    own_weights = [
        lax.dynamic_slice_in_dim(item.reshape(row_count, -1), own_index, 1, 0)[0]
        for item in weight_list
    ]
    rows = D // row_count
    fc1_sum = mlp_summed[0].reshape(4, rows, D).transpose(1, 0, 2).reshape(-1)
    fc2_sum = mlp_summed[1].reshape(-1)
    qkv_sum = jnp.concatenate(
        [rest_summed[0, :rows], rest_summed[0, rows : 2 * rows], rest_summed[1, :rows]], axis=1
    ).reshape(-1)
    proj_sum = rest_summed[1, rows : 2 * rows].reshape(-1)
    small = rest_summed[0, 2 * rows]
    widths = [item.size // row_count for item in weight_list]
    small_parts = {}
    start = 0
    for index, flag in enumerate(decay_flags):
        if flag == 0.0:
            small_parts[index] = small[start : start + widths[index]]
            start += widths[index]
    large_parts = {2: qkv_sum, 4: proj_sum, 8: fc1_sum, 10: fc2_sum}
    pieces = [
        small_parts[index] if index in small_parts else large_parts[index] for index in range(12)
    ]
    split = sum(widths[:8])
    grads_out, first_out, second_out, fresh = [], [], [], []
    for lead, tail, begin, end in ((8, 12, split, sum(widths)), (0, 8, 0, split)):
        summed_part = jnp.concatenate(pieces[lead:tail])
        current = jnp.concatenate(own_weights[lead:tail]).astype(jnp.float32)
        decay = jnp.concatenate(
            [
                jnp.full((width,), flag, jnp.float32)
                for width, flag in zip(widths[lead:tail], decay_flags[lead:tail])
            ]
        )
        new_first = beta_one * moments[0][0, begin:end] + (1.0 - beta_one) * summed_part
        new_second = (
            beta_two * moments[1][0, begin:end] + (1.0 - beta_two) * summed_part * summed_part
        )
        ratio = (
            new_first
            / (1.0 - beta_one**step_count)
            / (jnp.sqrt(new_second / (1.0 - beta_two**step_count)) + adam_eps)
        )
        fresh_low = (current - learn_rate * (ratio + decay_rate * decay * current)).astype(
            jnp.bfloat16
        )
        grads_out.insert(0, summed_part)
        first_out.insert(0, new_first)
        second_out.insert(0, new_second)
        fresh.insert(0, gather_rows(fresh_low))
    summed = jnp.concatenate(grads_out)[None]
    new_first = jnp.concatenate(first_out)[None]
    new_second = jnp.concatenate(second_out)[None]
    new_weights = jnp.concatenate(fresh, axis=1)
    summed_bias = pieces[11]
    return (block_out, input_grad, summed, new_weights, new_first, new_second, summed_bias)


def bit_of(position):
    return (lax.axis_index("dp") >> position) & 1


def halve(values, position, positions):
    axis = positions.index(position)
    own = bit_of(position)
    sent = lax.dynamic_index_in_dim(values, 1 - own, axis, keepdims=False)
    kept = lax.dynamic_index_in_dim(values, own, axis, keepdims=False)
    return kept, swap(sent, 1 << position), [p for p in positions if p != position]


def reduce_rows(values):
    count = lax.axis_size("dp")
    grp = lax.axis_index("grp")
    kept = lax.dynamic_index_in_dim(values, grp, 0, keepdims=False)
    came = swap(lax.dynamic_index_in_dim(values, 1 - grp, 0, keepdims=False), count)
    kept = add_low(kept, came)
    depth = count.bit_length() - 1
    positions = list(range(depth))[::-1]
    rows = kept.shape[1]
    parts = [kept[:, : rows // 2], kept[:, rows // 2 :]]
    left = [positions, positions]
    parts = [part.reshape((2,) * depth + part.shape[1:]) for part in parts]
    for order in ((0, 1), (1, 0)):
        for index in (0, 1):
            part, came, left[index] = halve(parts[index], order[index], left[index])
            parts[index] = add_low(part, came)
    whole = jnp.concatenate(parts, axis=depth - 2)
    rest = left[0]
    for position in range(2, depth):
        part, came, rest = halve(whole, position, rest)
        if rest:
            whole = add_low(part, came)
        else:
            whole = part.astype(jnp.float32) + came.astype(jnp.float32)
    other = swap(whole, count)
    return jnp.where(grp == 0, jnp.stack([whole, other]), jnp.stack([other, whole]))


def join(own, came, bit):
    return jnp.where(bit == 0, jnp.stack([own, came]), jnp.stack([came, own]))


def gather_rows(values):
    count = lax.axis_size("dp")
    depth = count.bit_length() - 1
    grp = lax.axis_index("grp")
    width = values.shape[0]
    padded = -(-width // 4096) * 4096
    halves = jnp.pad(values, (0, padded - width)).reshape(2, 2, padded // 512, 128)
    own = lax.dynamic_index_in_dim(halves, grp, 0, keepdims=False)
    for position in range(2, depth)[::-1]:
        own = join(own, swap(own, 1 << position), bit_of(position))
    lead = own.ndim - 3
    parts = [lax.index_in_dim(own, i, lead, keepdims=False) for i in (0, 1)]
    for order in ((1, 0), (0, 1)):
        for index in (0, 1):
            position = order[index]
            parts[index] = join(
                parts[index], swap(parts[index], 1 << position), bit_of(position)
            )
    parts[1] = jnp.swapaxes(parts[1], 0, 1)
    full = jnp.stack(parts, axis=depth)
    full = full.transpose(tuple(range(depth))[::-1] + tuple(range(depth, full.ndim)))
    full = full.reshape((count,) + full.shape[depth:])
    other = swap(full, count)
    whole = jnp.where(
        grp == 0, jnp.stack([full, other], axis=1), jnp.stack([other, full], axis=1)
    )
    return whole.reshape(count, padded)[:, :width]


def exchange_grads(front, back, factor):
    gain_one, shift_one, qkv, qkv_bias, proj, proj_bias = front
    gain_two, shift_two, fc1, fc1_bias, fc2, fc2_bias = back
    count = lax.axis_size("dp")
    rows = D // count
    fc1_blocks = fc1.reshape(count, rows, 4, D).transpose(0, 2, 1, 3).reshape(count, 4 * rows, D)
    fc2_blocks = fc2.reshape(count, 4 * rows, D)
    mlp = (jnp.stack([fc1_blocks, fc2_blocks]) * factor).astype(jnp.bfloat16)
    small = jnp.concatenate(
        [
            item.reshape(count, -1)
            for item in (
                gain_one,
                shift_one,
                qkv_bias,
                proj_bias,
                gain_two,
                shift_two,
                fc1_bias,
                fc2_bias,
            )
        ],
        axis=1,
    )
    small = jnp.pad(small, ((0, 0), (0, D - small.shape[1])))[:, None]
    small = jnp.pad(small, ((0, 0), (0, 7), (0, 0)))
    qkv_blocks = qkv.reshape(count, rows, 3, D)
    first_half = jnp.concatenate([qkv_blocks[:, :, 0], qkv_blocks[:, :, 1], small], axis=1)
    second_half = jnp.concatenate(
        [qkv_blocks[:, :, 2], proj.reshape(count, rows, D), jnp.zeros_like(small)], axis=1
    )
    rest = (jnp.stack([first_half, second_half]) * factor).astype(jnp.bfloat16)
    return reduce_rows(mlp), reduce_rows(rest)


def solution(mesh):
    in_specs = (
        P(("grp", "dp"), None),
        P(("grp", "dp"), None),
        P(("grp", "dp"), None),
        P(("grp", "dp")),
        P(),
        P(),
        P(),
        P(),
        P(),
        P(),
        P(),
        P(),
        P(),
        P(),
        P(),
        P(),
        P(),
        P("dp", None),
        P("dp", None),
    )
    out_specs = (
        P(("grp", "dp"), None),
        P(("grp", "dp"), None),
        P("dp", None),
        P(),
        P("dp", None),
        P("dp", None),
        P("dp"),
    )
    rows = D // mesh.shape["dp"]
    return jax.shard_map(
        on_device if rows % 16 == 0 and 8 * rows <= D else general_device, mesh=mesh, in_specs=in_specs, out_specs=out_specs, check_vma=False
    )
```

```python
import functools

import jax
import jax.numpy as jnp
from jax import lax
from jax.experimental import pallas as pl
from jax.experimental.pallas import tpu as pltpu
from jax.sharding import PartitionSpec as P

D = 768
HEADS = 12
HEAD_DIM = 64
NGROUPS = 3


beta_one = 0.9
beta_two = 0.999
adam_eps = 1e-08
decay_rate = 0.05
step_count = 10.0
learn_rate = 0.004 * 0.75**1
norm_eps = 1e-06
neg_fill = -1e30
decay_flags = (0.0, 0.0, 1.0, 0.0, 1.0, 0.0, 0.0, 0.0, 1.0, 0.0, 1.0, 0.0)


def layer_norm(values, gain, shift):
    center = values - jnp.mean(values, axis=-1, keepdims=True)
    spread = jnp.mean(center * center, axis=-1, keepdims=True)
    return center * lax.rsqrt(spread + norm_eps) * gain + shift


def gelu_tanh(values):
    return jax.nn.gelu(values, approximate=True)


def contract_rows(first_op, second_op):
    return lax.dot_general(
        first_op, second_op, (((0,), (0,)), ((), ())), preferred_element_type=jnp.float32
    )


def contract_cols(first_op, second_op):
    return lax.dot_general(
        first_op, second_op, (((1,), (1,)), ((), ())), preferred_element_type=jnp.float32
    )


def segment_info(counts_row, length):
    slots = lax.iota(jnp.int32, counts_row.shape[0])
    segment_ends = jnp.sum(
        jnp.where(slots[:, None] <= slots[None, :], counts_row[:, None], 0), axis=0
    )
    position = lax.iota(jnp.int32, length)
    segment = jnp.sum((position[:, None] >= segment_ends[None, :]).astype(jnp.int32), axis=1)
    return (segment, position < segment_ends[-1])


TILE = 128
WINDOW = 3 * TILE


def window_start(tile, tiles):
    return min(max(tile - 1, 0), tiles - 3) * TILE


def dot_nt(first, second):
    return lax.dot_general(first, second, (((1,), (1,)), ((), ())), preferred_element_type=jnp.float32)


def dot_tn(first, second):
    return lax.dot_general(first, second, (((0,), (0,)), ((), ())), preferred_element_type=jnp.float32)


def dot_nn(first, second):
    return jnp.dot(first, second, preferred_element_type=jnp.float32)


def stack_heads(block, low):
    zero = jnp.zeros_like(block)
    return jnp.concatenate([jnp.where(low, block, zero), jnp.where(low, zero, block)], axis=0)


def merge_heads(block, low):
    return jnp.where(low, block[:TILE], block[TILE:])


def find_segments(counts_ref, seg_col_ref, seg_row_ref):
    slots, length = counts_ref.shape[1], seg_col_ref.shape[0]
    down = lax.broadcasted_iota(jnp.int32, (slots, slots), 0)
    across = lax.broadcasted_iota(jnp.int32, (slots, slots), 1)
    counts = jnp.broadcast_to(counts_ref[...].astype(jnp.float32), (slots, slots))
    ends_col = jnp.sum(jnp.where(across <= down, counts, 0.0), axis=1, keepdims=True)
    ends_row = jnp.sum(jnp.where(across == down, ends_col, 0.0), axis=0, keepdims=True)
    place_col = lax.broadcasted_iota(jnp.int32, (length, slots), 0).astype(jnp.float32)
    place_row = lax.broadcasted_iota(jnp.int32, (slots, length), 1).astype(jnp.float32)
    seg_col_ref[...] = jnp.sum(jnp.where(place_col >= ends_row, 1.0, 0.0), axis=1, keepdims=True)
    seg_row_ref[...] = jnp.sum(jnp.where(place_row >= ends_col, 1.0, 0.0), axis=0, keepdims=True)


def fill_masks(bias_ref, seg_col_ref, seg_row_ref, tiles):
    for tile in range(tiles):
        start = window_start(tile, tiles)
        same = (
            seg_col_ref[tile * TILE : (tile + 1) * TILE, :]
            == seg_row_ref[:, start : start + WINDOW]
        )
        bias_ref[tile] = jnp.where(same, 0.0, neg_fill)


ANYWHERE = pl.BlockSpec(memory_space=pl.ANY)
VMEM_BYTES = 56 * 2**20


VECTORS = {
    "fc1_bias": (0, 3072),
    "gain_one": (3072, 768),
    "shift_one": (3840, 768),
    "qkv_bias": (4608, 2304),
    "proj_bias": (6912, 768),
    "gain_two": (7680, 768),
    "shift_two": (8448, 768),
    "fc2_bias": (9216, 768),
}


def vector_spec(name):
    begin, width = VECTORS[name]
    return pl.BlockSpec((1, width), lambda *_: (0, begin // width))


def ordered_kernel(kernel, first, extra, outs, *refs):
    token = refs[first + extra + outs]
    token[...] = jnp.zeros_like(token)
    kernel(*refs[:first], *refs[first + extra : first + extra + outs], *refs[first + extra + outs + 1 :])


def ordered_call(
    kernel, operands, in_specs, out_shape, out_specs, after=(), grid=(1,), scalars=(), scratch=(),
    cost=(0, 0, 0), aliases=None, name=None, room=56,
):
    call = pl.pallas_call(
        functools.partial(
            ordered_kernel, kernel, len(scalars) + len(operands), len(after), len(out_shape)
        ),
        out_shape=[*out_shape, jax.ShapeDtypeStruct((8, 128), jnp.float32)],
        grid_spec=pltpu.PrefetchScalarGridSpec(
            num_scalar_prefetch=len(scalars),
            grid=grid,
            in_specs=[*in_specs] + [ANYWHERE] * len(after),
            out_specs=[*out_specs, pl.BlockSpec((8, 128), lambda *_: (0, 0))],
            scratch_shapes=list(scratch),
        ),
        input_output_aliases=aliases or {},
        compiler_params=pltpu.CompilerParams(vmem_limit_bytes=room * 2**20),
        cost_estimate=pl.CostEstimate(
            flops=cost[0], bytes_accessed=cost[1], transcendentals=cost[2]
        ),
        name=name,
    )
    return call(*scalars, *operands, *after)


def whole(item):
    return pl.BlockSpec(item.shape, lambda *_: (0,) * len(item.shape))


def floats(*shape):
    return jax.ShapeDtypeStruct(shape, jnp.float32)


def halves(*shape):
    return jax.ShapeDtypeStruct(shape, jnp.bfloat16)


def attn_forward_kernel(
    pad_ref,
    query_ref,
    key_ref,
    value_ref,
    counts_ref,
    out_ref,
    weight_out,
    scale_out,
    bias_ref,
    seg_col_ref,
    seg_row_ref,
):
    length = query_ref.shape[0]
    tiles = length // TILE

    @pl.when(pl.program_id(0) == 0)
    def _():
        find_segments(counts_ref, seg_col_ref, seg_row_ref)
        fill_masks(bias_ref, seg_col_ref, seg_row_ref, tiles)

    low = lax.broadcasted_iota(jnp.int32, (TILE, 128), 1) < 64
    scale = jnp.asarray(0.125, jnp.bfloat16)

    def head_rows(queries, keys, values, bias):
        scores = dot_nt(queries, keys) + bias
        weights = jnp.exp(scores - jnp.max(scores, axis=1, keepdims=True)).astype(jnp.bfloat16)
        ones = jnp.ones((values.shape[0], 128), jnp.bfloat16)
        mixed = dot_nn(weights, jnp.concatenate([values, ones], axis=1))
        inverse = 1.0 / mixed[:, 128:]
        return weights, mixed[:, :128] * inverse, inverse

    for tile in range(tiles):
        span = pl.ds(window_start(tile, tiles), WINDOW)
        rows = slice(tile * TILE, (tile + 1) * TILE)
        queries = query_ref[rows, :] * scale
        zero = jnp.zeros_like(queries)
        first, second = (
            head_rows(part, key_ref[span, :], value_ref[span, :], bias_ref[tile])
            for part in (jnp.where(low, queries, zero), jnp.where(low, zero, queries))
        )
        weight_out[0, tile, 0:TILE, :] = first[0]
        weight_out[0, tile, TILE:, :] = second[0]
        out_ref[rows, :] = jnp.where(low, first[1], second[1]).astype(jnp.bfloat16)
        scale_out[rows, :] = jnp.where(low, first[2], second[2])

    @pl.loop(0, tiles)
    def _(tile):
        start = jnp.minimum(jnp.maximum(tile - 1, 0), tiles - 3) * TILE
        padding = (tile + 1) * TILE > pad_ref[0]
        outside = (pad_ref[0] < start) | (start + WINDOW < length)

        @pl.when(padding & outside)
        def _():
            rows = pl.ds(pl.multiple_of(tile * TILE, TILE), TILE)
            queries = query_ref[rows, :] * scale
            zero = jnp.zeros_like(queries)
            bias = jnp.where(seg_col_ref[rows, :] == seg_row_ref[...], 0.0, neg_fill)
            first, second = (
                head_rows(part, key_ref[...], value_ref[...], bias)
                for part in (jnp.where(low, queries, zero), jnp.where(low, zero, queries))
            )
            out_ref[rows, :] = jnp.where(low, first[1], second[1]).astype(jnp.bfloat16)


def attn_forward(projected, image_counts, pad_start, after=()):
    length, width = projected.shape
    pairs = width // 3 // 128
    tiles = length // TILE

    def part(offset):
        return pl.BlockSpec((length, 128), lambda pair, pad: (0, offset * pairs + pair))

    return ordered_call(
        attn_forward_kernel,
        (projected, projected, projected, image_counts),
        [part(0), part(1), part(2), whole(image_counts)],
        [
            halves(length, width // 3),
            halves(pairs, tiles, 2 * TILE, WINDOW),
            floats(length, width // 3),
        ],
        [
            part(0),
            pl.BlockSpec((1, tiles, 2 * TILE, WINDOW), lambda pair, pad: (pair, 0, 0, 0)),
            part(0),
        ],
        after,
        grid=(pairs,),
        scalars=(pad_start,),
        scratch=[
            pltpu.VMEM((tiles, TILE, WINDOW), jnp.float32),
            pltpu.VMEM((length, 1), jnp.float32),
            pltpu.VMEM((1, length), jnp.float32),
        ],
        cost=(
            16 * length * WINDOW * width // 3,
            14 * length * width // 3,
            length * WINDOW * 12,
        ),
        name="attn_forward",
    )


def attn_backward_kernel(
    query_ref,
    key_ref,
    value_ref,
    context_ref,
    grad_ref,
    weight_ref,
    scale_ref,
    query_out,
    key_out,
    value_out,
    key_sum,
    value_sum,
):
    length = query_ref.shape[0]
    tiles = length // TILE
    low = lax.broadcasted_iota(jnp.int32, (TILE, 128), 1) < 64
    scale = jnp.asarray(0.125, jnp.bfloat16)
    key_sum[...] = jnp.zeros_like(key_sum)
    value_sum[...] = jnp.zeros_like(value_sum)

    for tile in range(tiles):
        rows = slice(tile * TILE, (tile + 1) * TILE)
        span = pl.ds(window_start(tile, tiles), WINDOW)
        queries = stack_heads(query_ref[rows, :] * scale, low)
        scaled = grad_ref[rows, :].astype(jnp.float32) * scale_ref[rows, :]
        product = stack_heads(scaled * context_ref[rows, :].astype(jnp.float32), low)
        delta = jnp.sum(product, axis=1, keepdims=True)
        grads = stack_heads(scaled.astype(jnp.bfloat16), low)
        keys = key_ref[span, :]
        weights = weight_ref[0, tile]
        grad_probs = dot_nt(grads, value_ref[span, :])
        grad_scores = (weights.astype(jnp.float32) * (grad_probs - delta)).astype(jnp.bfloat16)
        query_out[rows, :] = (merge_heads(dot_nn(grad_scores, keys), low) * 0.125).astype(
            jnp.bfloat16
        )
        key_sum[span, :] += dot_tn(grad_scores, queries)
        value_sum[span, :] += dot_tn(weights, grads)
    key_out[...] = key_sum[...].astype(jnp.bfloat16)
    value_out[...] = value_sum[...].astype(jnp.bfloat16)


def attn_backward(projected, context, context_grad, weights, scales, begin, pairs, after=()):
    length, width = projected.shape
    wide = width // 3 // 128
    tiles = length // TILE

    def part(offset):
        return pl.BlockSpec((length, 128), lambda pair: (0, offset * wide + begin + pair))

    out = halves(length, pairs * 128)
    *grads, token = ordered_call(
        attn_backward_kernel,
        (projected, projected, projected, context, context_grad, weights, scales),
        [
            part(0),
            part(1),
            part(2),
            part(0),
            part(0),
            pl.BlockSpec((1, tiles, 2 * TILE, WINDOW), lambda pair: (begin + pair, 0, 0, 0)),
            part(0),
        ],
        [out] * 3,
        [pl.BlockSpec((length, 128), lambda pair: (0, pair))] * 3,
        after,
        grid=(pairs,),
        scratch=[
            pltpu.VMEM((length, 128), jnp.float32),
            pltpu.VMEM((length, 128), jnp.float32),
        ],
        cost=(40 * length * WINDOW * pairs * 128, 16 * length * pairs * 128, 0),
        name="attn_backward",
    )
    return grads, token


AXES = ("grp", "dp")


def swap(values, bit):
    count = lax.axis_size("grp") * lax.axis_size("dp")
    return lax.ppermute(values, AXES, [(i, i ^ bit) for i in range(count)])


def add_low(kept, came):
    return (kept.astype(jnp.float32) + came.astype(jnp.float32)).astype(jnp.bfloat16)


def pick(values, axis, index):
    return lax.index_in_dim(values, index, axis, keepdims=False)


def column_sums(block):
    ones = jnp.ones((8, block.shape[0]), jnp.bfloat16)
    return dot_nn(ones, block)


def mlp_grads_kernel(
    info, factor_ref, normed_ref, hidden_ref, active_ref, grad_ref, out_ref, bias_ref, small_ref
):
    step = pl.program_id(0)
    last = step == pl.num_programs(0) - 1
    own = info[1]
    count = out_ref.shape[0]
    rows = D // count
    factor = factor_ref[0]

    @pl.when(info[0] == 0)
    def _():
        grads = (dot_tn(normed_ref[...], hidden_ref[...]) * factor).astype(jnp.bfloat16)
        place = pl.ds(pl.multiple_of(step * rows, rows), rows)
        for dest in range(count):
            out_ref[dest ^ own, place, :] = grads[dest * rows : (dest + 1) * rows]
        bias_ref[:, pl.ds(pl.multiple_of(step * D, D), D)] = (
            column_sums(hidden_ref[...]) * factor
        )

        @pl.when(last)
        def _():
            small_ref[...] = jnp.zeros_like(small_ref)
            for dest in range(count):
                small_ref[0:1, 0 : 4 * rows] = bias_ref[
                    0:1, dest * 4 * rows : (dest + 1) * 4 * rows
                ]
                out_ref[dest ^ own, 4 * rows :, :] = small_ref[...].astype(jnp.bfloat16)

    @pl.when(info[0] == 1)
    def _():
        grads = (dot_tn(active_ref[...], grad_ref[...]) * factor).astype(jnp.bfloat16)
        per = count // 4
        for part in range(per):
            out_ref[(step * per + part) ^ own, 0 : 4 * rows, :] = grads[
                part * 4 * rows : (part + 1) * 4 * rows
            ]

        @pl.when(last)
        def _():
            bias_ref[:, 0:D] = column_sums(grad_ref[...]) * factor
            small_ref[...] = jnp.zeros_like(small_ref)
            for dest in range(count):
                small_ref[0:1, 0:rows] = bias_ref[0:1, dest * rows : (dest + 1) * rows]
                out_ref[dest ^ own, 4 * rows :, :] = small_ref[...].astype(jnp.bfloat16)


def mlp_grads(half, own, count, factor, normed, grad_hidden, active, grad_out, after=()):
    length = normed.shape[0]
    rows = D // count
    steps = grad_hidden.shape[1] // D
    shape = (count, 4 * rows + 8, D)
    return ordered_call(
        mlp_grads_kernel,
        (factor, normed, grad_hidden, active, grad_out),
        [
            pl.BlockSpec(memory_space=pltpu.SMEM),
            whole(normed),
            pl.BlockSpec((length, D), lambda i, info: (0, i * (1 - info[0]))),
            pl.BlockSpec((length, D), lambda i, info: (0, i * info[0])),
            whole(grad_out),
        ],
        [jax.ShapeDtypeStruct(shape, jnp.bfloat16)],
        [pl.BlockSpec(shape, lambda *_: (0, 0, 0))],
        after,
        grid=(steps,),
        scalars=(jnp.stack([half, own]),),
        scratch=[pltpu.VMEM((8, steps * D), jnp.float32), pltpu.VMEM((8, D), jnp.float32)],
        cost=(6 * length * D * D * steps, 16 * 2**20, 0),
        name="mlp_grads",
    )


def rest_grads_kernel(parts, info, factor_ref, normed_ref, context_ref, *refs):
    query_refs, refs = refs[:parts], refs[parts:]
    key_refs, refs = refs[:parts], refs[parts:]
    value_refs, refs = refs[:parts], refs[parts:]
    branch_ref, gain_one_ref, shift_one_ref, proj_bias_ref, gain_two_ref, shift_two_ref = refs[:6]
    out_ref, bias_ref, small_ref = refs[-3:]
    step = pl.program_id(0)
    own = info[1]
    count = out_ref.shape[0]
    rows = D // count
    factor = factor_ref[0]

    def block(first_ref, second_refs, position):
        begin = 0
        for second_ref in second_refs:
            end = begin + second_ref.shape[1]
            grads = (dot_tn(first_ref[...], second_ref[...]) * factor).astype(jnp.bfloat16)
            for dest in range(count):
                out_ref[dest ^ own, position * rows : (position + 1) * rows, begin:end] = grads[
                    dest * rows : (dest + 1) * rows
                ]
            begin = end

    @pl.when((info[0] == 0) & (step == 0))
    def _():
        block(normed_ref, query_refs, 0)

    @pl.when((info[0] == 0) & (step == 1))
    def _():
        block(normed_ref, key_refs, 1)
        begin = 0
        for ref in query_refs + key_refs + value_refs:
            end = begin + ref.shape[1]
            bias_ref[:, begin:end] = column_sums(ref[...])
            begin = end
        small_ref[...] = jnp.zeros_like(small_ref)
        for dest in range(count):
            part = slice(dest * rows, (dest + 1) * rows)
            wide = slice(dest * 3 * rows, (dest + 1) * 3 * rows)
            small_ref[0:1, 0:rows] = gain_one_ref[0:1, part]
            small_ref[0:1, rows : 2 * rows] = shift_one_ref[0:1, part]
            small_ref[0:1, 2 * rows : 5 * rows] = bias_ref[0:1, wide]
            small_ref[0:1, 5 * rows : 6 * rows] = proj_bias_ref[0:1, part]
            small_ref[0:1, 6 * rows : 7 * rows] = gain_two_ref[0:1, part]
            small_ref[0:1, 7 * rows : 8 * rows] = shift_two_ref[0:1, part]
            out_ref[dest ^ own, 2 * rows :, :] = (small_ref[...] * factor).astype(jnp.bfloat16)

    @pl.when((info[0] == 1) & (step == 0))
    def _():
        block(normed_ref, value_refs, 0)

    @pl.when((info[0] == 1) & (step == 1))
    def _():
        block(context_ref, (branch_ref,), 1)
        for dest in range(count):
            out_ref[dest, 2 * rows :, :] = jnp.zeros((8, D), jnp.bfloat16)


def rest_grads(
    half, own, count, factor, normed, context, query, key, value, branch, vectors, after=()
):
    length = normed.shape[0]
    rows = D // count
    operands = [normed, context, *query, *key, *value, branch]
    operands += vectors
    shape = (count, 2 * rows + 8, D)
    return ordered_call(
        functools.partial(rest_grads_kernel, len(query)),
        (factor, *operands),
        [pl.BlockSpec(memory_space=pltpu.SMEM)] + [whole(item) for item in operands],
        [jax.ShapeDtypeStruct(shape, jnp.bfloat16)],
        [pl.BlockSpec(shape, lambda *_: (0, 0, 0))],
        after,
        grid=(2,),
        scalars=(jnp.stack([half, own]),),
        scratch=[pltpu.VMEM((8, 3 * D), jnp.float32), pltpu.VMEM((8, D), jnp.float32)],
        cost=(16 * length * D * D, 12 * 2**20, 0),
        name="rest_grads",
    )


def first_split_kernel(cut, kept_ref, came_ref, *refs):
    first_stay, first_away, second_stay, second_away = refs
    for index in range(4):
        low, high = index % 2, index // 2
        target = first_away if low else first_stay
        target[high] = add_low(kept_ref[index, 0:cut, :], came_ref[index, 0:cut, :])
        target = second_away if high else second_stay
        target[low] = add_low(kept_ref[index, cut:, :], came_ref[index, cut:, :])


def first_split(kept, came, cut, after=()):
    count, rows, width = kept.shape
    sizes = (cut, cut, rows - cut, rows - cut)
    return ordered_call(
        functools.partial(first_split_kernel, cut),
        (kept, came),
        [pl.BlockSpec((4, rows, width), lambda i: (i, 0, 0))] * 2,
        [jax.ShapeDtypeStruct((count // 2, size, width), kept.dtype) for size in sizes],
        [pl.BlockSpec((2, size, width), lambda i: (i, 0, 0)) for size in sizes],
        after,
        grid=(count // 4,),
        cost=(count * rows * width, 6 * count * rows * width, 0),
        name="first_split",
        room=20,
    )


def next_split_kernel(parts, *refs):
    outs = refs[-2:] if parts == 1 else refs[-4:]
    for index in range(parts):
        kept_ref, came_ref = refs[2 * index : 2 * index + 2]
        for side in (0, 1):
            outs[2 * index + side][0] = add_low(kept_ref[side], came_ref[side])


def join_split_kernel(cut, *refs):
    first_kept, first_came, second_kept, second_came = refs[:4]
    for side, out in enumerate(refs[-2:]):
        out[0, 0:cut, :] = add_low(first_kept[side], first_came[side])
        out[0, cut:, :] = add_low(second_kept[side], second_came[side])


def next_split(pairs, joined, after=()):
    lead, _, width = pairs[0][0].shape
    heights = [kept.shape[1] for kept, _ in pairs]
    operands = [item for pair in pairs for item in pair]
    sizes = [sum(heights)] * 2 if joined else [size for size in heights for _ in (0, 1)]
    kernel = (
        functools.partial(join_split_kernel, heights[0])
        if joined
        else functools.partial(next_split_kernel, len(pairs))
    )
    total = lead * sum(heights) * width
    return ordered_call(
        kernel,
        operands,
        [pl.BlockSpec((2,) + item.shape[1:], lambda i: (i, 0, 0)) for item in operands],
        [jax.ShapeDtypeStruct((lead // 2, size, width), jnp.bfloat16) for size in sizes],
        [pl.BlockSpec((1, size, width), lambda i: (i, 0, 0)) for size in sizes],
        after,
        grid=(lead // 2,),
        cost=(total, 6 * total, 0),
        name="next_split",
        room=16,
    )


def reduce_blocks(came, kept):
    count = lax.axis_size("dp")
    depth = count.bit_length() - 1
    after = yield None
    cut = (kept.shape[1] - 8) // 2
    first, first_away, second, second_away, token = first_split(kept, came, cut, after)
    pairs = [(first, swap(first_away, 1)), (second, swap(second_away, 2))]
    after = yield token
    first, first_away, second, second_away, token = next_split(pairs, False, after)
    pairs = [(first, swap(first_away, 2)), (second, swap(second_away, 1))]
    after = yield token
    for position in range(2, depth):
        stay, away, token = next_split(pairs, position == 2, after)
        pairs = [(stay, swap(away, 1 << position))]
        after = yield token
    ((stay, came),) = pairs
    return final_sum(stay, came, after)


def finish(steps, works, sending):
    works = list(works)
    while True:
        after = (works.pop(0)(sending),) if works else ()
        try:
            sending = steps.send(after)
        except StopIteration as stop:
            for work in works:
                work(None)
            return stop.value


def final_sum_kernel(kept_ref, came_ref, out_ref):
    out_ref[...] = kept_ref[0].astype(jnp.float32) + came_ref[0].astype(jnp.float32)


def final_sum(kept, came, after=()):
    shape = jax.ShapeDtypeStruct(kept.shape[1:], jnp.float32)
    return ordered_call(
        final_sum_kernel,
        (kept, came),
        [whole(kept), whole(came)],
        [shape],
        [whole(shape)],
        after,
        name="final_sum",
        room=8,
    )


def tie_kernel(*refs):
    pass


def tie(values, *after):
    return pl.pallas_call(
        tie_kernel,
        out_shape=jax.ShapeDtypeStruct(values.shape, values.dtype),
        in_specs=[ANYWHERE] * (1 + len(after)),
        out_specs=ANYWHERE,
        input_output_aliases={0: 0},
        name="tie",
    )(values, *after)


def join_kernel(split, *refs):
    sems = refs[-1]
    ins = refs[: 2 if split else 4]
    outs = refs[len(ins) : -1]
    copies = []
    for index, out in enumerate(outs):
        for side in (0, 1):
            source = ins[side].at[:, index] if split else ins[2 * index + side]
            place = pl.ds(side * source.shape[0], source.shape[0])
            copies.append(pltpu.make_async_copy(source, out.at[place], sems.at[index, side]))
    for copy in copies:
        copy.start()
    for copy in copies:
        copy.wait()


def join_whole_kernel(first_ref, second_ref, out_ref, sems):
    copies = [
        pltpu.make_async_copy(
            ref, out_ref.at[pl.ds(side * ref.shape[0], ref.shape[0])], sems.at[0, side]
        )
        for side, ref in enumerate((first_ref, second_ref))
    ]
    for copy in copies:
        copy.start()
    for copy in copies:
        copy.wait()


def join_blocks(pairs, after=(), split=False):
    operands = [item for pair in pairs for item in pair]
    if split:
        lead, _, *rest = operands[0].shape
        shapes = [(2 * lead, *rest)] * 2
    else:
        shapes = [(2 * pair[0].shape[0], *pair[0].shape[1:]) for pair in pairs]
    shapes = [jax.ShapeDtypeStruct(shape, jnp.bfloat16) for shape in shapes]
    return ordered_call(
        join_whole_kernel if len(shapes) == 1 else functools.partial(join_kernel, split),
        operands,
        [ANYWHERE] * len(operands),
        shapes,
        [whole(shape) for shape in shapes],
        after,
        scratch=[pltpu.SemaphoreType.DMA((2, 2))],
        cost=(0, 4 * sum(shape.size for shape in shapes), 0),
        name="join_blocks",
        room=16,
    )


class Gather:
    def __init__(self, values):
        self.depth = lax.axis_size("dp").bit_length() - 1
        self.block = values.reshape(1, 2, -1, 128)
        self.slots = [0]
        self.position = self.depth - 1
        self.came = swap(self.block, 1 << self.position)

    def _grow(self, slots, position):
        return slots + [slot ^ (1 << position) for slot in slots]

    def outer(self, after=()):
        self.slots = self._grow(self.slots, self.position)
        if self.position > 2:
            self.block, token = join_blocks([(self.block, self.came)], after)
            self.position -= 1
            self.came = swap(self.block, 1 << self.position)
            return token
        *self.parts, token = join_blocks([(self.block, self.came)], after, split=True)
        self.came = [swap(self.parts[0], 2), swap(self.parts[1], 1)]
        return token

    def inner(self, after=()):
        *self.parts, token = join_blocks(list(zip(self.parts, self.came)), after)
        self.came = [swap(self.parts[0], 1), swap(self.parts[1], 2)]
        return token

    def others(self):
        count = lax.axis_size("dp")
        self.parts_other = [swap(part, count) for part in self.parts]

    def result(self, after=()):
        count = lax.axis_size("dp")
        came = [tie(item, *after) for item in self.came] if after else self.came
        came_other = [swap(item, count) for item in came]
        names = [self._grow(self.slots, 1), self._grow(self.slots, 0)]
        lists = []
        for name, bit in zip(names, (1, 2)):
            lists += [name, [slot ^ bit for slot in name]]
        arrays = [self.parts[0], came[0], self.parts[1], came[1]]
        others = [self.parts_other[0], came_other[0], self.parts_other[1], came_other[1]]
        return arrays, others, lists


def place(target, source_ref, rows, offset):
    row, lane = divmod(offset, 128)
    if lane == 0:
        target[row : row + rows, :] = source_ref[0:rows, :]
        return
    rolled = pltpu.roll(source_ref[0:rows, :], lane, 1)
    lanes = lax.broadcasted_iota(jnp.int32, (rows, 128), 1)
    target[row : row + rows, :] = jnp.where(lanes >= lane, rolled, target[row : row + rows, :])
    target[row + 1 : row + 1 + rows, :] = jnp.where(
        lanes < lane, rolled, target[row + 1 : row + 1 + rows, :]
    )


def place_line(target, line, offset):
    start, width = 0, line.shape[1]
    while start < width:
        row, lane = divmod(offset + start, 128)
        step = min(128 - lane, width - start)
        target[row : row + 1, lane : lane + step] = line[:, start : start + step]
        start += step


def spread(target, block, first, stride):
    for piece in range(block.shape[1] // 128):
        target[pl.ds(first + piece, block.shape[0], stride=stride), :] = block[
            :, piece * 128 : (piece + 1) * 128
        ]


def adam_rows(grads_ref, current_ref, first_ref, second_ref, outs, fresh_ref, start, width, plain):
    sum_out, first_out, second_out = outs

    def update(grads, current, old_first, old_second, position):
        new_first = beta_one * old_first + (1.0 - beta_one) * grads
        new_second = beta_two * old_second + (1.0 - beta_two) * grads * grads
        ratio = (
            new_first
            / (1.0 - beta_one**step_count)
            / (jnp.sqrt(new_second / (1.0 - beta_two**step_count)) + adam_eps)
        )
        decays = jnp.ones(grads.shape, jnp.bool_)
        for low, high in plain:
            decays = decays & ((position < low) | (position >= high))
        decay = jnp.where(decays, decay_rate, 0.0)
        fresh = current - learn_rate * (ratio + decay * current)
        return new_first, new_second, fresh

    group = 64
    loops = width // (group * 128)

    @pl.loop(0, loops)
    def _(index):
        rows = pl.ds(pl.multiple_of(index * group, group), group)
        begin = pl.multiple_of(index * (group * 128), 1024)
        there = pl.ds(pl.multiple_of(start + begin, 128), group * 128)
        here = pl.ds(begin, group * 128)
        shape = (group, 128)
        position = (
            begin
            + lax.broadcasted_iota(jnp.int32, shape, 0) * 128
            + lax.broadcasted_iota(jnp.int32, shape, 1)
        )
        grads = grads_ref[rows, :]
        new_first, new_second, fresh = update(
            grads,
            current_ref[rows, :],
            first_ref[0:1, there].reshape(shape),
            second_ref[0:1, there].reshape(shape),
            position,
        )
        sum_out[0:1, here] = grads.reshape(1, group * 128)
        first_out[0:1, here] = new_first.reshape(1, group * 128)
        second_out[0:1, here] = new_second.reshape(1, group * 128)
        fresh_ref[rows, :] = fresh

    begin = loops * group * 128
    while begin < width:
        size = min(128, width - begin)
        row = begin // 128
        grads = grads_ref[row : row + 1, 0:size]
        position = begin + lax.broadcasted_iota(jnp.int32, (1, size), 1)
        new_first, new_second, fresh = update(
            grads,
            current_ref[row : row + 1, 0:size],
            first_ref[0:1, start + begin : start + begin + size],
            second_ref[0:1, start + begin : start + begin + size],
            position,
        )
        sum_out[0:1, begin : begin + size] = grads
        first_out[0:1, begin : begin + size] = new_first
        second_out[0:1, begin : begin + size] = new_second
        fresh_ref[row : row + 1, 0:size] = fresh
        begin += size


def own_lines(target, info, count, lines, part_widths, offsets):
    for dest in range(count):

        @pl.when(info[1] == dest)
        def _():
            for line, width, offset in zip(lines, part_widths, offsets):
                place_line(
                    target,
                    line[:, dest * width : (dest + 1) * width].astype(jnp.float32),
                    offset,
                )


def send_half(info, fresh_ref, fresh_out):
    rows = fresh_out.shape[0]
    fresh_out[...] = fresh_ref[pl.ds(pl.multiple_of(info[0] * rows, 16), rows), :].astype(
        jnp.bfloat16
    )


def mlp_update_kernel(
    start,
    info,
    mine_ref,
    other_ref,
    fc1_ref,
    fc1_bias_ref,
    fc2_ref,
    fc2_bias_ref,
    first_ref,
    second_ref,
    sum_out,
    first_out,
    second_out,
    fresh_out,
    grads_ref,
    current_ref,
    fresh_ref,
    line_ref,
):
    rows = fc1_ref.shape[0]
    count = D // rows
    tiles = D // 128
    large = rows * 4 * D
    second = large + 4 * rows
    end = second + large

    def fill(fc1_half, fc2_half):
        for part in range(4):
            spread(
                grads_ref, fc1_half[part * rows : (part + 1) * rows, :], part * tiles, 4 * tiles
            )
        spread(line_ref, fc2_half[0 : 4 * rows, :], 0, tiles)
        place(grads_ref, line_ref, large // 128, second)
        place_line(grads_ref, fc1_half[4 * rows : 4 * rows + 1, 0 : 4 * rows], large)
        place_line(grads_ref, fc2_half[4 * rows : 4 * rows + 1, 0:rows], end)

    @pl.when(info[0] == 0)
    def _():
        fill(mine_ref, other_ref)

    @pl.when(info[0] != 0)
    def _():
        fill(other_ref, mine_ref)

    spread(current_ref, fc1_ref[...].astype(jnp.float32), 0, 4 * tiles)
    spread(line_ref, fc2_ref[...].astype(jnp.float32), 0, tiles)
    place(current_ref, line_ref, large // 128, second)
    own_lines(
        current_ref,
        info,
        count,
        (fc1_bias_ref[...], fc2_bias_ref[...]),
        (4 * rows, rows),
        (large, end),
    )
    adam_rows(
        grads_ref,
        current_ref,
        first_ref,
        second_ref,
        (sum_out, first_out, second_out),
        fresh_ref,
        start,
        end + rows,
        ((large, second), (end, end + rows)),
    )
    send_half(info, fresh_ref, fresh_out)


def rest_update_kernel(
    info,
    mine_ref,
    other_ref,
    qkv_ref,
    proj_ref,
    gain_one_ref,
    shift_one_ref,
    qkv_bias_ref,
    proj_bias_ref,
    gain_two_ref,
    shift_two_ref,
    first_ref,
    second_ref,
    sum_out,
    first_out,
    second_out,
    fresh_out,
    grads_ref,
    current_ref,
    fresh_ref,
    line_ref,
):
    rows = qkv_ref.shape[0]
    count = D // rows
    tiles = D // 128
    qkv_at = 2 * rows
    qkv_bias_at = qkv_at + 3 * rows * D
    proj_at = qkv_bias_at + 3 * rows
    proj_bias_at = proj_at + rows * D
    end = proj_bias_at + 3 * rows
    small = (0, rows, qkv_bias_at, proj_bias_at, proj_bias_at + rows, proj_bias_at + 2 * rows)
    widths = (rows, rows, 3 * rows, rows, rows, rows)

    def fill(first_half, second_half):
        spread(line_ref, first_half[0:rows, :], 0, 3 * tiles)
        spread(line_ref, first_half[rows : 2 * rows, :], tiles, 3 * tiles)
        spread(line_ref, second_half[0:rows, :], 2 * tiles, 3 * tiles)
        place(grads_ref, line_ref, 3 * rows * tiles, qkv_at)
        spread(line_ref, second_half[rows : 2 * rows, :], 0, tiles)
        place(grads_ref, line_ref, rows * tiles, proj_at)
        begin = 0
        for width, offset in zip(widths, small):
            place_line(
                grads_ref, first_half[2 * rows : 2 * rows + 1, begin : begin + width], offset
            )
            begin += width

    @pl.when(info[0] == 0)
    def _():
        fill(mine_ref, other_ref)

    @pl.when(info[0] != 0)
    def _():
        fill(other_ref, mine_ref)

    spread(line_ref, qkv_ref[...].astype(jnp.float32), 0, 3 * tiles)
    place(current_ref, line_ref, 3 * rows * tiles, qkv_at)
    spread(line_ref, proj_ref[...].astype(jnp.float32), 0, tiles)
    place(current_ref, line_ref, rows * tiles, proj_at)
    lines = (
        gain_one_ref[...],
        shift_one_ref[...],
        qkv_bias_ref[...],
        proj_bias_ref[...],
        gain_two_ref[...],
        shift_two_ref[...],
    )
    own_lines(current_ref, info, count, lines, widths, small)
    adam_rows(
        grads_ref,
        current_ref,
        first_ref,
        second_ref,
        (sum_out, first_out, second_out),
        fresh_ref,
        0,
        end,
        ((0, qkv_at), (qkv_bias_at, proj_at), (proj_bias_at, end)),
    )
    send_half(info, fresh_ref, fresh_out)


def update_call(
    kernel, name, info, mine, other, matrices, small, moments, width, order, after=()
):
    count = lax.axis_size("dp")
    half_rows = -(-width // 4096) * 16
    tall = 2 * half_rows

    operands = {("half", 0): (mine, whole(mine)), ("half", 1): (other, whole(other))}
    for index, item in enumerate(matrices):
        operands["matrix", index] = (
            item,
            pl.BlockSpec((item.shape[0] // count, item.shape[1]), lambda i, info: (info[1], 0)),
        )
    for index, item in enumerate(small[1:]):
        operands["small", index] = (small[0], vector_spec(item))
    for index, item in enumerate(moments):
        operands["moment", index] = (item, whole(item))
    chosen = [operands[key] for key in order]
    line = jax.ShapeDtypeStruct((1, width), jnp.float32)
    half_out = jax.ShapeDtypeStruct((half_rows, 128), jnp.bfloat16)
    return ordered_call(
        kernel,
        [item for item, _ in chosen],
        [spec for _, spec in chosen],
        [line, line, line, half_out],
        [whole(line)] * 3 + [whole(half_out)],
        after,
        scalars=(info,),
        scratch=[pltpu.VMEM((tall + 8, 128), jnp.float32) for _ in range(4)],
        cost=(2**20, 24 * 2**20, 0),
        name=name,
        room=36,
    )


def assemble_kernel(lists, start, width, extra, info, *refs):
    each = 1 if lists is None else 4
    mine, other = refs[0:each], refs[each : 2 * each]
    refs = refs[2 * each + extra :]
    out_ref, refs = refs[0], refs[1:]
    tail = width % 128
    if tail:
        tail_ref, refs = refs[0], refs[1:]
    held, wide, in_sems, out_sems = refs
    count, rows = held.shape[1], held.shape[2]

    def pieces(segment):
        part = segment % 2
        if lists is None:
            whole_part = pl.ds(part * rows, rows)
            return [(lambda refs: refs[0].at[:, whole_part], held.at[segment], 0)]
        found = []
        for index in range(count):
            array, slot = divmod(index, count // 2)
            array += 2 * part
            target = held.at[segment, lists[array][slot] ^ info[1]]
            found.append(
                (lambda refs, array=array, slot=slot: refs[array].at[slot], target, index)
            )
        return found

    def arrivals(segment, begin):
        for source, target, index in pieces(segment):

            def copy(refs):
                return pltpu.make_async_copy(source(refs), target, in_sems.at[segment, index])

            if begin:

                @pl.when(info[0] == segment // 2)
                def _():
                    copy(mine).start()

                @pl.when(info[0] != segment // 2)
                def _():
                    copy(other).start()

            else:
                copy(mine).wait()

    def departure(segment):
        length = min(rows * 128, width - tail - segment * rows * 128)
        return pltpu.make_async_copy(
            wide.at[segment % 2, :, pl.ds(0, length)],
            out_ref.at[:, pl.ds(start + segment * rows * 128, length)],
            out_sems.at[segment],
        )

    for segment in range(4):
        arrivals(segment, True)
    for segment in range(4):
        arrivals(segment, False)
        if segment >= 2:
            departure(segment - 2).wait()
        wide[segment % 2] = held[segment].reshape(count, rows * 128)
        departure(segment).start()
        if segment == 3 and tail:
            at = width - tail - segment * rows * 128
            tail_ref[...] = wide[segment % 2, :, at : at + 128]
    departure(2).wait()
    departure(3).wait()


def fill_tail_kernel(source_ref, target_ref, out_ref):
    out_ref[...] = source_ref[...]


def fill_tail(target, source, token):
    last = target.shape[1] // 128
    return ordered_call(
        fill_tail_kernel,
        (source, target),
        [whole(source), ANYWHERE],
        [jax.ShapeDtypeStruct(target.shape, target.dtype)],
        [pl.BlockSpec(source.shape, lambda *_: (0, last))],
        (token,),
        aliases={1: 0},
        name="fill_tail",
        room=4,
    )


def assemble(info, arrays, others, lists, start, width, total, target=None, after=()):
    count = lax.axis_size("dp")
    rows = arrays[0].shape[1] // (2 if lists is None else 1)
    aliased = 0 if target is None else 1
    tail = width % 128
    out_shape = [jax.ShapeDtypeStruct((count, total), jnp.bfloat16)]
    out_specs = [ANYWHERE]
    if tail:
        out_shape.append(jax.ShapeDtypeStruct((count, 128), jnp.bfloat16))
        out_specs.append(whole(out_shape[-1]))
    operands = (*arrays, *others, *(() if target is None else (target,)))
    *outs, token = ordered_call(
        functools.partial(assemble_kernel, lists, start, width, aliased),
        operands,
        [ANYWHERE] * len(operands),
        out_shape,
        out_specs,
        after,
        scalars=(info,),
        scratch=[
            pltpu.VMEM((4, count, rows, 128), jnp.bfloat16),
            pltpu.VMEM((2, count, rows * 128), jnp.bfloat16),
            pltpu.SemaphoreType.DMA((4, count)),
            pltpu.SemaphoreType.DMA((4,)),
        ],
        cost=(2**20, 4 * count * width, 0),
        aliases={len(operands): 0} if aliased else {},
        name="assemble",
        room=28,
    )
    if tail:
        return fill_tail(*outs, token)
    return outs[0], token


def join_lines_kernel(*refs):
    for index in range(3):
        low, high, out = refs[index], refs[3 + index], refs[6 + index]
        width = low.shape[1]
        out[0:1, 0:width] = low[...]
        out[0:1, width:] = high[...]


def join_lines(lows, highs, after=()):
    operands = (*lows, *highs)
    line = jax.ShapeDtypeStruct((1, lows[0].shape[1] + highs[0].shape[1]), jnp.float32)
    return ordered_call(
        join_lines_kernel,
        operands,
        [whole(item) for item in operands],
        [line] * 3,
        [whole(line)] * 3,
        after,
        cost=(0, 24 * line.size, 0),
        name="join_lines",
        room=30,
    )


MLP_ORDER = (
    ("half", 0),
    ("half", 1),
    ("matrix", 0),
    ("small", 0),
    ("matrix", 1),
    ("small", 1),
    ("moment", 0),
    ("moment", 1),
)
REST_ORDER = (
    (("half", 0), ("half", 1), ("matrix", 0), ("matrix", 1))
    + tuple(("small", index) for index in range(6))
    + (("moment", 0), ("moment", 1))
)


ROWS = 256


def norm_rows(values):
    center = values - jnp.mean(values, axis=-1, keepdims=True)
    spread = lax.rsqrt(jnp.mean(center * center, axis=-1, keepdims=True) + norm_eps)
    return center * spread, spread


def norm_back(grads, gain, hat, spread):
    scaled = grads * gain
    inner = scaled - jnp.mean(scaled, axis=-1, keepdims=True)
    inner = inner - hat * jnp.mean(scaled * hat, axis=-1, keepdims=True)
    return (
        spread * inner,
        jnp.sum(grads * hat, axis=0, keepdims=True),
        jnp.sum(grads, axis=0, keepdims=True),
    )


def add_lines(refs, lines):
    first = pl.program_id(0) == 0

    @pl.when(first)
    def _():
        for ref, line in zip(refs, lines):
            ref[...] = line

    @pl.when(jnp.logical_not(first))
    def _():
        for ref, line in zip(refs, lines):
            ref[...] += line


def rows_of(item):
    return pl.BlockSpec((ROWS, item.shape[1]), lambda i, *_: (i, 0))


def first_part_kernel(
    pad_ref,
    tokens_ref,
    grad_ref,
    gain_ref,
    bias_ref,
    weight_ref,
    shift_ref,
    normed_out,
    out_ref,
    grad_out,
):
    hat, _ = norm_rows(tokens_ref[...].astype(jnp.float32))
    normed = (
        hat * gain_ref[...].astype(jnp.float32) + bias_ref[...].astype(jnp.float32)
    ).astype(jnp.bfloat16)
    normed_out[...] = normed
    out_ref[...] = (
        dot_nn(normed, weight_ref[...]) + shift_ref[...].astype(jnp.float32)
    ).astype(jnp.bfloat16)
    row = pl.program_id(0) * ROWS + lax.broadcasted_iota(jnp.int32, grad_ref.shape, 0)
    grads = grad_ref[...].astype(jnp.float32)
    grad_out[...] = jnp.where(row < pad_ref[0], grads, 0.0).astype(jnp.bfloat16)


def first_part(tokens, out_grad, vectors, weight, pad_start):
    length = tokens.shape[0]
    outs = [halves(length, D), halves(length, weight.shape[1]), halves(length, D)]
    return ordered_call(
        first_part_kernel,
        (tokens, out_grad, vectors, vectors, weight, vectors),
        [
            rows_of(tokens),
            rows_of(out_grad),
            vector_spec("gain_one"),
            vector_spec("shift_one"),
            whole(weight),
            vector_spec("qkv_bias"),
        ],
        outs,
        [rows_of(item) for item in outs],
        grid=(length // ROWS,),
        scalars=(pad_start,),
        cost=(2 * length * weight.size, 8 * 2**20, 0),
        name="norm_qkv",
    )


def second_part_kernel(
    tokens_ref, context_ref, weight_ref, shift_ref, gain_ref, bias_ref, middle_out, normed_out
):
    middle = tokens_ref[...].astype(jnp.float32) + (
        dot_nn(context_ref[...], weight_ref[...]) + shift_ref[...].astype(jnp.float32)
    )
    middle_out[...] = middle
    hat, _ = norm_rows(middle)
    normed_out[...] = (
        hat * gain_ref[...].astype(jnp.float32) + bias_ref[...].astype(jnp.float32)
    ).astype(jnp.bfloat16)


def second_part(tokens, context, weight, vectors, after=()):
    length = tokens.shape[0]
    outs = [floats(length, D), halves(length, D)]
    return ordered_call(
        second_part_kernel,
        (tokens, context, weight, vectors, vectors, vectors),
        [
            rows_of(tokens),
            rows_of(context),
            whole(weight),
            vector_spec("proj_bias"),
            vector_spec("gain_two"),
            vector_spec("shift_two"),
        ],
        outs,
        [rows_of(item) for item in outs],
        after,
        grid=(length // ROWS,),
        cost=(2 * length * weight.size, 8 * 2**20, 0),
        name="proj_norm",
    )


def mlp_part_kernel(
    normed_ref, grad_ref, first_ref, shift_ref, second_ref, active_out, hidden_grad_out
):
    root = 0.7978845608028654
    for begin in range(0, normed_ref.shape[0], ROWS):
        rows = slice(begin, begin + ROWS)
        hidden = dot_nn(normed_ref[rows, :], first_ref[...]) + shift_ref[...].astype(jnp.float32)
        grad_active = dot_nt(grad_ref[rows, :], second_ref[...])
        square = hidden * hidden
        slope = jnp.tanh(hidden * (root + (root * 0.044715) * square))
        half = 0.5 + 0.5 * slope
        active_out[rows, :] = (hidden * half).astype(jnp.bfloat16)
        rise = half + (0.5 * hidden) * (1.0 - slope * slope) * (
            root + (3.0 * root * 0.044715) * square
        )
        hidden_grad_out[rows, :] = (grad_active * rise).astype(jnp.bfloat16)


def mlp_part(normed, grad_out, first, vectors, second, after=()):
    length, width = normed.shape[0], first.shape[1]
    step = D
    columns = pl.BlockSpec((length, step), lambda i: (0, i))
    outs = [halves(length, width)] * 2
    return ordered_call(
        mlp_part_kernel,
        (normed, grad_out, first, vectors, second),
        [
            whole(normed),
            whole(grad_out),
            pl.BlockSpec((D, step), lambda i: (0, i)),
            pl.BlockSpec((1, step), lambda i: (0, i)),
            pl.BlockSpec((step, D), lambda i: (i, 0)),
        ],
        outs,
        [columns, columns],
        after,
        grid=(width // step,),
        cost=(4 * length * D * width, 24 * 2**20, length * width),
        name="mlp_part",
    )


def middle_back_kernel(
    hidden_grad_ref,
    first_ref,
    middle_ref,
    gain_ref,
    grad_out_ref,
    proj_ref,
    middle_grad_out,
    branch_out,
    context_grad_out,
    gain_sum,
    bias_sum,
    proj_bias_sum,
):
    grads = dot_nt(hidden_grad_ref[...], first_ref[...])
    hat, spread = norm_rows(middle_ref[...])
    back, gain_line, bias_line = norm_back(
        grads, gain_ref[...].astype(jnp.float32), hat, spread
    )
    middle_grad = grad_out_ref[...].astype(jnp.float32) + back
    middle_grad_out[...] = middle_grad
    branch = middle_grad.astype(jnp.bfloat16)
    branch_out[...] = branch
    context_grad_out[...] = dot_nt(branch, proj_ref[...]).astype(jnp.bfloat16)
    proj_line = jnp.sum(branch.astype(jnp.float32), axis=0, keepdims=True)
    add_lines((gain_sum, bias_sum, proj_bias_sum), (gain_line, bias_line, proj_line))


def middle_back(hidden_grad, first, middle, vectors, grad_out, proj, after=()):
    length = middle.shape[0]
    line = floats(1, D)
    outs = [floats(length, D), halves(length, D), halves(length, D)]
    return ordered_call(
        middle_back_kernel,
        (hidden_grad, first, middle, vectors, grad_out, proj),
        [
            rows_of(hidden_grad),
            whole(first),
            rows_of(middle),
            vector_spec("gain_two"),
            rows_of(grad_out),
            whole(proj),
        ],
        outs + [line] * 3,
        [rows_of(item) for item in outs] + [whole(line)] * 3,
        after,
        grid=(length // ROWS,),
        cost=(2 * length * (first.size + proj.size), 24 * 2**20, 0),
        name="middle_back",
    )


def input_back_kernel(parts, tokens_ref, gain_ref, weight_ref, middle_grad_ref, *refs):
    pieces, (out_ref, gain_sum, bias_sum) = refs[: 3 * parts], refs[3 * parts :]
    joined = jnp.concatenate([piece[...] for piece in pieces], axis=1)
    grads = dot_nt(joined, weight_ref[...])
    hat, spread = norm_rows(tokens_ref[...].astype(jnp.float32))
    back, gain_line, bias_line = norm_back(
        grads, gain_ref[...].astype(jnp.float32), hat, spread
    )
    out_ref[...] = (middle_grad_ref[...] + back).astype(jnp.bfloat16)
    add_lines((gain_sum, bias_sum), (gain_line, bias_line))


def input_back(tokens, vectors, weight, middle_grad, pieces, after=()):
    length = tokens.shape[0]
    line = floats(1, D)
    out = halves(length, D)
    return ordered_call(
        functools.partial(input_back_kernel, len(pieces) // 3),
        (tokens, vectors, weight, middle_grad, *pieces),
        [rows_of(tokens), vector_spec("gain_one"), whole(weight), rows_of(middle_grad)]
        + [rows_of(item) for item in pieces],
        [out, line, line],
        [rows_of(out), whole(line), whole(line)],
        after,
        grid=(length // ROWS,),
        cost=(2 * length * weight.size, 16 * 2**20, 0),
        name="input_back",
    )


def block_out_kernel(active_ref, weight_ref, shift_ref, middle_ref, out_ref):
    out_ref[...] = (
        middle_ref[...]
        + (dot_nn(active_ref[...], weight_ref[...]) + shift_ref[...].astype(jnp.float32))
    ).astype(jnp.bfloat16)


def block_out_rows(active, weight, vectors, middle, after=()):
    length = middle.shape[0]
    out = halves(length, D)
    return ordered_call(
        block_out_kernel,
        (active, weight, vectors, middle),
        [rows_of(active), whole(weight), vector_spec("fc2_bias"), rows_of(middle)],
        [out],
        [rows_of(out)],
        after,
        grid=(length // ROWS,),
        cost=(2 * length * weight.size, 16 * 2**20, 0),
        name="block_out",
    )


def on_device(
    tokens,
    out_grad,
    image_counts,
    group_of_device,
    group_weight,
    norm1_gain,
    norm1_bias,
    qkv_weight,
    qkv_bias,
    proj_weight,
    proj_bias,
    norm2_gain,
    norm2_bias,
    fc1_weight,
    fc1_bias,
    fc2_weight,
    fc2_bias,
    first_moment,
    second_moment,
):
    count = lax.axis_size("dp")
    core = lax.axis_index("grp")
    own = lax.axis_index("dp")
    info = jnp.stack([core, own])
    pad_start = jnp.sum(image_counts[0], keepdims=True)
    vectors = jnp.concatenate(
        [
            fc1_bias,
            norm1_gain,
            norm1_bias,
            qkv_bias,
            proj_bias,
            norm2_gain,
            norm2_bias,
            fc2_bias,
        ]
    ).reshape(1, -1)
    member = (group_of_device[0] == lax.iota(jnp.int32, 128)).astype(jnp.float32)
    images = jnp.sum((image_counts[0] > 0).astype(jnp.float32))
    totals = jnp.broadcast_to(member * images, (8, 128))
    bits = iter([1 << place for place in range((2 * count).bit_length() - 1)])

    def count_on(totals, *after):
        return add_totals(totals, swap(totals, next(bits)), after)

    normed_one, projected, grad_out, token = first_part(
        tokens, out_grad, vectors, qkv_weight, pad_start
    )
    totals, token = count_on(totals, token)
    context, weights, scales, token = attn_forward(projected, image_counts, pad_start, (token,))
    totals, token = count_on(totals, token)
    middle, normed_two, token = second_part(tokens, context, proj_weight, vectors, (token,))
    totals, token = count_on(totals, token)
    active, grad_hidden, token = mlp_part(
        normed_two, grad_out, fc1_weight, vectors, fc2_weight, (token,)
    )
    totals, token = count_on(totals, token)
    for _ in range((2 * count).bit_length() - 5):
        totals, token = count_on(totals, token)
    share = jnp.sum(member[:NGROUPS] * group_weight.astype(jnp.float32))
    factor = (share / jnp.sum(member * totals[0])).reshape(1)

    mlp_make = functools.partial(
        mlp_grads,
        own=own,
        count=count,
        factor=factor,
        normed=normed_two,
        grad_hidden=grad_hidden,
        active=active,
        grad_out=grad_out,
    )
    sent, token = mlp_make(1 - core)
    came = swap(sent, count)
    kept, _ = mlp_make(core, after=(token,))
    mlp_steps = reduce_blocks(came, kept)
    next(mlp_steps)
    sending = mlp_steps.send(())
    middle_grad, branch, context_grad, gain_two_sum, shift_two_sum, proj_bias_sum, token = (
        middle_back(grad_hidden, fc1_weight, middle, vectors, grad_out, proj_weight, (sending,))
    )
    wide = D // 128
    (query_grad, key_grad, value_grad), token = attn_backward(
        projected, context, context_grad, weights, scales, 0, wide, (token,)
    )
    sending = mlp_steps.send((token,))
    input_grad, gain_one_sum, shift_one_sum, token = input_back(
        tokens,
        vectors,
        qkv_weight,
        middle_grad,
        (query_grad, key_grad, value_grad),
        (sending,),
    )
    sending = mlp_steps.send((token,))
    rest_make = functools.partial(
        rest_grads,
        own=own,
        count=count,
        factor=factor,
        normed=normed_one,
        context=context,
        query=(query_grad,),
        key=(key_grad,),
        value=(value_grad,),
        branch=branch,
        vectors=(gain_one_sum, shift_one_sum, proj_bias_sum, gain_two_sum, shift_two_sum),
    )
    rest_sent, rest_token = rest_make(1 - core, after=(sending,))
    rest_kept = []

    def keep_rest(sending):
        kept, token = rest_make(core, after=(rest_token,) if sending is None else (sending,))
        rest_kept.append(kept)
        return token

    mlp_mine, token = finish(mlp_steps, [lambda sending: rest_token, keep_rest], sending)
    mlp_parts = (mlp_mine, swap(mlp_mine, count))
    came = swap(tie(rest_sent, token), count)
    moments = (first_moment, second_moment)
    total = first_moment.shape[1]
    rest_width = (3 * D * D + D * D + 3 * D + 5 * D) // count
    mlp_width = total - rest_width
    *mlp_lines, mlp_fresh, update_token = update_call(
        functools.partial(mlp_update_kernel, rest_width),
        "mlp_update",
        info,
        *mlp_parts,
        (fc1_weight, fc2_weight),
        (vectors, "fc1_bias", "fc2_bias"),
        moments,
        mlp_width,
        MLP_ORDER,
    )
    mlp_gathered = lax.all_gather(mlp_fresh, "dp")
    rest_steps = reduce_blocks(came, rest_kept[0])
    next(rest_steps)
    sending = rest_steps.send((update_token,))
    block_state = []

    def block_rows(sending):
        block_state.extend(
            block_out_rows(active, fc2_weight, vectors, middle, (sending,))
        )
        return block_state[-1]

    rest_mine, _ = finish(rest_steps, [block_rows], sending)
    block_out, _ = block_state
    rest_parts = (rest_mine, swap(rest_mine, count))
    *rest_lines, rest_fresh, token = update_call(
        rest_update_kernel,
        "rest_update",
        info,
        *rest_parts,
        (qkv_weight, proj_weight),
        (vectors, "gain_one", "shift_one", "qkv_bias", "proj_bias", "gain_two", "shift_two"),
        moments,
        rest_width,
        REST_ORDER,
    )
    rest_gather = Gather(rest_fresh)
    mlp_gathered = tie(mlp_gathered, token)
    summed, new_first, new_second, token = join_lines(rest_lines, mlp_lines, (token,))
    mlp_other = swap(mlp_gathered, count)
    after = (token,)
    while rest_gather.position > 2:
        rest_gather.outer(after)
        after = ()
    token = rest_gather.outer(after)
    new_weights, token = assemble(
        info,
        [mlp_gathered],
        [mlp_other],
        None,
        rest_width,
        mlp_width,
        total,
        after=(token,),
    )
    rest_gather.inner((token,))
    rest_gather.others()
    new_weights, _ = assemble(info, *rest_gather.result(), 0, rest_width, total, new_weights)
    summed_bias = mlp_lines[0][0, mlp_width - D // count :]
    return (block_out, input_grad, summed, new_weights, new_first, new_second, summed_bias)


def add_totals_kernel(first_ref, second_ref, out_ref):
    out_ref[...] = first_ref[...] + second_ref[...]


def add_totals(first, second, after=()):
    return ordered_call(
        add_totals_kernel,
        (first, second),
        [whole(first), whole(second)],
        [floats(*first.shape)],
        [whole(first)],
        after,
        name="add_totals",
        room=4,
    )


def device_factor(counts_row, group_of_device, group_weight):
    images = jnp.sum((counts_row > 0).astype(jnp.int32))
    member = (group_of_device[0] == lax.iota(jnp.int32, NGROUPS)).astype(jnp.int32)
    totals = member * images
    for position in range((lax.axis_size("grp") * lax.axis_size("dp")).bit_length() - 1):
        totals = totals + swap(totals, 1 << position)
    return jnp.sum(member * group_weight).astype(jnp.float32) / jnp.sum(member * totals).astype(
        jnp.float32
    )


def general_device(
    tokens,
    out_grad,
    image_counts,
    group_of_device,
    group_weight,
    norm1_gain,
    norm1_bias,
    qkv_weight,
    qkv_bias,
    proj_weight,
    proj_bias,
    norm2_gain,
    norm2_bias,
    fc1_weight,
    fc1_bias,
    fc2_weight,
    fc2_bias,
    first_moment,
    second_moment,
):
    length = tokens.shape[0]
    segment, valid_rows = segment_info(image_counts[0], length)
    factor = device_factor(image_counts[0], group_of_device, group_weight)
    inputs = tokens.astype(jnp.float32)
    normed_one, norm_one_back = jax.vjp(
        layer_norm, inputs, norm1_gain.astype(jnp.float32), norm1_bias.astype(jnp.float32)
    )
    normed_one_low = normed_one.astype(jnp.bfloat16)
    projected = (
        jnp.dot(normed_one_low, qkv_weight, preferred_element_type=jnp.float32)
        + qkv_bias.astype(jnp.float32)
    ).astype(jnp.bfloat16)
    pad_start = jnp.sum(image_counts[0], keepdims=True)
    context, weights, scales, _ = attn_forward(projected, image_counts, pad_start)
    middle = inputs + (
        jnp.dot(context, proj_weight, preferred_element_type=jnp.float32)
        + proj_bias.astype(jnp.float32)
    )
    normed_two, norm_two_back = jax.vjp(
        layer_norm, middle, norm2_gain.astype(jnp.float32), norm2_bias.astype(jnp.float32)
    )
    normed_two_low = normed_two.astype(jnp.bfloat16)
    hidden = jnp.dot(
        normed_two_low, fc1_weight, preferred_element_type=jnp.float32
    ) + fc1_bias.astype(jnp.float32)
    activated, gelu_back = jax.vjp(gelu_tanh, hidden)
    activated_low = activated.astype(jnp.bfloat16)
    block_out = (
        middle
        + (
            jnp.dot(activated_low, fc2_weight, preferred_element_type=jnp.float32)
            + fc2_bias.astype(jnp.float32)
        )
    ).astype(jnp.bfloat16)
    grad_out = out_grad.astype(jnp.float32) * valid_rows[:, None].astype(jnp.float32)
    grad_out_low = grad_out.astype(jnp.bfloat16)
    fc2_grad = contract_rows(activated_low, grad_out_low)
    fc2_bias_grad = jnp.sum(grad_out, axis=0)
    grad_hidden = gelu_back(contract_cols(grad_out_low, fc2_weight))[0].astype(jnp.bfloat16)
    fc1_grad = contract_rows(normed_two_low, grad_hidden)
    fc1_bias_grad = jnp.sum(grad_hidden.astype(jnp.float32), axis=0)
    grad_middle_norm, gain_two_grad, shift_two_grad = norm_two_back(
        contract_cols(grad_hidden, fc1_weight)
    )
    grad_middle = grad_out + grad_middle_norm
    grad_branch = grad_middle.astype(jnp.bfloat16)
    proj_grad = contract_rows(context, grad_branch)
    proj_bias_grad = jnp.sum(grad_branch.astype(jnp.float32), axis=0)
    grad_context = contract_cols(grad_branch, proj_weight).astype(jnp.bfloat16)
    (query_grad, key_grad, value_grad), _ = attn_backward(
        projected, context, grad_context, weights, scales, 0, D // 128
    )
    grad_projected = jnp.concatenate([query_grad, key_grad, value_grad], axis=1)
    qkv_grad = contract_rows(normed_one_low, grad_projected)
    qkv_bias_grad = jnp.sum(grad_projected.astype(jnp.float32), axis=0)
    grad_input_norm, gain_one_grad, shift_one_grad = norm_one_back(
        contract_cols(grad_projected, qkv_weight)
    )
    input_grad = (grad_middle + grad_input_norm).astype(jnp.bfloat16)
    moments = (first_moment, second_moment)
    mlp_summed, rest_summed = exchange_grads(
        (gain_one_grad, shift_one_grad, qkv_grad, qkv_bias_grad, proj_grad, proj_bias_grad),
        (gain_two_grad, shift_two_grad, fc1_grad, fc1_bias_grad, fc2_grad, fc2_bias_grad),
        factor,
    )
    row_count = lax.axis_size("dp")
    own_index = lax.axis_index("dp")
    weight_list = (
        norm1_gain,
        norm1_bias,
        qkv_weight,
        qkv_bias,
        proj_weight,
        proj_bias,
        norm2_gain,
        norm2_bias,
        fc1_weight,
        fc1_bias,
        fc2_weight,
        fc2_bias,
    )
    own_weights = [
        lax.dynamic_slice_in_dim(item.reshape(row_count, -1), own_index, 1, 0)[0]
        for item in weight_list
    ]
    rows = D // row_count
    fc1_sum = mlp_summed[0].reshape(4, rows, D).transpose(1, 0, 2).reshape(-1)
    fc2_sum = mlp_summed[1].reshape(-1)
    qkv_sum = jnp.concatenate(
        [rest_summed[0, :rows], rest_summed[0, rows : 2 * rows], rest_summed[1, :rows]], axis=1
    ).reshape(-1)
    proj_sum = rest_summed[1, rows : 2 * rows].reshape(-1)
    small = rest_summed[0, 2 * rows]
    widths = [item.size // row_count for item in weight_list]
    small_parts = {}
    start = 0
    for index, flag in enumerate(decay_flags):
        if flag == 0.0:
            small_parts[index] = small[start : start + widths[index]]
            start += widths[index]
    large_parts = {2: qkv_sum, 4: proj_sum, 8: fc1_sum, 10: fc2_sum}
    pieces = [
        small_parts[index] if index in small_parts else large_parts[index] for index in range(12)
    ]
    split = sum(widths[:8])
    grads_out, first_out, second_out, fresh = [], [], [], []
    for lead, tail, begin, end in ((8, 12, split, sum(widths)), (0, 8, 0, split)):
        summed_part = jnp.concatenate(pieces[lead:tail])
        current = jnp.concatenate(own_weights[lead:tail]).astype(jnp.float32)
        decay = jnp.concatenate(
            [
                jnp.full((width,), flag, jnp.float32)
                for width, flag in zip(widths[lead:tail], decay_flags[lead:tail])
            ]
        )
        new_first = beta_one * moments[0][0, begin:end] + (1.0 - beta_one) * summed_part
        new_second = (
            beta_two * moments[1][0, begin:end] + (1.0 - beta_two) * summed_part * summed_part
        )
        ratio = (
            new_first
            / (1.0 - beta_one**step_count)
            / (jnp.sqrt(new_second / (1.0 - beta_two**step_count)) + adam_eps)
        )
        fresh_low = (current - learn_rate * (ratio + decay_rate * decay * current)).astype(
            jnp.bfloat16
        )
        grads_out.insert(0, summed_part)
        first_out.insert(0, new_first)
        second_out.insert(0, new_second)
        fresh.insert(0, gather_rows(fresh_low))
    summed = jnp.concatenate(grads_out)[None]
    new_first = jnp.concatenate(first_out)[None]
    new_second = jnp.concatenate(second_out)[None]
    new_weights = jnp.concatenate(fresh, axis=1)
    summed_bias = pieces[11]
    return (block_out, input_grad, summed, new_weights, new_first, new_second, summed_bias)


def bit_of(position):
    return (lax.axis_index("dp") >> position) & 1


def halve(values, position, positions):
    axis = positions.index(position)
    own = bit_of(position)
    sent = lax.dynamic_index_in_dim(values, 1 - own, axis, keepdims=False)
    kept = lax.dynamic_index_in_dim(values, own, axis, keepdims=False)
    return kept, swap(sent, 1 << position), [p for p in positions if p != position]


def reduce_rows(values):
    count = lax.axis_size("dp")
    grp = lax.axis_index("grp")
    kept = lax.dynamic_index_in_dim(values, grp, 0, keepdims=False)
    came = swap(lax.dynamic_index_in_dim(values, 1 - grp, 0, keepdims=False), count)
    kept = add_low(kept, came)
    depth = count.bit_length() - 1
    positions = list(range(depth))[::-1]
    rows = kept.shape[1]
    parts = [kept[:, : rows // 2], kept[:, rows // 2 :]]
    left = [positions, positions]
    parts = [part.reshape((2,) * depth + part.shape[1:]) for part in parts]
    for order in ((0, 1), (1, 0)):
        for index in (0, 1):
            part, came, left[index] = halve(parts[index], order[index], left[index])
            parts[index] = add_low(part, came)
    whole = jnp.concatenate(parts, axis=depth - 2)
    rest = left[0]
    for position in range(2, depth):
        part, came, rest = halve(whole, position, rest)
        if rest:
            whole = add_low(part, came)
        else:
            whole = part.astype(jnp.float32) + came.astype(jnp.float32)
    other = swap(whole, count)
    return jnp.where(grp == 0, jnp.stack([whole, other]), jnp.stack([other, whole]))


def join(own, came, bit):
    return jnp.where(bit == 0, jnp.stack([own, came]), jnp.stack([came, own]))


def gather_rows(values):
    count = lax.axis_size("dp")
    depth = count.bit_length() - 1
    grp = lax.axis_index("grp")
    width = values.shape[0]
    padded = -(-width // 4096) * 4096
    halves = jnp.pad(values, (0, padded - width)).reshape(2, 2, padded // 512, 128)
    own = lax.dynamic_index_in_dim(halves, grp, 0, keepdims=False)
    for position in range(2, depth)[::-1]:
        own = join(own, swap(own, 1 << position), bit_of(position))
    lead = own.ndim - 3
    parts = [lax.index_in_dim(own, i, lead, keepdims=False) for i in (0, 1)]
    for order in ((1, 0), (0, 1)):
        for index in (0, 1):
            position = order[index]
            parts[index] = join(
                parts[index], swap(parts[index], 1 << position), bit_of(position)
            )
    parts[1] = jnp.swapaxes(parts[1], 0, 1)
    full = jnp.stack(parts, axis=depth)
    full = full.transpose(tuple(range(depth))[::-1] + tuple(range(depth, full.ndim)))
    full = full.reshape((count,) + full.shape[depth:])
    other = swap(full, count)
    whole = jnp.where(
        grp == 0, jnp.stack([full, other], axis=1), jnp.stack([other, full], axis=1)
    )
    return whole.reshape(count, padded)[:, :width]


def exchange_grads(front, back, factor):
    gain_one, shift_one, qkv, qkv_bias, proj, proj_bias = front
    gain_two, shift_two, fc1, fc1_bias, fc2, fc2_bias = back
    count = lax.axis_size("dp")
    rows = D // count
    fc1_blocks = fc1.reshape(count, rows, 4, D).transpose(0, 2, 1, 3).reshape(count, 4 * rows, D)
    fc2_blocks = fc2.reshape(count, 4 * rows, D)
    mlp = (jnp.stack([fc1_blocks, fc2_blocks]) * factor).astype(jnp.bfloat16)
    small = jnp.concatenate(
        [
            item.reshape(count, -1)
            for item in (
                gain_one,
                shift_one,
                qkv_bias,
                proj_bias,
                gain_two,
                shift_two,
                fc1_bias,
                fc2_bias,
            )
        ],
        axis=1,
    )
    small = jnp.pad(small, ((0, 0), (0, D - small.shape[1])))[:, None]
    small = jnp.pad(small, ((0, 0), (0, 7), (0, 0)))
    qkv_blocks = qkv.reshape(count, rows, 3, D)
    first_half = jnp.concatenate([qkv_blocks[:, :, 0], qkv_blocks[:, :, 1], small], axis=1)
    second_half = jnp.concatenate(
        [qkv_blocks[:, :, 2], proj.reshape(count, rows, D), jnp.zeros_like(small)], axis=1
    )
    rest = (jnp.stack([first_half, second_half]) * factor).astype(jnp.bfloat16)
    return reduce_rows(mlp), reduce_rows(rest)


def solution(mesh):
    in_specs = (
        P(("grp", "dp"), None),
        P(("grp", "dp"), None),
        P(("grp", "dp"), None),
        P(("grp", "dp")),
        P(),
        P(),
        P(),
        P(),
        P(),
        P(),
        P(),
        P(),
        P(),
        P(),
        P(),
        P(),
        P(),
        P("dp", None),
        P("dp", None),
    )
    out_specs = (
        P(("grp", "dp"), None),
        P(("grp", "dp"), None),
        P("dp", None),
        P(),
        P("dp", None),
        P("dp", None),
        P("dp"),
    )
    rows = D // mesh.shape["dp"]
    return jax.shard_map(
        on_device if rows % 16 == 0 and 8 * rows <= D else general_device, mesh=mesh, in_specs=in_specs, out_specs=out_specs, check_vma=False
    )
```

```python
import functools

import jax
import jax.numpy as jnp
from jax import lax
from jax.experimental import pallas as pl
from jax.experimental.pallas import tpu as pltpu
from jax.sharding import PartitionSpec as P

D = 768
HEADS = 12
HEAD_DIM = 64
NGROUPS = 3


beta_one = 0.9
beta_two = 0.999
adam_eps = 1e-08
decay_rate = 0.05
step_count = 10.0
learn_rate = 0.004 * 0.75**1
norm_eps = 1e-06
neg_fill = -1e30
decay_flags = (0.0, 0.0, 1.0, 0.0, 1.0, 0.0, 0.0, 0.0, 1.0, 0.0, 1.0, 0.0)


def layer_norm(values, gain, shift):
    center = values - jnp.mean(values, axis=-1, keepdims=True)
    spread = jnp.mean(center * center, axis=-1, keepdims=True)
    return center * lax.rsqrt(spread + norm_eps) * gain + shift


def gelu_tanh(values):
    return jax.nn.gelu(values, approximate=True)


def contract_rows(first_op, second_op):
    return lax.dot_general(
        first_op, second_op, (((0,), (0,)), ((), ())), preferred_element_type=jnp.float32
    )


def contract_cols(first_op, second_op):
    return lax.dot_general(
        first_op, second_op, (((1,), (1,)), ((), ())), preferred_element_type=jnp.float32
    )


def segment_info(counts_row, length):
    slots = lax.iota(jnp.int32, counts_row.shape[0])
    segment_ends = jnp.sum(
        jnp.where(slots[:, None] <= slots[None, :], counts_row[:, None], 0), axis=0
    )
    position = lax.iota(jnp.int32, length)
    segment = jnp.sum((position[:, None] >= segment_ends[None, :]).astype(jnp.int32), axis=1)
    return (segment, position < segment_ends[-1])


TILE = 128
WINDOW = 3 * TILE


def window_start(tile, tiles):
    return min(max(tile - 1, 0), tiles - 3) * TILE


def dot_nt(first, second):
    return lax.dot_general(first, second, (((1,), (1,)), ((), ())), preferred_element_type=jnp.float32)


def dot_tn(first, second):
    return lax.dot_general(first, second, (((0,), (0,)), ((), ())), preferred_element_type=jnp.float32)


def dot_nn(first, second):
    return jnp.dot(first, second, preferred_element_type=jnp.float32)


def stack_heads(block, low):
    zero = jnp.zeros_like(block)
    return jnp.concatenate([jnp.where(low, block, zero), jnp.where(low, zero, block)], axis=0)


def merge_heads(block, low):
    return jnp.where(low, block[:TILE], block[TILE:])


def find_segments(counts_ref, seg_col_ref, seg_row_ref):
    slots, length = counts_ref.shape[1], seg_col_ref.shape[0]
    down = lax.broadcasted_iota(jnp.int32, (slots, slots), 0)
    across = lax.broadcasted_iota(jnp.int32, (slots, slots), 1)
    counts = jnp.broadcast_to(counts_ref[...].astype(jnp.float32), (slots, slots))
    ends_col = jnp.sum(jnp.where(across <= down, counts, 0.0), axis=1, keepdims=True)
    ends_row = jnp.sum(jnp.where(across == down, ends_col, 0.0), axis=0, keepdims=True)
    place_col = lax.broadcasted_iota(jnp.int32, (length, slots), 0).astype(jnp.float32)
    place_row = lax.broadcasted_iota(jnp.int32, (slots, length), 1).astype(jnp.float32)
    seg_col_ref[...] = jnp.sum(jnp.where(place_col >= ends_row, 1.0, 0.0), axis=1, keepdims=True)
    seg_row_ref[...] = jnp.sum(jnp.where(place_row >= ends_col, 1.0, 0.0), axis=0, keepdims=True)


def fill_masks(bias_ref, seg_col_ref, seg_row_ref, tiles):
    for tile in range(tiles):
        start = window_start(tile, tiles)
        same = (
            seg_col_ref[tile * TILE : (tile + 1) * TILE, :]
            == seg_row_ref[:, start : start + WINDOW]
        )
        bias_ref[tile] = jnp.where(same, 0.0, neg_fill)


ANYWHERE = pl.BlockSpec(memory_space=pl.ANY)
VMEM_BYTES = 56 * 2**20


VECTORS = {
    "fc1_bias": (0, 3072),
    "gain_one": (3072, 768),
    "shift_one": (3840, 768),
    "qkv_bias": (4608, 2304),
    "proj_bias": (6912, 768),
    "gain_two": (7680, 768),
    "shift_two": (8448, 768),
    "fc2_bias": (9216, 768),
}


def join_vectors_kernel(*refs):
    begin = 0
    for ref in refs[:-1]:
        width = ref.shape[0]
        refs[-1][0:1, begin : begin + width] = ref[...].reshape(1, width)
        begin += width


def join_vectors(*vectors):
    return pl.pallas_call(
        join_vectors_kernel,
        out_shape=halves(1, sum(item.shape[0] for item in vectors)),
        name="join_vectors",
    )(*vectors)


def vector_spec(name):
    begin, width = VECTORS[name]
    return pl.BlockSpec((1, width), lambda *_: (0, begin // width))


def ordered_kernel(kernel, first, extra, outs, *refs):
    token = refs[first + extra + outs]
    token[...] = jnp.zeros_like(token)
    kernel(*refs[:first], *refs[first + extra : first + extra + outs], *refs[first + extra + outs + 1 :])


def ordered_call(
    kernel, operands, in_specs, out_shape, out_specs, after=(), grid=(1,), scalars=(), scratch=(),
    cost=(0, 0, 0), aliases=None, name=None, room=56, far=(),
):
    out_shape = [
        pltpu.HBM(item.shape, item.dtype) if index in far else item
        for index, item in enumerate(out_shape)
    ]
    call = pl.pallas_call(
        functools.partial(
            ordered_kernel, kernel, len(scalars) + len(operands), len(after), len(out_shape)
        ),
        out_shape=[*out_shape, jax.ShapeDtypeStruct((8, 128), jnp.float32)],
        grid_spec=pltpu.PrefetchScalarGridSpec(
            num_scalar_prefetch=len(scalars),
            grid=grid,
            in_specs=[*in_specs] + [ANYWHERE] * len(after),
            out_specs=[*out_specs, pl.BlockSpec((8, 128), lambda *_: (0, 0))],
            scratch_shapes=list(scratch),
        ),
        input_output_aliases=aliases or {},
        compiler_params=pltpu.CompilerParams(vmem_limit_bytes=room * 2**20),
        cost_estimate=pl.CostEstimate(
            flops=cost[0], bytes_accessed=cost[1], transcendentals=cost[2]
        ),
        name=name,
    )
    return call(*scalars, *operands, *after)


def whole(item):
    return pl.BlockSpec(item.shape, lambda *_: (0,) * len(item.shape))


def floats(*shape):
    return jax.ShapeDtypeStruct(shape, jnp.float32)


def halves(*shape):
    return jax.ShapeDtypeStruct(shape, jnp.bfloat16)


def attn_forward_kernel(
    pad_ref,
    query_ref,
    key_ref,
    value_ref,
    counts_ref,
    out_ref,
    weight_out,
    scale_out,
    bias_ref,
    seg_col_ref,
    seg_row_ref,
):
    length = query_ref.shape[0]
    tiles = length // TILE

    @pl.when(pl.program_id(0) == 0)
    def _():
        find_segments(counts_ref, seg_col_ref, seg_row_ref)
        fill_masks(bias_ref, seg_col_ref, seg_row_ref, tiles)

    low = lax.broadcasted_iota(jnp.int32, (TILE, 128), 1) < 64
    scale = jnp.asarray(0.125, jnp.bfloat16)

    def head_rows(queries, keys, values, bias):
        scores = dot_nt(queries, keys) + bias
        weights = jnp.exp(scores - jnp.max(scores, axis=1, keepdims=True)).astype(jnp.bfloat16)
        ones = jnp.ones((values.shape[0], 128), jnp.bfloat16)
        mixed = dot_nn(weights, jnp.concatenate([values, ones], axis=1))
        inverse = 1.0 / mixed[:, 128:]
        return weights, mixed[:, :128] * inverse, inverse

    for tile in range(tiles):
        span = pl.ds(window_start(tile, tiles), WINDOW)
        rows = slice(tile * TILE, (tile + 1) * TILE)
        queries = query_ref[rows, :] * scale
        zero = jnp.zeros_like(queries)
        first, second = (
            head_rows(part, key_ref[span, :], value_ref[span, :], bias_ref[tile])
            for part in (jnp.where(low, queries, zero), jnp.where(low, zero, queries))
        )
        weight_out[0, tile, 0:TILE, :] = first[0]
        weight_out[0, tile, TILE:, :] = second[0]
        out_ref[rows, :] = jnp.where(low, first[1], second[1]).astype(jnp.bfloat16)
        scale_out[rows, :] = jnp.where(low, first[2], second[2])

    @pl.loop(0, tiles)
    def _(tile):
        start = jnp.minimum(jnp.maximum(tile - 1, 0), tiles - 3) * TILE
        padding = (tile + 1) * TILE > pad_ref[0]
        outside = (pad_ref[0] < start) | (start + WINDOW < length)

        @pl.when(padding & outside)
        def _():
            rows = pl.ds(pl.multiple_of(tile * TILE, TILE), TILE)
            queries = query_ref[rows, :] * scale
            zero = jnp.zeros_like(queries)
            bias = jnp.where(seg_col_ref[rows, :] == seg_row_ref[...], 0.0, neg_fill)
            first, second = (
                head_rows(part, key_ref[...], value_ref[...], bias)
                for part in (jnp.where(low, queries, zero), jnp.where(low, zero, queries))
            )
            out_ref[rows, :] = jnp.where(low, first[1], second[1]).astype(jnp.bfloat16)


def attn_forward(projected, image_counts, pad_start, after=()):
    length, width = projected.shape
    pairs = width // 3 // 128
    tiles = length // TILE

    def part(offset):
        return pl.BlockSpec((length, 128), lambda pair, pad: (0, offset * pairs + pair))

    return ordered_call(
        attn_forward_kernel,
        (projected, projected, projected, image_counts),
        [part(0), part(1), part(2), whole(image_counts)],
        [
            halves(length, width // 3),
            halves(pairs, tiles, 2 * TILE, WINDOW),
            floats(length, width // 3),
        ],
        [
            part(0),
            pl.BlockSpec((1, tiles, 2 * TILE, WINDOW), lambda pair, pad: (pair, 0, 0, 0)),
            part(0),
        ],
        after,
        grid=(pairs,),
        scalars=(pad_start,),
        scratch=[
            pltpu.VMEM((tiles, TILE, WINDOW), jnp.float32),
            pltpu.VMEM((length, 1), jnp.float32),
            pltpu.VMEM((1, length), jnp.float32),
        ],
        cost=(
            16 * length * WINDOW * width // 3,
            14 * length * width // 3,
            length * WINDOW * 12,
        ),
        name="attn_forward",
        room=16,
        far=(0, 1, 2),
    )


def attn_backward_kernel(
    query_ref,
    key_ref,
    value_ref,
    context_ref,
    grad_ref,
    weight_ref,
    scale_ref,
    query_out,
    key_out,
    value_out,
    key_sum,
    value_sum,
):
    length = query_ref.shape[0]
    tiles = length // TILE
    low = lax.broadcasted_iota(jnp.int32, (TILE, 128), 1) < 64
    scale = jnp.asarray(0.125, jnp.bfloat16)
    key_sum[...] = jnp.zeros_like(key_sum)
    value_sum[...] = jnp.zeros_like(value_sum)

    for tile in range(tiles):
        rows = slice(tile * TILE, (tile + 1) * TILE)
        span = pl.ds(window_start(tile, tiles), WINDOW)
        queries = stack_heads(query_ref[rows, :] * scale, low)
        scaled = grad_ref[rows, :].astype(jnp.float32) * scale_ref[rows, :]
        product = stack_heads(scaled * context_ref[rows, :].astype(jnp.float32), low)
        delta = jnp.sum(product, axis=1, keepdims=True)
        grads = stack_heads(scaled.astype(jnp.bfloat16), low)
        keys = key_ref[span, :]
        weights = weight_ref[0, tile]
        grad_probs = dot_nt(grads, value_ref[span, :])
        grad_scores = (weights.astype(jnp.float32) * (grad_probs - delta)).astype(jnp.bfloat16)
        query_out[rows, :] = (merge_heads(dot_nn(grad_scores, keys), low) * 0.125).astype(
            jnp.bfloat16
        )
        key_sum[span, :] += dot_tn(grad_scores, queries)
        value_sum[span, :] += dot_tn(weights, grads)
    key_out[...] = key_sum[...].astype(jnp.bfloat16)
    value_out[...] = value_sum[...].astype(jnp.bfloat16)


def attn_backward(projected, context, context_grad, weights, scales, begin, pairs, after=()):
    length, width = projected.shape
    wide = width // 3 // 128
    tiles = length // TILE

    def part(offset):
        return pl.BlockSpec((length, 128), lambda pair: (0, offset * wide + begin + pair))

    out = halves(length, pairs * 128)
    *grads, token = ordered_call(
        attn_backward_kernel,
        (projected, projected, projected, context, context_grad, weights, scales),
        [
            part(0),
            part(1),
            part(2),
            part(0),
            part(0),
            pl.BlockSpec((1, tiles, 2 * TILE, WINDOW), lambda pair: (begin + pair, 0, 0, 0)),
            part(0),
        ],
        [out] * 3,
        [pl.BlockSpec((length, 128), lambda pair: (0, pair))] * 3,
        after,
        grid=(pairs,),
        scratch=[
            pltpu.VMEM((length, 128), jnp.float32),
            pltpu.VMEM((length, 128), jnp.float32),
        ],
        cost=(40 * length * WINDOW * pairs * 128, 16 * length * pairs * 128, 0),
        name="attn_backward",
        room=56,
        far=(0, 1, 2),
    )
    return grads, token


AXES = ("grp", "dp")


def swap(values, bit):
    count = lax.axis_size("grp") * lax.axis_size("dp")
    return lax.ppermute(values, AXES, [(i, i ^ bit) for i in range(count)])


def add_low(kept, came):
    return (kept.astype(jnp.float32) + came.astype(jnp.float32)).astype(jnp.bfloat16)


def pick(values, axis, index):
    return lax.index_in_dim(values, index, axis, keepdims=False)


def column_sums(block):
    ones = jnp.ones((8, block.shape[0]), jnp.bfloat16)
    return dot_nn(ones, block)


def mlp_grads_kernel(
    info, factor_ref, normed_ref, hidden_ref, active_ref, grad_ref, out_ref, bias_ref, small_ref
):
    step = pl.program_id(0)
    last = step == pl.num_programs(0) - 1
    own = info[1]
    count = out_ref.shape[0]
    rows = D // count
    factor = factor_ref[0]

    @pl.when(info[0] == 0)
    def _():
        grads = (dot_tn(normed_ref[...], hidden_ref[...]) * factor).astype(jnp.bfloat16)
        place = pl.ds(pl.multiple_of(step * rows, rows), rows)
        for dest in range(count):
            out_ref[dest ^ own, place, :] = grads[dest * rows : (dest + 1) * rows]
        bias_ref[:, pl.ds(pl.multiple_of(step * D, D), D)] = (
            column_sums(hidden_ref[...]) * factor
        )

        @pl.when(last)
        def _():
            small_ref[...] = jnp.zeros_like(small_ref)
            for dest in range(count):
                small_ref[0:1, 0 : 4 * rows] = bias_ref[
                    0:1, dest * 4 * rows : (dest + 1) * 4 * rows
                ]
                out_ref[dest ^ own, 4 * rows :, :] = small_ref[...].astype(jnp.bfloat16)

    @pl.when(info[0] == 1)
    def _():
        grads = (dot_tn(active_ref[...], grad_ref[...]) * factor).astype(jnp.bfloat16)
        per = count // 4
        for part in range(per):
            out_ref[(step * per + part) ^ own, 0 : 4 * rows, :] = grads[
                part * 4 * rows : (part + 1) * 4 * rows
            ]

        @pl.when(last)
        def _():
            bias_ref[:, 0:D] = column_sums(grad_ref[...]) * factor
            small_ref[...] = jnp.zeros_like(small_ref)
            for dest in range(count):
                small_ref[0:1, 0:rows] = bias_ref[0:1, dest * rows : (dest + 1) * rows]
                out_ref[dest ^ own, 4 * rows :, :] = small_ref[...].astype(jnp.bfloat16)


def mlp_grads(half, own, count, factor, normed, grad_hidden, active, grad_out, after=()):
    length = normed.shape[0]
    rows = D // count
    steps = grad_hidden.shape[1] // D
    shape = (count, 4 * rows + 8, D)
    return ordered_call(
        mlp_grads_kernel,
        (factor, normed, grad_hidden, active, grad_out),
        [
            pl.BlockSpec(memory_space=pltpu.SMEM),
            whole(normed),
            pl.BlockSpec((length, D), lambda i, info: (0, i * (1 - info[0]))),
            pl.BlockSpec((length, D), lambda i, info: (0, i * info[0])),
            whole(grad_out),
        ],
        [jax.ShapeDtypeStruct(shape, jnp.bfloat16)],
        [pl.BlockSpec(shape, lambda *_: (0, 0, 0))],
        after,
        grid=(steps,),
        scalars=(jnp.stack([half, own]),),
        scratch=[pltpu.VMEM((8, steps * D), jnp.float32), pltpu.VMEM((8, D), jnp.float32)],
        cost=(6 * length * D * D * steps, 16 * 2**20, 0),
        name="mlp_grads",
        room=54,
    )


def rest_grads_kernel(parts, info, factor_ref, normed_ref, context_ref, *refs):
    query_refs, refs = refs[:parts], refs[parts:]
    key_refs, refs = refs[:parts], refs[parts:]
    value_refs, refs = refs[:parts], refs[parts:]
    branch_ref, gain_one_ref, shift_one_ref, proj_bias_ref, gain_two_ref, shift_two_ref = refs[:6]
    out_ref, bias_ref, small_ref = refs[-3:]
    step = pl.program_id(0)
    own = info[1]
    count = out_ref.shape[0]
    rows = D // count
    factor = factor_ref[0]

    def block(first_ref, second_refs, position):
        begin = 0
        for second_ref in second_refs:
            end = begin + second_ref.shape[1]
            grads = (dot_tn(first_ref[...], second_ref[...]) * factor).astype(jnp.bfloat16)
            for dest in range(count):
                out_ref[dest ^ own, position * rows : (position + 1) * rows, begin:end] = grads[
                    dest * rows : (dest + 1) * rows
                ]
            begin = end

    @pl.when((info[0] == 0) & (step == 0))
    def _():
        block(normed_ref, query_refs, 0)

    @pl.when((info[0] == 0) & (step == 1))
    def _():
        block(normed_ref, key_refs, 1)
        begin = 0
        for ref in query_refs + key_refs + value_refs:
            end = begin + ref.shape[1]
            bias_ref[:, begin:end] = column_sums(ref[...])
            begin = end
        small_ref[...] = jnp.zeros_like(small_ref)
        for dest in range(count):
            part = slice(dest * rows, (dest + 1) * rows)
            wide = slice(dest * 3 * rows, (dest + 1) * 3 * rows)
            small_ref[0:1, 0:rows] = gain_one_ref[0:1, part]
            small_ref[0:1, rows : 2 * rows] = shift_one_ref[0:1, part]
            small_ref[0:1, 2 * rows : 5 * rows] = bias_ref[0:1, wide]
            small_ref[0:1, 5 * rows : 6 * rows] = proj_bias_ref[0:1, part]
            small_ref[0:1, 6 * rows : 7 * rows] = gain_two_ref[0:1, part]
            small_ref[0:1, 7 * rows : 8 * rows] = shift_two_ref[0:1, part]
            out_ref[dest ^ own, 2 * rows :, :] = (small_ref[...] * factor).astype(jnp.bfloat16)

    @pl.when((info[0] == 1) & (step == 0))
    def _():
        block(normed_ref, value_refs, 0)

    @pl.when((info[0] == 1) & (step == 1))
    def _():
        block(context_ref, (branch_ref,), 1)
        for dest in range(count):
            out_ref[dest, 2 * rows :, :] = jnp.zeros((8, D), jnp.bfloat16)


def rest_grads(
    half, own, count, factor, normed, context, query, key, value, branch, vectors, after=()
):
    length = normed.shape[0]
    rows = D // count
    operands = [normed, context, *query, *key, *value, branch]
    operands += vectors
    shape = (count, 2 * rows + 8, D)
    return ordered_call(
        functools.partial(rest_grads_kernel, len(query)),
        (factor, *operands),
        [pl.BlockSpec(memory_space=pltpu.SMEM)] + [whole(item) for item in operands],
        [jax.ShapeDtypeStruct(shape, jnp.bfloat16)],
        [pl.BlockSpec(shape, lambda *_: (0, 0, 0))],
        after,
        grid=(2,),
        scalars=(jnp.stack([half, own]),),
        scratch=[pltpu.VMEM((8, 3 * D), jnp.float32), pltpu.VMEM((8, D), jnp.float32)],
        cost=(16 * length * D * D, 12 * 2**20, 0),
        name="rest_grads",
        room=36,
    )


def first_split_kernel(cut, kept_ref, came_ref, *refs):
    first_stay, first_away, second_stay, second_away = refs
    for index in range(4):
        low, high = index % 2, index // 2
        target = first_away if low else first_stay
        target[high] = add_low(kept_ref[index, 0:cut, :], came_ref[index, 0:cut, :])
        target = second_away if high else second_stay
        target[low] = add_low(kept_ref[index, cut:, :], came_ref[index, cut:, :])


def first_split(kept, came, cut, after=()):
    count, rows, width = kept.shape
    sizes = (cut, cut, rows - cut, rows - cut)
    return ordered_call(
        functools.partial(first_split_kernel, cut),
        (kept, came),
        [pl.BlockSpec((4, rows, width), lambda i: (i, 0, 0))] * 2,
        [jax.ShapeDtypeStruct((count // 2, size, width), kept.dtype) for size in sizes],
        [pl.BlockSpec((2, size, width), lambda i: (i, 0, 0)) for size in sizes],
        after,
        grid=(count // 4,),
        cost=(count * rows * width, 6 * count * rows * width, 0),
        name="first_split",
        room=20,
        far=(0, 2),
    )


def next_split_kernel(parts, *refs):
    outs = refs[-2:] if parts == 1 else refs[-4:]
    for index in range(parts):
        kept_ref, came_ref = refs[2 * index : 2 * index + 2]
        for side in (0, 1):
            outs[2 * index + side][0] = add_low(kept_ref[side], came_ref[side])


def join_split_kernel(cut, *refs):
    first_kept, first_came, second_kept, second_came = refs[:4]
    for side, out in enumerate(refs[-2:]):
        out[0, 0:cut, :] = add_low(first_kept[side], first_came[side])
        out[0, cut:, :] = add_low(second_kept[side], second_came[side])


def next_split(pairs, joined, after=()):
    lead, _, width = pairs[0][0].shape
    heights = [kept.shape[1] for kept, _ in pairs]
    operands = [item for pair in pairs for item in pair]
    sizes = [sum(heights)] * 2 if joined else [size for size in heights for _ in (0, 1)]
    kernel = (
        functools.partial(join_split_kernel, heights[0])
        if joined
        else functools.partial(next_split_kernel, len(pairs))
    )
    total = lead * sum(heights) * width
    return ordered_call(
        kernel,
        operands,
        [pl.BlockSpec((2,) + item.shape[1:], lambda i: (i, 0, 0)) for item in operands],
        [jax.ShapeDtypeStruct((lead // 2, size, width), jnp.bfloat16) for size in sizes],
        [pl.BlockSpec((1, size, width), lambda i: (i, 0, 0)) for size in sizes],
        after,
        grid=(lead // 2,),
        cost=(total, 6 * total, 0),
        name="next_split",
        room=16,
    )


def reduce_blocks(came, kept):
    count = lax.axis_size("dp")
    depth = count.bit_length() - 1
    after = yield None
    cut = (kept.shape[1] - 8) // 2
    first, first_away, second, second_away, token = first_split(kept, came, cut, after)
    pairs = [(first, swap(first_away, 1)), (second, swap(second_away, 2))]
    after = yield token
    first, first_away, second, second_away, token = next_split(pairs, False, after)
    pairs = [(first, swap(first_away, 2)), (second, swap(second_away, 1))]
    after = yield token
    for position in range(2, depth):
        stay, away, token = next_split(pairs, position == 2, after)
        pairs = [(stay, swap(away, 1 << position))]
        after = yield token
    ((stay, came),) = pairs
    return final_sum(stay, came, after)


def finish(steps, works, sending):
    works = list(works)
    while True:
        after = (works.pop(0)(sending),) if works else ()
        try:
            sending = steps.send(after)
        except StopIteration as stop:
            for work in works:
                work(None)
            return stop.value


def final_sum_kernel(kept_ref, came_ref, out_ref):
    out_ref[...] = kept_ref[0].astype(jnp.float32) + came_ref[0].astype(jnp.float32)


def final_sum(kept, came, after=()):
    shape = jax.ShapeDtypeStruct(kept.shape[1:], jnp.float32)
    return ordered_call(
        final_sum_kernel,
        (kept, came),
        [whole(kept), whole(came)],
        [shape],
        [whole(shape)],
        after,
        name="final_sum",
        room=8,
    )


def tie_kernel(*refs):
    pass


def tie(values, *after):
    return pl.pallas_call(
        tie_kernel,
        out_shape=jax.ShapeDtypeStruct(values.shape, values.dtype),
        in_specs=[ANYWHERE] * (1 + len(after)),
        out_specs=ANYWHERE,
        input_output_aliases={0: 0},
        name="tie",
    )(values, *after)


def join_kernel(split, *refs):
    sems = refs[-1]
    ins = refs[: 2 if split else 4]
    outs = refs[len(ins) : -1]
    copies = []
    for index, out in enumerate(outs):
        for side in (0, 1):
            source = ins[side].at[:, index] if split else ins[2 * index + side]
            place = pl.ds(side * source.shape[0], source.shape[0])
            copies.append(pltpu.make_async_copy(source, out.at[place], sems.at[index, side]))
    for copy in copies:
        copy.start()
    for copy in copies:
        copy.wait()


def join_whole_kernel(first_ref, second_ref, out_ref, sems):
    copies = [
        pltpu.make_async_copy(
            ref, out_ref.at[pl.ds(side * ref.shape[0], ref.shape[0])], sems.at[0, side]
        )
        for side, ref in enumerate((first_ref, second_ref))
    ]
    for copy in copies:
        copy.start()
    for copy in copies:
        copy.wait()


def join_blocks(pairs, after=(), split=False):
    operands = [item for pair in pairs for item in pair]
    if split:
        lead, _, *rest = operands[0].shape
        shapes = [(2 * lead, *rest)] * 2
    else:
        shapes = [(2 * pair[0].shape[0], *pair[0].shape[1:]) for pair in pairs]
    shapes = [jax.ShapeDtypeStruct(shape, jnp.bfloat16) for shape in shapes]
    return ordered_call(
        join_whole_kernel if len(shapes) == 1 else functools.partial(join_kernel, split),
        operands,
        [ANYWHERE] * len(operands),
        shapes,
        [whole(shape) for shape in shapes],
        after,
        scratch=[pltpu.SemaphoreType.DMA((2, 2))],
        cost=(0, 4 * sum(shape.size for shape in shapes), 0),
        name="join_blocks",
        room=16,
    )


class Gather:
    def __init__(self, values):
        self.depth = lax.axis_size("dp").bit_length() - 1
        self.block = values.reshape(1, 2, -1, 128)
        self.slots = [0]
        self.position = self.depth - 1
        self.came = swap(self.block, 1 << self.position)

    def _grow(self, slots, position):
        return slots + [slot ^ (1 << position) for slot in slots]

    def outer(self, after=()):
        self.slots = self._grow(self.slots, self.position)
        if self.position > 2:
            self.block, token = join_blocks([(self.block, self.came)], after)
            self.position -= 1
            self.came = swap(self.block, 1 << self.position)
            return token
        *self.parts, token = join_blocks([(self.block, self.came)], after, split=True)
        self.came = [swap(self.parts[0], 2), swap(self.parts[1], 1)]
        return token

    def inner(self, after=()):
        *self.parts, token = join_blocks(list(zip(self.parts, self.came)), after)
        self.came = [swap(self.parts[0], 1), swap(self.parts[1], 2)]
        return token

    def others(self):
        count = lax.axis_size("dp")
        self.parts_other = [swap(part, count) for part in self.parts]

    def result(self, after=()):
        count = lax.axis_size("dp")
        came = [tie(item, *after) for item in self.came] if after else self.came
        came_other = [swap(item, count) for item in came]
        names = [self._grow(self.slots, 1), self._grow(self.slots, 0)]
        lists = []
        for name, bit in zip(names, (1, 2)):
            lists += [name, [slot ^ bit for slot in name]]
        arrays = [self.parts[0], came[0], self.parts[1], came[1]]
        others = [self.parts_other[0], came_other[0], self.parts_other[1], came_other[1]]
        return arrays, others, lists


def place(target, source_ref, rows, offset):
    row, lane = divmod(offset, 128)
    if lane == 0:
        target[row : row + rows, :] = source_ref[0:rows, :]
        return
    rolled = pltpu.roll(source_ref[0:rows, :], lane, 1)
    lanes = lax.broadcasted_iota(jnp.int32, (rows, 128), 1)
    target[row : row + rows, :] = jnp.where(lanes >= lane, rolled, target[row : row + rows, :])
    target[row + 1 : row + 1 + rows, :] = jnp.where(
        lanes < lane, rolled, target[row + 1 : row + 1 + rows, :]
    )


def place_line(target, line, offset):
    start, width = 0, line.shape[1]
    while start < width:
        row, lane = divmod(offset + start, 128)
        step = min(128 - lane, width - start)
        target[row : row + 1, lane : lane + step] = line[:, start : start + step]
        start += step


def spread(target, block, first, stride):
    for piece in range(block.shape[1] // 128):
        target[pl.ds(first + piece, block.shape[0], stride=stride), :] = block[
            :, piece * 128 : (piece + 1) * 128
        ]


def adam_rows(grads_ref, current_ref, first_ref, second_ref, outs, fresh_ref, start, width, plain):
    sum_out, first_out, second_out = outs

    def update(grads, current, old_first, old_second, position):
        new_first = beta_one * old_first + (1.0 - beta_one) * grads
        new_second = beta_two * old_second + (1.0 - beta_two) * grads * grads
        ratio = (
            new_first
            / (1.0 - beta_one**step_count)
            / (jnp.sqrt(new_second / (1.0 - beta_two**step_count)) + adam_eps)
        )
        decays = jnp.ones(grads.shape, jnp.bool_)
        for low, high in plain:
            decays = decays & ((position < low) | (position >= high))
        decay = jnp.where(decays, decay_rate, 0.0)
        fresh = current - learn_rate * (ratio + decay * current)
        return new_first, new_second, fresh

    group = 64
    loops = width // (group * 128)

    @pl.loop(0, loops)
    def _(index):
        rows = pl.ds(pl.multiple_of(index * group, group), group)
        begin = pl.multiple_of(index * (group * 128), 1024)
        there = pl.ds(pl.multiple_of(start + begin, 128), group * 128)
        here = pl.ds(begin, group * 128)
        shape = (group, 128)
        position = (
            begin
            + lax.broadcasted_iota(jnp.int32, shape, 0) * 128
            + lax.broadcasted_iota(jnp.int32, shape, 1)
        )
        grads = grads_ref[rows, :]
        new_first, new_second, fresh = update(
            grads,
            current_ref[rows, :],
            first_ref[0:1, there].reshape(shape),
            second_ref[0:1, there].reshape(shape),
            position,
        )
        sum_out[0:1, here] = grads.reshape(1, group * 128)
        first_out[0:1, here] = new_first.reshape(1, group * 128)
        second_out[0:1, here] = new_second.reshape(1, group * 128)
        fresh_ref[rows, :] = fresh

    begin = loops * group * 128
    while begin < width:
        size = min(128, width - begin)
        row = begin // 128
        grads = grads_ref[row : row + 1, 0:size]
        position = begin + lax.broadcasted_iota(jnp.int32, (1, size), 1)
        new_first, new_second, fresh = update(
            grads,
            current_ref[row : row + 1, 0:size],
            first_ref[0:1, start + begin : start + begin + size],
            second_ref[0:1, start + begin : start + begin + size],
            position,
        )
        sum_out[0:1, begin : begin + size] = grads
        first_out[0:1, begin : begin + size] = new_first
        second_out[0:1, begin : begin + size] = new_second
        fresh_ref[row : row + 1, 0:size] = fresh
        begin += size


def own_lines(target, info, count, lines, part_widths, offsets):
    for dest in range(count):

        @pl.when(info[1] == dest)
        def _():
            for line, width, offset in zip(lines, part_widths, offsets):
                place_line(
                    target,
                    line[:, dest * width : (dest + 1) * width].astype(jnp.float32),
                    offset,
                )


def send_half(info, fresh_ref, fresh_out):
    rows = fresh_out.shape[0]
    fresh_out[...] = fresh_ref[pl.ds(pl.multiple_of(info[0] * rows, 16), rows), :].astype(
        jnp.bfloat16
    )


def mlp_update_kernel(
    start,
    info,
    mine_ref,
    other_ref,
    fc1_ref,
    fc1_bias_ref,
    fc2_ref,
    fc2_bias_ref,
    first_ref,
    second_ref,
    sum_out,
    first_out,
    second_out,
    fresh_out,
    grads_ref,
    current_ref,
    fresh_ref,
    line_ref,
):
    rows = fc1_ref.shape[0]
    count = D // rows
    tiles = D // 128
    large = rows * 4 * D
    second = large + 4 * rows
    end = second + large

    def fill(fc1_half, fc2_half):
        for part in range(4):
            spread(
                grads_ref, fc1_half[part * rows : (part + 1) * rows, :], part * tiles, 4 * tiles
            )
        spread(line_ref, fc2_half[0 : 4 * rows, :], 0, tiles)
        place(grads_ref, line_ref, large // 128, second)
        place_line(grads_ref, fc1_half[4 * rows : 4 * rows + 1, 0 : 4 * rows], large)
        place_line(grads_ref, fc2_half[4 * rows : 4 * rows + 1, 0:rows], end)

    @pl.when(info[0] == 0)
    def _():
        fill(mine_ref, other_ref)

    @pl.when(info[0] != 0)
    def _():
        fill(other_ref, mine_ref)

    spread(current_ref, fc1_ref[...].astype(jnp.float32), 0, 4 * tiles)
    spread(line_ref, fc2_ref[...].astype(jnp.float32), 0, tiles)
    place(current_ref, line_ref, large // 128, second)
    own_lines(
        current_ref,
        info,
        count,
        (fc1_bias_ref[...], fc2_bias_ref[...]),
        (4 * rows, rows),
        (large, end),
    )
    adam_rows(
        grads_ref,
        current_ref,
        first_ref,
        second_ref,
        (sum_out, first_out, second_out),
        fresh_ref,
        start,
        end + rows,
        ((large, second), (end, end + rows)),
    )
    send_half(info, fresh_ref, fresh_out)


def rest_update_kernel(
    info,
    mine_ref,
    other_ref,
    qkv_ref,
    proj_ref,
    gain_one_ref,
    shift_one_ref,
    qkv_bias_ref,
    proj_bias_ref,
    gain_two_ref,
    shift_two_ref,
    first_ref,
    second_ref,
    sum_out,
    first_out,
    second_out,
    fresh_out,
    grads_ref,
    current_ref,
    fresh_ref,
    line_ref,
):
    rows = qkv_ref.shape[0]
    count = D // rows
    tiles = D // 128
    qkv_at = 2 * rows
    qkv_bias_at = qkv_at + 3 * rows * D
    proj_at = qkv_bias_at + 3 * rows
    proj_bias_at = proj_at + rows * D
    end = proj_bias_at + 3 * rows
    small = (0, rows, qkv_bias_at, proj_bias_at, proj_bias_at + rows, proj_bias_at + 2 * rows)
    widths = (rows, rows, 3 * rows, rows, rows, rows)

    def fill(first_half, second_half):
        spread(line_ref, first_half[0:rows, :], 0, 3 * tiles)
        spread(line_ref, first_half[rows : 2 * rows, :], tiles, 3 * tiles)
        spread(line_ref, second_half[0:rows, :], 2 * tiles, 3 * tiles)
        place(grads_ref, line_ref, 3 * rows * tiles, qkv_at)
        spread(line_ref, second_half[rows : 2 * rows, :], 0, tiles)
        place(grads_ref, line_ref, rows * tiles, proj_at)
        begin = 0
        for width, offset in zip(widths, small):
            place_line(
                grads_ref, first_half[2 * rows : 2 * rows + 1, begin : begin + width], offset
            )
            begin += width

    @pl.when(info[0] == 0)
    def _():
        fill(mine_ref, other_ref)

    @pl.when(info[0] != 0)
    def _():
        fill(other_ref, mine_ref)

    spread(line_ref, qkv_ref[...].astype(jnp.float32), 0, 3 * tiles)
    place(current_ref, line_ref, 3 * rows * tiles, qkv_at)
    spread(line_ref, proj_ref[...].astype(jnp.float32), 0, tiles)
    place(current_ref, line_ref, rows * tiles, proj_at)
    lines = (
        gain_one_ref[...],
        shift_one_ref[...],
        qkv_bias_ref[...],
        proj_bias_ref[...],
        gain_two_ref[...],
        shift_two_ref[...],
    )
    own_lines(current_ref, info, count, lines, widths, small)
    adam_rows(
        grads_ref,
        current_ref,
        first_ref,
        second_ref,
        (sum_out, first_out, second_out),
        fresh_ref,
        0,
        end,
        ((0, qkv_at), (qkv_bias_at, proj_at), (proj_bias_at, end)),
    )
    send_half(info, fresh_ref, fresh_out)


def update_call(
    kernel, name, info, mine, other, matrices, small, moments, width, order, after=()
):
    count = lax.axis_size("dp")
    half_rows = -(-width // 4096) * 16
    tall = 2 * half_rows

    operands = {("half", 0): (mine, whole(mine)), ("half", 1): (other, whole(other))}
    for index, item in enumerate(matrices):
        operands["matrix", index] = (
            item,
            pl.BlockSpec((item.shape[0] // count, item.shape[1]), lambda i, info: (info[1], 0)),
        )
    for index, item in enumerate(small[1:]):
        operands["small", index] = (small[0], vector_spec(item))
    for index, item in enumerate(moments):
        operands["moment", index] = (item, whole(item))
    chosen = [operands[key] for key in order]
    line = jax.ShapeDtypeStruct((1, width), jnp.float32)
    half_out = jax.ShapeDtypeStruct((half_rows, 128), jnp.bfloat16)
    return ordered_call(
        kernel,
        [item for item, _ in chosen],
        [spec for _, spec in chosen],
        [line, line, line, half_out],
        [whole(line)] * 3 + [whole(half_out)],
        after,
        scalars=(info,),
        scratch=[pltpu.VMEM((tall + 8, 128), jnp.float32) for _ in range(4)],
        cost=(2**20, 24 * 2**20, 0),
        name=name,
        room=36,
        far=(0, 1, 2),
    )


def assemble_kernel(lists, start, width, extra, info, *refs):
    each = 1 if lists is None else 4
    mine, other = refs[0:each], refs[each : 2 * each]
    refs = refs[2 * each + extra :]
    out_ref, refs = refs[0], refs[1:]
    tail = width % 128
    if tail:
        tail_ref, refs = refs[0], refs[1:]
    held, wide, in_sems, out_sems = refs
    count, rows = held.shape[1], held.shape[2]

    def pieces(segment):
        part = segment % 2
        if lists is None:
            whole_part = pl.ds(part * rows, rows)
            return [(lambda refs: refs[0].at[:, whole_part], held.at[segment], 0)]
        found = []
        for index in range(count):
            array, slot = divmod(index, count // 2)
            array += 2 * part
            target = held.at[segment, lists[array][slot] ^ info[1]]
            found.append(
                (lambda refs, array=array, slot=slot: refs[array].at[slot], target, index)
            )
        return found

    def arrivals(segment, begin):
        for source, target, index in pieces(segment):

            def copy(refs):
                return pltpu.make_async_copy(source(refs), target, in_sems.at[segment, index])

            if begin:

                @pl.when(info[0] == segment // 2)
                def _():
                    copy(mine).start()

                @pl.when(info[0] != segment // 2)
                def _():
                    copy(other).start()

            else:
                copy(mine).wait()

    def departure(segment):
        length = min(rows * 128, width - tail - segment * rows * 128)
        return pltpu.make_async_copy(
            wide.at[segment % 2, :, pl.ds(0, length)],
            out_ref.at[:, pl.ds(start + segment * rows * 128, length)],
            out_sems.at[segment],
        )

    for segment in range(4):
        arrivals(segment, True)
    for segment in range(4):
        arrivals(segment, False)
        if segment >= 2:
            departure(segment - 2).wait()
        wide[segment % 2] = held[segment].reshape(count, rows * 128)
        departure(segment).start()
        if segment == 3 and tail:
            at = width - tail - segment * rows * 128
            tail_ref[...] = wide[segment % 2, :, at : at + 128]
    departure(2).wait()
    departure(3).wait()


def fill_tail_kernel(source_ref, target_ref, out_ref):
    out_ref[...] = source_ref[...]


def fill_tail(target, source, token):
    last = target.shape[1] // 128
    return ordered_call(
        fill_tail_kernel,
        (source, target),
        [whole(source), ANYWHERE],
        [jax.ShapeDtypeStruct(target.shape, target.dtype)],
        [pl.BlockSpec(source.shape, lambda *_: (0, last))],
        (token,),
        aliases={1: 0},
        name="fill_tail",
        room=4,
    )


def assemble(info, arrays, others, lists, start, width, total, target=None, after=()):
    count = lax.axis_size("dp")
    rows = arrays[0].shape[1] // (2 if lists is None else 1)
    aliased = 0 if target is None else 1
    tail = width % 128
    out_shape = [jax.ShapeDtypeStruct((count, total), jnp.bfloat16)]
    out_specs = [ANYWHERE]
    if tail:
        out_shape.append(jax.ShapeDtypeStruct((count, 128), jnp.bfloat16))
        out_specs.append(whole(out_shape[-1]))
    operands = (*arrays, *others, *(() if target is None else (target,)))
    *outs, token = ordered_call(
        functools.partial(assemble_kernel, lists, start, width, aliased),
        operands,
        [ANYWHERE] * len(operands),
        out_shape,
        out_specs,
        after,
        scalars=(info,),
        scratch=[
            pltpu.VMEM((4, count, rows, 128), jnp.bfloat16),
            pltpu.VMEM((2, count, rows * 128), jnp.bfloat16),
            pltpu.SemaphoreType.DMA((4, count)),
            pltpu.SemaphoreType.DMA((4,)),
        ],
        cost=(2**20, 4 * count * width, 0),
        aliases={len(operands): 0} if aliased else {},
        name="assemble",
        room=28 if target is None else 56,
    )
    if tail:
        return fill_tail(*outs, token)
    return outs[0], token


def join_lines_kernel(*refs):
    for index in range(3):
        low, high, out = refs[index], refs[3 + index], refs[6 + index]
        width = low.shape[1]
        out[0:1, 0:width] = low[...]
        out[0:1, width:] = high[...]


def join_lines(lows, highs, after=()):
    operands = (*lows, *highs)
    line = jax.ShapeDtypeStruct((1, lows[0].shape[1] + highs[0].shape[1]), jnp.float32)
    return ordered_call(
        join_lines_kernel,
        operands,
        [whole(item) for item in operands],
        [line] * 3,
        [whole(line)] * 3,
        after,
        cost=(0, 24 * line.size, 0),
        name="join_lines",
        room=56,
    )


MLP_ORDER = (
    ("half", 0),
    ("half", 1),
    ("matrix", 0),
    ("small", 0),
    ("matrix", 1),
    ("small", 1),
    ("moment", 0),
    ("moment", 1),
)
REST_ORDER = (
    (("half", 0), ("half", 1), ("matrix", 0), ("matrix", 1))
    + tuple(("small", index) for index in range(6))
    + (("moment", 0), ("moment", 1))
)


ROWS = 256


def norm_rows(values):
    center = values - jnp.mean(values, axis=-1, keepdims=True)
    spread = lax.rsqrt(jnp.mean(center * center, axis=-1, keepdims=True) + norm_eps)
    return center * spread, spread


def norm_back(grads, gain, hat, spread):
    scaled = grads * gain
    inner = scaled - jnp.mean(scaled, axis=-1, keepdims=True)
    inner = inner - hat * jnp.mean(scaled * hat, axis=-1, keepdims=True)
    return (
        spread * inner,
        jnp.sum(grads * hat, axis=0, keepdims=True),
        jnp.sum(grads, axis=0, keepdims=True),
    )


def add_lines(refs, lines):
    first = pl.program_id(0) == 0

    @pl.when(first)
    def _():
        for ref, line in zip(refs, lines):
            ref[...] = line

    @pl.when(jnp.logical_not(first))
    def _():
        for ref, line in zip(refs, lines):
            ref[...] += line


def rows_of(item):
    return pl.BlockSpec((ROWS, item.shape[1]), lambda i, *_: (i, 0))


def first_part_kernel(
    pad_ref,
    tokens_ref,
    grad_ref,
    gain_ref,
    bias_ref,
    weight_ref,
    shift_ref,
    normed_out,
    out_ref,
    grad_out,
):
    hat, _ = norm_rows(tokens_ref[...].astype(jnp.float32))
    normed = (
        hat * gain_ref[...].astype(jnp.float32) + bias_ref[...].astype(jnp.float32)
    ).astype(jnp.bfloat16)
    normed_out[...] = normed
    out_ref[...] = (
        dot_nn(normed, weight_ref[...]) + shift_ref[...].astype(jnp.float32)
    ).astype(jnp.bfloat16)
    row = pl.program_id(0) * ROWS + lax.broadcasted_iota(jnp.int32, grad_ref.shape, 0)
    grads = grad_ref[...].astype(jnp.float32)
    grad_out[...] = jnp.where(row < pad_ref[0], grads, 0.0).astype(jnp.bfloat16)


def first_part(tokens, out_grad, vectors, weight, pad_start):
    length = tokens.shape[0]
    outs = [halves(length, D), halves(length, weight.shape[1]), halves(length, D)]
    return ordered_call(
        first_part_kernel,
        (tokens, out_grad, vectors, vectors, weight, vectors),
        [
            rows_of(tokens),
            rows_of(out_grad),
            vector_spec("gain_one"),
            vector_spec("shift_one"),
            whole(weight),
            vector_spec("qkv_bias"),
        ],
        outs,
        [rows_of(item) for item in outs],
        grid=(length // ROWS,),
        scalars=(pad_start,),
        cost=(2 * length * weight.size, 8 * 2**20, 0),
        name="norm_qkv",
        room=56,
        far=(0, 1, 2),
    )


def second_part_kernel(
    tokens_ref, context_ref, weight_ref, shift_ref, gain_ref, bias_ref, middle_out, normed_out
):
    middle = tokens_ref[...].astype(jnp.float32) + (
        dot_nn(context_ref[...], weight_ref[...]) + shift_ref[...].astype(jnp.float32)
    )
    middle_out[...] = middle
    hat, _ = norm_rows(middle)
    normed_out[...] = (
        hat * gain_ref[...].astype(jnp.float32) + bias_ref[...].astype(jnp.float32)
    ).astype(jnp.bfloat16)


def second_part(tokens, context, weight, vectors, after=()):
    length = tokens.shape[0]
    outs = [floats(length, D), halves(length, D)]
    return ordered_call(
        second_part_kernel,
        (tokens, context, weight, vectors, vectors, vectors),
        [
            rows_of(tokens),
            rows_of(context),
            whole(weight),
            vector_spec("proj_bias"),
            vector_spec("gain_two"),
            vector_spec("shift_two"),
        ],
        outs,
        [rows_of(item) for item in outs],
        after,
        grid=(length // ROWS,),
        cost=(2 * length * weight.size, 8 * 2**20, 0),
        name="proj_norm",
        room=12,
        far=(0, 1),
    )


def mlp_part_kernel(
    normed_ref, grad_ref, first_ref, shift_ref, second_ref, active_out, hidden_grad_out
):
    root = 0.7978845608028654
    for begin in range(0, normed_ref.shape[0], ROWS):
        rows = slice(begin, begin + ROWS)
        hidden = dot_nn(normed_ref[rows, :], first_ref[...]) + shift_ref[...].astype(jnp.float32)
        grad_active = dot_nt(grad_ref[rows, :], second_ref[...])
        square = hidden * hidden
        slope = jnp.tanh(hidden * (root + (root * 0.044715) * square))
        half = 0.5 + 0.5 * slope
        active_out[rows, :] = (hidden * half).astype(jnp.bfloat16)
        rise = half + (0.5 * hidden) * (1.0 - slope * slope) * (
            root + (3.0 * root * 0.044715) * square
        )
        hidden_grad_out[rows, :] = (grad_active * rise).astype(jnp.bfloat16)


def mlp_part(normed, grad_out, first, vectors, second, after=()):
    length, width = normed.shape[0], first.shape[1]
    step = D
    columns = pl.BlockSpec((length, step), lambda i: (0, i))
    outs = [halves(length, width)] * 2
    return ordered_call(
        mlp_part_kernel,
        (normed, grad_out, first, vectors, second),
        [
            whole(normed),
            whole(grad_out),
            pl.BlockSpec((D, step), lambda i: (0, i)),
            pl.BlockSpec((1, step), lambda i: (0, i)),
            pl.BlockSpec((step, D), lambda i: (i, 0)),
        ],
        outs,
        [columns, columns],
        after,
        grid=(width // step,),
        cost=(4 * length * D * width, 24 * 2**20, length * width),
        name="mlp_part",
        room=30,
        far=(0, 1),
    )


def middle_back_kernel(
    hidden_grad_ref,
    first_ref,
    middle_ref,
    gain_ref,
    grad_out_ref,
    proj_ref,
    middle_grad_out,
    branch_out,
    context_grad_out,
    gain_sum,
    bias_sum,
    proj_bias_sum,
):
    grads = dot_nt(hidden_grad_ref[...], first_ref[...])
    hat, spread = norm_rows(middle_ref[...])
    back, gain_line, bias_line = norm_back(
        grads, gain_ref[...].astype(jnp.float32), hat, spread
    )
    middle_grad = grad_out_ref[...].astype(jnp.float32) + back
    middle_grad_out[...] = middle_grad
    branch = middle_grad.astype(jnp.bfloat16)
    branch_out[...] = branch
    context_grad_out[...] = dot_nt(branch, proj_ref[...]).astype(jnp.bfloat16)
    proj_line = jnp.sum(branch.astype(jnp.float32), axis=0, keepdims=True)
    add_lines((gain_sum, bias_sum, proj_bias_sum), (gain_line, bias_line, proj_line))


def middle_back(hidden_grad, first, middle, vectors, grad_out, proj, after=()):
    length = middle.shape[0]
    line = floats(1, D)
    outs = [floats(length, D), halves(length, D), halves(length, D)]
    return ordered_call(
        middle_back_kernel,
        (hidden_grad, first, middle, vectors, grad_out, proj),
        [
            rows_of(hidden_grad),
            whole(first),
            rows_of(middle),
            vector_spec("gain_two"),
            rows_of(grad_out),
            whole(proj),
        ],
        outs + [line] * 3,
        [rows_of(item) for item in outs] + [whole(line)] * 3,
        after,
        grid=(length // ROWS,),
        cost=(2 * length * (first.size + proj.size), 24 * 2**20, 0),
        name="middle_back",
        room=32,
        far=(0, 1, 2),
    )


def input_back_kernel(parts, tokens_ref, gain_ref, weight_ref, middle_grad_ref, *refs):
    pieces, (out_ref, gain_sum, bias_sum) = refs[: 3 * parts], refs[3 * parts :]
    joined = jnp.concatenate([piece[...] for piece in pieces], axis=1)
    grads = dot_nt(joined, weight_ref[...])
    hat, spread = norm_rows(tokens_ref[...].astype(jnp.float32))
    back, gain_line, bias_line = norm_back(
        grads, gain_ref[...].astype(jnp.float32), hat, spread
    )
    out_ref[...] = (middle_grad_ref[...] + back).astype(jnp.bfloat16)
    add_lines((gain_sum, bias_sum), (gain_line, bias_line))


def input_back(tokens, vectors, weight, middle_grad, pieces, after=()):
    length = tokens.shape[0]
    line = floats(1, D)
    out = halves(length, D)
    return ordered_call(
        functools.partial(input_back_kernel, len(pieces) // 3),
        (tokens, vectors, weight, middle_grad, *pieces),
        [rows_of(tokens), vector_spec("gain_one"), whole(weight), rows_of(middle_grad)]
        + [rows_of(item) for item in pieces],
        [out, line, line],
        [rows_of(out), whole(line), whole(line)],
        after,
        grid=(length // ROWS,),
        cost=(2 * length * weight.size, 16 * 2**20, 0),
        name="input_back",
        room=56,
    )


def block_out_kernel(active_ref, weight_ref, shift_ref, middle_ref, out_ref):
    out_ref[...] = (
        middle_ref[...]
        + (dot_nn(active_ref[...], weight_ref[...]) + shift_ref[...].astype(jnp.float32))
    ).astype(jnp.bfloat16)


def block_out_rows(active, weight, vectors, middle, after=()):
    length = middle.shape[0]
    out = halves(length, D)
    return ordered_call(
        block_out_kernel,
        (active, weight, vectors, middle),
        [rows_of(active), whole(weight), vector_spec("fc2_bias"), rows_of(middle)],
        [out],
        [rows_of(out)],
        after,
        grid=(length // ROWS,),
        cost=(2 * length * weight.size, 16 * 2**20, 0),
        name="block_out",
        room=56,
    )


def on_device(
    tokens,
    out_grad,
    image_counts,
    group_of_device,
    group_weight,
    norm1_gain,
    norm1_bias,
    qkv_weight,
    qkv_bias,
    proj_weight,
    proj_bias,
    norm2_gain,
    norm2_bias,
    fc1_weight,
    fc1_bias,
    fc2_weight,
    fc2_bias,
    first_moment,
    second_moment,
):
    count = lax.axis_size("dp")
    core = lax.axis_index("grp")
    own = lax.axis_index("dp")
    info = jnp.stack([core, own])
    pad_start = jnp.sum(image_counts[0], keepdims=True)
    vectors = join_vectors(
        fc1_bias,
        norm1_gain,
        norm1_bias,
        qkv_bias,
        proj_bias,
        norm2_gain,
        norm2_bias,
        fc2_bias,
    )
    member = (group_of_device[0] == lax.iota(jnp.int32, 128)).astype(jnp.float32)
    images = jnp.sum((image_counts[0] > 0).astype(jnp.float32))
    totals = jnp.broadcast_to(member * images, (8, 128))
    bits = iter([1 << place for place in range((2 * count).bit_length() - 1)])

    def count_on(totals, *after):
        return add_totals(totals, swap(totals, next(bits)), after)

    normed_one, projected, grad_out, token = first_part(
        tokens, out_grad, vectors, qkv_weight, pad_start
    )
    totals, token = count_on(totals, token)
    context, weights, scales, token = attn_forward(projected, image_counts, pad_start, (token,))
    totals, token = count_on(totals, token)
    middle, normed_two, token = second_part(tokens, context, proj_weight, vectors, (token,))
    totals, token = count_on(totals, token)
    active, grad_hidden, token = mlp_part(
        normed_two, grad_out, fc1_weight, vectors, fc2_weight, (token,)
    )
    totals, token = count_on(totals, token)
    for _ in range((2 * count).bit_length() - 5):
        totals, token = count_on(totals, token)
    share = jnp.sum(member[:NGROUPS] * group_weight.astype(jnp.float32))
    factor = (share / jnp.sum(member * totals[0])).reshape(1)

    mlp_make = functools.partial(
        mlp_grads,
        own=own,
        count=count,
        factor=factor,
        normed=normed_two,
        grad_hidden=grad_hidden,
        active=active,
        grad_out=grad_out,
    )
    sent, token = mlp_make(1 - core)
    came = swap(sent, count)
    kept, _ = mlp_make(core, after=(token,))
    mlp_steps = reduce_blocks(came, kept)
    next(mlp_steps)
    sending = mlp_steps.send(())
    middle_grad, branch, context_grad, gain_two_sum, shift_two_sum, proj_bias_sum, token = (
        middle_back(grad_hidden, fc1_weight, middle, vectors, grad_out, proj_weight, (sending,))
    )
    wide = D // 128
    (query_grad, key_grad, value_grad), token = attn_backward(
        projected, context, context_grad, weights, scales, 0, wide, (token,)
    )
    sending = mlp_steps.send((token,))
    input_grad, gain_one_sum, shift_one_sum, token = input_back(
        tokens,
        vectors,
        qkv_weight,
        middle_grad,
        (query_grad, key_grad, value_grad),
        (sending,),
    )
    sending = mlp_steps.send((token,))
    rest_make = functools.partial(
        rest_grads,
        own=own,
        count=count,
        factor=factor,
        normed=normed_one,
        context=context,
        query=(query_grad,),
        key=(key_grad,),
        value=(value_grad,),
        branch=branch,
        vectors=(gain_one_sum, shift_one_sum, proj_bias_sum, gain_two_sum, shift_two_sum),
    )
    rest_sent, rest_token = rest_make(1 - core, after=(sending,))
    rest_kept, rest_order = [], []

    def keep_rest(sending):
        kept, token = rest_make(core, after=(rest_token,) if sending is None else (sending,))
        rest_kept.append(kept)
        rest_order.append(rest_token if sending is None else sending)
        return token

    mlp_mine, token = finish(mlp_steps, [lambda sending: rest_token, keep_rest], sending)
    mlp_parts = (mlp_mine, swap(mlp_mine, count))
    came = swap(tie(rest_sent, *rest_order), count)
    moments = (first_moment, second_moment)
    total = first_moment.shape[1]
    rest_width = (3 * D * D + D * D + 3 * D + 5 * D) // count
    mlp_width = total - rest_width
    *mlp_lines, mlp_fresh, update_token = update_call(
        functools.partial(mlp_update_kernel, rest_width),
        "mlp_update",
        info,
        *mlp_parts,
        (fc1_weight, fc2_weight),
        (vectors, "fc1_bias", "fc2_bias"),
        moments,
        mlp_width,
        MLP_ORDER,
    )
    mlp_gathered = lax.all_gather(mlp_fresh, "dp")
    rest_steps = reduce_blocks(came, rest_kept[0])
    next(rest_steps)
    sending = rest_steps.send((update_token,))
    block_state = []

    def block_rows(sending):
        block_state.extend(
            block_out_rows(active, fc2_weight, vectors, middle, (sending,))
        )
        return block_state[-1]

    rest_mine, _ = finish(rest_steps, [block_rows], sending)
    block_out, _ = block_state
    rest_parts = (rest_mine, swap(rest_mine, count))
    *rest_lines, rest_fresh, token = update_call(
        rest_update_kernel,
        "rest_update",
        info,
        *rest_parts,
        (qkv_weight, proj_weight),
        (vectors, "gain_one", "shift_one", "qkv_bias", "proj_bias", "gain_two", "shift_two"),
        moments,
        rest_width,
        REST_ORDER,
    )
    rest_gather = Gather(rest_fresh)
    summed, new_first, new_second, token = join_lines(rest_lines, mlp_lines, (token,))
    while rest_gather.position > 2:
        token = rest_gather.outer((token,))
    mlp_gathered = tie(mlp_gathered, token)
    mlp_other = swap(mlp_gathered, count)
    token = rest_gather.outer((token,))
    new_weights, token = assemble(
        info,
        [mlp_gathered],
        [mlp_other],
        None,
        rest_width,
        mlp_width,
        total,
        after=(token,),
    )
    rest_gather.inner((token,))
    rest_gather.others()
    new_weights, _ = assemble(info, *rest_gather.result(), 0, rest_width, total, new_weights)
    summed_bias = mlp_lines[0][0, mlp_width - D // count :]
    return (block_out, input_grad, summed, new_weights, new_first, new_second, summed_bias)


def add_totals_kernel(first_ref, second_ref, out_ref):
    out_ref[...] = first_ref[...] + second_ref[...]


def add_totals(first, second, after=()):
    return ordered_call(
        add_totals_kernel,
        (first, second),
        [whole(first), whole(second)],
        [floats(*first.shape)],
        [whole(first)],
        after,
        name="add_totals",
        room=4,
    )


def device_factor(counts_row, group_of_device, group_weight):
    images = jnp.sum((counts_row > 0).astype(jnp.int32))
    member = (group_of_device[0] == lax.iota(jnp.int32, NGROUPS)).astype(jnp.int32)
    totals = member * images
    for position in range((lax.axis_size("grp") * lax.axis_size("dp")).bit_length() - 1):
        totals = totals + swap(totals, 1 << position)
    return jnp.sum(member * group_weight).astype(jnp.float32) / jnp.sum(member * totals).astype(
        jnp.float32
    )


def general_device(
    tokens,
    out_grad,
    image_counts,
    group_of_device,
    group_weight,
    norm1_gain,
    norm1_bias,
    qkv_weight,
    qkv_bias,
    proj_weight,
    proj_bias,
    norm2_gain,
    norm2_bias,
    fc1_weight,
    fc1_bias,
    fc2_weight,
    fc2_bias,
    first_moment,
    second_moment,
):
    length = tokens.shape[0]
    segment, valid_rows = segment_info(image_counts[0], length)
    factor = device_factor(image_counts[0], group_of_device, group_weight)
    inputs = tokens.astype(jnp.float32)
    normed_one, norm_one_back = jax.vjp(
        layer_norm, inputs, norm1_gain.astype(jnp.float32), norm1_bias.astype(jnp.float32)
    )
    normed_one_low = normed_one.astype(jnp.bfloat16)
    projected = (
        jnp.dot(normed_one_low, qkv_weight, preferred_element_type=jnp.float32)
        + qkv_bias.astype(jnp.float32)
    ).astype(jnp.bfloat16)
    pad_start = jnp.sum(image_counts[0], keepdims=True)
    context, weights, scales, _ = attn_forward(projected, image_counts, pad_start)
    middle = inputs + (
        jnp.dot(context, proj_weight, preferred_element_type=jnp.float32)
        + proj_bias.astype(jnp.float32)
    )
    normed_two, norm_two_back = jax.vjp(
        layer_norm, middle, norm2_gain.astype(jnp.float32), norm2_bias.astype(jnp.float32)
    )
    normed_two_low = normed_two.astype(jnp.bfloat16)
    hidden = jnp.dot(
        normed_two_low, fc1_weight, preferred_element_type=jnp.float32
    ) + fc1_bias.astype(jnp.float32)
    activated, gelu_back = jax.vjp(gelu_tanh, hidden)
    activated_low = activated.astype(jnp.bfloat16)
    block_out = (
        middle
        + (
            jnp.dot(activated_low, fc2_weight, preferred_element_type=jnp.float32)
            + fc2_bias.astype(jnp.float32)
        )
    ).astype(jnp.bfloat16)
    grad_out = out_grad.astype(jnp.float32) * valid_rows[:, None].astype(jnp.float32)
    grad_out_low = grad_out.astype(jnp.bfloat16)
    fc2_grad = contract_rows(activated_low, grad_out_low)
    fc2_bias_grad = jnp.sum(grad_out, axis=0)
    grad_hidden = gelu_back(contract_cols(grad_out_low, fc2_weight))[0].astype(jnp.bfloat16)
    fc1_grad = contract_rows(normed_two_low, grad_hidden)
    fc1_bias_grad = jnp.sum(grad_hidden.astype(jnp.float32), axis=0)
    grad_middle_norm, gain_two_grad, shift_two_grad = norm_two_back(
        contract_cols(grad_hidden, fc1_weight)
    )
    grad_middle = grad_out + grad_middle_norm
    grad_branch = grad_middle.astype(jnp.bfloat16)
    proj_grad = contract_rows(context, grad_branch)
    proj_bias_grad = jnp.sum(grad_branch.astype(jnp.float32), axis=0)
    grad_context = contract_cols(grad_branch, proj_weight).astype(jnp.bfloat16)
    (query_grad, key_grad, value_grad), _ = attn_backward(
        projected, context, grad_context, weights, scales, 0, D // 128
    )
    grad_projected = jnp.concatenate([query_grad, key_grad, value_grad], axis=1)
    qkv_grad = contract_rows(normed_one_low, grad_projected)
    qkv_bias_grad = jnp.sum(grad_projected.astype(jnp.float32), axis=0)
    grad_input_norm, gain_one_grad, shift_one_grad = norm_one_back(
        contract_cols(grad_projected, qkv_weight)
    )
    input_grad = (grad_middle + grad_input_norm).astype(jnp.bfloat16)
    moments = (first_moment, second_moment)
    mlp_summed, rest_summed = exchange_grads(
        (gain_one_grad, shift_one_grad, qkv_grad, qkv_bias_grad, proj_grad, proj_bias_grad),
        (gain_two_grad, shift_two_grad, fc1_grad, fc1_bias_grad, fc2_grad, fc2_bias_grad),
        factor,
    )
    row_count = lax.axis_size("dp")
    own_index = lax.axis_index("dp")
    weight_list = (
        norm1_gain,
        norm1_bias,
        qkv_weight,
        qkv_bias,
        proj_weight,
        proj_bias,
        norm2_gain,
        norm2_bias,
        fc1_weight,
        fc1_bias,
        fc2_weight,
        fc2_bias,
    )
    own_weights = [
        lax.dynamic_slice_in_dim(item.reshape(row_count, -1), own_index, 1, 0)[0]
        for item in weight_list
    ]
    rows = D // row_count
    fc1_sum = mlp_summed[0].reshape(4, rows, D).transpose(1, 0, 2).reshape(-1)
    fc2_sum = mlp_summed[1].reshape(-1)
    qkv_sum = jnp.concatenate(
        [rest_summed[0, :rows], rest_summed[0, rows : 2 * rows], rest_summed[1, :rows]], axis=1
    ).reshape(-1)
    proj_sum = rest_summed[1, rows : 2 * rows].reshape(-1)
    small = rest_summed[0, 2 * rows]
    widths = [item.size // row_count for item in weight_list]
    small_parts = {}
    start = 0
    for index, flag in enumerate(decay_flags):
        if flag == 0.0:
            small_parts[index] = small[start : start + widths[index]]
            start += widths[index]
    large_parts = {2: qkv_sum, 4: proj_sum, 8: fc1_sum, 10: fc2_sum}
    pieces = [
        small_parts[index] if index in small_parts else large_parts[index] for index in range(12)
    ]
    split = sum(widths[:8])
    grads_out, first_out, second_out, fresh = [], [], [], []
    for lead, tail, begin, end in ((8, 12, split, sum(widths)), (0, 8, 0, split)):
        summed_part = jnp.concatenate(pieces[lead:tail])
        current = jnp.concatenate(own_weights[lead:tail]).astype(jnp.float32)
        decay = jnp.concatenate(
            [
                jnp.full((width,), flag, jnp.float32)
                for width, flag in zip(widths[lead:tail], decay_flags[lead:tail])
            ]
        )
        new_first = beta_one * moments[0][0, begin:end] + (1.0 - beta_one) * summed_part
        new_second = (
            beta_two * moments[1][0, begin:end] + (1.0 - beta_two) * summed_part * summed_part
        )
        ratio = (
            new_first
            / (1.0 - beta_one**step_count)
            / (jnp.sqrt(new_second / (1.0 - beta_two**step_count)) + adam_eps)
        )
        fresh_low = (current - learn_rate * (ratio + decay_rate * decay * current)).astype(
            jnp.bfloat16
        )
        grads_out.insert(0, summed_part)
        first_out.insert(0, new_first)
        second_out.insert(0, new_second)
        fresh.insert(0, gather_rows(fresh_low))
    summed = jnp.concatenate(grads_out)[None]
    new_first = jnp.concatenate(first_out)[None]
    new_second = jnp.concatenate(second_out)[None]
    new_weights = jnp.concatenate(fresh, axis=1)
    summed_bias = pieces[11]
    return (block_out, input_grad, summed, new_weights, new_first, new_second, summed_bias)


def bit_of(position):
    return (lax.axis_index("dp") >> position) & 1


def halve(values, position, positions):
    axis = positions.index(position)
    own = bit_of(position)
    sent = lax.dynamic_index_in_dim(values, 1 - own, axis, keepdims=False)
    kept = lax.dynamic_index_in_dim(values, own, axis, keepdims=False)
    return kept, swap(sent, 1 << position), [p for p in positions if p != position]


def reduce_rows(values):
    count = lax.axis_size("dp")
    grp = lax.axis_index("grp")
    kept = lax.dynamic_index_in_dim(values, grp, 0, keepdims=False)
    came = swap(lax.dynamic_index_in_dim(values, 1 - grp, 0, keepdims=False), count)
    kept = add_low(kept, came)
    depth = count.bit_length() - 1
    positions = list(range(depth))[::-1]
    rows = kept.shape[1]
    parts = [kept[:, : rows // 2], kept[:, rows // 2 :]]
    left = [positions, positions]
    parts = [part.reshape((2,) * depth + part.shape[1:]) for part in parts]
    for order in ((0, 1), (1, 0)):
        for index in (0, 1):
            part, came, left[index] = halve(parts[index], order[index], left[index])
            parts[index] = add_low(part, came)
    whole = jnp.concatenate(parts, axis=depth - 2)
    rest = left[0]
    for position in range(2, depth):
        part, came, rest = halve(whole, position, rest)
        if rest:
            whole = add_low(part, came)
        else:
            whole = part.astype(jnp.float32) + came.astype(jnp.float32)
    other = swap(whole, count)
    return jnp.where(grp == 0, jnp.stack([whole, other]), jnp.stack([other, whole]))


def join(own, came, bit):
    return jnp.where(bit == 0, jnp.stack([own, came]), jnp.stack([came, own]))


def gather_rows(values):
    count = lax.axis_size("dp")
    depth = count.bit_length() - 1
    grp = lax.axis_index("grp")
    width = values.shape[0]
    padded = -(-width // 4096) * 4096
    halves = jnp.pad(values, (0, padded - width)).reshape(2, 2, padded // 512, 128)
    own = lax.dynamic_index_in_dim(halves, grp, 0, keepdims=False)
    for position in range(2, depth)[::-1]:
        own = join(own, swap(own, 1 << position), bit_of(position))
    lead = own.ndim - 3
    parts = [lax.index_in_dim(own, i, lead, keepdims=False) for i in (0, 1)]
    for order in ((1, 0), (0, 1)):
        for index in (0, 1):
            position = order[index]
            parts[index] = join(
                parts[index], swap(parts[index], 1 << position), bit_of(position)
            )
    parts[1] = jnp.swapaxes(parts[1], 0, 1)
    full = jnp.stack(parts, axis=depth)
    full = full.transpose(tuple(range(depth))[::-1] + tuple(range(depth, full.ndim)))
    full = full.reshape((count,) + full.shape[depth:])
    other = swap(full, count)
    whole = jnp.where(
        grp == 0, jnp.stack([full, other], axis=1), jnp.stack([other, full], axis=1)
    )
    return whole.reshape(count, padded)[:, :width]


def exchange_grads(front, back, factor):
    gain_one, shift_one, qkv, qkv_bias, proj, proj_bias = front
    gain_two, shift_two, fc1, fc1_bias, fc2, fc2_bias = back
    count = lax.axis_size("dp")
    rows = D // count
    fc1_blocks = fc1.reshape(count, rows, 4, D).transpose(0, 2, 1, 3).reshape(count, 4 * rows, D)
    fc2_blocks = fc2.reshape(count, 4 * rows, D)
    mlp = (jnp.stack([fc1_blocks, fc2_blocks]) * factor).astype(jnp.bfloat16)
    small = jnp.concatenate(
        [
            item.reshape(count, -1)
            for item in (
                gain_one,
                shift_one,
                qkv_bias,
                proj_bias,
                gain_two,
                shift_two,
                fc1_bias,
                fc2_bias,
            )
        ],
        axis=1,
    )
    small = jnp.pad(small, ((0, 0), (0, D - small.shape[1])))[:, None]
    small = jnp.pad(small, ((0, 0), (0, 7), (0, 0)))
    qkv_blocks = qkv.reshape(count, rows, 3, D)
    first_half = jnp.concatenate([qkv_blocks[:, :, 0], qkv_blocks[:, :, 1], small], axis=1)
    second_half = jnp.concatenate(
        [qkv_blocks[:, :, 2], proj.reshape(count, rows, D), jnp.zeros_like(small)], axis=1
    )
    rest = (jnp.stack([first_half, second_half]) * factor).astype(jnp.bfloat16)
    return reduce_rows(mlp), reduce_rows(rest)


def solution(mesh):
    in_specs = (
        P(("grp", "dp"), None),
        P(("grp", "dp"), None),
        P(("grp", "dp"), None),
        P(("grp", "dp")),
        P(),
        P(),
        P(),
        P(),
        P(),
        P(),
        P(),
        P(),
        P(),
        P(),
        P(),
        P(),
        P(),
        P("dp", None),
        P("dp", None),
    )
    out_specs = (
        P(("grp", "dp"), None),
        P(("grp", "dp"), None),
        P("dp", None),
        P(),
        P("dp", None),
        P("dp", None),
        P("dp"),
    )
    rows = D // mesh.shape["dp"]
    return jax.shard_map(
        on_device if rows % 16 == 0 and mesh.shape["dp"] == 16 else general_device, mesh=mesh, in_specs=in_specs, out_specs=out_specs, check_vma=False
    )
```

```python
import functools

import jax
import jax.numpy as jnp
from jax import lax
from jax.experimental import pallas as pl
from jax.experimental.pallas import tpu as pltpu
from jax.sharding import PartitionSpec as P

D = 768
HEADS = 12
HEAD_DIM = 64
NGROUPS = 3


beta_one = 0.9
beta_two = 0.999
adam_eps = 1e-08
decay_rate = 0.05
step_count = 10.0
learn_rate = 0.004 * 0.75**1
norm_eps = 1e-06
neg_fill = -1e30
decay_flags = (0.0, 0.0, 1.0, 0.0, 1.0, 0.0, 0.0, 0.0, 1.0, 0.0, 1.0, 0.0)


def layer_norm(values, gain, shift):
    center = values - jnp.mean(values, axis=-1, keepdims=True)
    spread = jnp.mean(center * center, axis=-1, keepdims=True)
    return center * lax.rsqrt(spread + norm_eps) * gain + shift


def gelu_tanh(values):
    return jax.nn.gelu(values, approximate=True)


def contract_rows(first_op, second_op):
    return lax.dot_general(
        first_op, second_op, (((0,), (0,)), ((), ())), preferred_element_type=jnp.float32
    )


def contract_cols(first_op, second_op):
    return lax.dot_general(
        first_op, second_op, (((1,), (1,)), ((), ())), preferred_element_type=jnp.float32
    )


def segment_info(counts_row, length):
    slots = lax.iota(jnp.int32, counts_row.shape[0])
    segment_ends = jnp.sum(
        jnp.where(slots[:, None] <= slots[None, :], counts_row[:, None], 0), axis=0
    )
    position = lax.iota(jnp.int32, length)
    segment = jnp.sum((position[:, None] >= segment_ends[None, :]).astype(jnp.int32), axis=1)
    return (segment, position < segment_ends[-1])


TILE = 128
WINDOW = 3 * TILE


def window_start(tile, tiles):
    return min(max(tile - 1, 0), tiles - 3) * TILE


def dot_nt(first, second):
    return lax.dot_general(first, second, (((1,), (1,)), ((), ())), preferred_element_type=jnp.float32)


def dot_tn(first, second):
    return lax.dot_general(first, second, (((0,), (0,)), ((), ())), preferred_element_type=jnp.float32)


def dot_nn(first, second):
    return jnp.dot(first, second, preferred_element_type=jnp.float32)


def stack_heads(block, low):
    zero = jnp.zeros_like(block)
    return jnp.concatenate([jnp.where(low, block, zero), jnp.where(low, zero, block)], axis=0)


def merge_heads(block, low):
    return jnp.where(low, block[:TILE], block[TILE:])


def find_segments(counts_ref, seg_col_ref, seg_row_ref):
    slots, length = counts_ref.shape[1], seg_col_ref.shape[0]
    down = lax.broadcasted_iota(jnp.int32, (slots, slots), 0)
    across = lax.broadcasted_iota(jnp.int32, (slots, slots), 1)
    counts = jnp.broadcast_to(counts_ref[...].astype(jnp.float32), (slots, slots))
    ends_col = jnp.sum(jnp.where(across <= down, counts, 0.0), axis=1, keepdims=True)
    ends_row = jnp.sum(jnp.where(across == down, ends_col, 0.0), axis=0, keepdims=True)
    place_col = lax.broadcasted_iota(jnp.int32, (length, slots), 0).astype(jnp.float32)
    place_row = lax.broadcasted_iota(jnp.int32, (slots, length), 1).astype(jnp.float32)
    seg_col_ref[...] = jnp.sum(jnp.where(place_col >= ends_row, 1.0, 0.0), axis=1, keepdims=True)
    seg_row_ref[...] = jnp.sum(jnp.where(place_row >= ends_col, 1.0, 0.0), axis=0, keepdims=True)


def fill_masks(bias_ref, seg_col_ref, seg_row_ref, tiles):
    for tile in range(tiles):
        start = window_start(tile, tiles)
        same = (
            seg_col_ref[tile * TILE : (tile + 1) * TILE, :]
            == seg_row_ref[:, start : start + WINDOW]
        )
        bias_ref[tile] = jnp.where(same, 0.0, neg_fill)


ANYWHERE = pl.BlockSpec(memory_space=pl.ANY)
VMEM_BYTES = 56 * 2**20


VECTORS = {
    "fc1_bias": (0, 3072),
    "gain_one": (3072, 768),
    "shift_one": (3840, 768),
    "qkv_bias": (4608, 2304),
    "proj_bias": (6912, 768),
    "gain_two": (7680, 768),
    "shift_two": (8448, 768),
    "fc2_bias": (9216, 768),
}


def join_vectors_kernel(*refs):
    begin = 0
    for ref in refs[:-1]:
        width = ref.shape[0]
        refs[-1][0:1, begin : begin + width] = ref[...].reshape(1, width)
        begin += width


def join_vectors(*vectors):
    return pl.pallas_call(
        join_vectors_kernel,
        out_shape=halves(1, sum(item.shape[0] for item in vectors)),
        name="join_vectors",
    )(*vectors)


def vector_spec(name):
    begin, width = VECTORS[name]
    return pl.BlockSpec((1, width), lambda *_: (0, begin // width))


def ordered_kernel(kernel, first, extra, outs, *refs):
    token = refs[first + extra + outs]
    token[...] = jnp.zeros_like(token)
    kernel(*refs[:first], *refs[first + extra : first + extra + outs], *refs[first + extra + outs + 1 :])


def ordered_call(
    kernel, operands, in_specs, out_shape, out_specs, after=(), grid=(1,), scalars=(), scratch=(),
    cost=(0, 0, 0), aliases=None, name=None, room=56, far=(),
):
    out_shape = [
        pltpu.HBM(item.shape, item.dtype) if index in far else item
        for index, item in enumerate(out_shape)
    ]
    call = pl.pallas_call(
        functools.partial(
            ordered_kernel, kernel, len(scalars) + len(operands), len(after), len(out_shape)
        ),
        out_shape=[*out_shape, jax.ShapeDtypeStruct((8, 128), jnp.float32)],
        grid_spec=pltpu.PrefetchScalarGridSpec(
            num_scalar_prefetch=len(scalars),
            grid=grid,
            in_specs=[*in_specs] + [ANYWHERE] * len(after),
            out_specs=[*out_specs, pl.BlockSpec((8, 128), lambda *_: (0, 0))],
            scratch_shapes=list(scratch),
        ),
        input_output_aliases=aliases or {},
        compiler_params=pltpu.CompilerParams(vmem_limit_bytes=room * 2**20),
        cost_estimate=pl.CostEstimate(
            flops=cost[0], bytes_accessed=cost[1], transcendentals=cost[2]
        ),
        name=name,
    )
    return call(*scalars, *operands, *after)


def whole(item):
    return pl.BlockSpec(item.shape, lambda *_: (0,) * len(item.shape))


def floats(*shape):
    return jax.ShapeDtypeStruct(shape, jnp.float32)


def halves(*shape):
    return jax.ShapeDtypeStruct(shape, jnp.bfloat16)


def attn_forward_kernel(
    pad_ref,
    query_ref,
    key_ref,
    value_ref,
    counts_ref,
    out_ref,
    weight_out,
    scale_out,
    bias_ref,
    seg_col_ref,
    seg_row_ref,
):
    length = query_ref.shape[0]
    tiles = length // TILE

    @pl.when(pl.program_id(0) == 0)
    def _():
        find_segments(counts_ref, seg_col_ref, seg_row_ref)
        fill_masks(bias_ref, seg_col_ref, seg_row_ref, tiles)

    low = lax.broadcasted_iota(jnp.int32, (TILE, 128), 1) < 64
    scale = jnp.asarray(0.125, jnp.bfloat16)

    def head_rows(queries, keys, values, bias):
        scores = dot_nt(queries, keys) + bias
        weights = jnp.exp(scores - jnp.max(scores, axis=1, keepdims=True)).astype(jnp.bfloat16)
        ones = jnp.ones((values.shape[0], 128), jnp.bfloat16)
        mixed = dot_nn(weights, jnp.concatenate([values, ones], axis=1))
        inverse = 1.0 / mixed[:, 128:]
        return weights, mixed[:, :128] * inverse, inverse

    for tile in range(tiles):
        span = pl.ds(window_start(tile, tiles), WINDOW)
        rows = slice(tile * TILE, (tile + 1) * TILE)
        queries = query_ref[rows, :] * scale
        zero = jnp.zeros_like(queries)
        first, second = (
            head_rows(part, key_ref[span, :], value_ref[span, :], bias_ref[tile])
            for part in (jnp.where(low, queries, zero), jnp.where(low, zero, queries))
        )
        weight_out[0, tile, 0:TILE, :] = first[0]
        weight_out[0, tile, TILE:, :] = second[0]
        out_ref[rows, :] = jnp.where(low, first[1], second[1]).astype(jnp.bfloat16)
        scale_out[rows, :] = jnp.where(low, first[2], second[2])

    @pl.loop(0, tiles)
    def _(tile):
        start = jnp.minimum(jnp.maximum(tile - 1, 0), tiles - 3) * TILE
        padding = (tile + 1) * TILE > pad_ref[0]
        outside = (pad_ref[0] < start) | (start + WINDOW < length)

        @pl.when(padding & outside)
        def _():
            rows = pl.ds(pl.multiple_of(tile * TILE, TILE), TILE)
            queries = query_ref[rows, :] * scale
            zero = jnp.zeros_like(queries)
            bias = jnp.where(seg_col_ref[rows, :] == seg_row_ref[...], 0.0, neg_fill)
            first, second = (
                head_rows(part, key_ref[...], value_ref[...], bias)
                for part in (jnp.where(low, queries, zero), jnp.where(low, zero, queries))
            )
            out_ref[rows, :] = jnp.where(low, first[1], second[1]).astype(jnp.bfloat16)


def attn_forward(projected, image_counts, pad_start, after=()):
    length, width = projected.shape
    pairs = width // 3 // 128
    tiles = length // TILE

    def part(offset):
        return pl.BlockSpec((length, 128), lambda pair, pad: (0, offset * pairs + pair))

    return ordered_call(
        attn_forward_kernel,
        (projected, projected, projected, image_counts),
        [part(0), part(1), part(2), whole(image_counts)],
        [
            halves(length, width // 3),
            halves(pairs, tiles, 2 * TILE, WINDOW),
            floats(length, width // 3),
        ],
        [
            part(0),
            pl.BlockSpec((1, tiles, 2 * TILE, WINDOW), lambda pair, pad: (pair, 0, 0, 0)),
            part(0),
        ],
        after,
        grid=(pairs,),
        scalars=(pad_start,),
        scratch=[
            pltpu.VMEM((tiles, TILE, WINDOW), jnp.float32),
            pltpu.VMEM((length, 1), jnp.float32),
            pltpu.VMEM((1, length), jnp.float32),
        ],
        cost=(
            16 * length * WINDOW * width // 3,
            14 * length * width // 3,
            length * WINDOW * 12,
        ),
        name="attn_forward",
        room=16,
        far=(0, 1, 2),
    )


def attn_backward_kernel(
    query_ref,
    key_ref,
    value_ref,
    context_ref,
    grad_ref,
    weight_ref,
    scale_ref,
    query_out,
    key_out,
    value_out,
    key_sum,
    value_sum,
):
    length = query_ref.shape[0]
    tiles = length // TILE
    low = lax.broadcasted_iota(jnp.int32, (TILE, 128), 1) < 64
    scale = jnp.asarray(0.125, jnp.bfloat16)
    key_sum[...] = jnp.zeros_like(key_sum)
    value_sum[...] = jnp.zeros_like(value_sum)

    for tile in range(tiles):
        rows = slice(tile * TILE, (tile + 1) * TILE)
        span = pl.ds(window_start(tile, tiles), WINDOW)
        queries = stack_heads(query_ref[rows, :] * scale, low)
        scaled = grad_ref[rows, :].astype(jnp.float32) * scale_ref[rows, :]
        product = stack_heads(scaled * context_ref[rows, :].astype(jnp.float32), low)
        delta = jnp.sum(product, axis=1, keepdims=True)
        grads = stack_heads(scaled.astype(jnp.bfloat16), low)
        keys = key_ref[span, :]
        weights = weight_ref[0, tile]
        grad_probs = dot_nt(grads, value_ref[span, :])
        grad_scores = (weights.astype(jnp.float32) * (grad_probs - delta)).astype(jnp.bfloat16)
        query_out[rows, :] = (merge_heads(dot_nn(grad_scores, keys), low) * 0.125).astype(
            jnp.bfloat16
        )
        key_sum[span, :] += dot_tn(grad_scores, queries)
        value_sum[span, :] += dot_tn(weights, grads)
    key_out[...] = key_sum[...].astype(jnp.bfloat16)
    value_out[...] = value_sum[...].astype(jnp.bfloat16)


def attn_backward(projected, context, context_grad, weights, scales, begin, pairs, after=()):
    length, width = projected.shape
    wide = width // 3 // 128
    tiles = length // TILE

    def part(offset):
        return pl.BlockSpec((length, 128), lambda pair: (0, offset * wide + begin + pair))

    out = halves(length, pairs * 128)
    *grads, token = ordered_call(
        attn_backward_kernel,
        (projected, projected, projected, context, context_grad, weights, scales),
        [
            part(0),
            part(1),
            part(2),
            part(0),
            part(0),
            pl.BlockSpec((1, tiles, 2 * TILE, WINDOW), lambda pair: (begin + pair, 0, 0, 0)),
            part(0),
        ],
        [out] * 3,
        [pl.BlockSpec((length, 128), lambda pair: (0, pair))] * 3,
        after,
        grid=(pairs,),
        scratch=[
            pltpu.VMEM((length, 128), jnp.float32),
            pltpu.VMEM((length, 128), jnp.float32),
        ],
        cost=(40 * length * WINDOW * pairs * 128, 16 * length * pairs * 128, 0),
        name="attn_backward",
        room=56,
        far=(0, 1, 2),
    )
    return grads, token


AXES = ("grp", "dp")


def swap(values, bit):
    count = lax.axis_size("grp") * lax.axis_size("dp")
    return lax.ppermute(values, AXES, [(i, i ^ bit) for i in range(count)])


def add_low(kept, came):
    return (kept.astype(jnp.float32) + came.astype(jnp.float32)).astype(jnp.bfloat16)


def pick(values, axis, index):
    return lax.index_in_dim(values, index, axis, keepdims=False)


def column_sums(block):
    ones = jnp.ones((8, block.shape[0]), jnp.bfloat16)
    return dot_nn(ones, block)


def mlp_grads_kernel(
    info, factor_ref, normed_ref, hidden_ref, active_ref, grad_ref, out_ref, bias_ref, small_ref
):
    step = pl.program_id(0)
    last = step == pl.num_programs(0) - 1
    own = info[1]
    count = out_ref.shape[0]
    rows = D // count
    factor = factor_ref[0]

    @pl.when(info[0] == 0)
    def _():
        grads = (dot_tn(normed_ref[...], hidden_ref[...]) * factor).astype(jnp.bfloat16)
        place = pl.ds(pl.multiple_of(step * rows, rows), rows)
        for dest in range(count):
            out_ref[dest ^ own, place, :] = grads[dest * rows : (dest + 1) * rows]
        bias_ref[:, pl.ds(pl.multiple_of(step * D, D), D)] = (
            column_sums(hidden_ref[...]) * factor
        )

        @pl.when(last)
        def _():
            small_ref[...] = jnp.zeros_like(small_ref)
            for dest in range(count):
                small_ref[0:1, 0 : 4 * rows] = bias_ref[
                    0:1, dest * 4 * rows : (dest + 1) * 4 * rows
                ]
                out_ref[dest ^ own, 4 * rows :, :] = small_ref[...].astype(jnp.bfloat16)

    @pl.when(info[0] == 1)
    def _():
        grads = (dot_tn(active_ref[...], grad_ref[...]) * factor).astype(jnp.bfloat16)
        per = count // 4
        for part in range(per):
            out_ref[(step * per + part) ^ own, 0 : 4 * rows, :] = grads[
                part * 4 * rows : (part + 1) * 4 * rows
            ]

        @pl.when(last)
        def _():
            bias_ref[:, 0:D] = column_sums(grad_ref[...]) * factor
            small_ref[...] = jnp.zeros_like(small_ref)
            for dest in range(count):
                small_ref[0:1, 0:rows] = bias_ref[0:1, dest * rows : (dest + 1) * rows]
                out_ref[dest ^ own, 4 * rows :, :] = small_ref[...].astype(jnp.bfloat16)


def mlp_grads(half, own, count, factor, normed, grad_hidden, active, grad_out, after=()):
    length = normed.shape[0]
    rows = D // count
    steps = grad_hidden.shape[1] // D
    shape = (count, 4 * rows + 8, D)
    return ordered_call(
        mlp_grads_kernel,
        (factor, normed, grad_hidden, active, grad_out),
        [
            pl.BlockSpec(memory_space=pltpu.SMEM),
            whole(normed),
            pl.BlockSpec((length, D), lambda i, info: (0, i * (1 - info[0]))),
            pl.BlockSpec((length, D), lambda i, info: (0, i * info[0])),
            whole(grad_out),
        ],
        [jax.ShapeDtypeStruct(shape, jnp.bfloat16)],
        [pl.BlockSpec(shape, lambda *_: (0, 0, 0))],
        after,
        grid=(steps,),
        scalars=(jnp.stack([half, own]),),
        scratch=[pltpu.VMEM((8, steps * D), jnp.float32), pltpu.VMEM((8, D), jnp.float32)],
        cost=(6 * length * D * D * steps, 16 * 2**20, 0),
        name="mlp_grads",
        room=47,
    )


def rest_grads_kernel(parts, info, factor_ref, normed_ref, context_ref, *refs):
    query_refs, refs = refs[:parts], refs[parts:]
    key_refs, refs = refs[:parts], refs[parts:]
    value_refs, refs = refs[:parts], refs[parts:]
    branch_ref, gain_one_ref, shift_one_ref, proj_bias_ref, gain_two_ref, shift_two_ref = refs[:6]
    out_ref, bias_ref, small_ref = refs[-3:]
    step = pl.program_id(0)
    own = info[1]
    count = out_ref.shape[0]
    rows = D // count
    factor = factor_ref[0]

    def block(first_ref, second_refs, position):
        begin = 0
        for second_ref in second_refs:
            end = begin + second_ref.shape[1]
            grads = (dot_tn(first_ref[...], second_ref[...]) * factor).astype(jnp.bfloat16)
            for dest in range(count):
                out_ref[dest ^ own, position * rows : (position + 1) * rows, begin:end] = grads[
                    dest * rows : (dest + 1) * rows
                ]
            begin = end

    @pl.when((info[0] == 0) & (step == 0))
    def _():
        block(normed_ref, query_refs, 0)

    @pl.when((info[0] == 0) & (step == 1))
    def _():
        block(normed_ref, key_refs, 1)
        begin = 0
        for ref in query_refs + key_refs + value_refs:
            end = begin + ref.shape[1]
            bias_ref[:, begin:end] = column_sums(ref[...])
            begin = end
        small_ref[...] = jnp.zeros_like(small_ref)
        for dest in range(count):
            part = slice(dest * rows, (dest + 1) * rows)
            wide = slice(dest * 3 * rows, (dest + 1) * 3 * rows)
            small_ref[0:1, 0:rows] = gain_one_ref[0:1, part]
            small_ref[0:1, rows : 2 * rows] = shift_one_ref[0:1, part]
            small_ref[0:1, 2 * rows : 5 * rows] = bias_ref[0:1, wide]
            small_ref[0:1, 5 * rows : 6 * rows] = proj_bias_ref[0:1, part]
            small_ref[0:1, 6 * rows : 7 * rows] = gain_two_ref[0:1, part]
            small_ref[0:1, 7 * rows : 8 * rows] = shift_two_ref[0:1, part]
            out_ref[dest ^ own, 2 * rows :, :] = (small_ref[...] * factor).astype(jnp.bfloat16)

    @pl.when((info[0] == 1) & (step == 0))
    def _():
        block(normed_ref, value_refs, 0)

    @pl.when((info[0] == 1) & (step == 1))
    def _():
        block(context_ref, (branch_ref,), 1)
        for dest in range(count):
            out_ref[dest, 2 * rows :, :] = jnp.zeros((8, D), jnp.bfloat16)


def rest_grads(
    half, own, count, factor, normed, context, query, key, value, branch, vectors, after=()
):
    length = normed.shape[0]
    rows = D // count
    operands = [normed, context, *query, *key, *value, branch]
    operands += vectors
    shape = (count, 2 * rows + 8, D)
    return ordered_call(
        functools.partial(rest_grads_kernel, len(query)),
        (factor, *operands),
        [pl.BlockSpec(memory_space=pltpu.SMEM)] + [whole(item) for item in operands],
        [jax.ShapeDtypeStruct(shape, jnp.bfloat16)],
        [pl.BlockSpec(shape, lambda *_: (0, 0, 0))],
        after,
        grid=(2,),
        scalars=(jnp.stack([half, own]),),
        scratch=[pltpu.VMEM((8, 3 * D), jnp.float32), pltpu.VMEM((8, D), jnp.float32)],
        cost=(16 * length * D * D, 12 * 2**20, 0),
        name="rest_grads",
        room=36,
    )


def first_split_kernel(cut, kept_ref, came_ref, *refs):
    first_stay, first_away, second_stay, second_away = refs
    for index in range(4):
        low, high = index % 2, index // 2
        target = first_away if low else first_stay
        target[high] = add_low(kept_ref[index, 0:cut, :], came_ref[index, 0:cut, :])
        target = second_away if high else second_stay
        target[low] = add_low(kept_ref[index, cut:, :], came_ref[index, cut:, :])


def first_split(kept, came, cut, after=()):
    count, rows, width = kept.shape
    sizes = (cut, cut, rows - cut, rows - cut)
    return ordered_call(
        functools.partial(first_split_kernel, cut),
        (kept, came),
        [pl.BlockSpec((4, rows, width), lambda i: (i, 0, 0))] * 2,
        [jax.ShapeDtypeStruct((count // 2, size, width), kept.dtype) for size in sizes],
        [pl.BlockSpec((2, size, width), lambda i: (i, 0, 0)) for size in sizes],
        after,
        grid=(count // 4,),
        cost=(count * rows * width, 6 * count * rows * width, 0),
        name="first_split",
        room=20,
        far=(0, 2),
    )


def next_split_kernel(parts, *refs):
    outs = refs[-2:] if parts == 1 else refs[-4:]
    for index in range(parts):
        kept_ref, came_ref = refs[2 * index : 2 * index + 2]
        for side in (0, 1):
            outs[2 * index + side][0] = add_low(kept_ref[side], came_ref[side])


def join_split_kernel(cut, *refs):
    first_kept, first_came, second_kept, second_came = refs[:4]
    for side, out in enumerate(refs[-2:]):
        out[0, 0:cut, :] = add_low(first_kept[side], first_came[side])
        out[0, cut:, :] = add_low(second_kept[side], second_came[side])


def next_split(pairs, joined, after=()):
    lead, _, width = pairs[0][0].shape
    heights = [kept.shape[1] for kept, _ in pairs]
    operands = [item for pair in pairs for item in pair]
    sizes = [sum(heights)] * 2 if joined else [size for size in heights for _ in (0, 1)]
    kernel = (
        functools.partial(join_split_kernel, heights[0])
        if joined
        else functools.partial(next_split_kernel, len(pairs))
    )
    total = lead * sum(heights) * width
    return ordered_call(
        kernel,
        operands,
        [pl.BlockSpec((2,) + item.shape[1:], lambda i: (i, 0, 0)) for item in operands],
        [jax.ShapeDtypeStruct((lead // 2, size, width), jnp.bfloat16) for size in sizes],
        [pl.BlockSpec((1, size, width), lambda i: (i, 0, 0)) for size in sizes],
        after,
        grid=(lead // 2,),
        cost=(total, 6 * total, 0),
        name="next_split",
        room=16,
    )


def reduce_blocks(came, kept):
    count = lax.axis_size("dp")
    depth = count.bit_length() - 1
    after = yield None
    cut = (kept.shape[1] - 8) // 2
    first, first_away, second, second_away, token = first_split(kept, came, cut, after)
    pairs = [(first, swap(first_away, 1)), (second, swap(second_away, 2))]
    after = yield token
    first, first_away, second, second_away, token = next_split(pairs, False, after)
    pairs = [(first, swap(first_away, 2)), (second, swap(second_away, 1))]
    after = yield token
    for position in range(2, depth):
        stay, away, token = next_split(pairs, position == 2, after)
        pairs = [(stay, swap(away, 1 << position))]
        after = yield token
    ((stay, came),) = pairs
    return final_sum(stay, came, after)


def finish(steps, works, sending):
    works = list(works)
    while True:
        after = (works.pop(0)(sending),) if works else ()
        try:
            sending = steps.send(after)
        except StopIteration as stop:
            for work in works:
                work(None)
            return stop.value


def final_sum_kernel(kept_ref, came_ref, out_ref):
    out_ref[...] = kept_ref[0].astype(jnp.float32) + came_ref[0].astype(jnp.float32)


def final_sum(kept, came, after=()):
    shape = jax.ShapeDtypeStruct(kept.shape[1:], jnp.float32)
    return ordered_call(
        final_sum_kernel,
        (kept, came),
        [whole(kept), whole(came)],
        [shape],
        [whole(shape)],
        after,
        name="final_sum",
        room=8,
    )


def tie_kernel(*refs):
    pass


def tie(values, *after):
    return pl.pallas_call(
        tie_kernel,
        out_shape=jax.ShapeDtypeStruct(values.shape, values.dtype),
        in_specs=[ANYWHERE] * (1 + len(after)),
        out_specs=ANYWHERE,
        input_output_aliases={0: 0},
        name="tie",
    )(values, *after)


def join_kernel(split, *refs):
    sems = refs[-1]
    ins = refs[: 2 if split else 4]
    outs = refs[len(ins) : -1]
    copies = []
    for index, out in enumerate(outs):
        for side in (0, 1):
            source = ins[side].at[:, index] if split else ins[2 * index + side]
            place = pl.ds(side * source.shape[0], source.shape[0])
            copies.append(pltpu.make_async_copy(source, out.at[place], sems.at[index, side]))
    for copy in copies:
        copy.start()
    for copy in copies:
        copy.wait()


def join_whole_kernel(first_ref, second_ref, out_ref, sems):
    copies = [
        pltpu.make_async_copy(
            ref, out_ref.at[pl.ds(side * ref.shape[0], ref.shape[0])], sems.at[0, side]
        )
        for side, ref in enumerate((first_ref, second_ref))
    ]
    for copy in copies:
        copy.start()
    for copy in copies:
        copy.wait()


def join_blocks(pairs, after=(), split=False):
    operands = [item for pair in pairs for item in pair]
    if split:
        lead, _, *rest = operands[0].shape
        shapes = [(2 * lead, *rest)] * 2
    else:
        shapes = [(2 * pair[0].shape[0], *pair[0].shape[1:]) for pair in pairs]
    shapes = [jax.ShapeDtypeStruct(shape, jnp.bfloat16) for shape in shapes]
    return ordered_call(
        join_whole_kernel if len(shapes) == 1 else functools.partial(join_kernel, split),
        operands,
        [ANYWHERE] * len(operands),
        shapes,
        [whole(shape) for shape in shapes],
        after,
        scratch=[pltpu.SemaphoreType.DMA((2, 2))],
        cost=(0, 4 * sum(shape.size for shape in shapes), 0),
        name="join_blocks",
        room=16,
    )


class Gather:
    def __init__(self, values):
        self.depth = lax.axis_size("dp").bit_length() - 1
        self.block = values.reshape(1, 2, -1, 128)
        self.slots = [0]
        self.position = self.depth - 1
        self.came = swap(self.block, 1 << self.position)

    def _grow(self, slots, position):
        return slots + [slot ^ (1 << position) for slot in slots]

    def outer(self, after=()):
        self.slots = self._grow(self.slots, self.position)
        if self.position > 2:
            self.block, token = join_blocks([(self.block, self.came)], after)
            self.position -= 1
            self.came = swap(self.block, 1 << self.position)
            return token
        *self.parts, token = join_blocks([(self.block, self.came)], after, split=True)
        self.came = [swap(self.parts[0], 2), swap(self.parts[1], 1)]
        return token

    def inner(self, after=()):
        *self.parts, token = join_blocks(list(zip(self.parts, self.came)), after)
        self.came = [swap(self.parts[0], 1), swap(self.parts[1], 2)]
        return token

    def others(self):
        count = lax.axis_size("dp")
        self.parts_other = [swap(part, count) for part in self.parts]

    def result(self, after=()):
        count = lax.axis_size("dp")
        came = [tie(item, *after) for item in self.came] if after else self.came
        came_other = [swap(item, count) for item in came]
        names = [self._grow(self.slots, 1), self._grow(self.slots, 0)]
        lists = []
        for name, bit in zip(names, (1, 2)):
            lists += [name, [slot ^ bit for slot in name]]
        arrays = [self.parts[0], came[0], self.parts[1], came[1]]
        others = [self.parts_other[0], came_other[0], self.parts_other[1], came_other[1]]
        return arrays, others, lists


def place(target, source_ref, rows, offset):
    row, lane = divmod(offset, 128)
    if lane == 0:
        target[row : row + rows, :] = source_ref[0:rows, :]
        return
    rolled = pltpu.roll(source_ref[0:rows, :], lane, 1)
    lanes = lax.broadcasted_iota(jnp.int32, (rows, 128), 1)
    target[row : row + rows, :] = jnp.where(lanes >= lane, rolled, target[row : row + rows, :])
    target[row + 1 : row + 1 + rows, :] = jnp.where(
        lanes < lane, rolled, target[row + 1 : row + 1 + rows, :]
    )


def place_line(target, line, offset):
    start, width = 0, line.shape[1]
    while start < width:
        row, lane = divmod(offset + start, 128)
        step = min(128 - lane, width - start)
        target[row : row + 1, lane : lane + step] = line[:, start : start + step]
        start += step


def spread(target, block, first, stride):
    for piece in range(block.shape[1] // 128):
        target[pl.ds(first + piece, block.shape[0], stride=stride), :] = block[
            :, piece * 128 : (piece + 1) * 128
        ]


def adam_rows(grads_ref, current_ref, first_ref, second_ref, outs, fresh_ref, start, width, plain):
    sum_out, first_out, second_out = outs

    def update(grads, current, old_first, old_second, position):
        new_first = beta_one * old_first + (1.0 - beta_one) * grads
        new_second = beta_two * old_second + (1.0 - beta_two) * grads * grads
        ratio = (
            new_first
            / (1.0 - beta_one**step_count)
            / (jnp.sqrt(new_second / (1.0 - beta_two**step_count)) + adam_eps)
        )
        decays = jnp.ones(grads.shape, jnp.bool_)
        for low, high in plain:
            decays = decays & ((position < low) | (position >= high))
        decay = jnp.where(decays, decay_rate, 0.0)
        fresh = current - learn_rate * (ratio + decay * current)
        return new_first, new_second, fresh

    group = 64
    loops = width // (group * 128)

    @pl.loop(0, loops)
    def _(index):
        rows = pl.ds(pl.multiple_of(index * group, group), group)
        begin = pl.multiple_of(index * (group * 128), 1024)
        there = pl.ds(pl.multiple_of(start + begin, 128), group * 128)
        here = pl.ds(begin, group * 128)
        shape = (group, 128)
        position = (
            begin
            + lax.broadcasted_iota(jnp.int32, shape, 0) * 128
            + lax.broadcasted_iota(jnp.int32, shape, 1)
        )
        grads = grads_ref[rows, :]
        new_first, new_second, fresh = update(
            grads,
            current_ref[rows, :],
            first_ref[0:1, there].reshape(shape),
            second_ref[0:1, there].reshape(shape),
            position,
        )
        sum_out[0:1, here] = grads.reshape(1, group * 128)
        first_out[0:1, here] = new_first.reshape(1, group * 128)
        second_out[0:1, here] = new_second.reshape(1, group * 128)
        fresh_ref[rows, :] = fresh

    begin = loops * group * 128
    while begin < width:
        size = min(128, width - begin)
        row = begin // 128
        grads = grads_ref[row : row + 1, 0:size]
        position = begin + lax.broadcasted_iota(jnp.int32, (1, size), 1)
        new_first, new_second, fresh = update(
            grads,
            current_ref[row : row + 1, 0:size],
            first_ref[0:1, start + begin : start + begin + size],
            second_ref[0:1, start + begin : start + begin + size],
            position,
        )
        sum_out[0:1, begin : begin + size] = grads
        first_out[0:1, begin : begin + size] = new_first
        second_out[0:1, begin : begin + size] = new_second
        fresh_ref[row : row + 1, 0:size] = fresh
        begin += size


def own_lines(target, info, count, lines, part_widths, offsets):
    for dest in range(count):

        @pl.when(info[1] == dest)
        def _():
            for line, width, offset in zip(lines, part_widths, offsets):
                place_line(
                    target,
                    line[:, dest * width : (dest + 1) * width].astype(jnp.float32),
                    offset,
                )


def send_half(info, fresh_ref, fresh_out):
    rows = fresh_out.shape[0]
    fresh_out[...] = fresh_ref[pl.ds(pl.multiple_of(info[0] * rows, 16), rows), :].astype(
        jnp.bfloat16
    )


def mlp_update_kernel(
    start,
    info,
    mine_ref,
    other_ref,
    fc1_ref,
    fc1_bias_ref,
    fc2_ref,
    fc2_bias_ref,
    first_ref,
    second_ref,
    sum_out,
    first_out,
    second_out,
    fresh_out,
    grads_ref,
    current_ref,
    fresh_ref,
    line_ref,
):
    rows = fc1_ref.shape[0]
    count = D // rows
    tiles = D // 128
    large = rows * 4 * D
    second = large + 4 * rows
    end = second + large

    def fill(fc1_half, fc2_half):
        for part in range(4):
            spread(
                grads_ref, fc1_half[part * rows : (part + 1) * rows, :], part * tiles, 4 * tiles
            )
        spread(line_ref, fc2_half[0 : 4 * rows, :], 0, tiles)
        place(grads_ref, line_ref, large // 128, second)
        place_line(grads_ref, fc1_half[4 * rows : 4 * rows + 1, 0 : 4 * rows], large)
        place_line(grads_ref, fc2_half[4 * rows : 4 * rows + 1, 0:rows], end)

    @pl.when(info[0] == 0)
    def _():
        fill(mine_ref, other_ref)

    @pl.when(info[0] != 0)
    def _():
        fill(other_ref, mine_ref)

    spread(current_ref, fc1_ref[...].astype(jnp.float32), 0, 4 * tiles)
    spread(line_ref, fc2_ref[...].astype(jnp.float32), 0, tiles)
    place(current_ref, line_ref, large // 128, second)
    own_lines(
        current_ref,
        info,
        count,
        (fc1_bias_ref[...], fc2_bias_ref[...]),
        (4 * rows, rows),
        (large, end),
    )
    adam_rows(
        grads_ref,
        current_ref,
        first_ref,
        second_ref,
        (sum_out, first_out, second_out),
        fresh_ref,
        start,
        end + rows,
        ((large, second), (end, end + rows)),
    )
    send_half(info, fresh_ref, fresh_out)


def rest_update_kernel(
    info,
    mine_ref,
    other_ref,
    qkv_ref,
    proj_ref,
    gain_one_ref,
    shift_one_ref,
    qkv_bias_ref,
    proj_bias_ref,
    gain_two_ref,
    shift_two_ref,
    first_ref,
    second_ref,
    sum_out,
    first_out,
    second_out,
    fresh_out,
    grads_ref,
    current_ref,
    fresh_ref,
    line_ref,
):
    rows = qkv_ref.shape[0]
    count = D // rows
    tiles = D // 128
    qkv_at = 2 * rows
    qkv_bias_at = qkv_at + 3 * rows * D
    proj_at = qkv_bias_at + 3 * rows
    proj_bias_at = proj_at + rows * D
    end = proj_bias_at + 3 * rows
    small = (0, rows, qkv_bias_at, proj_bias_at, proj_bias_at + rows, proj_bias_at + 2 * rows)
    widths = (rows, rows, 3 * rows, rows, rows, rows)

    def fill(first_half, second_half):
        spread(line_ref, first_half[0:rows, :], 0, 3 * tiles)
        spread(line_ref, first_half[rows : 2 * rows, :], tiles, 3 * tiles)
        spread(line_ref, second_half[0:rows, :], 2 * tiles, 3 * tiles)
        place(grads_ref, line_ref, 3 * rows * tiles, qkv_at)
        spread(line_ref, second_half[rows : 2 * rows, :], 0, tiles)
        place(grads_ref, line_ref, rows * tiles, proj_at)
        begin = 0
        for width, offset in zip(widths, small):
            place_line(
                grads_ref, first_half[2 * rows : 2 * rows + 1, begin : begin + width], offset
            )
            begin += width

    @pl.when(info[0] == 0)
    def _():
        fill(mine_ref, other_ref)

    @pl.when(info[0] != 0)
    def _():
        fill(other_ref, mine_ref)

    spread(line_ref, qkv_ref[...].astype(jnp.float32), 0, 3 * tiles)
    place(current_ref, line_ref, 3 * rows * tiles, qkv_at)
    spread(line_ref, proj_ref[...].astype(jnp.float32), 0, tiles)
    place(current_ref, line_ref, rows * tiles, proj_at)
    lines = (
        gain_one_ref[...],
        shift_one_ref[...],
        qkv_bias_ref[...],
        proj_bias_ref[...],
        gain_two_ref[...],
        shift_two_ref[...],
    )
    own_lines(current_ref, info, count, lines, widths, small)
    adam_rows(
        grads_ref,
        current_ref,
        first_ref,
        second_ref,
        (sum_out, first_out, second_out),
        fresh_ref,
        0,
        end,
        ((0, qkv_at), (qkv_bias_at, proj_at), (proj_bias_at, end)),
    )
    send_half(info, fresh_ref, fresh_out)


def update_call(
    kernel, name, info, mine, other, matrices, small, moments, width, order, after=()
):
    count = lax.axis_size("dp")
    half_rows = -(-width // 4096) * 16
    tall = 2 * half_rows

    operands = {("half", 0): (mine, whole(mine)), ("half", 1): (other, whole(other))}
    for index, item in enumerate(matrices):
        operands["matrix", index] = (
            item,
            pl.BlockSpec((item.shape[0] // count, item.shape[1]), lambda i, info: (info[1], 0)),
        )
    for index, item in enumerate(small[1:]):
        operands["small", index] = (small[0], vector_spec(item))
    for index, item in enumerate(moments):
        operands["moment", index] = (item, whole(item))
    chosen = [operands[key] for key in order]
    line = jax.ShapeDtypeStruct((1, width), jnp.float32)
    half_out = jax.ShapeDtypeStruct((half_rows, 128), jnp.bfloat16)
    return ordered_call(
        kernel,
        [item for item, _ in chosen],
        [spec for _, spec in chosen],
        [line, line, line, half_out],
        [whole(line)] * 3 + [whole(half_out)],
        after,
        scalars=(info,),
        scratch=[pltpu.VMEM((tall + 8, 128), jnp.float32) for _ in range(4)],
        cost=(2**20, 24 * 2**20, 0),
        name=name,
        room=36,
        far=(0, 1, 2),
    )


def assemble_kernel(lists, start, width, extra, info, *refs):
    each = 1 if lists is None else 4
    mine, other = refs[0:each], refs[each : 2 * each]
    refs = refs[2 * each + extra :]
    out_ref, refs = refs[0], refs[1:]
    tail = width % 128
    if tail:
        tail_ref, refs = refs[0], refs[1:]
    held, wide, in_sems, out_sems = refs
    count, rows = held.shape[1], held.shape[2]

    def pieces(segment):
        part = segment % 2
        if lists is None:
            whole_part = pl.ds(part * rows, rows)
            return [(lambda refs: refs[0].at[:, whole_part], held.at[segment], 0)]
        found = []
        for index in range(count):
            array, slot = divmod(index, count // 2)
            array += 2 * part
            target = held.at[segment, lists[array][slot] ^ info[1]]
            found.append(
                (lambda refs, array=array, slot=slot: refs[array].at[slot], target, index)
            )
        return found

    def arrivals(segment, begin):
        for source, target, index in pieces(segment):

            def copy(refs):
                return pltpu.make_async_copy(source(refs), target, in_sems.at[segment, index])

            if begin:

                @pl.when(info[0] == segment // 2)
                def _():
                    copy(mine).start()

                @pl.when(info[0] != segment // 2)
                def _():
                    copy(other).start()

            else:
                copy(mine).wait()

    def departure(segment):
        length = min(rows * 128, width - tail - segment * rows * 128)
        return pltpu.make_async_copy(
            wide.at[segment % 2, :, pl.ds(0, length)],
            out_ref.at[:, pl.ds(start + segment * rows * 128, length)],
            out_sems.at[segment],
        )

    for segment in range(4):
        arrivals(segment, True)
    for segment in range(4):
        arrivals(segment, False)
        if segment >= 2:
            departure(segment - 2).wait()
        wide[segment % 2] = held[segment].reshape(count, rows * 128)
        departure(segment).start()
        if segment == 3 and tail:
            at = width - tail - segment * rows * 128
            tail_ref[...] = wide[segment % 2, :, at : at + 128]
    departure(2).wait()
    departure(3).wait()


def fill_tail_kernel(source_ref, target_ref, out_ref):
    out_ref[...] = source_ref[...]


def fill_tail(target, source, token):
    last = target.shape[1] // 128
    return ordered_call(
        fill_tail_kernel,
        (source, target),
        [whole(source), ANYWHERE],
        [jax.ShapeDtypeStruct(target.shape, target.dtype)],
        [pl.BlockSpec(source.shape, lambda *_: (0, last))],
        (token,),
        aliases={1: 0},
        name="fill_tail",
        room=4,
    )


def assemble(info, arrays, others, lists, start, width, total, target=None, after=()):
    count = lax.axis_size("dp")
    rows = arrays[0].shape[1] // (2 if lists is None else 1)
    aliased = 0 if target is None else 1
    tail = width % 128
    out_shape = [jax.ShapeDtypeStruct((count, total), jnp.bfloat16)]
    out_specs = [ANYWHERE]
    if tail:
        out_shape.append(jax.ShapeDtypeStruct((count, 128), jnp.bfloat16))
        out_specs.append(whole(out_shape[-1]))
    operands = (*arrays, *others, *(() if target is None else (target,)))
    *outs, token = ordered_call(
        functools.partial(assemble_kernel, lists, start, width, aliased),
        operands,
        [ANYWHERE] * len(operands),
        out_shape,
        out_specs,
        after,
        scalars=(info,),
        scratch=[
            pltpu.VMEM((4, count, rows, 128), jnp.bfloat16),
            pltpu.VMEM((2, count, rows * 128), jnp.bfloat16),
            pltpu.SemaphoreType.DMA((4, count)),
            pltpu.SemaphoreType.DMA((4,)),
        ],
        cost=(2**20, 4 * count * width, 0),
        aliases={len(operands): 0} if aliased else {},
        name="assemble",
        room=28 if target is None else 56,
    )
    if tail:
        return fill_tail(*outs, token)
    return outs[0], token


def join_lines_kernel(*refs):
    for index in range(3):
        low, high, out = refs[index], refs[3 + index], refs[6 + index]
        width = low.shape[1]
        out[0:1, 0:width] = low[...]
        out[0:1, width:] = high[...]


def join_lines(lows, highs, after=()):
    operands = (*lows, *highs)
    line = jax.ShapeDtypeStruct((1, lows[0].shape[1] + highs[0].shape[1]), jnp.float32)
    return ordered_call(
        join_lines_kernel,
        operands,
        [whole(item) for item in operands],
        [line] * 3,
        [whole(line)] * 3,
        after,
        cost=(0, 24 * line.size, 0),
        name="join_lines",
        room=56,
    )


MLP_ORDER = (
    ("half", 0),
    ("half", 1),
    ("matrix", 0),
    ("small", 0),
    ("matrix", 1),
    ("small", 1),
    ("moment", 0),
    ("moment", 1),
)
REST_ORDER = (
    (("half", 0), ("half", 1), ("matrix", 0), ("matrix", 1))
    + tuple(("small", index) for index in range(6))
    + (("moment", 0), ("moment", 1))
)


ROWS = 256


def norm_rows(values):
    center = values - jnp.mean(values, axis=-1, keepdims=True)
    spread = lax.rsqrt(jnp.mean(center * center, axis=-1, keepdims=True) + norm_eps)
    return center * spread, spread


def norm_back(grads, gain, hat, spread):
    scaled = grads * gain
    inner = scaled - jnp.mean(scaled, axis=-1, keepdims=True)
    inner = inner - hat * jnp.mean(scaled * hat, axis=-1, keepdims=True)
    return (
        spread * inner,
        jnp.sum(grads * hat, axis=0, keepdims=True),
        jnp.sum(grads, axis=0, keepdims=True),
    )


def add_lines(refs, lines):
    first = pl.program_id(0) == 0

    @pl.when(first)
    def _():
        for ref, line in zip(refs, lines):
            ref[...] = line

    @pl.when(jnp.logical_not(first))
    def _():
        for ref, line in zip(refs, lines):
            ref[...] += line


def rows_of(item):
    return pl.BlockSpec((ROWS, item.shape[1]), lambda i, *_: (i, 0))


def first_part_kernel(
    pad_ref,
    tokens_ref,
    grad_ref,
    gain_ref,
    bias_ref,
    weight_ref,
    shift_ref,
    normed_out,
    out_ref,
    grad_out,
):
    hat, _ = norm_rows(tokens_ref[...].astype(jnp.float32))
    normed = (
        hat * gain_ref[...].astype(jnp.float32) + bias_ref[...].astype(jnp.float32)
    ).astype(jnp.bfloat16)
    normed_out[...] = normed
    out_ref[...] = (
        dot_nn(normed, weight_ref[...]) + shift_ref[...].astype(jnp.float32)
    ).astype(jnp.bfloat16)
    row = pl.program_id(0) * ROWS + lax.broadcasted_iota(jnp.int32, grad_ref.shape, 0)
    grads = grad_ref[...].astype(jnp.float32)
    grad_out[...] = jnp.where(row < pad_ref[0], grads, 0.0).astype(jnp.bfloat16)


def first_part(tokens, out_grad, vectors, weight, pad_start):
    length = tokens.shape[0]
    outs = [halves(length, D), halves(length, weight.shape[1]), halves(length, D)]
    return ordered_call(
        first_part_kernel,
        (tokens, out_grad, vectors, vectors, weight, vectors),
        [
            rows_of(tokens),
            rows_of(out_grad),
            vector_spec("gain_one"),
            vector_spec("shift_one"),
            whole(weight),
            vector_spec("qkv_bias"),
        ],
        outs,
        [rows_of(item) for item in outs],
        grid=(length // ROWS,),
        scalars=(pad_start,),
        cost=(2 * length * weight.size, 8 * 2**20, 0),
        name="norm_qkv",
        room=56,
        far=(0, 1, 2),
    )


def second_part_kernel(
    tokens_ref, context_ref, weight_ref, shift_ref, gain_ref, bias_ref, middle_out, normed_out
):
    middle = tokens_ref[...].astype(jnp.float32) + (
        dot_nn(context_ref[...], weight_ref[...]) + shift_ref[...].astype(jnp.float32)
    )
    middle_out[...] = middle
    hat, _ = norm_rows(middle)
    normed_out[...] = (
        hat * gain_ref[...].astype(jnp.float32) + bias_ref[...].astype(jnp.float32)
    ).astype(jnp.bfloat16)


def second_part(tokens, context, weight, vectors, after=()):
    length = tokens.shape[0]
    outs = [floats(length, D), halves(length, D)]
    return ordered_call(
        second_part_kernel,
        (tokens, context, weight, vectors, vectors, vectors),
        [
            rows_of(tokens),
            rows_of(context),
            whole(weight),
            vector_spec("proj_bias"),
            vector_spec("gain_two"),
            vector_spec("shift_two"),
        ],
        outs,
        [rows_of(item) for item in outs],
        after,
        grid=(length // ROWS,),
        cost=(2 * length * weight.size, 8 * 2**20, 0),
        name="proj_norm",
        room=12,
        far=(0, 1),
    )


def mlp_part_kernel(
    normed_ref, grad_ref, first_ref, shift_ref, second_ref, active_out, hidden_grad_out
):
    root = 0.7978845608028654
    for begin in range(0, normed_ref.shape[0], ROWS):
        rows = slice(begin, begin + ROWS)
        hidden = dot_nn(normed_ref[rows, :], first_ref[...]) + shift_ref[...].astype(jnp.float32)
        grad_active = dot_nt(grad_ref[rows, :], second_ref[...])
        square = hidden * hidden
        slope = jnp.tanh(hidden * (root + (root * 0.044715) * square))
        half = 0.5 + 0.5 * slope
        active_out[rows, :] = (hidden * half).astype(jnp.bfloat16)
        rise = half + (0.5 * hidden) * (1.0 - slope * slope) * (
            root + (3.0 * root * 0.044715) * square
        )
        hidden_grad_out[rows, :] = (grad_active * rise).astype(jnp.bfloat16)


def mlp_part(normed, grad_out, first, vectors, second, after=()):
    length, width = normed.shape[0], first.shape[1]
    step = D
    columns = pl.BlockSpec((length, step), lambda i: (0, i))
    outs = [halves(length, width)] * 2
    return ordered_call(
        mlp_part_kernel,
        (normed, grad_out, first, vectors, second),
        [
            whole(normed),
            whole(grad_out),
            pl.BlockSpec((D, step), lambda i: (0, i)),
            pl.BlockSpec((1, step), lambda i: (0, i)),
            pl.BlockSpec((step, D), lambda i: (i, 0)),
        ],
        outs,
        [columns, columns],
        after,
        grid=(width // step,),
        cost=(4 * length * D * width, 24 * 2**20, length * width),
        name="mlp_part",
        room=30,
        far=(0, 1),
    )


def middle_back_kernel(
    hidden_grad_ref,
    first_ref,
    middle_ref,
    gain_ref,
    grad_out_ref,
    proj_ref,
    middle_grad_out,
    branch_out,
    context_grad_out,
    gain_sum,
    bias_sum,
    proj_bias_sum,
):
    grads = dot_nt(hidden_grad_ref[...], first_ref[...])
    hat, spread = norm_rows(middle_ref[...])
    back, gain_line, bias_line = norm_back(
        grads, gain_ref[...].astype(jnp.float32), hat, spread
    )
    middle_grad = grad_out_ref[...].astype(jnp.float32) + back
    middle_grad_out[...] = middle_grad
    branch = middle_grad.astype(jnp.bfloat16)
    branch_out[...] = branch
    context_grad_out[...] = dot_nt(branch, proj_ref[...]).astype(jnp.bfloat16)
    proj_line = jnp.sum(branch.astype(jnp.float32), axis=0, keepdims=True)
    add_lines((gain_sum, bias_sum, proj_bias_sum), (gain_line, bias_line, proj_line))


def middle_back(hidden_grad, first, middle, vectors, grad_out, proj, after=()):
    length = middle.shape[0]
    line = floats(1, D)
    outs = [floats(length, D), halves(length, D), halves(length, D)]
    return ordered_call(
        middle_back_kernel,
        (hidden_grad, first, middle, vectors, grad_out, proj),
        [
            rows_of(hidden_grad),
            whole(first),
            rows_of(middle),
            vector_spec("gain_two"),
            rows_of(grad_out),
            whole(proj),
        ],
        outs + [line] * 3,
        [rows_of(item) for item in outs] + [whole(line)] * 3,
        after,
        grid=(length // ROWS,),
        cost=(2 * length * (first.size + proj.size), 24 * 2**20, 0),
        name="middle_back",
        room=32,
        far=(0, 1, 2),
    )


def input_back_kernel(parts, tokens_ref, gain_ref, weight_ref, middle_grad_ref, *refs):
    pieces, (out_ref, gain_sum, bias_sum) = refs[: 3 * parts], refs[3 * parts :]
    joined = jnp.concatenate([piece[...] for piece in pieces], axis=1)
    grads = dot_nt(joined, weight_ref[...])
    hat, spread = norm_rows(tokens_ref[...].astype(jnp.float32))
    back, gain_line, bias_line = norm_back(
        grads, gain_ref[...].astype(jnp.float32), hat, spread
    )
    out_ref[...] = (middle_grad_ref[...] + back).astype(jnp.bfloat16)
    add_lines((gain_sum, bias_sum), (gain_line, bias_line))


def input_back(tokens, vectors, weight, middle_grad, pieces, after=()):
    length = tokens.shape[0]
    line = floats(1, D)
    out = halves(length, D)
    return ordered_call(
        functools.partial(input_back_kernel, len(pieces) // 3),
        (tokens, vectors, weight, middle_grad, *pieces),
        [rows_of(tokens), vector_spec("gain_one"), whole(weight), rows_of(middle_grad)]
        + [rows_of(item) for item in pieces],
        [out, line, line],
        [rows_of(out), whole(line), whole(line)],
        after,
        grid=(length // ROWS,),
        cost=(2 * length * weight.size, 16 * 2**20, 0),
        name="input_back",
        room=56,
    )


def block_out_kernel(active_ref, weight_ref, shift_ref, middle_ref, out_ref):
    out_ref[...] = (
        middle_ref[...]
        + (dot_nn(active_ref[...], weight_ref[...]) + shift_ref[...].astype(jnp.float32))
    ).astype(jnp.bfloat16)


def block_out_rows(active, weight, vectors, middle, after=()):
    length = middle.shape[0]
    out = halves(length, D)
    return ordered_call(
        block_out_kernel,
        (active, weight, vectors, middle),
        [rows_of(active), whole(weight), vector_spec("fc2_bias"), rows_of(middle)],
        [out],
        [rows_of(out)],
        after,
        grid=(length // ROWS,),
        cost=(2 * length * weight.size, 16 * 2**20, 0),
        name="block_out",
        room=56,
    )


def on_device(
    tokens,
    out_grad,
    image_counts,
    group_of_device,
    group_weight,
    norm1_gain,
    norm1_bias,
    qkv_weight,
    qkv_bias,
    proj_weight,
    proj_bias,
    norm2_gain,
    norm2_bias,
    fc1_weight,
    fc1_bias,
    fc2_weight,
    fc2_bias,
    first_moment,
    second_moment,
):
    count = lax.axis_size("dp")
    core = lax.axis_index("grp")
    own = lax.axis_index("dp")
    info = jnp.stack([core, own])
    pad_start = jnp.sum(image_counts[0], keepdims=True)
    vectors = join_vectors(
        fc1_bias,
        norm1_gain,
        norm1_bias,
        qkv_bias,
        proj_bias,
        norm2_gain,
        norm2_bias,
        fc2_bias,
    )
    member = (group_of_device[0] == lax.iota(jnp.int32, 128)).astype(jnp.float32)
    images = jnp.sum((image_counts[0] > 0).astype(jnp.float32))
    totals = jnp.broadcast_to(member * images, (8, 128))
    bits = iter([1 << place for place in range((2 * count).bit_length() - 1)])

    def count_on(totals, *after):
        return add_totals(totals, swap(totals, next(bits)), after)

    normed_one, projected, grad_out, token = first_part(
        tokens, out_grad, vectors, qkv_weight, pad_start
    )
    totals, token = count_on(totals, token)
    context, weights, scales, token = attn_forward(projected, image_counts, pad_start, (token,))
    totals, token = count_on(totals, token)
    middle, normed_two, token = second_part(tokens, context, proj_weight, vectors, (token,))
    totals, token = count_on(totals, token)
    active, grad_hidden, token = mlp_part(
        normed_two, grad_out, fc1_weight, vectors, fc2_weight, (token,)
    )
    totals, token = count_on(totals, token)
    for _ in range((2 * count).bit_length() - 5):
        totals, token = count_on(totals, token)
    share = jnp.sum(member[:NGROUPS] * group_weight.astype(jnp.float32))
    factor = (share / jnp.sum(member * totals[0])).reshape(1)

    mlp_make = functools.partial(
        mlp_grads,
        own=own,
        count=count,
        factor=factor,
        normed=normed_two,
        grad_hidden=grad_hidden,
        active=active,
        grad_out=grad_out,
    )
    sent, token = mlp_make(1 - core)
    came = swap(sent, count)
    kept, _ = mlp_make(core, after=(token,))
    mlp_steps = reduce_blocks(came, kept)
    next(mlp_steps)
    sending = mlp_steps.send(())
    middle_grad, branch, context_grad, gain_two_sum, shift_two_sum, proj_bias_sum, token = (
        middle_back(grad_hidden, fc1_weight, middle, vectors, grad_out, proj_weight, (sending,))
    )
    wide = D // 128
    (query_grad, key_grad, value_grad), token = attn_backward(
        projected, context, context_grad, weights, scales, 0, wide, (token,)
    )
    sending = mlp_steps.send((token,))
    input_grad, gain_one_sum, shift_one_sum, token = input_back(
        tokens,
        vectors,
        qkv_weight,
        middle_grad,
        (query_grad, key_grad, value_grad),
        (sending,),
    )
    sending = mlp_steps.send((token,))
    rest_make = functools.partial(
        rest_grads,
        own=own,
        count=count,
        factor=factor,
        normed=normed_one,
        context=context,
        query=(query_grad,),
        key=(key_grad,),
        value=(value_grad,),
        branch=branch,
        vectors=(gain_one_sum, shift_one_sum, proj_bias_sum, gain_two_sum, shift_two_sum),
    )
    rest_sent, rest_token = rest_make(1 - core, after=(sending,))
    rest_kept, rest_order = [], []

    def keep_rest(sending):
        kept, token = rest_make(core, after=(rest_token,) if sending is None else (sending,))
        rest_kept.append(kept)
        rest_order.append(rest_token if sending is None else sending)
        return token

    mlp_mine, token = finish(mlp_steps, [lambda sending: rest_token, keep_rest], sending)
    mlp_parts = (mlp_mine, swap(mlp_mine, count))
    came = swap(tie(rest_sent, *rest_order), count)
    moments = (first_moment, second_moment)
    total = first_moment.shape[1]
    rest_width = (3 * D * D + D * D + 3 * D + 5 * D) // count
    mlp_width = total - rest_width
    *mlp_lines, mlp_fresh, update_token = update_call(
        functools.partial(mlp_update_kernel, rest_width),
        "mlp_update",
        info,
        *mlp_parts,
        (fc1_weight, fc2_weight),
        (vectors, "fc1_bias", "fc2_bias"),
        moments,
        mlp_width,
        MLP_ORDER,
        (came,),
    )
    mlp_gathered = lax.all_gather(mlp_fresh, "dp")
    rest_steps = reduce_blocks(came, rest_kept[0])
    next(rest_steps)
    sending = rest_steps.send((update_token,))
    block_state = []

    def block_rows(sending):
        block_state.extend(
            block_out_rows(active, fc2_weight, vectors, middle, (sending,))
        )
        return block_state[-1]

    rest_mine, _ = finish(rest_steps, [block_rows], sending)
    block_out, _ = block_state
    rest_parts = (rest_mine, swap(rest_mine, count))
    *rest_lines, rest_fresh, token = update_call(
        rest_update_kernel,
        "rest_update",
        info,
        *rest_parts,
        (qkv_weight, proj_weight),
        (vectors, "gain_one", "shift_one", "qkv_bias", "proj_bias", "gain_two", "shift_two"),
        moments,
        rest_width,
        REST_ORDER,
    )
    rest_gather = Gather(rest_fresh)
    summed, new_first, new_second, token = join_lines(rest_lines, mlp_lines, (token,))
    while rest_gather.position > 2:
        token = rest_gather.outer((token,))
    mlp_gathered = tie(mlp_gathered, token)
    mlp_other = swap(mlp_gathered, count)
    token = rest_gather.outer((token,))
    new_weights, token = assemble(
        info,
        [mlp_gathered],
        [mlp_other],
        None,
        rest_width,
        mlp_width,
        total,
        after=(token,),
    )
    rest_gather.inner((token,))
    rest_gather.others()
    new_weights, _ = assemble(info, *rest_gather.result(), 0, rest_width, total, new_weights)
    summed_bias = mlp_lines[0][0, mlp_width - D // count :]
    return (block_out, input_grad, summed, new_weights, new_first, new_second, summed_bias)


def add_totals_kernel(first_ref, second_ref, out_ref):
    out_ref[...] = first_ref[...] + second_ref[...]


def add_totals(first, second, after=()):
    return ordered_call(
        add_totals_kernel,
        (first, second),
        [whole(first), whole(second)],
        [floats(*first.shape)],
        [whole(first)],
        after,
        name="add_totals",
        room=4,
    )


def device_factor(counts_row, group_of_device, group_weight):
    images = jnp.sum((counts_row > 0).astype(jnp.int32))
    member = (group_of_device[0] == lax.iota(jnp.int32, NGROUPS)).astype(jnp.int32)
    totals = member * images
    for position in range((lax.axis_size("grp") * lax.axis_size("dp")).bit_length() - 1):
        totals = totals + swap(totals, 1 << position)
    return jnp.sum(member * group_weight).astype(jnp.float32) / jnp.sum(member * totals).astype(
        jnp.float32
    )


def general_device(
    tokens,
    out_grad,
    image_counts,
    group_of_device,
    group_weight,
    norm1_gain,
    norm1_bias,
    qkv_weight,
    qkv_bias,
    proj_weight,
    proj_bias,
    norm2_gain,
    norm2_bias,
    fc1_weight,
    fc1_bias,
    fc2_weight,
    fc2_bias,
    first_moment,
    second_moment,
):
    length = tokens.shape[0]
    segment, valid_rows = segment_info(image_counts[0], length)
    factor = device_factor(image_counts[0], group_of_device, group_weight)
    inputs = tokens.astype(jnp.float32)
    normed_one, norm_one_back = jax.vjp(
        layer_norm, inputs, norm1_gain.astype(jnp.float32), norm1_bias.astype(jnp.float32)
    )
    normed_one_low = normed_one.astype(jnp.bfloat16)
    projected = (
        jnp.dot(normed_one_low, qkv_weight, preferred_element_type=jnp.float32)
        + qkv_bias.astype(jnp.float32)
    ).astype(jnp.bfloat16)
    pad_start = jnp.sum(image_counts[0], keepdims=True)
    context, weights, scales, _ = attn_forward(projected, image_counts, pad_start)
    middle = inputs + (
        jnp.dot(context, proj_weight, preferred_element_type=jnp.float32)
        + proj_bias.astype(jnp.float32)
    )
    normed_two, norm_two_back = jax.vjp(
        layer_norm, middle, norm2_gain.astype(jnp.float32), norm2_bias.astype(jnp.float32)
    )
    normed_two_low = normed_two.astype(jnp.bfloat16)
    hidden = jnp.dot(
        normed_two_low, fc1_weight, preferred_element_type=jnp.float32
    ) + fc1_bias.astype(jnp.float32)
    activated, gelu_back = jax.vjp(gelu_tanh, hidden)
    activated_low = activated.astype(jnp.bfloat16)
    block_out = (
        middle
        + (
            jnp.dot(activated_low, fc2_weight, preferred_element_type=jnp.float32)
            + fc2_bias.astype(jnp.float32)
        )
    ).astype(jnp.bfloat16)
    grad_out = out_grad.astype(jnp.float32) * valid_rows[:, None].astype(jnp.float32)
    grad_out_low = grad_out.astype(jnp.bfloat16)
    fc2_grad = contract_rows(activated_low, grad_out_low)
    fc2_bias_grad = jnp.sum(grad_out, axis=0)
    grad_hidden = gelu_back(contract_cols(grad_out_low, fc2_weight))[0].astype(jnp.bfloat16)
    fc1_grad = contract_rows(normed_two_low, grad_hidden)
    fc1_bias_grad = jnp.sum(grad_hidden.astype(jnp.float32), axis=0)
    grad_middle_norm, gain_two_grad, shift_two_grad = norm_two_back(
        contract_cols(grad_hidden, fc1_weight)
    )
    grad_middle = grad_out + grad_middle_norm
    grad_branch = grad_middle.astype(jnp.bfloat16)
    proj_grad = contract_rows(context, grad_branch)
    proj_bias_grad = jnp.sum(grad_branch.astype(jnp.float32), axis=0)
    grad_context = contract_cols(grad_branch, proj_weight).astype(jnp.bfloat16)
    (query_grad, key_grad, value_grad), _ = attn_backward(
        projected, context, grad_context, weights, scales, 0, D // 128
    )
    grad_projected = jnp.concatenate([query_grad, key_grad, value_grad], axis=1)
    qkv_grad = contract_rows(normed_one_low, grad_projected)
    qkv_bias_grad = jnp.sum(grad_projected.astype(jnp.float32), axis=0)
    grad_input_norm, gain_one_grad, shift_one_grad = norm_one_back(
        contract_cols(grad_projected, qkv_weight)
    )
    input_grad = (grad_middle + grad_input_norm).astype(jnp.bfloat16)
    moments = (first_moment, second_moment)
    mlp_summed, rest_summed = exchange_grads(
        (gain_one_grad, shift_one_grad, qkv_grad, qkv_bias_grad, proj_grad, proj_bias_grad),
        (gain_two_grad, shift_two_grad, fc1_grad, fc1_bias_grad, fc2_grad, fc2_bias_grad),
        factor,
    )
    row_count = lax.axis_size("dp")
    own_index = lax.axis_index("dp")
    weight_list = (
        norm1_gain,
        norm1_bias,
        qkv_weight,
        qkv_bias,
        proj_weight,
        proj_bias,
        norm2_gain,
        norm2_bias,
        fc1_weight,
        fc1_bias,
        fc2_weight,
        fc2_bias,
    )
    own_weights = [
        lax.dynamic_slice_in_dim(item.reshape(row_count, -1), own_index, 1, 0)[0]
        for item in weight_list
    ]
    rows = D // row_count
    fc1_sum = mlp_summed[0].reshape(4, rows, D).transpose(1, 0, 2).reshape(-1)
    fc2_sum = mlp_summed[1].reshape(-1)
    qkv_sum = jnp.concatenate(
        [rest_summed[0, :rows], rest_summed[0, rows : 2 * rows], rest_summed[1, :rows]], axis=1
    ).reshape(-1)
    proj_sum = rest_summed[1, rows : 2 * rows].reshape(-1)
    small = rest_summed[0, 2 * rows]
    widths = [item.size // row_count for item in weight_list]
    small_parts = {}
    start = 0
    for index, flag in enumerate(decay_flags):
        if flag == 0.0:
            small_parts[index] = small[start : start + widths[index]]
            start += widths[index]
    large_parts = {2: qkv_sum, 4: proj_sum, 8: fc1_sum, 10: fc2_sum}
    pieces = [
        small_parts[index] if index in small_parts else large_parts[index] for index in range(12)
    ]
    split = sum(widths[:8])
    grads_out, first_out, second_out, fresh = [], [], [], []
    for lead, tail, begin, end in ((8, 12, split, sum(widths)), (0, 8, 0, split)):
        summed_part = jnp.concatenate(pieces[lead:tail])
        current = jnp.concatenate(own_weights[lead:tail]).astype(jnp.float32)
        decay = jnp.concatenate(
            [
                jnp.full((width,), flag, jnp.float32)
                for width, flag in zip(widths[lead:tail], decay_flags[lead:tail])
            ]
        )
        new_first = beta_one * moments[0][0, begin:end] + (1.0 - beta_one) * summed_part
        new_second = (
            beta_two * moments[1][0, begin:end] + (1.0 - beta_two) * summed_part * summed_part
        )
        ratio = (
            new_first
            / (1.0 - beta_one**step_count)
            / (jnp.sqrt(new_second / (1.0 - beta_two**step_count)) + adam_eps)
        )
        fresh_low = (current - learn_rate * (ratio + decay_rate * decay * current)).astype(
            jnp.bfloat16
        )
        grads_out.insert(0, summed_part)
        first_out.insert(0, new_first)
        second_out.insert(0, new_second)
        fresh.insert(0, gather_rows(fresh_low))
    summed = jnp.concatenate(grads_out)[None]
    new_first = jnp.concatenate(first_out)[None]
    new_second = jnp.concatenate(second_out)[None]
    new_weights = jnp.concatenate(fresh, axis=1)
    summed_bias = pieces[11]
    return (block_out, input_grad, summed, new_weights, new_first, new_second, summed_bias)


def bit_of(position):
    return (lax.axis_index("dp") >> position) & 1


def halve(values, position, positions):
    axis = positions.index(position)
    own = bit_of(position)
    sent = lax.dynamic_index_in_dim(values, 1 - own, axis, keepdims=False)
    kept = lax.dynamic_index_in_dim(values, own, axis, keepdims=False)
    return kept, swap(sent, 1 << position), [p for p in positions if p != position]


def reduce_rows(values):
    count = lax.axis_size("dp")
    grp = lax.axis_index("grp")
    kept = lax.dynamic_index_in_dim(values, grp, 0, keepdims=False)
    came = swap(lax.dynamic_index_in_dim(values, 1 - grp, 0, keepdims=False), count)
    kept = add_low(kept, came)
    depth = count.bit_length() - 1
    positions = list(range(depth))[::-1]
    rows = kept.shape[1]
    parts = [kept[:, : rows // 2], kept[:, rows // 2 :]]
    left = [positions, positions]
    parts = [part.reshape((2,) * depth + part.shape[1:]) for part in parts]
    for order in ((0, 1), (1, 0)):
        for index in (0, 1):
            part, came, left[index] = halve(parts[index], order[index], left[index])
            parts[index] = add_low(part, came)
    whole = jnp.concatenate(parts, axis=depth - 2)
    rest = left[0]
    for position in range(2, depth):
        part, came, rest = halve(whole, position, rest)
        if rest:
            whole = add_low(part, came)
        else:
            whole = part.astype(jnp.float32) + came.astype(jnp.float32)
    other = swap(whole, count)
    return jnp.where(grp == 0, jnp.stack([whole, other]), jnp.stack([other, whole]))


def join(own, came, bit):
    return jnp.where(bit == 0, jnp.stack([own, came]), jnp.stack([came, own]))


def gather_rows(values):
    count = lax.axis_size("dp")
    depth = count.bit_length() - 1
    grp = lax.axis_index("grp")
    width = values.shape[0]
    padded = -(-width // 4096) * 4096
    halves = jnp.pad(values, (0, padded - width)).reshape(2, 2, padded // 512, 128)
    own = lax.dynamic_index_in_dim(halves, grp, 0, keepdims=False)
    for position in range(2, depth)[::-1]:
        own = join(own, swap(own, 1 << position), bit_of(position))
    lead = own.ndim - 3
    parts = [lax.index_in_dim(own, i, lead, keepdims=False) for i in (0, 1)]
    for order in ((1, 0), (0, 1)):
        for index in (0, 1):
            position = order[index]
            parts[index] = join(
                parts[index], swap(parts[index], 1 << position), bit_of(position)
            )
    parts[1] = jnp.swapaxes(parts[1], 0, 1)
    full = jnp.stack(parts, axis=depth)
    full = full.transpose(tuple(range(depth))[::-1] + tuple(range(depth, full.ndim)))
    full = full.reshape((count,) + full.shape[depth:])
    other = swap(full, count)
    whole = jnp.where(
        grp == 0, jnp.stack([full, other], axis=1), jnp.stack([other, full], axis=1)
    )
    return whole.reshape(count, padded)[:, :width]


def exchange_grads(front, back, factor):
    gain_one, shift_one, qkv, qkv_bias, proj, proj_bias = front
    gain_two, shift_two, fc1, fc1_bias, fc2, fc2_bias = back
    count = lax.axis_size("dp")
    rows = D // count
    fc1_blocks = fc1.reshape(count, rows, 4, D).transpose(0, 2, 1, 3).reshape(count, 4 * rows, D)
    fc2_blocks = fc2.reshape(count, 4 * rows, D)
    mlp = (jnp.stack([fc1_blocks, fc2_blocks]) * factor).astype(jnp.bfloat16)
    small = jnp.concatenate(
        [
            item.reshape(count, -1)
            for item in (
                gain_one,
                shift_one,
                qkv_bias,
                proj_bias,
                gain_two,
                shift_two,
                fc1_bias,
                fc2_bias,
            )
        ],
        axis=1,
    )
    small = jnp.pad(small, ((0, 0), (0, D - small.shape[1])))[:, None]
    small = jnp.pad(small, ((0, 0), (0, 7), (0, 0)))
    qkv_blocks = qkv.reshape(count, rows, 3, D)
    first_half = jnp.concatenate([qkv_blocks[:, :, 0], qkv_blocks[:, :, 1], small], axis=1)
    second_half = jnp.concatenate(
        [qkv_blocks[:, :, 2], proj.reshape(count, rows, D), jnp.zeros_like(small)], axis=1
    )
    rest = (jnp.stack([first_half, second_half]) * factor).astype(jnp.bfloat16)
    return reduce_rows(mlp), reduce_rows(rest)


def solution(mesh):
    in_specs = (
        P(("grp", "dp"), None),
        P(("grp", "dp"), None),
        P(("grp", "dp"), None),
        P(("grp", "dp")),
        P(),
        P(),
        P(),
        P(),
        P(),
        P(),
        P(),
        P(),
        P(),
        P(),
        P(),
        P(),
        P(),
        P("dp", None),
        P("dp", None),
    )
    out_specs = (
        P(("grp", "dp"), None),
        P(("grp", "dp"), None),
        P("dp", None),
        P(),
        P("dp", None),
        P("dp", None),
        P("dp"),
    )
    rows = D // mesh.shape["dp"]
    return jax.shard_map(
        on_device if rows % 16 == 0 and mesh.shape["dp"] == 16 else general_device, mesh=mesh, in_specs=in_specs, out_specs=out_specs, check_vma=False
    )
```

```python
import functools

import jax
import jax.numpy as jnp
from jax import lax
from jax.experimental import pallas as pl
from jax.experimental.pallas import tpu as pltpu
from jax.sharding import PartitionSpec as P

D = 768
HEADS = 12
HEAD_DIM = 64
NGROUPS = 3


beta_one = 0.9
beta_two = 0.999
adam_eps = 1e-08
decay_rate = 0.05
step_count = 10.0
learn_rate = 0.004 * 0.75**1
norm_eps = 1e-06
neg_fill = -1e30
decay_flags = (0.0, 0.0, 1.0, 0.0, 1.0, 0.0, 0.0, 0.0, 1.0, 0.0, 1.0, 0.0)


def layer_norm(values, gain, shift):
    center = values - jnp.mean(values, axis=-1, keepdims=True)
    spread = jnp.mean(center * center, axis=-1, keepdims=True)
    return center * lax.rsqrt(spread + norm_eps) * gain + shift


def gelu_tanh(values):
    return jax.nn.gelu(values, approximate=True)


def contract_rows(first_op, second_op):
    return lax.dot_general(
        first_op, second_op, (((0,), (0,)), ((), ())), preferred_element_type=jnp.float32
    )


def contract_cols(first_op, second_op):
    return lax.dot_general(
        first_op, second_op, (((1,), (1,)), ((), ())), preferred_element_type=jnp.float32
    )


def segment_info(counts_row, length):
    slots = lax.iota(jnp.int32, counts_row.shape[0])
    segment_ends = jnp.sum(
        jnp.where(slots[:, None] <= slots[None, :], counts_row[:, None], 0), axis=0
    )
    position = lax.iota(jnp.int32, length)
    segment = jnp.sum((position[:, None] >= segment_ends[None, :]).astype(jnp.int32), axis=1)
    return (segment, position < segment_ends[-1])


TILE = 128
WINDOW = 3 * TILE


def window_start(tile, tiles):
    return min(max(tile - 1, 0), tiles - 3) * TILE


def dot_nt(first, second):
    return lax.dot_general(first, second, (((1,), (1,)), ((), ())), preferred_element_type=jnp.float32)


def dot_tn(first, second):
    return lax.dot_general(first, second, (((0,), (0,)), ((), ())), preferred_element_type=jnp.float32)


def dot_nn(first, second):
    return jnp.dot(first, second, preferred_element_type=jnp.float32)


def stack_heads(block, low):
    zero = jnp.zeros_like(block)
    return jnp.concatenate([jnp.where(low, block, zero), jnp.where(low, zero, block)], axis=0)


def merge_heads(block, low):
    return jnp.where(low, block[:TILE], block[TILE:])


def find_segments(counts_ref, seg_col_ref, seg_row_ref):
    slots, length = counts_ref.shape[1], seg_col_ref.shape[0]
    down = lax.broadcasted_iota(jnp.int32, (slots, slots), 0)
    across = lax.broadcasted_iota(jnp.int32, (slots, slots), 1)
    counts = jnp.broadcast_to(counts_ref[...].astype(jnp.float32), (slots, slots))
    ends_col = jnp.sum(jnp.where(across <= down, counts, 0.0), axis=1, keepdims=True)
    ends_row = jnp.sum(jnp.where(across == down, ends_col, 0.0), axis=0, keepdims=True)
    place_col = lax.broadcasted_iota(jnp.int32, (length, slots), 0).astype(jnp.float32)
    place_row = lax.broadcasted_iota(jnp.int32, (slots, length), 1).astype(jnp.float32)
    seg_col_ref[...] = jnp.sum(jnp.where(place_col >= ends_row, 1.0, 0.0), axis=1, keepdims=True)
    seg_row_ref[...] = jnp.sum(jnp.where(place_row >= ends_col, 1.0, 0.0), axis=0, keepdims=True)


def fill_masks(bias_ref, seg_col_ref, seg_row_ref, tiles):
    for tile in range(tiles):
        start = window_start(tile, tiles)
        same = (
            seg_col_ref[tile * TILE : (tile + 1) * TILE, :]
            == seg_row_ref[:, start : start + WINDOW]
        )
        bias_ref[tile] = jnp.where(same, 0.0, neg_fill)


ANYWHERE = pl.BlockSpec(memory_space=pl.ANY)
VMEM_BYTES = 56 * 2**20


VECTORS = {
    "fc1_bias": (0, 3072),
    "gain_one": (3072, 768),
    "shift_one": (3840, 768),
    "qkv_bias": (4608, 2304),
    "proj_bias": (6912, 768),
    "gain_two": (7680, 768),
    "shift_two": (8448, 768),
    "fc2_bias": (9216, 768),
}


def join_vectors_kernel(*refs):
    begin = 0
    for ref in refs[:-1]:
        width = ref.shape[0]
        refs[-1][0:1, begin : begin + width] = ref[...].reshape(1, width)
        begin += width


def join_vectors(*vectors):
    return pl.pallas_call(
        join_vectors_kernel,
        out_shape=halves(1, sum(item.shape[0] for item in vectors)),
        name="join_vectors",
    )(*vectors)


def vector_spec(name):
    begin, width = VECTORS[name]
    return pl.BlockSpec((1, width), lambda *_: (0, begin // width))


def ordered_kernel(kernel, first, extra, outs, *refs):
    token = refs[first + extra + outs]
    token[...] = jnp.zeros_like(token)
    kernel(*refs[:first], *refs[first + extra : first + extra + outs], *refs[first + extra + outs + 1 :])


def ordered_call(
    kernel, operands, in_specs, out_shape, out_specs, after=(), grid=(1,), scalars=(), scratch=(),
    cost=(0, 0, 0), aliases=None, name=None, room=56, far=(),
):
    out_shape = [
        pltpu.HBM(item.shape, item.dtype) if index in far else item
        for index, item in enumerate(out_shape)
    ]
    call = pl.pallas_call(
        functools.partial(
            ordered_kernel, kernel, len(scalars) + len(operands), len(after), len(out_shape)
        ),
        out_shape=[*out_shape, jax.ShapeDtypeStruct((8, 128), jnp.float32)],
        grid_spec=pltpu.PrefetchScalarGridSpec(
            num_scalar_prefetch=len(scalars),
            grid=grid,
            in_specs=[*in_specs] + [ANYWHERE] * len(after),
            out_specs=[*out_specs, pl.BlockSpec((8, 128), lambda *_: (0, 0))],
            scratch_shapes=list(scratch),
        ),
        input_output_aliases=aliases or {},
        compiler_params=pltpu.CompilerParams(vmem_limit_bytes=room * 2**20),
        cost_estimate=pl.CostEstimate(
            flops=cost[0], bytes_accessed=cost[1], transcendentals=cost[2]
        ),
        name=name,
    )
    return call(*scalars, *operands, *after)


def whole(item):
    return pl.BlockSpec(item.shape, lambda *_: (0,) * len(item.shape))


def floats(*shape):
    return jax.ShapeDtypeStruct(shape, jnp.float32)


def halves(*shape):
    return jax.ShapeDtypeStruct(shape, jnp.bfloat16)


def attn_forward_kernel(
    pad_ref,
    query_ref,
    key_ref,
    value_ref,
    counts_ref,
    out_ref,
    weight_out,
    scale_out,
    bias_ref,
    seg_col_ref,
    seg_row_ref,
):
    length = query_ref.shape[0]
    tiles = length // TILE

    @pl.when(pl.program_id(0) == 0)
    def _():
        find_segments(counts_ref, seg_col_ref, seg_row_ref)
        fill_masks(bias_ref, seg_col_ref, seg_row_ref, tiles)

    low = lax.broadcasted_iota(jnp.int32, (TILE, 128), 1) < 64
    scale = jnp.asarray(0.125, jnp.bfloat16)

    def head_rows(queries, keys, values, bias):
        scores = dot_nt(queries, keys) + bias
        weights = jnp.exp(scores - jnp.max(scores, axis=1, keepdims=True)).astype(jnp.bfloat16)
        ones = jnp.ones((values.shape[0], 128), jnp.bfloat16)
        mixed = dot_nn(weights, jnp.concatenate([values, ones], axis=1))
        inverse = 1.0 / mixed[:, 128:]
        return weights, mixed[:, :128] * inverse, inverse

    for tile in range(tiles):
        span = pl.ds(window_start(tile, tiles), WINDOW)
        rows = slice(tile * TILE, (tile + 1) * TILE)
        queries = query_ref[rows, :] * scale
        zero = jnp.zeros_like(queries)
        first, second = (
            head_rows(part, key_ref[span, :], value_ref[span, :], bias_ref[tile])
            for part in (jnp.where(low, queries, zero), jnp.where(low, zero, queries))
        )
        weight_out[0, tile, 0:TILE, :] = first[0]
        weight_out[0, tile, TILE:, :] = second[0]
        out_ref[rows, :] = jnp.where(low, first[1], second[1]).astype(jnp.bfloat16)
        scale_out[rows, :] = jnp.where(low, first[2], second[2])

    @pl.loop(0, tiles)
    def _(tile):
        start = jnp.minimum(jnp.maximum(tile - 1, 0), tiles - 3) * TILE
        padding = (tile + 1) * TILE > pad_ref[0]
        outside = (pad_ref[0] < start) | (start + WINDOW < length)

        @pl.when(padding & outside)
        def _():
            rows = pl.ds(pl.multiple_of(tile * TILE, TILE), TILE)
            queries = query_ref[rows, :] * scale
            zero = jnp.zeros_like(queries)
            bias = jnp.where(seg_col_ref[rows, :] == seg_row_ref[...], 0.0, neg_fill)
            first, second = (
                head_rows(part, key_ref[...], value_ref[...], bias)
                for part in (jnp.where(low, queries, zero), jnp.where(low, zero, queries))
            )
            out_ref[rows, :] = jnp.where(low, first[1], second[1]).astype(jnp.bfloat16)


def attn_forward(projected, image_counts, pad_start, after=()):
    length, width = projected.shape
    pairs = width // 3 // 128
    tiles = length // TILE

    def part(offset):
        return pl.BlockSpec((length, 128), lambda pair, pad: (0, offset * pairs + pair))

    return ordered_call(
        attn_forward_kernel,
        (projected, projected, projected, image_counts),
        [part(0), part(1), part(2), whole(image_counts)],
        [
            halves(length, width // 3),
            halves(pairs, tiles, 2 * TILE, WINDOW),
            floats(length, width // 3),
        ],
        [
            part(0),
            pl.BlockSpec((1, tiles, 2 * TILE, WINDOW), lambda pair, pad: (pair, 0, 0, 0)),
            part(0),
        ],
        after,
        grid=(pairs,),
        scalars=(pad_start,),
        scratch=[
            pltpu.VMEM((tiles, TILE, WINDOW), jnp.float32),
            pltpu.VMEM((length, 1), jnp.float32),
            pltpu.VMEM((1, length), jnp.float32),
        ],
        cost=(
            16 * length * WINDOW * width // 3,
            14 * length * width // 3,
            length * WINDOW * 12,
        ),
        name="attn_forward",
        room=52,
        far=(0, 1, 2),
    )


def attn_backward_kernel(
    query_ref,
    key_ref,
    value_ref,
    context_ref,
    grad_ref,
    weight_ref,
    scale_ref,
    query_out,
    key_out,
    value_out,
    key_sum,
    value_sum,
):
    length = query_ref.shape[0]
    tiles = length // TILE
    low = lax.broadcasted_iota(jnp.int32, (TILE, 128), 1) < 64
    scale = jnp.asarray(0.125, jnp.bfloat16)
    key_sum[...] = jnp.zeros_like(key_sum)
    value_sum[...] = jnp.zeros_like(value_sum)

    for tile in range(tiles):
        rows = slice(tile * TILE, (tile + 1) * TILE)
        span = pl.ds(window_start(tile, tiles), WINDOW)
        queries = stack_heads(query_ref[rows, :] * scale, low)
        scaled = grad_ref[rows, :].astype(jnp.float32) * scale_ref[rows, :]
        product = stack_heads(scaled * context_ref[rows, :].astype(jnp.float32), low)
        delta = jnp.sum(product, axis=1, keepdims=True)
        grads = stack_heads(scaled.astype(jnp.bfloat16), low)
        keys = key_ref[span, :]
        weights = weight_ref[0, tile]
        grad_probs = dot_nt(grads, value_ref[span, :])
        grad_scores = (weights.astype(jnp.float32) * (grad_probs - delta)).astype(jnp.bfloat16)
        query_out[rows, :] = (merge_heads(dot_nn(grad_scores, keys), low) * 0.125).astype(
            jnp.bfloat16
        )
        key_sum[span, :] += dot_tn(grad_scores, queries)
        value_sum[span, :] += dot_tn(weights, grads)
    key_out[...] = key_sum[...].astype(jnp.bfloat16)
    value_out[...] = value_sum[...].astype(jnp.bfloat16)


def attn_backward(projected, context, context_grad, weights, scales, begin, pairs, after=()):
    length, width = projected.shape
    wide = width // 3 // 128
    tiles = length // TILE

    def part(offset):
        return pl.BlockSpec((length, 128), lambda pair: (0, offset * wide + begin + pair))

    out = halves(length, pairs * 128)
    *grads, token = ordered_call(
        attn_backward_kernel,
        (projected, projected, projected, context, context_grad, weights, scales),
        [
            part(0),
            part(1),
            part(2),
            part(0),
            part(0),
            pl.BlockSpec((1, tiles, 2 * TILE, WINDOW), lambda pair: (begin + pair, 0, 0, 0)),
            part(0),
        ],
        [out] * 3,
        [pl.BlockSpec((length, 128), lambda pair: (0, pair))] * 3,
        after,
        grid=(pairs,),
        scratch=[
            pltpu.VMEM((length, 128), jnp.float32),
            pltpu.VMEM((length, 128), jnp.float32),
        ],
        cost=(40 * length * WINDOW * pairs * 128, 16 * length * pairs * 128, 0),
        name="attn_backward",
        room=56,
        far=(0, 1, 2),
    )
    return grads, token


AXES = ("grp", "dp")


def swap(values, bit):
    count = lax.axis_size("grp") * lax.axis_size("dp")
    return lax.ppermute(values, AXES, [(i, i ^ bit) for i in range(count)])


def add_low(kept, came):
    return (kept.astype(jnp.float32) + came.astype(jnp.float32)).astype(jnp.bfloat16)


def pick(values, axis, index):
    return lax.index_in_dim(values, index, axis, keepdims=False)


def column_sums(block):
    ones = jnp.ones((8, block.shape[0]), jnp.bfloat16)
    return dot_nn(ones, block)


def mlp_grads_kernel(
    info, factor_ref, normed_ref, hidden_ref, active_ref, grad_ref, out_ref, bias_ref, small_ref
):
    step = pl.program_id(0)
    last = step == pl.num_programs(0) - 1
    own = info[1]
    count = out_ref.shape[0]
    rows = D // count
    factor = factor_ref[0]

    @pl.when(info[0] == 0)
    def _():
        grads = (dot_tn(normed_ref[...], hidden_ref[...]) * factor).astype(jnp.bfloat16)
        place = pl.ds(pl.multiple_of(step * rows, rows), rows)
        for dest in range(count):
            out_ref[dest ^ own, place, :] = grads[dest * rows : (dest + 1) * rows]
        bias_ref[:, pl.ds(pl.multiple_of(step * D, D), D)] = (
            column_sums(hidden_ref[...]) * factor
        )

        @pl.when(last)
        def _():
            small_ref[...] = jnp.zeros_like(small_ref)
            for dest in range(count):
                small_ref[0:1, 0 : 4 * rows] = bias_ref[
                    0:1, dest * 4 * rows : (dest + 1) * 4 * rows
                ]
                out_ref[dest ^ own, 4 * rows :, :] = small_ref[...].astype(jnp.bfloat16)

    @pl.when(info[0] == 1)
    def _():
        grads = (dot_tn(active_ref[...], grad_ref[...]) * factor).astype(jnp.bfloat16)
        per = count // 4
        for part in range(per):
            out_ref[(step * per + part) ^ own, 0 : 4 * rows, :] = grads[
                part * 4 * rows : (part + 1) * 4 * rows
            ]

        @pl.when(last)
        def _():
            bias_ref[:, 0:D] = column_sums(grad_ref[...]) * factor
            small_ref[...] = jnp.zeros_like(small_ref)
            for dest in range(count):
                small_ref[0:1, 0:rows] = bias_ref[0:1, dest * rows : (dest + 1) * rows]
                out_ref[dest ^ own, 4 * rows :, :] = small_ref[...].astype(jnp.bfloat16)


def mlp_grads(half, own, count, factor, normed, grad_hidden, active, grad_out, after=()):
    length = normed.shape[0]
    rows = D // count
    steps = grad_hidden.shape[1] // D
    shape = (count, 4 * rows + 8, D)
    return ordered_call(
        mlp_grads_kernel,
        (factor, normed, grad_hidden, active, grad_out),
        [
            pl.BlockSpec(memory_space=pltpu.SMEM),
            whole(normed),
            pl.BlockSpec((length, D), lambda i, info: (0, i * (1 - info[0]))),
            pl.BlockSpec((length, D), lambda i, info: (0, i * info[0])),
            whole(grad_out),
        ],
        [jax.ShapeDtypeStruct(shape, jnp.bfloat16)],
        [pl.BlockSpec(shape, lambda *_: (0, 0, 0))],
        after,
        grid=(steps,),
        scalars=(jnp.stack([half, own]),),
        scratch=[pltpu.VMEM((8, steps * D), jnp.float32), pltpu.VMEM((8, D), jnp.float32)],
        cost=(6 * length * D * D * steps, 16 * 2**20, 0),
        name="mlp_grads",
        room=47,
    )


def rest_grads_kernel(parts, info, factor_ref, normed_ref, context_ref, *refs):
    query_refs, refs = refs[:parts], refs[parts:]
    key_refs, refs = refs[:parts], refs[parts:]
    value_refs, refs = refs[:parts], refs[parts:]
    branch_ref, gain_one_ref, shift_one_ref, proj_bias_ref, gain_two_ref, shift_two_ref = refs[:6]
    out_ref, bias_ref, small_ref = refs[-3:]
    step = pl.program_id(0)
    own = info[1]
    count = out_ref.shape[0]
    rows = D // count
    factor = factor_ref[0]

    def block(first_ref, second_refs, position):
        begin = 0
        for second_ref in second_refs:
            end = begin + second_ref.shape[1]
            grads = (dot_tn(first_ref[...], second_ref[...]) * factor).astype(jnp.bfloat16)
            for dest in range(count):
                out_ref[dest ^ own, position * rows : (position + 1) * rows, begin:end] = grads[
                    dest * rows : (dest + 1) * rows
                ]
            begin = end

    @pl.when((info[0] == 0) & (step == 0))
    def _():
        block(normed_ref, query_refs, 0)

    @pl.when((info[0] == 0) & (step == 1))
    def _():
        block(normed_ref, key_refs, 1)
        begin = 0
        for ref in query_refs + key_refs + value_refs:
            end = begin + ref.shape[1]
            bias_ref[:, begin:end] = column_sums(ref[...])
            begin = end
        small_ref[...] = jnp.zeros_like(small_ref)
        for dest in range(count):
            part = slice(dest * rows, (dest + 1) * rows)
            wide = slice(dest * 3 * rows, (dest + 1) * 3 * rows)
            small_ref[0:1, 0:rows] = gain_one_ref[0:1, part]
            small_ref[0:1, rows : 2 * rows] = shift_one_ref[0:1, part]
            small_ref[0:1, 2 * rows : 5 * rows] = bias_ref[0:1, wide]
            small_ref[0:1, 5 * rows : 6 * rows] = proj_bias_ref[0:1, part]
            small_ref[0:1, 6 * rows : 7 * rows] = gain_two_ref[0:1, part]
            small_ref[0:1, 7 * rows : 8 * rows] = shift_two_ref[0:1, part]
            out_ref[dest ^ own, 2 * rows :, :] = (small_ref[...] * factor).astype(jnp.bfloat16)

    @pl.when((info[0] == 1) & (step == 0))
    def _():
        block(normed_ref, value_refs, 0)

    @pl.when((info[0] == 1) & (step == 1))
    def _():
        block(context_ref, (branch_ref,), 1)
        for dest in range(count):
            out_ref[dest, 2 * rows :, :] = jnp.zeros((8, D), jnp.bfloat16)


def rest_grads(
    half, own, count, factor, normed, context, query, key, value, branch, vectors, after=()
):
    length = normed.shape[0]
    rows = D // count
    operands = [normed, context, *query, *key, *value, branch]
    operands += vectors
    shape = (count, 2 * rows + 8, D)
    return ordered_call(
        functools.partial(rest_grads_kernel, len(query)),
        (factor, *operands),
        [pl.BlockSpec(memory_space=pltpu.SMEM)] + [whole(item) for item in operands],
        [jax.ShapeDtypeStruct(shape, jnp.bfloat16)],
        [pl.BlockSpec(shape, lambda *_: (0, 0, 0))],
        after,
        grid=(2,),
        scalars=(jnp.stack([half, own]),),
        scratch=[pltpu.VMEM((8, 3 * D), jnp.float32), pltpu.VMEM((8, D), jnp.float32)],
        cost=(16 * length * D * D, 12 * 2**20, 0),
        name="rest_grads",
        room=36,
    )


def first_split_kernel(cut, kept_ref, came_ref, *refs):
    first_stay, first_away, second_stay, second_away = refs
    for index in range(4):
        low, high = index % 2, index // 2
        target = first_away if low else first_stay
        target[high] = add_low(kept_ref[index, 0:cut, :], came_ref[index, 0:cut, :])
        target = second_away if high else second_stay
        target[low] = add_low(kept_ref[index, cut:, :], came_ref[index, cut:, :])


def first_split(kept, came, cut, after=()):
    count, rows, width = kept.shape
    sizes = (cut, cut, rows - cut, rows - cut)
    return ordered_call(
        functools.partial(first_split_kernel, cut),
        (kept, came),
        [pl.BlockSpec((4, rows, width), lambda i: (i, 0, 0))] * 2,
        [jax.ShapeDtypeStruct((count // 2, size, width), kept.dtype) for size in sizes],
        [pl.BlockSpec((2, size, width), lambda i: (i, 0, 0)) for size in sizes],
        after,
        grid=(count // 4,),
        cost=(count * rows * width, 6 * count * rows * width, 0),
        name="first_split",
        room=20,
        far=(0, 2),
    )


def next_split_kernel(parts, *refs):
    outs = refs[-2:] if parts == 1 else refs[-4:]
    for index in range(parts):
        kept_ref, came_ref = refs[2 * index : 2 * index + 2]
        for side in (0, 1):
            outs[2 * index + side][0] = add_low(kept_ref[side], came_ref[side])


def join_split_kernel(cut, *refs):
    first_kept, first_came, second_kept, second_came = refs[:4]
    for side, out in enumerate(refs[-2:]):
        out[0, 0:cut, :] = add_low(first_kept[side], first_came[side])
        out[0, cut:, :] = add_low(second_kept[side], second_came[side])


def next_split(pairs, joined, after=()):
    lead, _, width = pairs[0][0].shape
    heights = [kept.shape[1] for kept, _ in pairs]
    operands = [item for pair in pairs for item in pair]
    sizes = [sum(heights)] * 2 if joined else [size for size in heights for _ in (0, 1)]
    kernel = (
        functools.partial(join_split_kernel, heights[0])
        if joined
        else functools.partial(next_split_kernel, len(pairs))
    )
    total = lead * sum(heights) * width
    return ordered_call(
        kernel,
        operands,
        [pl.BlockSpec((2,) + item.shape[1:], lambda i: (i, 0, 0)) for item in operands],
        [jax.ShapeDtypeStruct((lead // 2, size, width), jnp.bfloat16) for size in sizes],
        [pl.BlockSpec((1, size, width), lambda i: (i, 0, 0)) for size in sizes],
        after,
        grid=(lead // 2,),
        cost=(total, 6 * total, 0),
        name="next_split",
        room=16,
    )


def reduce_blocks(came, kept):
    count = lax.axis_size("dp")
    depth = count.bit_length() - 1
    after = yield None
    cut = (kept.shape[1] - 8) // 2
    first, first_away, second, second_away, token = first_split(kept, came, cut, after)
    pairs = [(first, swap(first_away, 1)), (second, swap(second_away, 2))]
    after = yield token
    first, first_away, second, second_away, token = next_split(pairs, False, after)
    pairs = [(first, swap(first_away, 2)), (second, swap(second_away, 1))]
    after = yield token
    for position in range(2, depth):
        stay, away, token = next_split(pairs, position == 2, after)
        pairs = [(stay, swap(away, 1 << position))]
        after = yield token
    ((stay, came),) = pairs
    return final_sum(stay, came, after)


def finish(steps, works, sending):
    works = list(works)
    while True:
        after = (works.pop(0)(sending),) if works else ()
        try:
            sending = steps.send(after)
        except StopIteration as stop:
            for work in works:
                work(None)
            return stop.value


def final_sum_kernel(kept_ref, came_ref, out_ref):
    out_ref[...] = kept_ref[0].astype(jnp.float32) + came_ref[0].astype(jnp.float32)


def final_sum(kept, came, after=()):
    shape = jax.ShapeDtypeStruct(kept.shape[1:], jnp.float32)
    return ordered_call(
        final_sum_kernel,
        (kept, came),
        [whole(kept), whole(came)],
        [shape],
        [whole(shape)],
        after,
        name="final_sum",
        room=8,
    )


def tie_kernel(*refs):
    pass


def tie(values, *after):
    return pl.pallas_call(
        tie_kernel,
        out_shape=jax.ShapeDtypeStruct(values.shape, values.dtype),
        in_specs=[ANYWHERE] * (1 + len(after)),
        out_specs=ANYWHERE,
        input_output_aliases={0: 0},
        name="tie",
    )(values, *after)


def join_kernel(split, *refs):
    sems = refs[-1]
    ins = refs[: 2 if split else 4]
    outs = refs[len(ins) : -1]
    copies = []
    for index, out in enumerate(outs):
        for side in (0, 1):
            source = ins[side].at[:, index] if split else ins[2 * index + side]
            place = pl.ds(side * source.shape[0], source.shape[0])
            copies.append(pltpu.make_async_copy(source, out.at[place], sems.at[index, side]))
    for copy in copies:
        copy.start()
    for copy in copies:
        copy.wait()


def join_whole_kernel(first_ref, second_ref, out_ref, sems):
    copies = [
        pltpu.make_async_copy(
            ref, out_ref.at[pl.ds(side * ref.shape[0], ref.shape[0])], sems.at[0, side]
        )
        for side, ref in enumerate((first_ref, second_ref))
    ]
    for copy in copies:
        copy.start()
    for copy in copies:
        copy.wait()


def join_blocks(pairs, after=(), split=False):
    operands = [item for pair in pairs for item in pair]
    if split:
        lead, _, *rest = operands[0].shape
        shapes = [(2 * lead, *rest)] * 2
    else:
        shapes = [(2 * pair[0].shape[0], *pair[0].shape[1:]) for pair in pairs]
    shapes = [jax.ShapeDtypeStruct(shape, jnp.bfloat16) for shape in shapes]
    return ordered_call(
        join_whole_kernel if len(shapes) == 1 else functools.partial(join_kernel, split),
        operands,
        [ANYWHERE] * len(operands),
        shapes,
        [whole(shape) for shape in shapes],
        after,
        scratch=[pltpu.SemaphoreType.DMA((2, 2))],
        cost=(0, 4 * sum(shape.size for shape in shapes), 0),
        name="join_blocks",
        room=16,
    )


class Gather:
    def __init__(self, values):
        self.depth = lax.axis_size("dp").bit_length() - 1
        self.block = values.reshape(1, 2, -1, 128)
        self.slots = [0]
        self.position = self.depth - 1
        self.came = swap(self.block, 1 << self.position)

    def _grow(self, slots, position):
        return slots + [slot ^ (1 << position) for slot in slots]

    def outer(self, after=()):
        self.slots = self._grow(self.slots, self.position)
        if self.position > 2:
            self.block, token = join_blocks([(self.block, self.came)], after)
            self.position -= 1
            self.came = swap(self.block, 1 << self.position)
            return token
        *self.parts, token = join_blocks([(self.block, self.came)], after, split=True)
        self.came = [swap(self.parts[0], 2), swap(self.parts[1], 1)]
        return token

    def inner(self, after=()):
        *self.parts, token = join_blocks(list(zip(self.parts, self.came)), after)
        self.came = [swap(self.parts[0], 1), swap(self.parts[1], 2)]
        return token

    def others(self):
        count = lax.axis_size("dp")
        self.parts_other = [swap(part, count) for part in self.parts]

    def result(self, after=()):
        count = lax.axis_size("dp")
        came = [tie(item, *after) for item in self.came] if after else self.came
        came_other = [swap(item, count) for item in came]
        names = [self._grow(self.slots, 1), self._grow(self.slots, 0)]
        lists = []
        for name, bit in zip(names, (1, 2)):
            lists += [name, [slot ^ bit for slot in name]]
        arrays = [self.parts[0], came[0], self.parts[1], came[1]]
        others = [self.parts_other[0], came_other[0], self.parts_other[1], came_other[1]]
        return arrays, others, lists


def place(target, source_ref, rows, offset):
    row, lane = divmod(offset, 128)
    if lane == 0:
        target[row : row + rows, :] = source_ref[0:rows, :]
        return
    rolled = pltpu.roll(source_ref[0:rows, :], lane, 1)
    lanes = lax.broadcasted_iota(jnp.int32, (rows, 128), 1)
    target[row : row + rows, :] = jnp.where(lanes >= lane, rolled, target[row : row + rows, :])
    target[row + 1 : row + 1 + rows, :] = jnp.where(
        lanes < lane, rolled, target[row + 1 : row + 1 + rows, :]
    )


def place_line(target, line, offset):
    start, width = 0, line.shape[1]
    while start < width:
        row, lane = divmod(offset + start, 128)
        step = min(128 - lane, width - start)
        target[row : row + 1, lane : lane + step] = line[:, start : start + step]
        start += step


def spread(target, block, first, stride):
    for piece in range(block.shape[1] // 128):
        target[pl.ds(first + piece, block.shape[0], stride=stride), :] = block[
            :, piece * 128 : (piece + 1) * 128
        ]


def adam_rows(grads_ref, current_ref, first_ref, second_ref, outs, fresh_ref, start, width, plain):
    sum_out, first_out, second_out = outs

    def update(grads, current, old_first, old_second, position):
        new_first = beta_one * old_first + (1.0 - beta_one) * grads
        new_second = beta_two * old_second + (1.0 - beta_two) * grads * grads
        ratio = (
            new_first
            / (1.0 - beta_one**step_count)
            / (jnp.sqrt(new_second / (1.0 - beta_two**step_count)) + adam_eps)
        )
        decays = jnp.ones(grads.shape, jnp.bool_)
        for low, high in plain:
            decays = decays & ((position < low) | (position >= high))
        decay = jnp.where(decays, decay_rate, 0.0)
        fresh = current - learn_rate * (ratio + decay * current)
        return new_first, new_second, fresh

    group = 64
    loops = width // (group * 128)

    @pl.loop(0, loops)
    def _(index):
        rows = pl.ds(pl.multiple_of(index * group, group), group)
        begin = pl.multiple_of(index * (group * 128), 1024)
        there = pl.ds(pl.multiple_of(start + begin, 128), group * 128)
        here = pl.ds(begin, group * 128)
        shape = (group, 128)
        position = (
            begin
            + lax.broadcasted_iota(jnp.int32, shape, 0) * 128
            + lax.broadcasted_iota(jnp.int32, shape, 1)
        )
        grads = grads_ref[rows, :]
        new_first, new_second, fresh = update(
            grads,
            current_ref[rows, :],
            first_ref[0:1, there].reshape(shape),
            second_ref[0:1, there].reshape(shape),
            position,
        )
        sum_out[0:1, here] = grads.reshape(1, group * 128)
        first_out[0:1, here] = new_first.reshape(1, group * 128)
        second_out[0:1, here] = new_second.reshape(1, group * 128)
        fresh_ref[rows, :] = fresh

    begin = loops * group * 128
    while begin < width:
        size = min(128, width - begin)
        row = begin // 128
        grads = grads_ref[row : row + 1, 0:size]
        position = begin + lax.broadcasted_iota(jnp.int32, (1, size), 1)
        new_first, new_second, fresh = update(
            grads,
            current_ref[row : row + 1, 0:size],
            first_ref[0:1, start + begin : start + begin + size],
            second_ref[0:1, start + begin : start + begin + size],
            position,
        )
        sum_out[0:1, begin : begin + size] = grads
        first_out[0:1, begin : begin + size] = new_first
        second_out[0:1, begin : begin + size] = new_second
        fresh_ref[row : row + 1, 0:size] = fresh
        begin += size


def own_lines(target, info, count, lines, part_widths, offsets):
    for dest in range(count):

        @pl.when(info[1] == dest)
        def _():
            for line, width, offset in zip(lines, part_widths, offsets):
                place_line(
                    target,
                    line[:, dest * width : (dest + 1) * width].astype(jnp.float32),
                    offset,
                )


def send_half(info, fresh_ref, fresh_out):
    rows = fresh_out.shape[0]
    fresh_out[...] = fresh_ref[pl.ds(pl.multiple_of(info[0] * rows, 16), rows), :].astype(
        jnp.bfloat16
    )


def mlp_update_kernel(
    start,
    info,
    mine_ref,
    other_ref,
    fc1_ref,
    fc1_bias_ref,
    fc2_ref,
    fc2_bias_ref,
    first_ref,
    second_ref,
    sum_out,
    first_out,
    second_out,
    fresh_out,
    grads_ref,
    current_ref,
    fresh_ref,
    line_ref,
):
    rows = fc1_ref.shape[0]
    count = D // rows
    tiles = D // 128
    large = rows * 4 * D
    second = large + 4 * rows
    end = second + large

    def fill(fc1_half, fc2_half):
        for part in range(4):
            spread(
                grads_ref, fc1_half[part * rows : (part + 1) * rows, :], part * tiles, 4 * tiles
            )
        spread(line_ref, fc2_half[0 : 4 * rows, :], 0, tiles)
        place(grads_ref, line_ref, large // 128, second)
        place_line(grads_ref, fc1_half[4 * rows : 4 * rows + 1, 0 : 4 * rows], large)
        place_line(grads_ref, fc2_half[4 * rows : 4 * rows + 1, 0:rows], end)

    @pl.when(info[0] == 0)
    def _():
        fill(mine_ref, other_ref)

    @pl.when(info[0] != 0)
    def _():
        fill(other_ref, mine_ref)

    spread(current_ref, fc1_ref[...].astype(jnp.float32), 0, 4 * tiles)
    spread(line_ref, fc2_ref[...].astype(jnp.float32), 0, tiles)
    place(current_ref, line_ref, large // 128, second)
    own_lines(
        current_ref,
        info,
        count,
        (fc1_bias_ref[...], fc2_bias_ref[...]),
        (4 * rows, rows),
        (large, end),
    )
    adam_rows(
        grads_ref,
        current_ref,
        first_ref,
        second_ref,
        (sum_out, first_out, second_out),
        fresh_ref,
        start,
        end + rows,
        ((large, second), (end, end + rows)),
    )
    send_half(info, fresh_ref, fresh_out)


def rest_update_kernel(
    info,
    mine_ref,
    other_ref,
    qkv_ref,
    proj_ref,
    gain_one_ref,
    shift_one_ref,
    qkv_bias_ref,
    proj_bias_ref,
    gain_two_ref,
    shift_two_ref,
    first_ref,
    second_ref,
    sum_out,
    first_out,
    second_out,
    fresh_out,
    grads_ref,
    current_ref,
    fresh_ref,
    line_ref,
):
    rows = qkv_ref.shape[0]
    count = D // rows
    tiles = D // 128
    qkv_at = 2 * rows
    qkv_bias_at = qkv_at + 3 * rows * D
    proj_at = qkv_bias_at + 3 * rows
    proj_bias_at = proj_at + rows * D
    end = proj_bias_at + 3 * rows
    small = (0, rows, qkv_bias_at, proj_bias_at, proj_bias_at + rows, proj_bias_at + 2 * rows)
    widths = (rows, rows, 3 * rows, rows, rows, rows)

    def fill(first_half, second_half):
        spread(line_ref, first_half[0:rows, :], 0, 3 * tiles)
        spread(line_ref, first_half[rows : 2 * rows, :], tiles, 3 * tiles)
        spread(line_ref, second_half[0:rows, :], 2 * tiles, 3 * tiles)
        place(grads_ref, line_ref, 3 * rows * tiles, qkv_at)
        spread(line_ref, second_half[rows : 2 * rows, :], 0, tiles)
        place(grads_ref, line_ref, rows * tiles, proj_at)
        begin = 0
        for width, offset in zip(widths, small):
            place_line(
                grads_ref, first_half[2 * rows : 2 * rows + 1, begin : begin + width], offset
            )
            begin += width

    @pl.when(info[0] == 0)
    def _():
        fill(mine_ref, other_ref)

    @pl.when(info[0] != 0)
    def _():
        fill(other_ref, mine_ref)

    spread(line_ref, qkv_ref[...].astype(jnp.float32), 0, 3 * tiles)
    place(current_ref, line_ref, 3 * rows * tiles, qkv_at)
    spread(line_ref, proj_ref[...].astype(jnp.float32), 0, tiles)
    place(current_ref, line_ref, rows * tiles, proj_at)
    lines = (
        gain_one_ref[...],
        shift_one_ref[...],
        qkv_bias_ref[...],
        proj_bias_ref[...],
        gain_two_ref[...],
        shift_two_ref[...],
    )
    own_lines(current_ref, info, count, lines, widths, small)
    adam_rows(
        grads_ref,
        current_ref,
        first_ref,
        second_ref,
        (sum_out, first_out, second_out),
        fresh_ref,
        0,
        end,
        ((0, qkv_at), (qkv_bias_at, proj_at), (proj_bias_at, end)),
    )
    send_half(info, fresh_ref, fresh_out)


def update_call(
    kernel, name, info, mine, other, matrices, small, moments, width, order, after=()
):
    count = lax.axis_size("dp")
    half_rows = -(-width // 4096) * 16
    tall = 2 * half_rows

    operands = {("half", 0): (mine, whole(mine)), ("half", 1): (other, whole(other))}
    for index, item in enumerate(matrices):
        operands["matrix", index] = (
            item,
            pl.BlockSpec((item.shape[0] // count, item.shape[1]), lambda i, info: (info[1], 0)),
        )
    for index, item in enumerate(small[1:]):
        operands["small", index] = (small[0], vector_spec(item))
    for index, item in enumerate(moments):
        operands["moment", index] = (item, whole(item))
    chosen = [operands[key] for key in order]
    line = jax.ShapeDtypeStruct((1, width), jnp.float32)
    half_out = jax.ShapeDtypeStruct((half_rows, 128), jnp.bfloat16)
    return ordered_call(
        kernel,
        [item for item, _ in chosen],
        [spec for _, spec in chosen],
        [line, line, line, half_out],
        [whole(line)] * 3 + [whole(half_out)],
        after,
        scalars=(info,),
        scratch=[pltpu.VMEM((tall + 8, 128), jnp.float32) for _ in range(4)],
        cost=(2**20, 24 * 2**20, 0),
        name=name,
        room=36,
        far=(0, 1, 2),
    )


def assemble_kernel(lists, start, width, extra, info, *refs):
    each = 1 if lists is None else 4
    mine, other = refs[0:each], refs[each : 2 * each]
    refs = refs[2 * each + extra :]
    out_ref, refs = refs[0], refs[1:]
    tail = width % 128
    if tail:
        tail_ref, refs = refs[0], refs[1:]
    held, wide, in_sems, out_sems = refs
    count, rows = held.shape[1], held.shape[2]

    def pieces(segment):
        part = segment % 2
        if lists is None:
            whole_part = pl.ds(part * rows, rows)
            return [(lambda refs: refs[0].at[:, whole_part], held.at[segment], 0)]
        found = []
        for index in range(count):
            array, slot = divmod(index, count // 2)
            array += 2 * part
            target = held.at[segment, lists[array][slot] ^ info[1]]
            found.append(
                (lambda refs, array=array, slot=slot: refs[array].at[slot], target, index)
            )
        return found

    def arrivals(segment, begin):
        for source, target, index in pieces(segment):

            def copy(refs):
                return pltpu.make_async_copy(source(refs), target, in_sems.at[segment, index])

            if begin:

                @pl.when(info[0] == segment // 2)
                def _():
                    copy(mine).start()

                @pl.when(info[0] != segment // 2)
                def _():
                    copy(other).start()

            else:
                copy(mine).wait()

    def departure(segment):
        length = min(rows * 128, width - tail - segment * rows * 128)
        return pltpu.make_async_copy(
            wide.at[segment % 2, :, pl.ds(0, length)],
            out_ref.at[:, pl.ds(start + segment * rows * 128, length)],
            out_sems.at[segment],
        )

    for segment in range(4):
        arrivals(segment, True)
    for segment in range(4):
        arrivals(segment, False)
        if segment >= 2:
            departure(segment - 2).wait()
        wide[segment % 2] = held[segment].reshape(count, rows * 128)
        departure(segment).start()
        if segment == 3 and tail:
            at = width - tail - segment * rows * 128
            tail_ref[...] = wide[segment % 2, :, at : at + 128]
    departure(2).wait()
    departure(3).wait()


def fill_tail_kernel(source_ref, target_ref, out_ref):
    out_ref[...] = source_ref[...]


def fill_tail(target, source, token):
    last = target.shape[1] // 128
    return ordered_call(
        fill_tail_kernel,
        (source, target),
        [whole(source), ANYWHERE],
        [jax.ShapeDtypeStruct(target.shape, target.dtype)],
        [pl.BlockSpec(source.shape, lambda *_: (0, last))],
        (token,),
        aliases={1: 0},
        name="fill_tail",
        room=4,
    )


def assemble(info, arrays, others, lists, start, width, total, target=None, after=()):
    count = lax.axis_size("dp")
    rows = arrays[0].shape[1] // (2 if lists is None else 1)
    aliased = 0 if target is None else 1
    tail = width % 128
    out_shape = [jax.ShapeDtypeStruct((count, total), jnp.bfloat16)]
    out_specs = [ANYWHERE]
    if tail:
        out_shape.append(jax.ShapeDtypeStruct((count, 128), jnp.bfloat16))
        out_specs.append(whole(out_shape[-1]))
    operands = (*arrays, *others, *(() if target is None else (target,)))
    *outs, token = ordered_call(
        functools.partial(assemble_kernel, lists, start, width, aliased),
        operands,
        [ANYWHERE] * len(operands),
        out_shape,
        out_specs,
        after,
        scalars=(info,),
        scratch=[
            pltpu.VMEM((4, count, rows, 128), jnp.bfloat16),
            pltpu.VMEM((2, count, rows * 128), jnp.bfloat16),
            pltpu.SemaphoreType.DMA((4, count)),
            pltpu.SemaphoreType.DMA((4,)),
        ],
        cost=(2**20, 4 * count * width, 0),
        aliases={len(operands): 0} if aliased else {},
        name="assemble",
        room=28 if target is None else 56,
    )
    if tail:
        return fill_tail(*outs, token)
    return outs[0], token


def join_lines_kernel(*refs):
    for index in range(3):
        low, high, out = refs[index], refs[3 + index], refs[6 + index]
        width = low.shape[1]
        out[0:1, 0:width] = low[...]
        out[0:1, width:] = high[...]


def join_lines(lows, highs, after=()):
    operands = (*lows, *highs)
    line = jax.ShapeDtypeStruct((1, lows[0].shape[1] + highs[0].shape[1]), jnp.float32)
    return ordered_call(
        join_lines_kernel,
        operands,
        [whole(item) for item in operands],
        [line] * 3,
        [whole(line)] * 3,
        after,
        cost=(0, 24 * line.size, 0),
        name="join_lines",
        room=56,
    )


MLP_ORDER = (
    ("half", 0),
    ("half", 1),
    ("matrix", 0),
    ("small", 0),
    ("matrix", 1),
    ("small", 1),
    ("moment", 0),
    ("moment", 1),
)
REST_ORDER = (
    (("half", 0), ("half", 1), ("matrix", 0), ("matrix", 1))
    + tuple(("small", index) for index in range(6))
    + (("moment", 0), ("moment", 1))
)


ROWS = 256


def norm_rows(values):
    center = values - jnp.mean(values, axis=-1, keepdims=True)
    spread = lax.rsqrt(jnp.mean(center * center, axis=-1, keepdims=True) + norm_eps)
    return center * spread, spread


def norm_back(grads, gain, hat, spread):
    scaled = grads * gain
    inner = scaled - jnp.mean(scaled, axis=-1, keepdims=True)
    inner = inner - hat * jnp.mean(scaled * hat, axis=-1, keepdims=True)
    return (
        spread * inner,
        jnp.sum(grads * hat, axis=0, keepdims=True),
        jnp.sum(grads, axis=0, keepdims=True),
    )


def add_lines(refs, lines):
    first = pl.program_id(0) == 0

    @pl.when(first)
    def _():
        for ref, line in zip(refs, lines):
            ref[...] = line

    @pl.when(jnp.logical_not(first))
    def _():
        for ref, line in zip(refs, lines):
            ref[...] += line


def rows_of(item):
    return pl.BlockSpec((ROWS, item.shape[1]), lambda i, *_: (i, 0))


def first_part_kernel(
    pad_ref,
    tokens_ref,
    grad_ref,
    gain_ref,
    bias_ref,
    weight_ref,
    shift_ref,
    normed_out,
    out_ref,
    grad_out,
):
    hat, _ = norm_rows(tokens_ref[...].astype(jnp.float32))
    normed = (
        hat * gain_ref[...].astype(jnp.float32) + bias_ref[...].astype(jnp.float32)
    ).astype(jnp.bfloat16)
    normed_out[...] = normed
    out_ref[...] = (
        dot_nn(normed, weight_ref[...]) + shift_ref[...].astype(jnp.float32)
    ).astype(jnp.bfloat16)
    row = pl.program_id(0) * ROWS + lax.broadcasted_iota(jnp.int32, grad_ref.shape, 0)
    grads = grad_ref[...].astype(jnp.float32)
    grad_out[...] = jnp.where(row < pad_ref[0], grads, 0.0).astype(jnp.bfloat16)


def first_part(tokens, out_grad, vectors, weight, pad_start):
    length = tokens.shape[0]
    outs = [halves(length, D), halves(length, weight.shape[1]), halves(length, D)]
    return ordered_call(
        first_part_kernel,
        (tokens, out_grad, vectors, vectors, weight, vectors),
        [
            rows_of(tokens),
            rows_of(out_grad),
            vector_spec("gain_one"),
            vector_spec("shift_one"),
            whole(weight),
            vector_spec("qkv_bias"),
        ],
        outs,
        [rows_of(item) for item in outs],
        grid=(length // ROWS,),
        scalars=(pad_start,),
        cost=(2 * length * weight.size, 8 * 2**20, 0),
        name="norm_qkv",
        room=56,
        far=(0, 1, 2),
    )


def second_part_kernel(
    tokens_ref, context_ref, weight_ref, shift_ref, gain_ref, bias_ref, middle_out, normed_out
):
    middle = tokens_ref[...].astype(jnp.float32) + (
        dot_nn(context_ref[...], weight_ref[...]) + shift_ref[...].astype(jnp.float32)
    )
    middle_out[...] = middle
    hat, _ = norm_rows(middle)
    normed_out[...] = (
        hat * gain_ref[...].astype(jnp.float32) + bias_ref[...].astype(jnp.float32)
    ).astype(jnp.bfloat16)


def second_part(tokens, context, weight, vectors, after=()):
    length = tokens.shape[0]
    outs = [floats(length, D), halves(length, D)]
    return ordered_call(
        second_part_kernel,
        (tokens, context, weight, vectors, vectors, vectors),
        [
            rows_of(tokens),
            rows_of(context),
            whole(weight),
            vector_spec("proj_bias"),
            vector_spec("gain_two"),
            vector_spec("shift_two"),
        ],
        outs,
        [rows_of(item) for item in outs],
        after,
        grid=(length // ROWS,),
        cost=(2 * length * weight.size, 8 * 2**20, 0),
        name="proj_norm",
        room=12,
        far=(0, 1),
    )


def mlp_part_kernel(
    normed_ref, grad_ref, first_ref, shift_ref, second_ref, active_out, hidden_grad_out
):
    root = 0.7978845608028654
    for begin in range(0, normed_ref.shape[0], ROWS):
        rows = slice(begin, begin + ROWS)
        hidden = dot_nn(normed_ref[rows, :], first_ref[...]) + shift_ref[...].astype(jnp.float32)
        grad_active = dot_nt(grad_ref[rows, :], second_ref[...])
        square = hidden * hidden
        slope = jnp.tanh(hidden * (root + (root * 0.044715) * square))
        half = 0.5 + 0.5 * slope
        active_out[rows, :] = (hidden * half).astype(jnp.bfloat16)
        rise = half + (0.5 * hidden) * (1.0 - slope * slope) * (
            root + (3.0 * root * 0.044715) * square
        )
        hidden_grad_out[rows, :] = (grad_active * rise).astype(jnp.bfloat16)


def mlp_part(normed, grad_out, first, vectors, second, after=()):
    length, width = normed.shape[0], first.shape[1]
    step = D
    columns = pl.BlockSpec((length, step), lambda i: (0, i))
    outs = [halves(length, width)] * 2
    return ordered_call(
        mlp_part_kernel,
        (normed, grad_out, first, vectors, second),
        [
            whole(normed),
            whole(grad_out),
            pl.BlockSpec((D, step), lambda i: (0, i)),
            pl.BlockSpec((1, step), lambda i: (0, i)),
            pl.BlockSpec((step, D), lambda i: (i, 0)),
        ],
        outs,
        [columns, columns],
        after,
        grid=(width // step,),
        cost=(4 * length * D * width, 24 * 2**20, length * width),
        name="mlp_part",
        room=30,
        far=(0, 1),
    )


def middle_back_kernel(
    hidden_grad_ref,
    first_ref,
    middle_ref,
    gain_ref,
    grad_out_ref,
    proj_ref,
    middle_grad_out,
    branch_out,
    context_grad_out,
    gain_sum,
    bias_sum,
    proj_bias_sum,
):
    grads = dot_nt(hidden_grad_ref[...], first_ref[...])
    hat, spread = norm_rows(middle_ref[...])
    back, gain_line, bias_line = norm_back(
        grads, gain_ref[...].astype(jnp.float32), hat, spread
    )
    middle_grad = grad_out_ref[...].astype(jnp.float32) + back
    middle_grad_out[...] = middle_grad
    branch = middle_grad.astype(jnp.bfloat16)
    branch_out[...] = branch
    context_grad_out[...] = dot_nt(branch, proj_ref[...]).astype(jnp.bfloat16)
    proj_line = jnp.sum(branch.astype(jnp.float32), axis=0, keepdims=True)
    add_lines((gain_sum, bias_sum, proj_bias_sum), (gain_line, bias_line, proj_line))


def middle_back(hidden_grad, first, middle, vectors, grad_out, proj, after=()):
    length = middle.shape[0]
    line = floats(1, D)
    outs = [floats(length, D), halves(length, D), halves(length, D)]
    return ordered_call(
        middle_back_kernel,
        (hidden_grad, first, middle, vectors, grad_out, proj),
        [
            rows_of(hidden_grad),
            whole(first),
            rows_of(middle),
            vector_spec("gain_two"),
            rows_of(grad_out),
            whole(proj),
        ],
        outs + [line] * 3,
        [rows_of(item) for item in outs] + [whole(line)] * 3,
        after,
        grid=(length // ROWS,),
        cost=(2 * length * (first.size + proj.size), 24 * 2**20, 0),
        name="middle_back",
        room=32,
        far=(0, 1, 2),
    )


def input_back_kernel(parts, tokens_ref, gain_ref, weight_ref, middle_grad_ref, *refs):
    pieces, (out_ref, gain_sum, bias_sum) = refs[: 3 * parts], refs[3 * parts :]
    joined = jnp.concatenate([piece[...] for piece in pieces], axis=1)
    grads = dot_nt(joined, weight_ref[...])
    hat, spread = norm_rows(tokens_ref[...].astype(jnp.float32))
    back, gain_line, bias_line = norm_back(
        grads, gain_ref[...].astype(jnp.float32), hat, spread
    )
    out_ref[...] = (middle_grad_ref[...] + back).astype(jnp.bfloat16)
    add_lines((gain_sum, bias_sum), (gain_line, bias_line))


def input_back(tokens, vectors, weight, middle_grad, pieces, after=()):
    length = tokens.shape[0]
    line = floats(1, D)
    out = halves(length, D)
    return ordered_call(
        functools.partial(input_back_kernel, len(pieces) // 3),
        (tokens, vectors, weight, middle_grad, *pieces),
        [rows_of(tokens), vector_spec("gain_one"), whole(weight), rows_of(middle_grad)]
        + [rows_of(item) for item in pieces],
        [out, line, line],
        [rows_of(out), whole(line), whole(line)],
        after,
        grid=(length // ROWS,),
        cost=(2 * length * weight.size, 16 * 2**20, 0),
        name="input_back",
        room=56,
    )


def block_out_kernel(active_ref, weight_ref, shift_ref, middle_ref, out_ref):
    out_ref[...] = (
        middle_ref[...]
        + (dot_nn(active_ref[...], weight_ref[...]) + shift_ref[...].astype(jnp.float32))
    ).astype(jnp.bfloat16)


def block_out_rows(active, weight, vectors, middle, after=()):
    length = middle.shape[0]
    out = halves(length, D)
    return ordered_call(
        block_out_kernel,
        (active, weight, vectors, middle),
        [rows_of(active), whole(weight), vector_spec("fc2_bias"), rows_of(middle)],
        [out],
        [rows_of(out)],
        after,
        grid=(length // ROWS,),
        cost=(2 * length * weight.size, 16 * 2**20, 0),
        name="block_out",
        room=50,
    )


def on_device(
    tokens,
    out_grad,
    image_counts,
    group_of_device,
    group_weight,
    norm1_gain,
    norm1_bias,
    qkv_weight,
    qkv_bias,
    proj_weight,
    proj_bias,
    norm2_gain,
    norm2_bias,
    fc1_weight,
    fc1_bias,
    fc2_weight,
    fc2_bias,
    first_moment,
    second_moment,
):
    count = lax.axis_size("dp")
    core = lax.axis_index("grp")
    own = lax.axis_index("dp")
    info = jnp.stack([core, own])
    pad_start = jnp.sum(image_counts[0], keepdims=True)
    vectors = join_vectors(
        fc1_bias,
        norm1_gain,
        norm1_bias,
        qkv_bias,
        proj_bias,
        norm2_gain,
        norm2_bias,
        fc2_bias,
    )
    member = (group_of_device[0] == lax.iota(jnp.int32, 128)).astype(jnp.float32)
    images = jnp.sum((image_counts[0] > 0).astype(jnp.float32))
    totals = jnp.broadcast_to(member * images, (8, 128))
    bits = iter([1 << place for place in range((2 * count).bit_length() - 1)])

    def count_on(totals, *after):
        return add_totals(totals, swap(totals, next(bits)), after)

    normed_one, projected, grad_out, token = first_part(
        tokens, out_grad, vectors, qkv_weight, pad_start
    )
    totals, token = count_on(totals, token)
    context, weights, scales, token = attn_forward(projected, image_counts, pad_start, (token,))
    totals, token = count_on(totals, token)
    middle, normed_two, token = second_part(tokens, context, proj_weight, vectors, (token,))
    totals, token = count_on(totals, token)
    active, grad_hidden, token = mlp_part(
        normed_two, grad_out, fc1_weight, vectors, fc2_weight, (token,)
    )
    totals, token = count_on(totals, token)
    for _ in range((2 * count).bit_length() - 5):
        totals, token = count_on(totals, token)
    share = jnp.sum(member[:NGROUPS] * group_weight.astype(jnp.float32))
    factor = (share / jnp.sum(member * totals[0])).reshape(1)

    mlp_make = functools.partial(
        mlp_grads,
        own=own,
        count=count,
        factor=factor,
        normed=normed_two,
        grad_hidden=grad_hidden,
        active=active,
        grad_out=grad_out,
    )
    sent, token = mlp_make(1 - core)
    came = swap(sent, count)
    kept, _ = mlp_make(core, after=(token,))
    mlp_steps = reduce_blocks(came, kept)
    next(mlp_steps)
    sending = mlp_steps.send(())
    middle_grad, branch, context_grad, gain_two_sum, shift_two_sum, proj_bias_sum, token = (
        middle_back(grad_hidden, fc1_weight, middle, vectors, grad_out, proj_weight, (sending,))
    )
    wide = D // 128
    (query_grad, key_grad, value_grad), token = attn_backward(
        projected, context, context_grad, weights, scales, 0, wide, (token,)
    )
    sending = mlp_steps.send((token,))
    input_grad, gain_one_sum, shift_one_sum, token = input_back(
        tokens,
        vectors,
        qkv_weight,
        middle_grad,
        (query_grad, key_grad, value_grad),
        (sending,),
    )
    sending = mlp_steps.send((token,))
    rest_make = functools.partial(
        rest_grads,
        own=own,
        count=count,
        factor=factor,
        normed=normed_one,
        context=context,
        query=(query_grad,),
        key=(key_grad,),
        value=(value_grad,),
        branch=branch,
        vectors=(gain_one_sum, shift_one_sum, proj_bias_sum, gain_two_sum, shift_two_sum),
    )
    rest_sent, rest_token = rest_make(1 - core, after=(sending,))
    rest_kept, rest_order = [], []

    def keep_rest(sending):
        kept, token = rest_make(core, after=(rest_token,) if sending is None else (sending,))
        rest_kept.append(kept)
        rest_order.append(rest_token if sending is None else sending)
        return token

    mlp_mine, token = finish(mlp_steps, [lambda sending: rest_token, keep_rest], sending)
    mlp_parts = (mlp_mine, swap(mlp_mine, count))
    came = swap(tie(rest_sent, *rest_order), count)
    moments = (first_moment, second_moment)
    total = first_moment.shape[1]
    rest_width = (3 * D * D + D * D + 3 * D + 5 * D) // count
    mlp_width = total - rest_width
    *mlp_lines, mlp_fresh, update_token = update_call(
        functools.partial(mlp_update_kernel, rest_width),
        "mlp_update",
        info,
        *mlp_parts,
        (fc1_weight, fc2_weight),
        (vectors, "fc1_bias", "fc2_bias"),
        moments,
        mlp_width,
        MLP_ORDER,
        (came,),
    )
    mlp_gathered = lax.all_gather(mlp_fresh, "dp")
    rest_steps = reduce_blocks(came, rest_kept[0])
    next(rest_steps)
    sending = rest_steps.send((update_token,))
    block_state = []

    def block_rows(sending):
        block_state.extend(
            block_out_rows(active, fc2_weight, vectors, middle, (sending,))
        )
        return block_state[-1]

    rest_mine, _ = finish(rest_steps, [block_rows], sending)
    block_out, _ = block_state
    rest_parts = (rest_mine, swap(rest_mine, count))
    *rest_lines, rest_fresh, token = update_call(
        rest_update_kernel,
        "rest_update",
        info,
        *rest_parts,
        (qkv_weight, proj_weight),
        (vectors, "gain_one", "shift_one", "qkv_bias", "proj_bias", "gain_two", "shift_two"),
        moments,
        rest_width,
        REST_ORDER,
    )
    rest_gather = Gather(rest_fresh)
    summed, new_first, new_second, token = join_lines(rest_lines, mlp_lines, (token,))
    while rest_gather.position > 2:
        token = rest_gather.outer((token,))
    mlp_gathered = tie(mlp_gathered, token)
    mlp_other = swap(mlp_gathered, count)
    token = rest_gather.outer((token,))
    new_weights, token = assemble(
        info,
        [mlp_gathered],
        [mlp_other],
        None,
        rest_width,
        mlp_width,
        total,
        after=(token,),
    )
    rest_gather.inner((token,))
    rest_gather.others()
    new_weights, _ = assemble(info, *rest_gather.result(), 0, rest_width, total, new_weights)
    summed_bias = mlp_lines[0][0, mlp_width - D // count :]
    return (block_out, input_grad, summed, new_weights, new_first, new_second, summed_bias)


def add_totals_kernel(first_ref, second_ref, out_ref):
    out_ref[...] = first_ref[...] + second_ref[...]


def add_totals(first, second, after=()):
    return ordered_call(
        add_totals_kernel,
        (first, second),
        [whole(first), whole(second)],
        [floats(*first.shape)],
        [whole(first)],
        after,
        name="add_totals",
        room=4,
    )


def device_factor(counts_row, group_of_device, group_weight):
    images = jnp.sum((counts_row > 0).astype(jnp.int32))
    member = (group_of_device[0] == lax.iota(jnp.int32, NGROUPS)).astype(jnp.int32)
    totals = member * images
    for position in range((lax.axis_size("grp") * lax.axis_size("dp")).bit_length() - 1):
        totals = totals + swap(totals, 1 << position)
    return jnp.sum(member * group_weight).astype(jnp.float32) / jnp.sum(member * totals).astype(
        jnp.float32
    )


def general_device(
    tokens,
    out_grad,
    image_counts,
    group_of_device,
    group_weight,
    norm1_gain,
    norm1_bias,
    qkv_weight,
    qkv_bias,
    proj_weight,
    proj_bias,
    norm2_gain,
    norm2_bias,
    fc1_weight,
    fc1_bias,
    fc2_weight,
    fc2_bias,
    first_moment,
    second_moment,
):
    length = tokens.shape[0]
    segment, valid_rows = segment_info(image_counts[0], length)
    factor = device_factor(image_counts[0], group_of_device, group_weight)
    inputs = tokens.astype(jnp.float32)
    normed_one, norm_one_back = jax.vjp(
        layer_norm, inputs, norm1_gain.astype(jnp.float32), norm1_bias.astype(jnp.float32)
    )
    normed_one_low = normed_one.astype(jnp.bfloat16)
    projected = (
        jnp.dot(normed_one_low, qkv_weight, preferred_element_type=jnp.float32)
        + qkv_bias.astype(jnp.float32)
    ).astype(jnp.bfloat16)
    pad_start = jnp.sum(image_counts[0], keepdims=True)
    context, weights, scales, _ = attn_forward(projected, image_counts, pad_start)
    middle = inputs + (
        jnp.dot(context, proj_weight, preferred_element_type=jnp.float32)
        + proj_bias.astype(jnp.float32)
    )
    normed_two, norm_two_back = jax.vjp(
        layer_norm, middle, norm2_gain.astype(jnp.float32), norm2_bias.astype(jnp.float32)
    )
    normed_two_low = normed_two.astype(jnp.bfloat16)
    hidden = jnp.dot(
        normed_two_low, fc1_weight, preferred_element_type=jnp.float32
    ) + fc1_bias.astype(jnp.float32)
    activated, gelu_back = jax.vjp(gelu_tanh, hidden)
    activated_low = activated.astype(jnp.bfloat16)
    block_out = (
        middle
        + (
            jnp.dot(activated_low, fc2_weight, preferred_element_type=jnp.float32)
            + fc2_bias.astype(jnp.float32)
        )
    ).astype(jnp.bfloat16)
    grad_out = out_grad.astype(jnp.float32) * valid_rows[:, None].astype(jnp.float32)
    grad_out_low = grad_out.astype(jnp.bfloat16)
    fc2_grad = contract_rows(activated_low, grad_out_low)
    fc2_bias_grad = jnp.sum(grad_out, axis=0)
    grad_hidden = gelu_back(contract_cols(grad_out_low, fc2_weight))[0].astype(jnp.bfloat16)
    fc1_grad = contract_rows(normed_two_low, grad_hidden)
    fc1_bias_grad = jnp.sum(grad_hidden.astype(jnp.float32), axis=0)
    grad_middle_norm, gain_two_grad, shift_two_grad = norm_two_back(
        contract_cols(grad_hidden, fc1_weight)
    )
    grad_middle = grad_out + grad_middle_norm
    grad_branch = grad_middle.astype(jnp.bfloat16)
    proj_grad = contract_rows(context, grad_branch)
    proj_bias_grad = jnp.sum(grad_branch.astype(jnp.float32), axis=0)
    grad_context = contract_cols(grad_branch, proj_weight).astype(jnp.bfloat16)
    (query_grad, key_grad, value_grad), _ = attn_backward(
        projected, context, grad_context, weights, scales, 0, D // 128
    )
    grad_projected = jnp.concatenate([query_grad, key_grad, value_grad], axis=1)
    qkv_grad = contract_rows(normed_one_low, grad_projected)
    qkv_bias_grad = jnp.sum(grad_projected.astype(jnp.float32), axis=0)
    grad_input_norm, gain_one_grad, shift_one_grad = norm_one_back(
        contract_cols(grad_projected, qkv_weight)
    )
    input_grad = (grad_middle + grad_input_norm).astype(jnp.bfloat16)
    moments = (first_moment, second_moment)
    mlp_summed, rest_summed = exchange_grads(
        (gain_one_grad, shift_one_grad, qkv_grad, qkv_bias_grad, proj_grad, proj_bias_grad),
        (gain_two_grad, shift_two_grad, fc1_grad, fc1_bias_grad, fc2_grad, fc2_bias_grad),
        factor,
    )
    row_count = lax.axis_size("dp")
    own_index = lax.axis_index("dp")
    weight_list = (
        norm1_gain,
        norm1_bias,
        qkv_weight,
        qkv_bias,
        proj_weight,
        proj_bias,
        norm2_gain,
        norm2_bias,
        fc1_weight,
        fc1_bias,
        fc2_weight,
        fc2_bias,
    )
    own_weights = [
        lax.dynamic_slice_in_dim(item.reshape(row_count, -1), own_index, 1, 0)[0]
        for item in weight_list
    ]
    rows = D // row_count
    fc1_sum = mlp_summed[0].reshape(4, rows, D).transpose(1, 0, 2).reshape(-1)
    fc2_sum = mlp_summed[1].reshape(-1)
    qkv_sum = jnp.concatenate(
        [rest_summed[0, :rows], rest_summed[0, rows : 2 * rows], rest_summed[1, :rows]], axis=1
    ).reshape(-1)
    proj_sum = rest_summed[1, rows : 2 * rows].reshape(-1)
    small = rest_summed[0, 2 * rows]
    widths = [item.size // row_count for item in weight_list]
    small_parts = {}
    start = 0
    for index, flag in enumerate(decay_flags):
        if flag == 0.0:
            small_parts[index] = small[start : start + widths[index]]
            start += widths[index]
    large_parts = {2: qkv_sum, 4: proj_sum, 8: fc1_sum, 10: fc2_sum}
    pieces = [
        small_parts[index] if index in small_parts else large_parts[index] for index in range(12)
    ]
    split = sum(widths[:8])
    grads_out, first_out, second_out, fresh = [], [], [], []
    for lead, tail, begin, end in ((8, 12, split, sum(widths)), (0, 8, 0, split)):
        summed_part = jnp.concatenate(pieces[lead:tail])
        current = jnp.concatenate(own_weights[lead:tail]).astype(jnp.float32)
        decay = jnp.concatenate(
            [
                jnp.full((width,), flag, jnp.float32)
                for width, flag in zip(widths[lead:tail], decay_flags[lead:tail])
            ]
        )
        new_first = beta_one * moments[0][0, begin:end] + (1.0 - beta_one) * summed_part
        new_second = (
            beta_two * moments[1][0, begin:end] + (1.0 - beta_two) * summed_part * summed_part
        )
        ratio = (
            new_first
            / (1.0 - beta_one**step_count)
            / (jnp.sqrt(new_second / (1.0 - beta_two**step_count)) + adam_eps)
        )
        fresh_low = (current - learn_rate * (ratio + decay_rate * decay * current)).astype(
            jnp.bfloat16
        )
        grads_out.insert(0, summed_part)
        first_out.insert(0, new_first)
        second_out.insert(0, new_second)
        fresh.insert(0, gather_rows(fresh_low))
    summed = jnp.concatenate(grads_out)[None]
    new_first = jnp.concatenate(first_out)[None]
    new_second = jnp.concatenate(second_out)[None]
    new_weights = jnp.concatenate(fresh, axis=1)
    summed_bias = pieces[11]
    return (block_out, input_grad, summed, new_weights, new_first, new_second, summed_bias)


def bit_of(position):
    return (lax.axis_index("dp") >> position) & 1


def halve(values, position, positions):
    axis = positions.index(position)
    own = bit_of(position)
    sent = lax.dynamic_index_in_dim(values, 1 - own, axis, keepdims=False)
    kept = lax.dynamic_index_in_dim(values, own, axis, keepdims=False)
    return kept, swap(sent, 1 << position), [p for p in positions if p != position]


def reduce_rows(values):
    count = lax.axis_size("dp")
    grp = lax.axis_index("grp")
    kept = lax.dynamic_index_in_dim(values, grp, 0, keepdims=False)
    came = swap(lax.dynamic_index_in_dim(values, 1 - grp, 0, keepdims=False), count)
    kept = add_low(kept, came)
    depth = count.bit_length() - 1
    positions = list(range(depth))[::-1]
    rows = kept.shape[1]
    parts = [kept[:, : rows // 2], kept[:, rows // 2 :]]
    left = [positions, positions]
    parts = [part.reshape((2,) * depth + part.shape[1:]) for part in parts]
    for order in ((0, 1), (1, 0)):
        for index in (0, 1):
            part, came, left[index] = halve(parts[index], order[index], left[index])
            parts[index] = add_low(part, came)
    whole = jnp.concatenate(parts, axis=depth - 2)
    rest = left[0]
    for position in range(2, depth):
        part, came, rest = halve(whole, position, rest)
        if rest:
            whole = add_low(part, came)
        else:
            whole = part.astype(jnp.float32) + came.astype(jnp.float32)
    other = swap(whole, count)
    return jnp.where(grp == 0, jnp.stack([whole, other]), jnp.stack([other, whole]))


def join(own, came, bit):
    return jnp.where(bit == 0, jnp.stack([own, came]), jnp.stack([came, own]))


def gather_rows(values):
    count = lax.axis_size("dp")
    depth = count.bit_length() - 1
    grp = lax.axis_index("grp")
    width = values.shape[0]
    padded = -(-width // 4096) * 4096
    halves = jnp.pad(values, (0, padded - width)).reshape(2, 2, padded // 512, 128)
    own = lax.dynamic_index_in_dim(halves, grp, 0, keepdims=False)
    for position in range(2, depth)[::-1]:
        own = join(own, swap(own, 1 << position), bit_of(position))
    lead = own.ndim - 3
    parts = [lax.index_in_dim(own, i, lead, keepdims=False) for i in (0, 1)]
    for order in ((1, 0), (0, 1)):
        for index in (0, 1):
            position = order[index]
            parts[index] = join(
                parts[index], swap(parts[index], 1 << position), bit_of(position)
            )
    parts[1] = jnp.swapaxes(parts[1], 0, 1)
    full = jnp.stack(parts, axis=depth)
    full = full.transpose(tuple(range(depth))[::-1] + tuple(range(depth, full.ndim)))
    full = full.reshape((count,) + full.shape[depth:])
    other = swap(full, count)
    whole = jnp.where(
        grp == 0, jnp.stack([full, other], axis=1), jnp.stack([other, full], axis=1)
    )
    return whole.reshape(count, padded)[:, :width]


def exchange_grads(front, back, factor):
    gain_one, shift_one, qkv, qkv_bias, proj, proj_bias = front
    gain_two, shift_two, fc1, fc1_bias, fc2, fc2_bias = back
    count = lax.axis_size("dp")
    rows = D // count
    fc1_blocks = fc1.reshape(count, rows, 4, D).transpose(0, 2, 1, 3).reshape(count, 4 * rows, D)
    fc2_blocks = fc2.reshape(count, 4 * rows, D)
    mlp = (jnp.stack([fc1_blocks, fc2_blocks]) * factor).astype(jnp.bfloat16)
    small = jnp.concatenate(
        [
            item.reshape(count, -1)
            for item in (
                gain_one,
                shift_one,
                qkv_bias,
                proj_bias,
                gain_two,
                shift_two,
                fc1_bias,
                fc2_bias,
            )
        ],
        axis=1,
    )
    small = jnp.pad(small, ((0, 0), (0, D - small.shape[1])))[:, None]
    small = jnp.pad(small, ((0, 0), (0, 7), (0, 0)))
    qkv_blocks = qkv.reshape(count, rows, 3, D)
    first_half = jnp.concatenate([qkv_blocks[:, :, 0], qkv_blocks[:, :, 1], small], axis=1)
    second_half = jnp.concatenate(
        [qkv_blocks[:, :, 2], proj.reshape(count, rows, D), jnp.zeros_like(small)], axis=1
    )
    rest = (jnp.stack([first_half, second_half]) * factor).astype(jnp.bfloat16)
    return reduce_rows(mlp), reduce_rows(rest)


def solution(mesh):
    in_specs = (
        P(("grp", "dp"), None),
        P(("grp", "dp"), None),
        P(("grp", "dp"), None),
        P(("grp", "dp")),
        P(),
        P(),
        P(),
        P(),
        P(),
        P(),
        P(),
        P(),
        P(),
        P(),
        P(),
        P(),
        P(),
        P("dp", None),
        P("dp", None),
    )
    out_specs = (
        P(("grp", "dp"), None),
        P(("grp", "dp"), None),
        P("dp", None),
        P(),
        P("dp", None),
        P("dp", None),
        P("dp"),
    )
    rows = D // mesh.shape["dp"]
    return jax.shard_map(
        on_device if rows % 16 == 0 and mesh.shape["dp"] == 16 else general_device, mesh=mesh, in_specs=in_specs, out_specs=out_specs, check_vma=False
    )
```
